32 devices in a mesh: dp: 4 (over y, x), fsdp: 8 (over z, core).
Axes of the slice: x: 2, y: 2, z: 4, core: 2. Of those that a mesh axis runs over, the one named last changes fastest.
Arguments:
- text_ids: int32 [32, 128], P(('dp', 'fsdp')), may hold values from 0 to 15999
- text_segments: int32 [32, 128], P(('dp', 'fsdp')), may hold values from 0 to 1, never falling along the last dimension, each value on 1 to 127 neighbouring positions
- codes: int32 [64, 256], P(('dp', 'fsdp')), may hold values from 0 to 8191
- caption_of: int32 [64], P(('dp', 'fsdp')), may hold values from 0 to 1
- mix_in: float32 [3, 1024, 3072], P(None, ('dp', 'fsdp')), may hold values from -0.1875 to 0.1875
- mix_out: float32 [3, 1024, 1024], P(None, ('dp', 'fsdp')), may hold values from -1.5 to 1.5
- ffn_up: float32 [2, 1024, 4096], P(None, ('dp', 'fsdp')), may hold values from -0.1875 to 0.1875
- ffn_down: float32 [2, 4096, 1024], P(None, ('dp', 'fsdp')), may hold values from -0.09375 to 0.09375
- norm_gains: float32 [7, 1024], P(None, ('dp', 'fsdp')), may hold values from 0 to 3, as said below
- text_table: float32 [16000, 1024], P(('dp', 'fsdp')), may hold values from -0.1875 to 0.1875
- code_table: float32 [8192, 1024], P('fsdp', 'dp'), may hold values from -2 to 2
- mix_in_first: float32 [3, 1024, 3072], P(None, ('dp', 'fsdp')), may hold values from -3.8146973e-05 to 3.8146973e-05
- mix_out_first: float32 [3, 1024, 1024], P(None, ('dp', 'fsdp')), may hold values from -3.8146973e-05 to 3.8146973e-05
- ffn_up_first: float32 [2, 1024, 4096], P(None, ('dp', 'fsdp')), may hold values from -3.8146973e-05 to 3.8146973e-05
- ffn_down_first: float32 [2, 4096, 1024], P(None, ('dp', 'fsdp')), may hold values from -3.8146973e-05 to 3.8146973e-05
- gains_first: float32 [7, 1024], P(None, ('dp', 'fsdp')), may hold values from -0.00015258789 to 0.00015258789
- text_first: float32 [16000, 1024], P(('dp', 'fsdp')), may hold values from -3.8146973e-05 to 3.8146973e-05
- code_first: float32 [8192, 1024], P('fsdp', 'dp'), may hold values from -3.8146973e-05 to 3.8146973e-05
- mix_in_second: float32 [3, 1024, 3072], P(None, ('dp', 'fsdp')), may hold values from 7.3e-12 to 2.9e-11
- mix_out_second: float32 [3, 1024, 1024], P(None, ('dp', 'fsdp')), may hold values from 7.3e-12 to 2.9e-11
- ffn_up_second: float32 [2, 1024, 4096], P(None, ('dp', 'fsdp')), may hold values from 7.3e-12 to 2.9e-11
- ffn_down_second: float32 [2, 4096, 1024], P(None, ('dp', 'fsdp')), may hold values from 7.3e-12 to 2.9e-11
- gains_second: float32 [7, 1024], P(None, ('dp', 'fsdp')), may hold values from 1.2e-10 to 4.8e-10
- text_second: float32 [16000, 1024], P(('dp', 'fsdp')), may hold values from 7.3e-12 to 2.9e-11
- code_second: float32 [8192, 1024], P('fsdp', 'dp'), may hold values from 7.3e-12 to 2.9e-11
Outputs:
- loss_sum: float32 [], replicated
- grad_norm: float32 [], replicated
- mix_in_new: float32 [3, 1024, 3072], P(None, ('dp', 'fsdp'))
- mix_out_new: float32 [3, 1024, 1024], P(None, ('dp', 'fsdp'))
- ffn_up_new: float32 [2, 1024, 4096], P(None, ('dp', 'fsdp'))
- ffn_down_new: float32 [2, 4096, 1024], P(None, ('dp', 'fsdp'))
- gains_new: float32 [7, 1024], P(None, ('dp', 'fsdp'))
- text_new: float32 [16000, 1024], P(('dp', 'fsdp'))
- code_new: float32 [8192, 1024], P('fsdp', 'dp')
- mix_in_first_new: float32 [3, 1024, 3072], P(None, ('dp', 'fsdp'))
- mix_out_first_new: float32 [3, 1024, 1024], P(None, ('dp', 'fsdp'))
- ffn_up_first_new: float32 [2, 1024, 4096], P(None, ('dp', 'fsdp'))
- ffn_down_first_new: float32 [2, 4096, 1024], P(None, ('dp', 'fsdp'))
- gains_first_new: float32 [7, 1024], P(None, ('dp', 'fsdp'))
- text_first_new: float32 [16000, 1024], P(('dp', 'fsdp'))
- code_first_new: float32 [8192, 1024], P('fsdp', 'dp')
- mix_in_second_new: float32 [3, 1024, 3072], P(None, ('dp', 'fsdp'))
- mix_out_second_new: float32 [3, 1024, 1024], P(None, ('dp', 'fsdp'))
- ffn_up_second_new: float32 [2, 1024, 4096], P(None, ('dp', 'fsdp'))
- ffn_down_second_new: float32 [2, 4096, 1024], P(None, ('dp', 'fsdp'))
- gains_second_new: float32 [7, 1024], P(None, ('dp', 'fsdp'))
- text_second_new: float32 [16000, 1024], P(('dp', 'fsdp'))
- code_second_new: float32 [8192, 1024], P('fsdp', 'dp')
The draws below stay inside these ranges and needn't reach their ends.
Inputs may be any that keep to these rules, and one draw needn't show every extreme that they name: `text_segments`: in each row the segment numbers run 0 to 1 in order, every one present. Image i reads segment caption_of[i] of caption row i // 2. `norm_gains`: positive gains.
All inputs are finite; a program needn't handle non-finite values.
Results may differ from the reference program's by a relative error of at most 0.017.
Values may be sent and summed in bfloat16 or wider, within the bound.
A program may use at most 512 MiB of HBM per device.

```python
import math
from functools import partial
import jax
import jax.numpy as jnp
import numpy as np
from jax import lax

D = 1024
HEADS = 16
HEAD = 64
FF = 4096
VOCAB = 8192
TVOC = 16000
IMG_LEN = 256
TXT_LEN = 128
STEP = 5
IMGS_DEV = 2
CAPTION_ROWS = 32
IMAGES = 64


def draw_norm_gains(key, part):
    key = jax.random.fold_in(key, 11)
    fraction = jnp.arange(D, dtype=jnp.float32) / D
    rising = 0.5 + fraction
    jitter = jax.random.uniform(key, (7, D), jnp.float32, 0.8, 1.2)
    return rising[None, :] * jitter


def draw_code_table(key, part):
    key = jax.random.fold_in(key, 12)
    fraction = jnp.arange(VOCAB, dtype=jnp.float32)[:, None] / VOCAB
    values = jnp.clip(jax.random.normal(key, (VOCAB, D), jnp.float32), -4.0, 4.0)
    rising = 1.0 + 2.0 * fraction
    return values * rising / math.sqrt(D)


def touch_ends(entries, key, smallest, top_value):
    longest = entries.shape.index(max(entries.shape))
    spots = []
    for shift in (0, 1):
        where = [jax.random.randint(jax.random.fold_in(key, axis), (), 0, length) for axis, length in enumerate(entries.shape)]
        where[longest] = (where[longest] + shift) % entries.shape[longest]
        spots.append(tuple(where))
    return entries.at[spots[0]].set(smallest).at[spots[1]].set(top_value)


def level_of(key, shape, shards, low, top_value):
    def one(dim, blocks):
        steps = jax.random.uniform(jax.random.fold_in(jax.random.fold_in(key, 6), dim), (blocks,), jnp.float32, low / len(shards), top_value / len(shards))
        return jnp.repeat(jnp.exp(steps), shape[dim] // blocks).reshape((-1,) + (1,) * (len(shape) - dim - 1))

    factor_of = one(*shards[0])
    for cut in shards[1:]:
        factor_of = factor_of * one(*cut)
    return factor_of


def length_profile(number_of, total, most, lean):
    portions = [(1 << 20) // math.isqrt(rank ** lean) + 1 for rank in range(2, number_of + 1)]
    rest, counts = total - most - (number_of - 1), [1] * (number_of - 1)
    while rest > 0:
        candidates = [i for i in range(number_of - 1) if counts[i] < most]
        whole, left = sum([portions[i] for i in candidates]), rest
        for i in candidates:
            addition = min(most - counts[i], max(1, left * portions[i] // whole), rest)
            counts[i] = counts[i] + addition
            rest = rest - addition
    return np.array([most] + counts)


def uneven(key, count, total, limit, lean):
    if count == 2:
        one = jax.random.randint(key, (), max(1, total - limit), min(limit, total - 1) + 1)
        return jnp.stack([one, total - one])
    lengths = jnp.asarray(length_profile(count, total, limit, lean), jnp.int32)
    pairs = (count - 1) // 2
    source_of, taker = lengths[1:1 + 2 * pairs:2], lengths[2:2 + 2 * pairs:2]
    room = jnp.minimum(source_of - 1, limit - taker)
    moved = jax.random.randint(jax.random.fold_in(key, 1), (pairs,), 0, 1 << 20) % (room + 1)
    lengths = lengths.at[1:1 + 2 * pairs:2].set(source_of - moved).at[2:2 + 2 * pairs:2].set(taker + moved)
    return lengths[jax.random.permutation(jax.random.fold_in(key, 2), count)]


def gaussian(stream_key, extent, deviation, bound, shards=(), kind=jnp.bfloat16):
    factor_of = level_of(stream_key, extent, shards, -0.22, 0.18) if shards else 1.0
    drawn = jax.random.normal(stream_key, extent, jnp.float32) * deviation * factor_of
    return jnp.minimum(jnp.maximum(drawn, -bound), bound).astype(kind)


def setup_inputs(seed: int = 0) -> dict:
    key_of = jax.random.split(jax.random.key(seed), 26)
    text_ids = touch_ends(jax.random.randint(key_of[0], (CAPTION_ROWS, TXT_LEN), 0, TVOC), jax.random.fold_in(key_of[0], 1), 0, TVOC - 1).astype(jnp.int32)
    text_segments = jax.vmap(lambda own: jnp.searchsorted(jnp.cumsum(uneven(own, IMGS_DEV, TXT_LEN, TXT_LEN - IMGS_DEV + 1, 0)), jnp.arange(TXT_LEN), side="right"))(jax.random.split(key_of[1], CAPTION_ROWS)).reshape((CAPTION_ROWS, TXT_LEN)).astype(jnp.int32)
    codes = touch_ends(jax.random.randint(key_of[2], (IMAGES, IMG_LEN), 0, VOCAB), jax.random.fold_in(key_of[2], 1), 0, VOCAB - 1).astype(jnp.int32)
    caption_of = touch_ends(jax.random.randint(key_of[3], (IMAGES,), 0, IMGS_DEV), jax.random.fold_in(key_of[3], 1), 0, IMGS_DEV - 1).astype(jnp.int32)
    mix_in = gaussian(key_of[4], (3, D, 3 * D), D ** -0.5, 0.1875, ((1, 32),), jnp.float32)
    mix_out = gaussian(key_of[5], (3, D, D), (D // 64) ** -0.5, 1.5, ((1, 32),), jnp.float32)
    ffn_up = gaussian(key_of[6], (2, D, FF), D ** -0.5, 0.1875, ((1, 32),), jnp.float32)
    ffn_down = gaussian(key_of[7], (2, FF, D), FF ** -0.5, 0.09375, ((1, 32),), jnp.float32)
    norm_gains = draw_norm_gains(jax.random.fold_in(key_of[25], 71), 0)
    text_table = gaussian(key_of[9], (TVOC, D), D ** -0.5, 0.1875, ((0, 32),), jnp.float32)
    code_table = draw_code_table(jax.random.fold_in(key_of[25], 71), 0)
    mix_in_first = gaussian(key_of[11], (3, D, 3 * D), 0.0000027, 3.814697265625e-05, ((1, 32),), jnp.float32)
    mix_out_first = gaussian(key_of[12], (3, D, D), 0.0000027, 3.814697265625e-05, ((1, 32),), jnp.float32)
    ffn_up_first = gaussian(key_of[13], (2, D, FF), 0.0000027, 3.814697265625e-05, ((1, 32),), jnp.float32)
    ffn_down_first = gaussian(key_of[14], (2, FF, D), 0.0000027, 3.814697265625e-05, ((1, 32),), jnp.float32)
    gains_first = gaussian(key_of[15], (7, D), 0.000011, 0.00015258789, ((1, 32),), jnp.float32)
    text_first = gaussian(key_of[16], (TVOC, D), 0.0000027, 3.814697265625e-05, ((0, 32),), jnp.float32)
    code_first = gaussian(key_of[17], (VOCAB, D), 0.0000027, 3.814697265625e-05, ((0, 8), (1, 4)), jnp.float32)
    mix_in_second = jnp.clip(jnp.exp(math.log(2.9000000317802588e-11) - 1.3794215 * jax.random.uniform(key_of[18], (3, D, 3 * D), jnp.float32) ** level_of(key_of[18], (3, D, 3 * D), ((1, 32),), -0.2, 0.2)), 7.300000014198726e-12, 2.9000000317802588e-11)
    mix_out_second = jnp.clip(jnp.exp(math.log(2.9000000317802588e-11) - 1.3794215 * jax.random.uniform(key_of[19], (3, D, D), jnp.float32) ** level_of(key_of[19], (3, D, D), ((1, 32),), -0.2, 0.2)), 7.300000014198726e-12, 2.9000000317802588e-11)
    ffn_up_second = jnp.clip(jnp.exp(math.log(2.9000000317802588e-11) - 1.3794215 * jax.random.uniform(key_of[20], (2, D, FF), jnp.float32) ** level_of(key_of[20], (2, D, FF), ((1, 32),), -0.2, 0.2)), 7.300000014198726e-12, 2.9000000317802588e-11)
    ffn_down_second = jnp.clip(jnp.exp(math.log(2.9000000317802588e-11) - 1.3794215 * jax.random.uniform(key_of[21], (2, FF, D), jnp.float32) ** level_of(key_of[21], (2, FF, D), ((1, 32),), -0.2, 0.2)), 7.300000014198726e-12, 2.9000000317802588e-11)
    gains_second = jnp.clip(jnp.exp(math.log(4.799999842042268e-10) - 1.3862944 * jax.random.uniform(key_of[22], (7, D), jnp.float32) ** level_of(key_of[22], (7, D), ((1, 32),), -0.2, 0.2)), 1.199999960510567e-10, 4.799999842042268e-10)
    text_second = jnp.clip(jnp.exp(math.log(2.9000000317802588e-11) - 1.3794215 * jax.random.uniform(key_of[23], (TVOC, D), jnp.float32) ** level_of(key_of[23], (TVOC, D), ((0, 32),), -0.2, 0.2)), 7.300000014198726e-12, 2.9000000317802588e-11)
    code_second = jnp.clip(jnp.exp(math.log(2.9000000317802588e-11) - 1.3794215 * jax.random.uniform(key_of[24], (VOCAB, D), jnp.float32) ** level_of(key_of[24], (VOCAB, D), ((0, 8), (1, 4)), -0.2, 0.2)), 7.300000014198726e-12, 2.9000000317802588e-11)
    return dict(text_ids=text_ids, text_segments=text_segments, codes=codes, caption_of=caption_of, mix_in=mix_in, mix_out=mix_out, ffn_up=ffn_up, ffn_down=ffn_down, norm_gains=norm_gains, text_table=text_table, code_table=code_table, mix_in_first=mix_in_first, mix_out_first=mix_out_first, ffn_up_first=ffn_up_first, ffn_down_first=ffn_down_first, gains_first=gains_first, text_first=text_first, code_first=code_first, mix_in_second=mix_in_second, mix_out_second=mix_out_second, ffn_up_second=ffn_up_second, ffn_down_second=ffn_down_second, gains_second=gains_second, text_second=text_second, code_second=code_second)


@jax.custom_vjp
def low(v):
    return lax.optimization_barrier(v.astype(jnp.bfloat16)).astype(jnp.float32)

@jax.custom_vjp
def low_back(v):
    return v

def low_keep(v):
    return (low(v), None)

def low_pass(kept, grad):
    return (grad,)

def back_keep(v):
    return (v, None)

def back_low(kept, grad):
    return (low(grad),)
low.defvjp(low_keep, low_pass)
low_back.defvjp(back_keep, back_low)
SMOOTH = 0.1
BETA_ONE = 0.5
BETA_TWO = 0.5
WEIGHT_DECAY = 0.1
ADAM_EPS = 1e-08
CLIP_NORM = 0.02
MASKED = -1e+30
PRECISE = lax.Precision.HIGHEST
STEP_RATES = (0.02, 0.15, 0.02, 0.01, 0.3, 0.02, 0.03)

def rounded(value):
    return low(low_back(value))

def layer_norm(stream, gain):
    centred = stream - lax.optimization_barrier(jnp.mean(stream, axis=-1, keepdims=True))
    return centred * lax.rsqrt(lax.optimization_barrier(jnp.mean(centred * centred, axis=-1, keepdims=True)) + 1e-05) * gain

def positions(length, width):
    position = jnp.arange(length, dtype=jnp.float32)[:, None]
    speeds = jnp.exp(-math.log(10000.0) * 2.0 * jnp.arange(width // 2, dtype=jnp.float32)[None, :] / width)
    return jnp.concatenate([jnp.sin(position * speeds), jnp.cos(position * speeds)], axis=1)

def matmul(first_op, second_op):
    return jnp.dot(first_op, second_op, precision=PRECISE)

def head_split(matrix):
    return matrix.reshape(matrix.shape[0], HEADS, HEAD)

def attend(inputs):
    queries, keys_in, values, visible = inputs
    scores = low_back(jnp.einsum('qhd,khd->hqk', head_split(queries), head_split(keys_in), precision=PRECISE) * HEAD ** (-0.5))
    scores = jnp.where(visible[None], scores, MASKED)
    shares = jax.nn.softmax(scores, axis=-1)
    attended = jnp.einsum('hqk,khd->qhd', low(shares), head_split(values), precision=PRECISE)
    return rounded(attended.reshape(queries.shape))

def attention(queries, keys_in, values, visible):
    blocks = visible.shape[0]
    attended = lax.map(jax.checkpoint(attend), (queries.reshape(blocks, -1, queries.shape[1]), keys_in, values, visible))
    return attended.reshape(queries.shape)

def layer_pass(stream, weights, self_visible, memory, cross_visible):
    mix_in, mix_out, ffn_up, ffn_down, gain_rows = weights
    width = stream.shape[1]
    blocks = self_visible.shape[0]
    normed = low(layer_norm(stream, gain_rows[0]))
    project = rounded(matmul(normed, mix_in[0]))
    queries, keys_in, values = jnp.split(project, 3, axis=1)
    attended = attention(queries, keys_in.reshape(blocks, -1, width), values.reshape(blocks, -1, width), self_visible)
    stream = stream + low_back(matmul(attended, mix_out[0]))
    if memory is not None:
        cross_in = low(layer_norm(stream, gain_rows[1]))
        cross_query = rounded(matmul(cross_in, mix_in[1][:, :width]))
        memory_kv = rounded(matmul(memory, mix_in[1][:, width:]))
        memory_keys, memory_values = jnp.split(memory_kv, 2, axis=1)
        stacked_shape = (blocks,) + memory_keys.shape
        attended = attention(cross_query, jnp.broadcast_to(memory_keys, stacked_shape), jnp.broadcast_to(memory_values, stacked_shape), cross_visible)
        stream = stream + low_back(matmul(attended, mix_out[1]))
    ffn_in = low(layer_norm(stream, gain_rows[-2]))
    hidden_pre = low_back(matmul(ffn_in, ffn_up))
    hidden = low(jax.nn.gelu(hidden_pre, approximate=True))
    stream = stream + low_back(matmul(hidden, ffn_down))
    return low(layer_norm(stream, gain_rows[-1]))

def block_loss(table, inputs):
    final_out, targets = inputs
    logits = low_back(matmul(final_out, table.T))
    log_total = jax.nn.logsumexp(logits, axis=-1)
    picked = jnp.take_along_axis(logits, targets[:, None], axis=1)[:, 0]
    return jnp.sum(log_total - (1.0 - SMOOTH) * picked - SMOOTH * lax.optimization_barrier(jnp.mean(logits, axis=-1)))

def group_loss(params, token_ids, segments, group_codes, captions):
    mix_in, mix_out, ffn_up, ffn_down, gain_rows, text_table, code_table = [low(param) for param in params]
    scale_in = math.sqrt(D)
    text_in = text_table[token_ids] * scale_in + positions(TXT_LEN, D)
    text_visible = (segments[:, None] == segments[None, :])[None]
    memory = layer_pass(text_in, (mix_in[0:1], mix_out[0:1], ffn_up[0], ffn_down[0], gain_rows[0:3]), text_visible, None, None)
    looked = code_table[group_codes] * scale_in
    shifted = jnp.concatenate([jnp.zeros_like(looked[:, :1]), looked[:, :-1]], axis=1)
    image_in = (shifted + positions(IMG_LEN, D)[None]).reshape(-1, D)
    blocks = IMGS_DEV // 2
    rows_block = 2 * IMG_LEN
    position = jnp.arange(rows_block)
    image_of = position // IMG_LEN
    self_one = (image_of[:, None] == image_of[None, :]) & (position[None, :] <= position[:, None])
    self_visible = jnp.broadcast_to(self_one, (blocks, rows_block, rows_block))
    wanted = jnp.repeat(captions, IMG_LEN).reshape(blocks, rows_block)
    cross_visible = segments[None, None, :] == wanted[:, :, None]
    final_out = layer_pass(image_in, (mix_in[1:3], mix_out[1:3], ffn_up[1], ffn_down[1], gain_rows[3:7]), self_visible, memory, cross_visible)
    losses = lax.map(jax.checkpoint(partial(block_loss, code_table)), (final_out.reshape(blocks, rows_block, D), group_codes.reshape(blocks, rows_block)))
    return jnp.sum(losses)

def adam_step(weight, moment_one, second, gradient, rate):
    moment_one = BETA_ONE * moment_one + (1.0 - BETA_ONE) * gradient
    second = BETA_TWO * second + (1.0 - BETA_TWO) * gradient * gradient
    first_hat = moment_one / (1.0 - BETA_ONE ** STEP)
    second_hat = second / (1.0 - BETA_TWO ** STEP)
    weight = weight - rate * (first_hat / (jnp.sqrt(second_hat) + ADAM_EPS) + WEIGHT_DECAY * weight)
    return (weight, moment_one, second)

def reference(text_ids, text_segments, codes, caption_of, mix_in, mix_out, ffn_up, ffn_down, norm_gains, text_table, code_table, mix_in_first, mix_out_first, ffn_up_first, ffn_down_first, gains_first, text_first, code_first, mix_in_second, mix_out_second, ffn_up_second, ffn_down_second, gains_second, text_second, code_second):
    params = (mix_in, mix_out, ffn_up, ffn_down, norm_gains, text_table, code_table)
    firsts = (mix_in_first, mix_out_first, ffn_up_first, ffn_down_first, gains_first, text_first, code_first)
    seconds = (mix_in_second, mix_out_second, ffn_up_second, ffn_down_second, gains_second, text_second, code_second)
    token_total = IMAGES * IMG_LEN
    items = (text_ids, text_segments, codes.reshape(CAPTION_ROWS, IMGS_DEV, IMG_LEN), caption_of.reshape(CAPTION_ROWS, IMGS_DEV))

    def step_group(state_now, group_item):
        running, gradients = state_now
        token_ids, segments, group_codes, captions = group_item
        group_value, pullback = jax.vjp(lambda weights: group_loss(weights, token_ids, segments, group_codes, captions), params)
        group_grads = pullback(jnp.ones_like(group_value) / token_total)[0]
        return ((running + group_value, jax.tree.map(jnp.add, gradients, group_grads)), None)
    initial = (jnp.zeros((), text_table.dtype), jax.tree.map(jnp.zeros_like, params))
    (loss_sum, gradients), _ = lax.scan(step_group, initial, items)
    grad_norm = jnp.sqrt(sum((jnp.sum(gradient * gradient) for gradient in gradients)))
    factor = CLIP_NORM / jnp.maximum(grad_norm, CLIP_NORM)
    updated = [adam_step(params[index], firsts[index], seconds[index], gradients[index] * factor, STEP_RATES[index]) for index in range(7)]
    return (loss_sum, grad_norm, updated[0][0], updated[1][0], updated[2][0], updated[3][0], updated[4][0], updated[5][0], updated[6][0], updated[0][1], updated[1][1], updated[2][1], updated[3][1], updated[4][1], updated[5][1], updated[6][1], updated[0][2], updated[1][2], updated[2][2], updated[3][2], updated[4][2], updated[5][2], updated[6][2])
```

```python
from functools import partial
import math

import jax
import jax.numpy as jnp
from jax import lax
from jax.experimental import pallas as pl
from jax.experimental.pallas import tpu as pltpu
from jax.sharding import PartitionSpec as P

D = 1024
HEADS = 16
HEAD = 64
VOCAB = 8192
TVOC = 16000
IMG_LEN = 256
TXT_LEN = 128
STEP = 5


SMOOTH = 0.1
BETA_ONE = 0.5
BETA_TWO = 0.5
WEIGHT_DECAY = 0.1
ADAM_EPS = 1e-08
CLIP_NORM = 0.02
MASKED = -1e30
STEP_RATES = (0.02, 0.15, 0.02, 0.01, 0.3, 0.02, 0.03)

BF = jnp.bfloat16
F32 = jnp.float32
AXES = ("dp", "fsdp")
MESH = pl.DeviceIdType.MESH
LAG = 2


def sum_kernel(
    units, Z, p_ref, out_ref, own, from_core, held, from_x, from_y, all_x, all_y, kept, from_line,
    own_sem, core_send, core_recv, one_send, one_recv, two_send, two_recv, line_send, line_recv,
):
    depth = 2 * LAG
    dp, fs = lax.axis_index("dp"), lax.axis_index("fsdp")
    z, core = fs // 2, fs % 2
    x_mate, y_mate = dp + 1 - 2 * (dp % 2), (dp + 2) % 4
    across_dp = (x_mate + 2) % 4
    core_dev, x_dev, y_dev = (dp, fs + 1 - 2 * core), (x_mate, fs), (y_mate, fs)
    up_dev, down_dev = (dp, fs + 2), (dp, fs - 2)
    has_up, has_down = z < Z - 1, z > 0

    barrier = pltpu.get_barrier_semaphore()
    for device in (core_dev, x_dev, y_dev):
        pl.semaphore_signal(barrier, inc=1, device_id=device, device_id_type=MESH)

    @pl.when(has_up)
    def _():
        pl.semaphore_signal(barrier, inc=1, device_id=up_dev, device_id_type=MESH)

    @pl.when(has_down)
    def _():
        pl.semaphore_signal(barrier, inc=1, device_id=down_dev, device_id_type=MESH)

    pl.semaphore_wait(barrier, 3 + has_up.astype(jnp.int32) + has_down.astype(jnp.int32))
    half = Z // 2
    own_slots, held_slots, kept_slots = own.shape[0], held.shape[0], kept.shape[0]

    def add(a, b):
        return (a.astype(F32) + b.astype(F32)).astype(BF)

    def remote(src, dst, send, recv, device):
        return pltpu.make_async_remote_copy(
            src_ref=src, dst_ref=dst, send_sem=send, recv_sem=recv, device_id=device, device_id_type=MESH
        )

    def own_copy(k):
        return pltpu.make_async_copy(
            p_ref.at[k, :, :, core], own.at[k % own_slots], own_sem.at[k % own_slots]
        )

    def core_copy(k):
        s = k % depth
        return remote(
            p_ref.at[k, :, :, 1 - core], from_core.at[s], core_send.at[s], core_recv.at[s], core_dev
        )

    def one_copies(k):
        s, block = k % depth, held.at[k % held_slots, across_dp]
        return (
            remote(block.at[pl.ds(0, half)], from_x.at[s], one_send.at[0, s], one_recv.at[0, s], x_dev),
            remote(block.at[pl.ds(half, Z - half)], from_y.at[s], one_send.at[1, s], one_recv.at[1, s], y_dev),
        )

    def two_copies(k):
        s, h = k % depth, k % held_slots
        return (
            remote(held.at[h, x_mate], all_x.at[s], two_send.at[0, s], two_recv.at[0, s], x_dev),
            remote(held.at[h, y_mate], all_y.at[s], two_send.at[1, s], two_recv.at[1, s], y_dev),
        )

    def up_block(step):
        return jnp.minimum(z + Z - step, Z - 1)

    def down_block(step):
        return jnp.maximum(z - Z + step, 0)

    def up_copy(k, step):
        s = k % depth
        return remote(
            kept.at[k % kept_slots, up_block(step)], from_line.at[0, step - 1, s],
            line_send.at[0, step - 1, s], line_recv.at[0, step - 1, s], up_dev,
        )

    def down_copy(k, step):
        s = k % depth
        return remote(
            kept.at[k % kept_slots, down_block(step)], from_line.at[1, step - 1, s],
            line_send.at[1, step - 1, s], line_recv.at[1, step - 1, s], down_dev,
        )

    def line_start(k, step):
        @pl.when(has_up)
        def _():
            up_copy(k, step).start()

        @pl.when(has_down)
        def _():
            down_copy(k, step).start()

    def line_wait(k, step):
        @pl.when(has_down)
        def _():
            up_copy(k, step).wait_recv()
            down_copy(k, step).wait_send()

        @pl.when(has_up)
        def _():
            down_copy(k, step).wait_recv()
            up_copy(k, step).wait_send()

    def begin(k):
        own_copy(k).start()
        core_copy(k).start()

    def after_core(k):
        own_copy(k).wait()
        core_copy(k).wait()

        def one(block, carry):
            for q in range(Z):
                held[k % held_slots, block, q] = add(
                    own[k % own_slots, block, q], from_core[k % depth, block, q]
                )
            return carry

        lax.fori_loop(0, 4, one, 0)
        for copy in one_copies(k):
            copy.start()

    def after_one(k):
        s, h = k % depth, k % held_slots
        for copy in one_copies(k):
            copy.wait()
        for q in range(half):
            held[h, y_mate, q] = add(held[h, y_mate, q], from_x[s, q])
        for q in range(Z - half):
            held[h, x_mate, half + q] = add(held[h, x_mate, half + q], from_y[s, q])
        for copy in two_copies(k):
            copy.start()

    def after_two(k):
        s, h = k % depth, k % held_slots
        for copy in two_copies(k):
            copy.wait()
        for q in range(Z):
            kept[k % kept_slots, q] = (
                held[h, dp, q].astype(F32) + all_x[s, q].astype(F32) + all_y[s, q].astype(F32)
            ).astype(BF)
        line_start(k, 1)

    def along_line(step):
        def run(k):
            s, h = k % depth, k % kept_slots
            line_wait(k, step - 1)

            @pl.when(has_down & (z + Z - step <= Z - 1))
            def _():
                kept[h, up_block(step)] = add(kept[h, up_block(step)], from_line[0, step - 2, s])

            @pl.when(has_up & (z - Z + step >= 0))
            def _():
                kept[h, down_block(step)] = add(kept[h, down_block(step)], from_line[1, step - 2, s])

            line_start(k, step)

        return run

    def finish(k):
        s = k % depth
        line_wait(k, Z - 1)
        out_ref[k] = kept[k % kept_slots, z].astype(F32)

        @pl.when(has_down)
        def _():
            out_ref[k] = out_ref[k] + from_line[0, Z - 2, s].astype(F32)

        @pl.when(has_up)
        def _():
            out_ref[k] = out_ref[k] + from_line[1, Z - 2, s].astype(F32)

    stages = [begin, after_core, after_one, after_two]
    stages += [along_line(step) for step in range(2, Z)] + [finish]

    def loop_step(j, carry):
        for place in reversed(range(len(stages))):
            k = j - place * LAG

            @pl.when((k >= 0) & (k < units))
            def _(k=k, run=stages[place]):
                run(k)

        return carry

    lax.fori_loop(0, units + (len(stages) - 1) * LAG, loop_step, 0)


def sum_units(partial_sums, call_id):
    units, devices, m, n = partial_sums.shape
    Z = lax.axis_size("fsdp") // 2
    if lax.axis_size("dp") != 4 or Z != 4 or m % 16:
        return lax.psum_scatter(
            partial_sums, AXES, scatter_dimension=1, tiled=True
        ).reshape(units, m, n).astype(F32)
    depth, half = 2 * LAG, Z // 2
    own_slots, held_slots, kept_slots = LAG + 1, 2 * LAG + 1, Z * LAG + 1
    dma = pltpu.SemaphoreType.DMA
    return pl.pallas_call(
        partial(sum_kernel, units, Z),
        out_shape=jax.ShapeDtypeStruct((units, m, n), F32),
        in_specs=[pl.BlockSpec(memory_space=pl.ANY)],
        out_specs=pl.BlockSpec(memory_space=pltpu.VMEM),
        scratch_shapes=[
            pltpu.VMEM((own_slots, 4, Z, m, n), BF),
            pltpu.VMEM((depth, 4, Z, m, n), BF),
            pltpu.VMEM((held_slots, 4, Z, m, n), BF),
            pltpu.VMEM((depth, half, m, n), BF),
            pltpu.VMEM((depth, Z - half, m, n), BF),
            pltpu.VMEM((depth, Z, m, n), BF),
            pltpu.VMEM((depth, Z, m, n), BF),
            pltpu.VMEM((kept_slots, Z, m, n), BF),
            pltpu.VMEM((2, Z - 1, depth, m, n), BF),
            dma((own_slots,)),
            dma((depth,)),
            dma((depth,)),
            dma((2, depth)),
            dma((2, depth)),
            dma((2, depth)),
            dma((2, depth)),
            dma((2, Z - 1, depth)),
            dma((2, Z - 1, depth)),
        ],
        compiler_params=pltpu.CompilerParams(
            collective_id=call_id, has_side_effects=True, vmem_limit_bytes=48 << 20
        ),
    )(partial_sums.reshape(units, 4, Z, 2, m, n))


def layer_norm(stream, gain):
    centred = stream - jnp.mean(stream, axis=-1, keepdims=True)
    return centred * lax.rsqrt(jnp.mean(centred * centred, axis=-1, keepdims=True) + 1e-05) * gain


def norm_back(stream, gain, grad_out):
    _, pullback = jax.vjp(layer_norm, stream, gain)
    return pullback(grad_out)


def positions(length, width):
    position = jnp.arange(length, dtype=jnp.float32)[:, None]
    speeds = jnp.exp(
        -math.log(10000.0) * 2.0 * jnp.arange(width // 2, dtype=jnp.float32)[None, :] / width
    )
    return jnp.concatenate([jnp.sin(position * speeds), jnp.cos(position * speeds)], axis=1)


def matmul(first_op, second_op):
    return jnp.dot(first_op, second_op, preferred_element_type=jnp.float32)


def across(first_op, second_op):
    return lax.dot_general(
        first_op, second_op, (((0,), (0,)), ((), ())), preferred_element_type=jnp.float32
    )


def against(first_op, second_op):
    return lax.dot_general(
        first_op, second_op, (((1,), (1,)), ((), ())), preferred_element_type=jnp.float32
    )


def heads_first(matrix, blocks):
    return matrix.reshape(blocks, -1, HEADS, HEAD).transpose(0, 2, 1, 3)


def heads_last(array):
    return array.transpose(0, 2, 1, 3).reshape(-1, HEADS * HEAD)


def attention(queries, keys_in, values, visible):
    scores = jnp.einsum(
        "bhqd,bhkd->bhqk", queries, keys_in, preferred_element_type=F32
    ) * HEAD ** (-0.5)
    scores = jnp.where(visible[:, None], scores, MASKED)
    weights = jnp.exp(scores - jnp.max(scores, axis=-1, keepdims=True))
    shares = weights / jnp.sum(weights, axis=-1, keepdims=True)
    low = shares.astype(BF)
    attended = jnp.einsum("bhqk,bhkd->bhqd", low, values, preferred_element_type=F32)
    return heads_last(attended.astype(BF)), low


def attention_back(queries, keys_in, values, shares, grad_mixed):
    grad_heads = heads_first(grad_mixed, queries.shape[0])
    grad_shares = jnp.einsum(
        "bhqd,bhkd->bhqk", grad_heads, values, preferred_element_type=F32
    )
    wide = shares.astype(F32)
    grad_scores = (
        wide * (grad_shares - jnp.sum(wide * grad_shares, axis=-1, keepdims=True))
    ).astype(BF)
    grad_query = jnp.einsum(
        "bhqk,bhkd->bhqd", grad_scores, keys_in, preferred_element_type=F32
    ) * HEAD ** (-0.5)
    grad_keys = jnp.einsum(
        "bhqk,bhqd->bhkd", grad_scores, queries, preferred_element_type=F32
    ) * HEAD ** (-0.5)
    grad_values = jnp.einsum(
        "bhqk,bhqd->bhkd", shares, grad_heads, preferred_element_type=F32
    )
    return grad_query, grad_keys, grad_values


def layer_forward(stream, weights, gains, self_visible, memory, cross_visible):
    project, mix_out, cross, cross_out, ffn_up, ffn_down = weights
    blocks = self_visible.shape[0]
    stored = {"stream": stream}
    normed = layer_norm(stream, gains[0]).astype(BF)
    queries, keys_in, values = [
        heads_first(matmul(normed, project[i]).astype(BF), blocks) for i in range(3)
    ]
    attended, shares = attention(queries, keys_in, values, self_visible)
    stream = stream + matmul(attended, mix_out)
    stored.update(
        normed=normed, self_attention=(queries, keys_in, values, shares), attended=attended, after_self=stream
    )
    if memory is not None:
        cross_in = layer_norm(stream, gains[1]).astype(BF)
        cross_query = heads_first(matmul(cross_in, cross[0]).astype(BF), 1)
        memory_keys = heads_first(matmul(memory, cross[1]).astype(BF), 1)
        memory_values = heads_first(matmul(memory, cross[2]).astype(BF), 1)
        cross_mixed, cross_shares = attention(cross_query, memory_keys, memory_values, cross_visible)
        stream = stream + matmul(cross_mixed, cross_out)
        stored.update(
            cross_in=cross_in,
            cross_attention=(cross_query, memory_keys, memory_values, cross_shares),
            cross_mixed=cross_mixed,
        )
    stored["before_ffn"] = stream
    ffn_in = layer_norm(stream, gains[-2]).astype(BF)
    hidden_pre = [matmul(ffn_in, up) for up in ffn_up]
    hidden = [jax.nn.gelu(pre, approximate=True).astype(BF) for pre in hidden_pre]
    for low, down in zip(hidden, ffn_down):
        stream = stream + matmul(low, down)
    stored.update(ffn_in=ffn_in, hidden_pre=hidden_pre, hidden=hidden, before_final=stream)
    return layer_norm(stream, gains[-1]).astype(BF), stored


def layer_backward(grad_final, weights, gains, stored, memory):
    project, mix_out, cross, cross_out, ffn_up, ffn_down = weights
    gain_grads = [None] * len(gains)
    grad_stream, gain_grads[-1] = norm_back(stored["before_final"], gains[-1], grad_final)
    grad_low = grad_stream.astype(BF)
    up_pairs, down_pairs = [], []
    grad_ffn = 0.0
    for pre, low, up, down in zip(stored["hidden_pre"], stored["hidden"], ffn_up, ffn_down):
        down_pairs.append((low, grad_low))
        _, gelu_pull = jax.vjp(partial(jax.nn.gelu, approximate=True), pre)
        grad_pre = gelu_pull(against(grad_low, down))[0].astype(BF)
        up_pairs.append((stored["ffn_in"], grad_pre))
        grad_ffn = grad_ffn + against(grad_pre, up)
    grad_normed, gain_grads[-2] = norm_back(stored["before_ffn"], gains[-2], grad_ffn)
    grad_stream = grad_stream + grad_normed
    cross_pairs, cross_out_pairs = [], []
    grad_memory = None
    if memory is not None:
        grad_low = grad_stream.astype(BF)
        cross_out_pairs.append((stored["cross_mixed"], grad_low))
        grad_mixed = against(grad_low, cross_out).astype(BF)
        grads = [
            heads_last(grad.astype(BF)) for grad in attention_back(*stored["cross_attention"], grad_mixed)
        ]
        cross_pairs = [(stored["cross_in"], grads[0]), (memory, grads[1]), (memory, grads[2])]
        grad_memory = against(grads[1], cross[1]) + against(grads[2], cross[2])
        grad_normed, gain_grads[1] = norm_back(
            stored["after_self"], gains[1], against(grads[0], cross[0])
        )
        grad_stream = grad_stream + grad_normed
    grad_low = grad_stream.astype(BF)
    out_pairs = [(stored["attended"], grad_low)]
    grad_mixed = against(grad_low, mix_out).astype(BF)
    grads = [
        heads_last(grad.astype(BF)) for grad in attention_back(*stored["self_attention"], grad_mixed)
    ]
    project_pairs = [(stored["normed"], grad) for grad in grads]
    grad_normed, gain_grads[0] = norm_back(
        stored["stream"],
        gains[0],
        sum(against(grads[i], project[i]) for i in range(3)),
    )
    grad_stream = grad_stream + grad_normed
    pairs = (project_pairs, out_pairs, cross_pairs, cross_out_pairs, up_pairs, down_pairs)
    return grad_stream, grad_memory, gain_grads, pairs


def adam_step(weight, moment_one, second, gradient, rate):
    moment_one = BETA_ONE * moment_one + (1.0 - BETA_ONE) * gradient
    second = BETA_TWO * second + (1.0 - BETA_TWO) * gradient * gradient
    first_hat = moment_one / (1.0 - BETA_ONE**STEP)
    second_hat = second / (1.0 - BETA_TWO**STEP)
    weight = weight - rate * (first_hat / (jnp.sqrt(second_hat) + ADAM_EPS) + WEIGHT_DECAY * weight)
    return (weight, moment_one, second)


def column_units(matrix):
    return matrix.reshape(matrix.shape[0], -1, D).transpose(1, 0, 2)


def from_column_units(units):
    return units.transpose(1, 0, 2).reshape(units.shape[1], -1)


def hidden_units(matrix, devices):
    rows, width = matrix.shape
    return (
        matrix.reshape(rows, devices, 4, width // devices // 4)
        .transpose(2, 0, 1, 3)
        .reshape(4, rows, width // 4)
    )


def from_hidden_units(units, devices):
    quarters, rows, width = units.shape
    return (
        units.reshape(quarters, rows, devices, width // devices)
        .transpose(1, 2, 0, 3)
        .reshape(rows, quarters * width)
    )


def on_device(
    text_ids,
    text_segments,
    codes,
    caption_of,
    mix_in,
    mix_out,
    ffn_up,
    ffn_down,
    norm_gains,
    text_table,
    code_table,
    mix_in_first,
    mix_out_first,
    ffn_up_first,
    ffn_down_first,
    gains_first,
    text_first,
    code_first,
    mix_in_second,
    mix_out_second,
    ffn_up_second,
    ffn_down_second,
    gains_second,
    text_second,
    code_second,
):
    image_count = codes.shape[0]
    dp_size, fsdp_size = lax.axis_size("dp"), lax.axis_size("fsdp")
    devices = dp_size * fsdp_size
    me = lax.axis_index("dp") * fsdp_size + lax.axis_index("fsdp")
    token_total = image_count * IMG_LEN * devices
    inverse = 1.0 / token_total
    scale_in = math.sqrt(D)
    rows = mix_in.shape[1]
    segments = text_segments[0]
    text_visible = (segments[:, None] == segments[None, :])[None]
    place = jnp.arange(IMG_LEN)
    self_visible = jnp.broadcast_to(
        place[None, :] <= place[:, None], (image_count, IMG_LEN, IMG_LEN)
    )
    wanted = jnp.repeat(caption_of, IMG_LEN)
    cross_visible = (segments[None, :] == wanted[:, None])[None]

    small = jnp.concatenate([text_ids[0].astype(F32), norm_gains.reshape(-1)])
    small = lax.all_gather(small, AXES)
    all_ids = small[:, :TXT_LEN].astype(jnp.int32).reshape(-1)
    gains = small[:, TXT_LEN:].reshape(devices, 7, -1).transpose(1, 0, 2).reshape(7, D)
    gains = gains.astype(BF).astype(F32)

    def gather(units):
        return lax.all_gather(units.astype(BF), AXES, axis=1, tiled=True)

    code_cols = lax.all_gather(code_table.astype(BF), "dp", axis=1, tiled=True)
    code_full = lax.all_gather(code_cols, "fsdp", axis=0, tiled=True)

    def layer_units(which):
        return [
            column_units(mix_in[which]),
            mix_out[which][None],
            hidden_units(ffn_up[min(which, 1)], devices),
            ffn_down[min(which, 1)].reshape(4, rows, D),
        ]

    enc_units = gather(jnp.concatenate(layer_units(0)))
    self_units = gather(jnp.concatenate(layer_units(1)[:2]))
    late_units = gather(jnp.concatenate(layer_units(2)))
    enc_weights = (enc_units[:3], enc_units[3], None, None, enc_units[4:8], enc_units[8:])
    dec_weights = (
        self_units[:3], self_units[3], late_units[:3], late_units[3], late_units[4:8], late_units[8:]
    )

    base = me * text_table.shape[0]
    owned = (all_ids[:, None] - base == jnp.arange(text_table.shape[0])[None, :]).astype(BF)
    looked = matmul(owned, text_table.astype(BF)).astype(BF)
    looked = looked.reshape(devices, TXT_LEN // rows, rows, D).transpose(1, 0, 2, 3)
    text_in = sum_units(looked, 0).reshape(TXT_LEN, D) * scale_in + positions(TXT_LEN, D)
    enc_gains = [gains[i] for i in range(3)]
    dec_gains = [gains[i] for i in range(3, 7)]
    memory, enc_stored = layer_forward(text_in, enc_weights, enc_gains, text_visible, None, None)

    image_rows = code_full[codes].astype(F32) * scale_in
    shifted = jnp.concatenate([jnp.zeros_like(image_rows[:, :1]), image_rows[:, :-1]], axis=1)
    image_in = (shifted + positions(IMG_LEN, D)[None]).reshape(-1, D)
    final_out, dec_stored = layer_forward(
        image_in, dec_weights, dec_gains, self_visible, memory, cross_visible
    )

    targets = codes.reshape(-1)
    logits = against(final_out, code_full)
    hit = targets[:, None] == jnp.arange(VOCAB)[None, :]
    top = jnp.max(logits, axis=1, keepdims=True)
    log_total = top + jnp.log(jnp.sum(jnp.exp(logits - top), axis=1, keepdims=True))
    weighted = jnp.sum(
        logits * jnp.where(hit, 1.0 - SMOOTH + SMOOTH / VOCAB, SMOOTH / VOCAB), axis=1, keepdims=True
    )
    loss_part = jnp.sum(log_total - weighted)
    grad_logits = (
        (jnp.exp(logits - log_total) - jnp.where(hit, 1.0 - SMOOTH, 0.0) - SMOOTH / VOCAB) * inverse
    ).astype(BF)
    grad_final = matmul(grad_logits, code_full)

    grad_image, grad_memory, dec_gain_grads, dec_pairs = layer_backward(
        grad_final, dec_weights, dec_gains, dec_stored, memory
    )
    grad_text, _, enc_gain_grads, enc_pairs = layer_backward(
        grad_memory, enc_weights, enc_gains, enc_stored, None
    )
    gain_part = jnp.stack(enc_gain_grads + dec_gain_grads)

    grad_rows = lax.all_gather((grad_text * scale_in).astype(BF), AXES, axis=0, tiled=True)
    text_grad = across(owned, grad_rows)

    grad_looked = grad_image.reshape(image_count, IMG_LEN, D)[:, 1:] * scale_in
    grad_looked = jnp.pad(grad_looked, ((0, 0), (0, 1), (0, 0))).reshape(-1, D).astype(BF)
    code_part = across(
        jnp.concatenate([grad_logits, hit.astype(BF)]), jnp.concatenate([final_out, grad_looked])
    ).astype(BF)
    code_parts = 8
    code_part = (
        code_part.reshape(fsdp_size, code_parts, -1, dp_size, D // dp_size)
        .transpose(1, 3, 0, 2, 4)
        .reshape(code_parts, devices, -1, D // dp_size)
    )
    pairs = [pair for group in (*enc_pairs, *dec_pairs) for pair in group]
    weight_part = jnp.stack([across(*pair).astype(BF) for pair in pairs])
    weight_sum = sum_units(weight_part.reshape(len(pairs), devices, rows, D), 1)
    code_grad = sum_units(code_part, 2).reshape(code_table.shape)

    enc_sum, dec_sum = weight_sum[:12], weight_sum[12:]
    small_sum = lax.psum(jnp.concatenate([gain_part.reshape(-1), loss_part[None]]), AXES)
    loss_sum = small_sum[-1]
    gains_grad = lax.dynamic_slice_in_dim(small_sum[:-1].reshape(7, D), me * rows, rows, 1)
    gradients = (
        jnp.stack(
            [from_column_units(part) for part in (enc_sum[:3], dec_sum[:3], dec_sum[4:7])]
        ),
        jnp.stack([enc_sum[3], dec_sum[3], dec_sum[7]]),
        jnp.stack(
            [from_hidden_units(part, devices) for part in (enc_sum[4:8], dec_sum[8:12])]
        ),
        jnp.stack([part.reshape(-1, D) for part in (enc_sum[8:], dec_sum[12:])]),
        gains_grad,
        text_grad,
        code_grad,
    )
    square_part = sum((jnp.sum(gradient * gradient) for gradient in gradients))
    grad_norm = jnp.sqrt(lax.psum(square_part, AXES))
    factor = CLIP_NORM / jnp.maximum(grad_norm, CLIP_NORM)
    params = (mix_in, mix_out, ffn_up, ffn_down, norm_gains, text_table, code_table)
    firsts = (
        mix_in_first,
        mix_out_first,
        ffn_up_first,
        ffn_down_first,
        gains_first,
        text_first,
        code_first,
    )
    seconds = (
        mix_in_second,
        mix_out_second,
        ffn_up_second,
        ffn_down_second,
        gains_second,
        text_second,
        code_second,
    )
    updated = [
        adam_step(
            params[index],
            firsts[index],
            seconds[index],
            gradients[index] * factor,
            STEP_RATES[index],
        )
        for index in range(7)
    ]
    return (
        loss_sum,
        grad_norm,
        updated[0][0],
        updated[1][0],
        updated[2][0],
        updated[3][0],
        updated[4][0],
        updated[5][0],
        updated[6][0],
        updated[0][1],
        updated[1][1],
        updated[2][1],
        updated[3][1],
        updated[4][1],
        updated[5][1],
        updated[6][1],
        updated[0][2],
        updated[1][2],
        updated[2][2],
        updated[3][2],
        updated[4][2],
        updated[5][2],
        updated[6][2],
    )


def solution(mesh):
    return jax.shard_map(
        on_device,
        mesh=mesh,
        in_specs=(
            P(("dp", "fsdp"), None),
            P(("dp", "fsdp"), None),
            P(("dp", "fsdp"), None),
            P(("dp", "fsdp")),
            P(None, ("dp", "fsdp"), None),
            P(None, ("dp", "fsdp"), None),
            P(None, ("dp", "fsdp"), None),
            P(None, ("dp", "fsdp"), None),
            P(None, ("dp", "fsdp")),
            P(("dp", "fsdp"), None),
            P("fsdp", "dp"),
            P(None, ("dp", "fsdp"), None),
            P(None, ("dp", "fsdp"), None),
            P(None, ("dp", "fsdp"), None),
            P(None, ("dp", "fsdp"), None),
            P(None, ("dp", "fsdp")),
            P(("dp", "fsdp"), None),
            P("fsdp", "dp"),
            P(None, ("dp", "fsdp"), None),
            P(None, ("dp", "fsdp"), None),
            P(None, ("dp", "fsdp"), None),
            P(None, ("dp", "fsdp"), None),
            P(None, ("dp", "fsdp")),
            P(("dp", "fsdp"), None),
            P("fsdp", "dp"),
        ),
        out_specs=(
            P(),
            P(),
            P(None, ("dp", "fsdp"), None),
            P(None, ("dp", "fsdp"), None),
            P(None, ("dp", "fsdp"), None),
            P(None, ("dp", "fsdp"), None),
            P(None, ("dp", "fsdp")),
            P(("dp", "fsdp"), None),
            P("fsdp", "dp"),
            P(None, ("dp", "fsdp"), None),
            P(None, ("dp", "fsdp"), None),
            P(None, ("dp", "fsdp"), None),
            P(None, ("dp", "fsdp"), None),
            P(None, ("dp", "fsdp")),
            P(("dp", "fsdp"), None),
            P("fsdp", "dp"),
            P(None, ("dp", "fsdp"), None),
            P(None, ("dp", "fsdp"), None),
            P(None, ("dp", "fsdp"), None),
            P(None, ("dp", "fsdp"), None),
            P(None, ("dp", "fsdp")),
            P(("dp", "fsdp"), None),
            P("fsdp", "dp"),
        ),
        check_vma=False,
    )
```

```python
from functools import partial
import math

import jax
import jax.numpy as jnp
from jax import lax
from jax.experimental import pallas as pl
from jax.experimental.pallas import tpu as pltpu
from jax.sharding import PartitionSpec as P

D = 1024
HEADS = 16
HEAD = 64
VOCAB = 8192
TVOC = 16000
IMG_LEN = 256
TXT_LEN = 128
STEP = 5


SMOOTH = 0.1
BETA_ONE = 0.5
BETA_TWO = 0.5
WEIGHT_DECAY = 0.1
ADAM_EPS = 1e-08
CLIP_NORM = 0.02
MASKED = -1e30
STEP_RATES = (0.02, 0.15, 0.02, 0.01, 0.3, 0.02, 0.03)

BF = jnp.bfloat16
F32 = jnp.float32
AXES = ("dp", "fsdp")
MESH = pl.DeviceIdType.MESH
LAG = 2


DEC_INPUTS = (0, 0, 0, 1, 2, 3, 4, 4, 4, 4, 5, 6, 7, 8)
ENC_INPUTS = (0, 0, 1, 1, 1, 2, 3, 3, 3, 3, 4, 5, 6, 7)
CODE_UNITS = 8


def stepped(table, k):
    rises = [i for i in range(1, len(table)) if table[i] > table[i - 1]]
    return sum((k >= i).astype(jnp.int32) for i in rises)


def sum_kernel(
    Z, dec_x, dec_g, enc_x, enc_g, code_x, code_g, out_ref,
    dec_xs, dec_gs, enc_xs, enc_gs, code_xs, code_gs, to_core,
    own, from_core, held, from_x, from_y, all_x, all_y, kept, from_line,
    load_sem, code_sem, core_send, core_recv, one_send, one_recv, two_send, two_recv, line_send, line_recv,
):
    dec_units, enc_units = len(DEC_INPUTS), len(ENC_INPUTS)
    plain_units = dec_units + enc_units
    units = plain_units + CODE_UNITS
    depth = 2 * LAG
    dp, fs = lax.axis_index("dp"), lax.axis_index("fsdp")
    z, core = fs // 2, fs % 2
    x_mate, y_mate = dp + 1 - 2 * (dp % 2), (dp + 2) % 4
    across_dp = (x_mate + 2) % 4
    core_dev, x_dev, y_dev = (dp, fs + 1 - 2 * core), (x_mate, fs), (y_mate, fs)
    up_dev, down_dev = (dp, fs + 2), (dp, fs - 2)
    has_up, has_down = z < Z - 1, z > 0

    barrier = pltpu.get_barrier_semaphore()
    for device in (core_dev, x_dev, y_dev):
        pl.semaphore_signal(barrier, inc=1, device_id=device, device_id_type=MESH)

    @pl.when(has_up)
    def _():
        pl.semaphore_signal(barrier, inc=1, device_id=up_dev, device_id_type=MESH)

    @pl.when(has_down)
    def _():
        pl.semaphore_signal(barrier, inc=1, device_id=down_dev, device_id_type=MESH)

    pl.semaphore_wait(barrier, 3 + has_up.astype(jnp.int32) + has_down.astype(jnp.int32))
    half = Z // 2
    own_slots, held_slots, kept_slots = own.shape[0], held.shape[0], kept.shape[0]

    def add(a, b):
        return (a.astype(F32) + b.astype(F32)).astype(BF)

    def remote(src, dst, send, recv, device):
        return pltpu.make_async_remote_copy(
            src_ref=src, dst_ref=dst, send_sem=send, recv_sem=recv, device_id=device, device_id_type=MESH
        )

    def loads(k):
        slot, e = k % 2, k - dec_units
        dec_place, enc_place = stepped(DEC_INPUTS, k), stepped(ENC_INPUTS, e)

        def three(x, g, xs, gs, x_place, g_place):
            return [
                pltpu.make_async_copy(x.at[x_place, :, side], xs.at[slot, own_side], load_sem.at[own_side, slot])
                for own_side, side in ((0, core), (1, 1 - core))
            ] + [pltpu.make_async_copy(g.at[g_place], gs.at[slot], load_sem.at[2, slot])]

        return (
            (k < dec_units, three(dec_x, dec_g, dec_xs, dec_gs, dec_place, jnp.minimum(k, 10))),
            (
                (k >= dec_units) & (k < plain_units),
                three(enc_x, enc_g, enc_xs, enc_gs, enc_place, jnp.minimum(e, 10)),
            ),
        )

    def start_loads(k):
        for here, copies in loads(k):

            @pl.when(here)
            def _(copies=copies):
                for copy in copies:
                    copy.start()

    code_loads = [
        pltpu.make_async_copy(code_x, code_xs, code_sem.at[0]),
        pltpu.make_async_copy(code_g, code_gs, code_sem.at[1]),
    ]
    for copy in code_loads:
        copy.start()
    start_loads(jnp.int32(0))

    def core_copy(k):
        s = k % depth
        return remote(
            to_core.at[k % own_slots], from_core.at[s], core_send.at[s], core_recv.at[s], core_dev
        )

    def one_copies(k):
        s, block = k % depth, held.at[k % held_slots, across_dp]
        return (
            remote(block.at[pl.ds(0, half)], from_x.at[s], one_send.at[0, s], one_recv.at[0, s], x_dev),
            remote(block.at[pl.ds(half, Z - half)], from_y.at[s], one_send.at[1, s], one_recv.at[1, s], y_dev),
        )

    def two_copies(k):
        s, h = k % depth, k % held_slots
        return (
            remote(held.at[h, x_mate], all_x.at[s], two_send.at[0, s], two_recv.at[0, s], x_dev),
            remote(held.at[h, y_mate], all_y.at[s], two_send.at[1, s], two_recv.at[1, s], y_dev),
        )

    def up_block(step):
        return jnp.minimum(z + Z - step, Z - 1)

    def down_block(step):
        return jnp.maximum(z - Z + step, 0)

    def up_copy(k, step):
        s = k % depth
        return remote(
            kept.at[k % kept_slots, up_block(step)], from_line.at[0, step - 1, s],
            line_send.at[0, step - 1, s], line_recv.at[0, step - 1, s], up_dev,
        )

    def down_copy(k, step):
        s = k % depth
        return remote(
            kept.at[k % kept_slots, down_block(step)], from_line.at[1, step - 1, s],
            line_send.at[1, step - 1, s], line_recv.at[1, step - 1, s], down_dev,
        )

    def line_start(k, step):
        @pl.when(has_up)
        def _():
            up_copy(k, step).start()

        @pl.when(has_down)
        def _():
            down_copy(k, step).start()

    def line_wait(k, step):
        @pl.when(has_down)
        def _():
            up_copy(k, step).wait_recv()
            down_copy(k, step).wait_send()

        @pl.when(has_up)
        def _():
            down_copy(k, step).wait_recv()
            up_copy(k, step).wait_send()

    def product(xs, gs, slot, side, into):
        def rows(block, carry):
            value = xs[slot, side, pl.ds(block * Z, Z)].reshape(-1, xs.shape[-1])
            result = jnp.dot(value, gs[slot], preferred_element_type=F32).astype(BF)
            into[block] = result.reshape(into.shape[1:])
            return carry

        lax.fori_loop(0, 4, rows, 0)

    def code_product(k, side, into):
        value = code_gs[:, k - plain_units].reshape(-1, code_gs.shape[-1])
        width = into.shape[-1]

        def columns(place, carry):
            start = pl.multiple_of((2 * place + side) * width, width)
            result = jnp.dot(value, code_xs[:, pl.ds(start, width)], preferred_element_type=F32).astype(BF)
            into[:, place] = result.reshape(4, -1, width)
            return carry

        lax.fori_loop(0, Z, columns, 0)

    def begin(k):
        slot, o = k % 2, k % own_slots
        for (here, copies), xs, gs in zip(loads(k), (dec_xs, enc_xs), (dec_gs, enc_gs)):

            @pl.when(here)
            def _(copies=copies, xs=xs, gs=gs):
                for copy in copies:
                    copy.wait()
                start_loads(k + 1)
                product(xs, gs, slot, 1, to_core.at[o])
                core_copy(k).start()
                product(xs, gs, slot, 0, own.at[o])

        @pl.when(k == plain_units)
        def _():
            for copy in code_loads:
                copy.wait()

        @pl.when(k >= plain_units)
        def _():
            code_product(k, 1 - core, to_core.at[o])
            core_copy(k).start()
            code_product(k, core, own.at[o])

    def after_core(k):
        core_copy(k).wait()

        def one(block, carry):
            for q in range(Z):
                held[k % held_slots, block, q] = add(
                    own[k % own_slots, block, q], from_core[k % depth, block, q]
                )
            return carry

        lax.fori_loop(0, 4, one, 0)
        for copy in one_copies(k):
            copy.start()

    def after_one(k):
        s, h = k % depth, k % held_slots
        for copy in one_copies(k):
            copy.wait()
        for q in range(half):
            held[h, y_mate, q] = add(held[h, y_mate, q], from_x[s, q])
        for q in range(Z - half):
            held[h, x_mate, half + q] = add(held[h, x_mate, half + q], from_y[s, q])
        for copy in two_copies(k):
            copy.start()

    def after_two(k):
        s, h = k % depth, k % held_slots
        for copy in two_copies(k):
            copy.wait()
        for q in range(Z):
            kept[k % kept_slots, q] = (
                held[h, dp, q].astype(F32) + all_x[s, q].astype(F32) + all_y[s, q].astype(F32)
            ).astype(BF)
        line_start(k, 1)

    def along_line(step):
        def run(k):
            s, h = k % depth, k % kept_slots
            line_wait(k, step - 1)

            @pl.when(has_down & (z + Z - step <= Z - 1))
            def _():
                kept[h, up_block(step)] = add(kept[h, up_block(step)], from_line[0, step - 2, s])

            @pl.when(has_up & (z - Z + step >= 0))
            def _():
                kept[h, down_block(step)] = add(kept[h, down_block(step)], from_line[1, step - 2, s])

            line_start(k, step)

        return run

    def finish(k):
        s = k % depth
        line_wait(k, Z - 1)
        out_ref[k] = kept[k % kept_slots, z].astype(F32)

        @pl.when(has_down)
        def _():
            out_ref[k] = out_ref[k] + from_line[0, Z - 2, s].astype(F32)

        @pl.when(has_up)
        def _():
            out_ref[k] = out_ref[k] + from_line[1, Z - 2, s].astype(F32)

    stages = [begin, after_core, after_one, after_two]
    stages += [along_line(step) for step in range(2, Z)] + [finish]

    def loop_step(j, carry):
        for place in reversed(range(len(stages))):
            k = j - place * LAG

            @pl.when((k >= 0) & (k < units))
            def _(k=k, run=stages[place]):
                run(k)

        return carry

    lax.fori_loop(0, units + (len(stages) - 1) * LAG, loop_step, 0)


def sum_products(dec_x, dec_g, enc_x, enc_g, code_x, code_g, call_id):
    dp_size, fsdp_size = lax.axis_size("dp"), lax.axis_size("fsdp")
    devices, Z = dp_size * fsdp_size, fsdp_size // 2
    m = D // devices
    if dp_size != 4 or Z != 4 or m % 32:
        products = [matmul(dec_x[i], dec_g[min(k, 10)]) for k, i in enumerate(DEC_INPUTS)]
        products += [matmul(enc_x[i], enc_g[min(k, 10)]) for k, i in enumerate(ENC_INPUTS)]
        plain = jnp.stack(products).astype(BF).reshape(len(products), devices, m, D)
        code = matmul(code_g, code_x).astype(BF).reshape(dp_size, D // dp_size, fsdp_size, VOCAB // fsdp_size)
        code = code.transpose(0, 2, 1, 3).reshape(devices, D // dp_size, VOCAB // fsdp_size)
        plain = lax.psum_scatter(plain, AXES, scatter_dimension=1, tiled=True)
        code = lax.psum_scatter(code, AXES, scatter_dimension=0, tiled=True)
        return plain.reshape(-1, m, D).astype(F32), code.reshape(D // dp_size, -1).astype(F32)
    n, units = D, len(DEC_INPUTS) + len(ENC_INPUTS) + CODE_UNITS
    depth, half = 2 * LAG, Z // 2
    own_slots, held_slots, kept_slots = LAG + 1, 2 * LAG + 1, Z * LAG + 1
    dec_rows, enc_rows, code_rows = dec_x.shape[2], enc_x.shape[2], code_g.shape[1]
    dma = pltpu.SemaphoreType.DMA
    out = pl.pallas_call(
        partial(sum_kernel, Z),
        out_shape=jax.ShapeDtypeStruct((units, m, n), F32),
        in_specs=[pl.BlockSpec(memory_space=pl.ANY)] * 6,
        out_specs=pl.BlockSpec(memory_space=pltpu.VMEM),
        scratch_shapes=[
            pltpu.VMEM((2, 2, 4 * Z, m, dec_rows), BF),
            pltpu.VMEM((2, dec_rows, n), BF),
            pltpu.VMEM((2, 2, 4 * Z, m, enc_rows), BF),
            pltpu.VMEM((2, enc_rows, n), BF),
            pltpu.VMEM(code_x.shape, BF),
            pltpu.VMEM((4, CODE_UNITS, m, code_rows), BF),
            pltpu.VMEM((own_slots, 4, Z, m, n), BF),
            pltpu.VMEM((own_slots, 4, Z, m, n), BF),
            pltpu.VMEM((depth, 4, Z, m, n), BF),
            pltpu.VMEM((held_slots, 4, Z, m, n), BF),
            pltpu.VMEM((depth, half, m, n), BF),
            pltpu.VMEM((depth, Z - half, m, n), BF),
            pltpu.VMEM((depth, Z, m, n), BF),
            pltpu.VMEM((depth, Z, m, n), BF),
            pltpu.VMEM((kept_slots, Z, m, n), BF),
            pltpu.VMEM((2, Z - 1, depth, m, n), BF),
            dma((3, 2)),
            dma((2,)),
            dma((depth,)),
            dma((depth,)),
            dma((2, depth)),
            dma((2, depth)),
            dma((2, depth)),
            dma((2, depth)),
            dma((2, Z - 1, depth)),
            dma((2, Z - 1, depth)),
        ],
        compiler_params=pltpu.CompilerParams(
            collective_id=call_id, has_side_effects=True, vmem_limit_bytes=60 << 20
        ),
    )(
        dec_x.reshape(-1, 4 * Z, 2, m, dec_rows),
        dec_g,
        enc_x.reshape(-1, 4 * Z, 2, m, enc_rows),
        enc_g,
        code_x,
        code_g.reshape(4, CODE_UNITS, m, code_rows),
    )
    return out[:-CODE_UNITS], out[-CODE_UNITS:].reshape(-1, n)


def spread_kernel(
    tables, units, Z, table_ref, unit_ref, table_out, unit_out,
    own_sem, line_send, line_recv, square_send, square_recv, core_send, core_recv,
):
    dp, fs = lax.axis_index("dp"), lax.axis_index("fsdp")
    z, core = fs // 2, fs % 2
    x_mate, y_mate = dp + 1 - 2 * (dp % 2), (dp + 2) % 4
    across_dp = (x_mate + 2) % 4
    core_dev, x_dev, y_dev = (dp, fs + 1 - 2 * core), (x_mate, fs), (y_mate, fs)
    up_dev, down_dev = (dp, fs + 2), (dp, fs - 2)
    has_up, has_down = z < Z - 1, z > 0
    total, half = tables + units, Z // 2
    every = slice(None)
    table_rows, table_columns = table_out.shape[2] // tables, table_out.shape[3] // 4

    def at(is_table, k, dp_at, z_at, core_at, part=None):
        if is_table:
            size = table_rows if part is None else table_rows // 2
            rows = pl.ds(k * table_rows + (part or 0) * size, size)
            columns = every if isinstance(dp_at, slice) else pl.ds(dp_at * table_columns, table_columns)
            return table_out.at[z_at, core_at, rows, columns]
        if part is None:
            return unit_out.at[k - tables, dp_at, z_at, core_at]
        size = unit_out.shape[4] // 2
        return unit_out.at[k - tables, dp_at, z_at, core_at, pl.ds(part * size, size)]

    def remote(ref, send, recv, device):
        return pltpu.make_async_remote_copy(
            src_ref=ref, dst_ref=ref, send_sem=send, recv_sem=recv, device_id=device, device_id_type=MESH
        )

    own = (
        pltpu.make_async_copy(
            table_ref, table_out.at[z, core, :, pl.ds(dp * table_columns, table_columns)], own_sem.at[0]
        ),
        pltpu.make_async_copy(unit_ref, unit_out.at[:, dp, z, core], own_sem.at[1]),
    )
    for copy in own:
        copy.start()

    barrier = pltpu.get_barrier_semaphore()
    for device in (core_dev, x_dev, y_dev):
        pl.semaphore_signal(barrier, inc=1, device_id=device, device_id_type=MESH)

    @pl.when(has_up)
    def _():
        pl.semaphore_signal(barrier, inc=1, device_id=up_dev, device_id_type=MESH)

    @pl.when(has_down)
    def _():
        pl.semaphore_signal(barrier, inc=1, device_id=down_dev, device_id_type=MESH)

    for copy in own:
        copy.wait()
    pl.semaphore_wait(barrier, 3 + has_up.astype(jnp.int32) + has_down.astype(jnp.int32))

    def line_copies(view, k, step):
        s = step - 1
        return (
            (remote(view(jnp.maximum(z - s, 0)), line_send.at[0, s, k], line_recv.at[0, s, k], up_dev),
             has_up & (z >= s), has_down & (z >= s + 1)),
            (remote(view(jnp.minimum(z + s, Z - 1)), line_send.at[1, s, k], line_recv.at[1, s, k], down_dev),
             has_down & (z + s <= Z - 1), has_up & (z + s + 1 <= Z - 1)),
        )

    def line_start(view, k, step):
        for copy, sends, _ in line_copies(view, k, step):
            pl.when(sends)(copy.start)

    def line_wait(view, k, step):
        for copy, sends, receives in line_copies(view, k, step):
            pl.when(sends)(copy.wait_send)
            pl.when(receives)(copy.wait_recv)

    def to_core(ref, k, slot):
        return remote(ref, core_send.at[slot, k], core_recv.at[slot, k], core_dev)

    def square_copy(ref, k, slot):
        return remote(
            ref, square_send.at[slot, k], square_recv.at[slot, k], x_dev if slot % 2 == 0 else y_dev
        )

    def line_first(is_table):
        def view(k):
            return lambda place: at(is_table, k, dp, place, core)

        def row(k, dp_at):
            return at(is_table, k, dp_at, every, core)

        def ones(k):
            return square_copy(row(k, dp), k, 0), square_copy(row(k, dp), k, 1)

        def twos(k):
            return (
                square_copy(at(is_table, k, y_mate, pl.ds(0, half), core), k, 2),
                square_copy(at(is_table, k, x_mate, pl.ds(half, Z - half), core), k, 3),
            )

        def line(step):
            def run(k):
                if step > 1:
                    line_wait(view(k), k, step - 1)
                if step < Z:
                    line_start(view(k), k, step)
                else:
                    for copy in ones(k):
                        copy.start()
                    to_core(row(k, dp), k, 0).start()
            return run

        def after_one(k):
            for copy in ones(k):
                copy.wait()
            for copy in twos(k):
                copy.start()
            to_core(row(k, x_mate), k, 1).start()
            to_core(row(k, y_mate), k, 2).start()

        def after_two(k):
            for copy in twos(k):
                copy.wait()
            to_core(row(k, across_dp), k, 3).start()

        def finish(k):
            for slot in range(4):
                to_core(row(k, dp), k, slot).wait()

        return [line(step) for step in range(1, Z + 1)] + [after_one, after_two, finish]

    def square_first(is_table):
        def plane(k):
            return lambda place: at(is_table, k, every, place, core)

        def ones(k):
            ref = at(is_table, k, dp, z, core)
            return square_copy(ref, k, 0), square_copy(ref, k, 1)

        def twos(k):
            return (
                square_copy(at(is_table, k, y_mate, z, core, 0), k, 2),
                square_copy(at(is_table, k, x_mate, z, core, 1), k, 3),
            )

        def begin(k):
            for copy in ones(k):
                copy.start()

        def after_one(k):
            for copy in ones(k):
                copy.wait()
            for copy in twos(k):
                copy.start()

        def after_two(k):
            for copy in twos(k):
                copy.wait()
            line_start(plane(k), k, 1)
            to_core(plane(k)(z), k, z).start()

        def line(step):
            def run(k):
                line_wait(plane(k), k, step)
                if step + 1 < Z:
                    line_start(plane(k), k, step + 1)

                @pl.when(z - step >= 0)
                def _():
                    to_core(plane(k)(jnp.maximum(z - step, 0)), k, jnp.maximum(z - step, 0)).start()

                @pl.when(z + step <= Z - 1)
                def _():
                    to_core(plane(k)(jnp.minimum(z + step, Z - 1)), k, jnp.minimum(z + step, Z - 1)).start()
            return run

        def finish(k):
            for place in range(Z):
                to_core(plane(k)(place), k, place).wait()

        return [begin, after_one, after_two] + [line(step) for step in range(1, Z)] + [finish]

    forms = [(is_table, first, form(is_table))
             for is_table in (True, False) for first, form in ((True, line_first), (False, square_first))]
    n_stages = Z + 3

    def loop_step(j, carry):
        for place in reversed(range(n_stages)):
            k = j - place * LAG
            turn = k % 9
            by_line = (turn != 3) & (turn != 7)
            for is_table, first, stages in forms:
                here = (k >= 0) & (k < tables) if is_table else (k >= tables) & (k < total)
                here = here & (by_line if first else jnp.logical_not(by_line))

                @pl.when(here)
                def _(k=k, run=stages[place]):
                    run(k)

        return carry

    lax.fori_loop(0, total + (n_stages - 1) * LAG, loop_step, 0)


def spread(table, units, call_id):
    count, m, n = units.shape
    Z = lax.axis_size("fsdp") // 2
    if lax.axis_size("dp") != 4 or Z != 4 or m % 32:
        whole = lax.all_gather(lax.all_gather(table, "dp", axis=1, tiled=True), "fsdp", axis=0, tiled=True)
        return whole, lax.all_gather(units, AXES, axis=1, tiled=True)
    tables, dma = 8, pltpu.SemaphoreType.DMA
    total = tables + count
    whole, units = pl.pallas_call(
        partial(spread_kernel, tables, count, Z),
        out_shape=(
            jax.ShapeDtypeStruct((Z, 2, table.shape[0], 4 * table.shape[1]), BF),
            jax.ShapeDtypeStruct((count, 4, Z, 2, m, n), BF),
        ),
        in_specs=[pl.BlockSpec(memory_space=pl.ANY)] * 2,
        out_specs=[pl.BlockSpec(memory_space=pl.ANY)] * 2,
        scratch_shapes=[
            dma((2,)),
            dma((2, Z - 1, total)),
            dma((2, Z - 1, total)),
            dma((4, total)),
            dma((4, total)),
            dma((4, total)),
            dma((4, total)),
        ],
        compiler_params=pltpu.CompilerParams(collective_id=call_id, has_side_effects=True),
    )(table, units)
    return whole.reshape(-1, 4 * table.shape[1]), units.reshape(count, -1, n)


def exchange_kernel(size, inner, in_ref, out_ref, send_sem, recv_sem):
    me = lax.axis_index("dp") * inner + lax.axis_index("fsdp")

    def peer(i):
        other = lax.rem(me + i, size)
        return other, (other // inner, lax.rem(other, inner))

    barrier = pltpu.get_barrier_semaphore()

    def greet(i, carry):
        pl.semaphore_signal(barrier, inc=1, device_id=peer(i)[1], device_id_type=MESH)
        return carry

    def copy(i):
        other, device = peer(i)
        return pltpu.make_async_remote_copy(
            src_ref=in_ref.at[other], dst_ref=out_ref.at[me], send_sem=send_sem.at[i],
            recv_sem=recv_sem.at[i], device_id=device, device_id_type=MESH,
        )

    def begin(i, carry):
        copy(i).start()
        return carry

    def end(i, carry):
        copy(i).wait()
        return carry

    lax.fori_loop(1, size, greet, 0)
    out_ref[me] = in_ref[me]
    pl.semaphore_wait(barrier, size - 1)
    lax.fori_loop(1, size, begin, 0)
    lax.fori_loop(1, size, end, 0)


def exchange(blocks, call_id):
    size, inner = blocks.shape[0], lax.axis_size("fsdp")
    return pl.pallas_call(
        partial(exchange_kernel, size, inner),
        out_shape=jax.ShapeDtypeStruct(blocks.shape, F32),
        in_specs=[pl.BlockSpec(memory_space=pltpu.VMEM)],
        out_specs=pl.BlockSpec(memory_space=pltpu.VMEM),
        scratch_shapes=[pltpu.SemaphoreType.DMA((size,)), pltpu.SemaphoreType.DMA((size,))],
        compiler_params=pltpu.CompilerParams(collective_id=call_id, has_side_effects=True),
    )(blocks)


def tiles(values, count):
    padded = jnp.pad(values, ((0, 1024 - values.shape[0]),)).reshape(1, 8, 128)
    return jnp.broadcast_to(padded, (count, 8, 128))


def layer_norm(stream, gain):
    centred = stream - jnp.mean(stream, axis=-1, keepdims=True)
    return centred * lax.rsqrt(jnp.mean(centred * centred, axis=-1, keepdims=True) + 1e-05) * gain


def norm_back(stream, gain, grad_out):
    _, pullback = jax.vjp(layer_norm, stream, gain)
    return pullback(grad_out)


def positions(length, width):
    position = jnp.arange(length, dtype=jnp.float32)[:, None]
    speeds = jnp.exp(
        -math.log(10000.0) * 2.0 * jnp.arange(width // 2, dtype=jnp.float32)[None, :] / width
    )
    return jnp.concatenate([jnp.sin(position * speeds), jnp.cos(position * speeds)], axis=1)


def matmul(first_op, second_op):
    return jnp.dot(first_op, second_op, preferred_element_type=jnp.float32)


def across(first_op, second_op):
    return lax.dot_general(
        first_op, second_op, (((0,), (0,)), ((), ())), preferred_element_type=jnp.float32
    )


def against(first_op, second_op):
    return lax.dot_general(
        first_op, second_op, (((1,), (1,)), ((), ())), preferred_element_type=jnp.float32
    )


def heads_first(matrix, blocks):
    return matrix.reshape(blocks, -1, HEADS, HEAD).transpose(0, 2, 1, 3)


def heads_last(array):
    return array.transpose(0, 2, 1, 3).reshape(-1, HEADS * HEAD)


def attention(queries, keys_in, values, visible):
    scores = jnp.einsum(
        "bhqd,bhkd->bhqk", queries, keys_in, preferred_element_type=F32
    ) * HEAD ** (-0.5)
    scores = jnp.where(visible[:, None], scores, MASKED)
    weights = jnp.exp(scores - jnp.max(scores, axis=-1, keepdims=True))
    shares = weights / jnp.sum(weights, axis=-1, keepdims=True)
    low = shares.astype(BF)
    attended = jnp.einsum("bhqk,bhkd->bhqd", low, values, preferred_element_type=F32)
    return heads_last(attended.astype(BF)), low


def attention_back(queries, keys_in, values, shares, grad_mixed):
    grad_heads = heads_first(grad_mixed, queries.shape[0])
    grad_shares = jnp.einsum(
        "bhqd,bhkd->bhqk", grad_heads, values, preferred_element_type=F32
    )
    wide = shares.astype(F32)
    grad_scores = (
        wide * (grad_shares - jnp.sum(wide * grad_shares, axis=-1, keepdims=True))
    ).astype(BF)
    grad_query = jnp.einsum(
        "bhqk,bhkd->bhqd", grad_scores, keys_in, preferred_element_type=F32
    ) * HEAD ** (-0.5)
    grad_keys = jnp.einsum(
        "bhqk,bhqd->bhkd", grad_scores, queries, preferred_element_type=F32
    ) * HEAD ** (-0.5)
    grad_values = jnp.einsum(
        "bhqk,bhqd->bhkd", shares, grad_heads, preferred_element_type=F32
    )
    return grad_query, grad_keys, grad_values


def layer_forward(stream, weights, gains, self_visible, memory, cross_visible):
    project, mix_out, cross, cross_out, ffn_up, ffn_down = weights
    blocks = self_visible.shape[0]
    stored = {"stream": stream}
    normed = layer_norm(stream, gains[0]).astype(BF)
    queries, keys_in, values = [
        heads_first(matmul(normed, project[i]).astype(BF), blocks) for i in range(3)
    ]
    attended, shares = attention(queries, keys_in, values, self_visible)
    stream = stream + matmul(attended, mix_out)
    stored.update(
        normed=normed, self_attention=(queries, keys_in, values, shares), attended=attended, after_self=stream
    )
    if memory is not None:
        cross_in = layer_norm(stream, gains[1]).astype(BF)
        cross_query = heads_first(matmul(cross_in, cross[0]).astype(BF), 1)
        memory_keys = heads_first(matmul(memory, cross[1]).astype(BF), 1)
        memory_values = heads_first(matmul(memory, cross[2]).astype(BF), 1)
        cross_mixed, cross_shares = attention(cross_query, memory_keys, memory_values, cross_visible)
        stream = stream + matmul(cross_mixed, cross_out)
        stored.update(
            cross_in=cross_in,
            cross_attention=(cross_query, memory_keys, memory_values, cross_shares),
            cross_mixed=cross_mixed,
        )
    stored["before_ffn"] = stream
    ffn_in = layer_norm(stream, gains[-2]).astype(BF)
    hidden_pre = [matmul(ffn_in, up) for up in ffn_up]
    hidden = [jax.nn.gelu(pre, approximate=True).astype(BF) for pre in hidden_pre]
    for low, down in zip(hidden, ffn_down):
        stream = stream + matmul(low, down)
    stored.update(ffn_in=ffn_in, hidden_pre=hidden_pre, hidden=hidden, before_final=stream)
    return layer_norm(stream, gains[-1]).astype(BF), stored


def layer_backward(grad_final, weights, gains, stored, memory):
    project, mix_out, cross, cross_out, ffn_up, ffn_down = weights
    gain_grads = [None] * len(gains)
    grad_stream, gain_grads[-1] = norm_back(stored["before_final"], gains[-1], grad_final)
    ffn_low = grad_stream.astype(BF)
    grad_pres = []
    grad_ffn = 0.0
    for pre, up, down in zip(stored["hidden_pre"], ffn_up, ffn_down):
        _, gelu_pull = jax.vjp(partial(jax.nn.gelu, approximate=True), pre)
        grad_pres.append(gelu_pull(against(ffn_low, down))[0].astype(BF))
        grad_ffn = grad_ffn + against(grad_pres[-1], up)
    grad_normed, gain_grads[-2] = norm_back(stored["before_ffn"], gains[-2], grad_ffn)
    grad_stream = grad_stream + grad_normed
    cross_inputs, cross_grads, memory_grads = [], [], []
    grad_memory = None
    if memory is not None:
        cross_low = grad_stream.astype(BF)
        grad_mixed = against(cross_low, cross_out).astype(BF)
        grads = [
            heads_last(grad.astype(BF)) for grad in attention_back(*stored["cross_attention"], grad_mixed)
        ]
        cross_inputs = [stored["cross_in"], stored["cross_mixed"]]
        cross_grads = [grads[0], cross_low]
        memory_grads = grads[1:]
        grad_memory = against(grads[1], cross[1]) + against(grads[2], cross[2])
        grad_normed, gain_grads[1] = norm_back(
            stored["after_self"], gains[1], against(grads[0], cross[0])
        )
        grad_stream = grad_stream + grad_normed
    self_low = grad_stream.astype(BF)
    grad_mixed = against(self_low, mix_out).astype(BF)
    grads = [
        heads_last(grad.astype(BF)) for grad in attention_back(*stored["self_attention"], grad_mixed)
    ]
    grad_normed, gain_grads[0] = norm_back(
        stored["stream"],
        gains[0],
        sum(against(grads[i], project[i]) for i in range(3)),
    )
    grad_stream = grad_stream + grad_normed
    inputs = [stored["normed"], stored["attended"], *cross_inputs, stored["ffn_in"], *stored["hidden"]]
    outputs = [*grads, self_low, *cross_grads, *grad_pres, ffn_low]
    parts = (inputs, outputs) if memory is None else (inputs, outputs, memory_grads)
    return grad_stream, grad_memory, gain_grads, parts


def adam_step(weight, moment_one, second, gradient, rate):
    moment_one = BETA_ONE * moment_one + (1.0 - BETA_ONE) * gradient
    second = BETA_TWO * second + (1.0 - BETA_TWO) * gradient * gradient
    first_hat = moment_one / (1.0 - BETA_ONE**STEP)
    second_hat = second / (1.0 - BETA_TWO**STEP)
    weight = weight - rate * (first_hat / (jnp.sqrt(second_hat) + ADAM_EPS) + WEIGHT_DECAY * weight)
    return (weight, moment_one, second)


def column_units(matrix):
    return matrix.reshape(matrix.shape[0], -1, D).transpose(1, 0, 2)


def from_column_units(units):
    return units.transpose(1, 0, 2).reshape(units.shape[1], -1)


def hidden_units(matrix, devices):
    rows, width = matrix.shape
    return (
        matrix.reshape(rows, devices, 4, width // devices // 4)
        .transpose(2, 0, 1, 3)
        .reshape(4, rows, width // 4)
    )


def from_hidden_units(units, devices):
    quarters, rows, width = units.shape
    return (
        units.reshape(quarters, rows, devices, width // devices)
        .transpose(1, 2, 0, 3)
        .reshape(rows, quarters * width)
    )


def on_device(
    text_ids,
    text_segments,
    codes,
    caption_of,
    mix_in,
    mix_out,
    ffn_up,
    ffn_down,
    norm_gains,
    text_table,
    code_table,
    mix_in_first,
    mix_out_first,
    ffn_up_first,
    ffn_down_first,
    gains_first,
    text_first,
    code_first,
    mix_in_second,
    mix_out_second,
    ffn_up_second,
    ffn_down_second,
    gains_second,
    text_second,
    code_second,
):
    image_count = codes.shape[0]
    dp_size, fsdp_size = lax.axis_size("dp"), lax.axis_size("fsdp")
    devices = dp_size * fsdp_size
    me = lax.axis_index("dp") * fsdp_size + lax.axis_index("fsdp")
    token_total = image_count * IMG_LEN * devices
    inverse = 1.0 / token_total
    scale_in = math.sqrt(D)
    rows = mix_in.shape[1]
    segments = text_segments[0]
    text_visible = (segments[:, None] == segments[None, :])[None]
    place = jnp.arange(IMG_LEN)
    self_visible = jnp.broadcast_to(
        place[None, :] <= place[:, None], (image_count, IMG_LEN, IMG_LEN)
    )
    wanted = jnp.repeat(caption_of, IMG_LEN)
    cross_visible = (segments[None, :] == wanted[:, None])[None]

    small = tiles(jnp.concatenate([text_ids[0].astype(F32), norm_gains.reshape(-1)]), devices)
    small = exchange(small, 3).reshape(devices, 1024)[:, : TXT_LEN + 7 * norm_gains.shape[1]]
    all_ids = small[:, :TXT_LEN].astype(jnp.int32).reshape(-1)
    gains = small[:, TXT_LEN:].reshape(devices, 7, -1).transpose(1, 0, 2).reshape(7, D)
    gains = gains.astype(BF).astype(F32)

    base = me * text_table.shape[0]
    owned = (all_ids[:, None] - base == jnp.arange(text_table.shape[0])[None, :]).astype(BF)
    looked = matmul(owned, text_table.astype(BF)).astype(BF)
    text_rows = lax.psum_scatter(looked, AXES, scatter_dimension=0, tiled=True)

    def layer_units(which):
        return [
            column_units(mix_in[which]),
            mix_out[which][None],
            hidden_units(ffn_up[min(which, 1)], devices),
            ffn_down[min(which, 1)].reshape(4, rows, D),
        ]

    shards = layer_units(0) + layer_units(1)[:2] + layer_units(2)
    code_full, units = spread(code_table.astype(BF), jnp.concatenate(shards).astype(BF), 4)
    enc_units, self_units, late_units = units[:12], units[12:16], units[16:]
    enc_weights = (enc_units[:3], enc_units[3], None, None, enc_units[4:8], enc_units[8:])
    dec_weights = (
        self_units[:3], self_units[3], late_units[:3], late_units[3], late_units[4:8], late_units[8:]
    )

    text_in = text_rows.astype(F32) * scale_in + positions(TXT_LEN, D)
    enc_gains = [gains[i] for i in range(3)]
    dec_gains = [gains[i] for i in range(3, 7)]
    memory, enc_stored = layer_forward(text_in, enc_weights, enc_gains, text_visible, None, None)

    image_rows = code_full[codes].astype(F32) * scale_in
    shifted = jnp.concatenate([jnp.zeros_like(image_rows[:, :1]), image_rows[:, :-1]], axis=1)
    image_in = (shifted + positions(IMG_LEN, D)[None]).reshape(-1, D)
    final_out, dec_stored = layer_forward(
        image_in, dec_weights, dec_gains, self_visible, memory, cross_visible
    )

    targets = codes.reshape(-1)
    logits = against(final_out, code_full)
    hit = targets[:, None] == jnp.arange(VOCAB)[None, :]
    top = jnp.max(logits, axis=1, keepdims=True)
    log_total = top + jnp.log(jnp.sum(jnp.exp(logits - top), axis=1, keepdims=True))
    weighted = jnp.sum(
        logits * jnp.where(hit, 1.0 - SMOOTH + SMOOTH / VOCAB, SMOOTH / VOCAB), axis=1, keepdims=True
    )
    loss_part = jnp.sum(log_total - weighted)
    grad_logits = (
        (jnp.exp(logits - log_total) - jnp.where(hit, 1.0 - SMOOTH, 0.0) - SMOOTH / VOCAB) * inverse
    ).astype(BF)
    grad_final = matmul(grad_logits, code_full)

    grad_image, grad_memory, dec_gain_grads, dec_parts = layer_backward(
        grad_final, dec_weights, dec_gains, dec_stored, memory
    )
    grad_text, _, enc_gain_grads, enc_parts = layer_backward(
        grad_memory, enc_weights, enc_gains, enc_stored, None
    )
    gain_part = jnp.stack(enc_gain_grads + dec_gain_grads)

    grad_rows = lax.all_gather((grad_text * scale_in).astype(BF), AXES, axis=0, tiled=True)
    text_grad = across(owned, grad_rows)

    grad_looked = grad_image.reshape(image_count, IMG_LEN, D)[:, 1:] * scale_in
    grad_looked = jnp.pad(grad_looked, ((0, 0), (0, 1), (0, 0))).reshape(-1, D).astype(BF)
    code_x = jnp.concatenate([grad_logits, hit.astype(BF)])
    code_g = jnp.concatenate([final_out, grad_looked]).T

    def inputs(values):
        return jnp.stack([value.T for value in values])

    def gradients_of(values):
        return jnp.stack(values)

    enc_x, enc_g = enc_parts
    dec_x, dec_g, memory_g = dec_parts
    plain_sum, code_sum = sum_products(
        inputs(dec_x),
        gradients_of(dec_g),
        inputs([memory] + enc_x),
        gradients_of(memory_g + enc_g),
        code_x,
        code_g,
        1,
    )
    code_grad = code_sum.T
    dec_sum, enc_sum = plain_sum[:14], plain_sum[14:]

    gain_blocks = gain_part.reshape(7, devices, rows).transpose(1, 0, 2).reshape(devices, 7 * rows)
    gain_blocks = jnp.concatenate([gain_blocks, jnp.full((devices, 1), loss_part)], axis=1)
    gain_blocks = jnp.pad(gain_blocks, ((0, 0), (0, 1024 - gain_blocks.shape[1])))
    small_sum = jnp.sum(exchange(gain_blocks.reshape(devices, 8, 128), 5), axis=0).reshape(-1)
    loss_sum = small_sum[7 * rows]
    gains_grad = small_sum[: 7 * rows].reshape(7, rows)
    gradients = (
        jnp.stack(
            [
                from_column_units(part)
                for part in (enc_sum[2:5], dec_sum[:3], jnp.concatenate([dec_sum[4:5], enc_sum[:2]]))
            ]
        ),
        jnp.stack([enc_sum[5], dec_sum[3], dec_sum[5]]),
        jnp.stack([from_hidden_units(part, devices) for part in (enc_sum[6:10], dec_sum[6:10])]),
        jnp.stack([part.reshape(-1, D) for part in (enc_sum[10:], dec_sum[10:])]),
        gains_grad,
        text_grad,
        code_grad,
    )
    square_part = sum((jnp.sum(gradient * gradient) for gradient in gradients))
    squares = exchange(tiles(square_part[None], devices), 6)[:, 0, 0]
    grad_norm = jnp.sqrt(jnp.sum(squares))
    factor = CLIP_NORM / jnp.maximum(grad_norm, CLIP_NORM)
    params = (mix_in, mix_out, ffn_up, ffn_down, norm_gains, text_table, code_table)
    firsts = (
        mix_in_first,
        mix_out_first,
        ffn_up_first,
        ffn_down_first,
        gains_first,
        text_first,
        code_first,
    )
    seconds = (
        mix_in_second,
        mix_out_second,
        ffn_up_second,
        ffn_down_second,
        gains_second,
        text_second,
        code_second,
    )
    updated = [
        adam_step(
            params[index],
            firsts[index],
            seconds[index],
            gradients[index] * factor,
            STEP_RATES[index],
        )
        for index in range(7)
    ]
    return (
        loss_sum,
        grad_norm,
        updated[0][0],
        updated[1][0],
        updated[2][0],
        updated[3][0],
        updated[4][0],
        updated[5][0],
        updated[6][0],
        updated[0][1],
        updated[1][1],
        updated[2][1],
        updated[3][1],
        updated[4][1],
        updated[5][1],
        updated[6][1],
        updated[0][2],
        updated[1][2],
        updated[2][2],
        updated[3][2],
        updated[4][2],
        updated[5][2],
        updated[6][2],
    )


def solution(mesh):
    return jax.shard_map(
        on_device,
        mesh=mesh,
        in_specs=(
            P(("dp", "fsdp"), None),
            P(("dp", "fsdp"), None),
            P(("dp", "fsdp"), None),
            P(("dp", "fsdp")),
            P(None, ("dp", "fsdp"), None),
            P(None, ("dp", "fsdp"), None),
            P(None, ("dp", "fsdp"), None),
            P(None, ("dp", "fsdp"), None),
            P(None, ("dp", "fsdp")),
            P(("dp", "fsdp"), None),
            P("fsdp", "dp"),
            P(None, ("dp", "fsdp"), None),
            P(None, ("dp", "fsdp"), None),
            P(None, ("dp", "fsdp"), None),
            P(None, ("dp", "fsdp"), None),
            P(None, ("dp", "fsdp")),
            P(("dp", "fsdp"), None),
            P("fsdp", "dp"),
            P(None, ("dp", "fsdp"), None),
            P(None, ("dp", "fsdp"), None),
            P(None, ("dp", "fsdp"), None),
            P(None, ("dp", "fsdp"), None),
            P(None, ("dp", "fsdp")),
            P(("dp", "fsdp"), None),
            P("fsdp", "dp"),
        ),
        out_specs=(
            P(),
            P(),
            P(None, ("dp", "fsdp"), None),
            P(None, ("dp", "fsdp"), None),
            P(None, ("dp", "fsdp"), None),
            P(None, ("dp", "fsdp"), None),
            P(None, ("dp", "fsdp")),
            P(("dp", "fsdp"), None),
            P("fsdp", "dp"),
            P(None, ("dp", "fsdp"), None),
            P(None, ("dp", "fsdp"), None),
            P(None, ("dp", "fsdp"), None),
            P(None, ("dp", "fsdp"), None),
            P(None, ("dp", "fsdp")),
            P(("dp", "fsdp"), None),
            P("fsdp", "dp"),
            P(None, ("dp", "fsdp"), None),
            P(None, ("dp", "fsdp"), None),
            P(None, ("dp", "fsdp"), None),
            P(None, ("dp", "fsdp"), None),
            P(None, ("dp", "fsdp")),
            P(("dp", "fsdp"), None),
            P("fsdp", "dp"),
        ),
        check_vma=False,
    )
```

```python
from functools import partial
import math

import jax
import jax.numpy as jnp
from jax import lax
from jax.experimental import pallas as pl
from jax.experimental.pallas import tpu as pltpu
from jax.sharding import PartitionSpec as P

D = 1024
HEADS = 16
HEAD = 64
VOCAB = 8192
TVOC = 16000
IMG_LEN = 256
TXT_LEN = 128
STEP = 5


SMOOTH = 0.1
BETA_ONE = 0.5
BETA_TWO = 0.5
WEIGHT_DECAY = 0.1
ADAM_EPS = 1e-08
CLIP_NORM = 0.02
MASKED = -1e30
STEP_RATES = (0.02, 0.15, 0.02, 0.01, 0.3, 0.02, 0.03)

BF = jnp.bfloat16
F32 = jnp.float32
AXES = ("dp", "fsdp")
MESH = pl.DeviceIdType.MESH
LAG = 2


DEC_INPUTS = (0, 0, 0, 1, 2, 3, 4, 4, 4, 4, 5, 6, 7, 8)
ENC_INPUTS = (0, 0, 1, 1, 1, 2, 3, 3, 3, 3, 4, 5, 6, 7)
CODE_UNITS = 8


def sum_kernel(Z, *refs):
    dec_x, refs = refs[:9], refs[9:]
    dec_g, refs = refs[:11], refs[11:]
    enc_x, refs = refs[:8], refs[8:]
    enc_g, refs = refs[:11], refs[11:]
    (
        code_x, targets, code_g, look_g, out_ref,
        dec_xs, dec_gs, dec_turned, enc_xs, enc_gs, enc_turned, code_xs, code_loaded, code_gs, to_core,
        own, from_core, held, from_x, from_y, all_x, all_y, kept, from_line,
        load_sem, code_sem, core_send, core_recv, one_send, one_recv, two_send, two_recv, line_send, line_recv,
    ) = refs
    dec_units, enc_units = len(DEC_INPUTS), len(ENC_INPUTS)
    plain_units = dec_units + enc_units
    units = plain_units + CODE_UNITS
    depth = 2 * LAG
    dp, fs = lax.axis_index("dp"), lax.axis_index("fsdp")
    z, core = fs // 2, fs % 2
    x_mate, y_mate = dp + 1 - 2 * (dp % 2), (dp + 2) % 4
    across_dp = (x_mate + 2) % 4
    core_dev, x_dev, y_dev = (dp, fs + 1 - 2 * core), (x_mate, fs), (y_mate, fs)
    up_dev, down_dev = (dp, fs + 2), (dp, fs - 2)
    has_up, has_down = z < Z - 1, z > 0

    barrier = pltpu.get_barrier_semaphore()
    for device in (core_dev, x_dev, y_dev):
        pl.semaphore_signal(barrier, inc=1, device_id=device, device_id_type=MESH)

    @pl.when(has_up)
    def _():
        pl.semaphore_signal(barrier, inc=1, device_id=up_dev, device_id_type=MESH)

    @pl.when(has_down)
    def _():
        pl.semaphore_signal(barrier, inc=1, device_id=down_dev, device_id_type=MESH)

    pl.semaphore_wait(barrier, 3 + has_up.astype(jnp.int32) + has_down.astype(jnp.int32))
    half = Z // 2
    own_slots, held_slots, kept_slots = own.shape[0], held.shape[0], kept.shape[0]

    def add(a, b):
        return (a.astype(F32) + b.astype(F32)).astype(BF)

    def remote(src, dst, send, recv, device):
        return pltpu.make_async_remote_copy(
            src_ref=src, dst_ref=dst, send_sem=send, recv_sem=recv, device_id=device, device_id_type=MESH
        )

    def pair(x, g, xs, gs, slot):
        return (
            pltpu.make_async_copy(x, xs.at[slot], load_sem.at[0, slot]),
            pltpu.make_async_copy(g, gs.at[slot], load_sem.at[1, slot]),
        )

    def start_loads(k):
        for i, place in enumerate(DEC_INPUTS):

            @pl.when(k == i)
            def _(i=i, place=place):
                for copy in pair(dec_x[place], dec_g[min(i, 10)], dec_xs, dec_gs, i % 2):
                    copy.start()

        for i, place in enumerate(ENC_INPUTS):

            @pl.when(k == dec_units + i)
            def _(i=i, place=place):
                for copy in pair(enc_x[place], enc_g[min(i, 10)], enc_xs, enc_gs, (dec_units + i) % 2):
                    copy.start()

    code_rows = code_x.shape[0]
    code_loads = [
        pltpu.make_async_copy(code_x, code_xs.at[pl.ds(0, code_rows)], code_sem.at[0]),
        pltpu.make_async_copy(code_g, code_loaded.at[0], code_sem.at[1]),
        pltpu.make_async_copy(look_g, code_loaded.at[1], code_sem.at[2]),
    ]
    for copy in code_loads:
        copy.start()
    start_loads(jnp.int32(0))

    def core_copy(k):
        s = k % depth
        return remote(
            to_core.at[k % own_slots], from_core.at[s], core_send.at[s], core_recv.at[s], core_dev
        )

    def one_copies(k):
        s, block = k % depth, held.at[k % held_slots, across_dp]
        return (
            remote(block.at[pl.ds(0, half)], from_x.at[s], one_send.at[0, s], one_recv.at[0, s], x_dev),
            remote(block.at[pl.ds(half, Z - half)], from_y.at[s], one_send.at[1, s], one_recv.at[1, s], y_dev),
        )

    def two_copies(k):
        s, h = k % depth, k % held_slots
        return (
            remote(held.at[h, x_mate], all_x.at[s], two_send.at[0, s], two_recv.at[0, s], x_dev),
            remote(held.at[h, y_mate], all_y.at[s], two_send.at[1, s], two_recv.at[1, s], y_dev),
        )

    def up_block(step):
        return jnp.minimum(z + Z - step, Z - 1)

    def down_block(step):
        return jnp.maximum(z - Z + step, 0)

    def up_copy(k, step):
        s = k % depth
        return remote(
            kept.at[k % kept_slots, up_block(step)], from_line.at[0, step - 1, s],
            line_send.at[0, step - 1, s], line_recv.at[0, step - 1, s], up_dev,
        )

    def down_copy(k, step):
        s = k % depth
        return remote(
            kept.at[k % kept_slots, down_block(step)], from_line.at[1, step - 1, s],
            line_send.at[1, step - 1, s], line_recv.at[1, step - 1, s], down_dev,
        )

    def line_start(k, step):
        @pl.when(has_up)
        def _():
            up_copy(k, step).start()

        @pl.when(has_down)
        def _():
            down_copy(k, step).start()

    def line_wait(k, step):
        @pl.when(has_down)
        def _():
            up_copy(k, step).wait_recv()
            down_copy(k, step).wait_send()

        @pl.when(has_up)
        def _():
            down_copy(k, step).wait_recv()
            up_copy(k, step).wait_send()

    def turn(xs, slot, turned):
        size = 256

        def columns(i, carry):
            part = xs[slot, :, pl.ds(pl.multiple_of(i * size, size), size)].T
            count = size // (2 * turned.shape[2])
            turned[pl.ds(i * count, count)] = part.reshape(count, *turned.shape[1:])
            return carry

        lax.fori_loop(0, xs.shape[2] // size, columns, 0)

    def product(turned, gs, slot, side, into):
        def rows(block, carry):
            value = turned[pl.ds(block * Z, Z), side].reshape(-1, turned.shape[-1])
            result = jnp.dot(value, gs[slot], preferred_element_type=F32).astype(BF)
            into[block] = result.reshape(into.shape[1:])
            return carry

        lax.fori_loop(0, 4, rows, 0)

    def code_inputs():
        for copy in code_loads:
            copy.wait()
        size = D // 4
        for half_rows in range(2):

            def turn_columns(i, carry, half_rows=half_rows):
                part = code_loaded[half_rows, :, pl.ds(pl.multiple_of(i * size, size), size)].T
                code_gs[i, :, :, pl.ds(half_rows * code_rows, code_rows)] = part.reshape(
                    CODE_UNITS, size // CODE_UNITS, code_rows
                )
                return carry

            lax.fori_loop(0, 4, turn_columns, 0)

        width = 512

        def hits(i, carry):
            start = pl.multiple_of(i * width, width)
            column = lax.broadcasted_iota(jnp.int32, (code_rows, width), 1) + i * width
            code_xs[pl.ds(code_rows, code_rows), pl.ds(start, width)] = jnp.where(
                targets[...] == column, 1.0, 0.0
            ).astype(BF)
            return carry

        lax.fori_loop(0, VOCAB // width, hits, 0)

    def code_product(k, side, into):
        value = code_gs[:, k - plain_units].reshape(-1, code_gs.shape[-1])
        width = into.shape[-1]

        def columns(place, carry):
            start = pl.multiple_of((2 * place + side) * width, width)
            result = jnp.dot(value, code_xs[:, pl.ds(start, width)], preferred_element_type=F32).astype(BF)
            into[:, place] = result.reshape(4, -1, width)
            return carry

        lax.fori_loop(0, Z, columns, 0)

    def begin(k):
        slot, o = k % 2, k % own_slots
        for here, x, g, xs, gs, turned in (
            (k < dec_units, dec_x[0], dec_g[0], dec_xs, dec_gs, dec_turned),
            ((k >= dec_units) & (k < plain_units), enc_x[0], enc_g[0], enc_xs, enc_gs, enc_turned),
        ):

            @pl.when(here)
            def _(x=x, g=g, xs=xs, gs=gs, turned=turned):
                for copy in pair(x, g, xs, gs, slot):
                    copy.wait()
                start_loads(k + 1)
                turn(xs, slot, turned)
                product(turned, gs, slot, 1 - core, to_core.at[o])
                core_copy(k).start()
                product(turned, gs, slot, core, own.at[o])

        @pl.when(k == dec_units)
        def _():
            code_inputs()

        @pl.when(k >= plain_units)
        def _():
            code_product(k, 1 - core, to_core.at[o])
            core_copy(k).start()
            code_product(k, core, own.at[o])

    def after_core(k):
        core_copy(k).wait()

        def one(block, carry):
            for q in range(Z):
                held[k % held_slots, block, q] = add(
                    own[k % own_slots, block, q], from_core[k % depth, block, q]
                )
            return carry

        lax.fori_loop(0, 4, one, 0)
        for copy in one_copies(k):
            copy.start()

    def after_one(k):
        s, h = k % depth, k % held_slots
        for copy in one_copies(k):
            copy.wait()
        for q in range(half):
            held[h, y_mate, q] = add(held[h, y_mate, q], from_x[s, q])
        for q in range(Z - half):
            held[h, x_mate, half + q] = add(held[h, x_mate, half + q], from_y[s, q])
        for copy in two_copies(k):
            copy.start()

    def after_two(k):
        s, h = k % depth, k % held_slots
        for copy in two_copies(k):
            copy.wait()
        for q in range(Z):
            kept[k % kept_slots, q] = (
                held[h, dp, q].astype(F32) + all_x[s, q].astype(F32) + all_y[s, q].astype(F32)
            ).astype(BF)
        line_start(k, 1)

    def along_line(step):
        def run(k):
            s, h = k % depth, k % kept_slots
            line_wait(k, step - 1)

            @pl.when(has_down & (z + Z - step <= Z - 1))
            def _():
                kept[h, up_block(step)] = add(kept[h, up_block(step)], from_line[0, step - 2, s])

            @pl.when(has_up & (z - Z + step >= 0))
            def _():
                kept[h, down_block(step)] = add(kept[h, down_block(step)], from_line[1, step - 2, s])

            line_start(k, step)

        return run

    def finish(k):
        s = k % depth
        line_wait(k, Z - 1)
        out_ref[k] = kept[k % kept_slots, z].astype(F32)

        @pl.when(has_down)
        def _():
            out_ref[k] = out_ref[k] + from_line[0, Z - 2, s].astype(F32)

        @pl.when(has_up)
        def _():
            out_ref[k] = out_ref[k] + from_line[1, Z - 2, s].astype(F32)

    stages = [begin, after_core, after_one, after_two]
    stages += [along_line(step) for step in range(2, Z)] + [finish]

    def loop_step(j, carry):
        for place in reversed(range(len(stages))):
            k = j - place * LAG

            @pl.when((k >= 0) & (k < units))
            def _(k=k, run=stages[place]):
                run(k)

        return carry

    lax.fori_loop(0, units + (len(stages) - 1) * LAG, loop_step, 0)


def sum_products(dec_x, dec_g, enc_x, enc_g, code_x, targets, code_g, look_g, call_id):
    dp_size, fsdp_size = lax.axis_size("dp"), lax.axis_size("fsdp")
    devices, Z = dp_size * fsdp_size, fsdp_size // 2
    m = D // devices
    if dp_size != 4 or Z != 4 or m % 32:
        products = [across(dec_x[i], dec_g[min(k, 10)]) for k, i in enumerate(DEC_INPUTS)]
        products += [across(enc_x[i], enc_g[min(k, 10)]) for k, i in enumerate(ENC_INPUTS)]
        plain = jnp.stack(products).astype(BF).reshape(len(products), devices, m, D)
        hit = (targets[:, None] == jnp.arange(VOCAB)[None, :]).astype(BF)
        code = across(jnp.concatenate([code_g, look_g]), jnp.concatenate([code_x, hit])).astype(BF)
        code = code.reshape(dp_size, D // dp_size, fsdp_size, VOCAB // fsdp_size)
        code = code.transpose(0, 2, 1, 3).reshape(devices, D // dp_size, VOCAB // fsdp_size)
        plain = lax.psum_scatter(plain, AXES, scatter_dimension=1, tiled=True)
        code = lax.psum_scatter(code, AXES, scatter_dimension=0, tiled=True)
        return plain.reshape(-1, m, D).astype(F32), code.reshape(D // dp_size, -1).astype(F32)
    n, units = D, len(DEC_INPUTS) + len(ENC_INPUTS) + CODE_UNITS
    depth, half = 2 * LAG, Z // 2
    own_slots, held_slots, kept_slots = LAG + 1, 2 * LAG + 1, Z * LAG + 1
    dec_rows, enc_rows, code_rows = dec_x[0].shape[0], enc_x[0].shape[0], code_x.shape[0]
    dma = pltpu.SemaphoreType.DMA
    whole = pl.BlockSpec(memory_space=pl.ANY)
    out = pl.pallas_call(
        partial(sum_kernel, Z),
        out_shape=jax.ShapeDtypeStruct((units, m, n), F32),
        in_specs=[whole] * 40 + [pl.BlockSpec(memory_space=pltpu.VMEM)] + [whole] * 2,
        out_specs=pl.BlockSpec(memory_space=pltpu.VMEM),
        scratch_shapes=[
            pltpu.VMEM((2, dec_rows, n), BF),
            pltpu.VMEM((2, dec_rows, n), BF),
            pltpu.VMEM((4 * Z, 2, m, dec_rows), BF),
            pltpu.VMEM((2, enc_rows, n), BF),
            pltpu.VMEM((2, enc_rows, n), BF),
            pltpu.VMEM((4 * Z, 2, m, enc_rows), BF),
            pltpu.VMEM((2 * code_rows, VOCAB), BF),
            pltpu.VMEM((2, code_rows, n), BF),
            pltpu.VMEM((4, CODE_UNITS, m, 2 * code_rows), BF),
            pltpu.VMEM((own_slots, 4, Z, m, n), BF),
            pltpu.VMEM((own_slots, 4, Z, m, n), BF),
            pltpu.VMEM((depth, 4, Z, m, n), BF),
            pltpu.VMEM((held_slots, 4, Z, m, n), BF),
            pltpu.VMEM((depth, half, m, n), BF),
            pltpu.VMEM((depth, Z - half, m, n), BF),
            pltpu.VMEM((depth, Z, m, n), BF),
            pltpu.VMEM((depth, Z, m, n), BF),
            pltpu.VMEM((kept_slots, Z, m, n), BF),
            pltpu.VMEM((2, Z - 1, depth, m, n), BF),
            dma((2, 2)),
            dma((3,)),
            dma((depth,)),
            dma((depth,)),
            dma((2, depth)),
            dma((2, depth)),
            dma((2, depth)),
            dma((2, depth)),
            dma((2, Z - 1, depth)),
            dma((2, Z - 1, depth)),
        ],
        compiler_params=pltpu.CompilerParams(
            collective_id=call_id, has_side_effects=True, vmem_limit_bytes=60 << 20
        ),
    )(*dec_x, *dec_g, *enc_x, *enc_g, code_x, targets[:, None], code_g, look_g)
    return out[:-CODE_UNITS], out[-CODE_UNITS:].reshape(-1, n)


def spread_kernel(
    tables, units, Z, table_ref, unit_ref, table_out, unit_out,
    own_sem, line_send, line_recv, square_send, square_recv, core_send, core_recv,
):
    dp, fs = lax.axis_index("dp"), lax.axis_index("fsdp")
    z, core = fs // 2, fs % 2
    x_mate, y_mate = dp + 1 - 2 * (dp % 2), (dp + 2) % 4
    across_dp = (x_mate + 2) % 4
    core_dev, x_dev, y_dev = (dp, fs + 1 - 2 * core), (x_mate, fs), (y_mate, fs)
    up_dev, down_dev = (dp, fs + 2), (dp, fs - 2)
    has_up, has_down = z < Z - 1, z > 0
    total, half = tables + units, Z // 2
    every = slice(None)
    table_rows, table_columns = table_out.shape[2] // tables, table_out.shape[3] // 4

    def at(is_table, k, dp_at, z_at, core_at, part=None):
        if is_table:
            size = table_rows if part is None else table_rows // 2
            rows = pl.ds(k * table_rows + (part or 0) * size, size)
            columns = every if isinstance(dp_at, slice) else pl.ds(dp_at * table_columns, table_columns)
            return table_out.at[z_at, core_at, rows, columns]
        if part is None:
            return unit_out.at[k - tables, dp_at, z_at, core_at]
        size = unit_out.shape[4] // 2
        return unit_out.at[k - tables, dp_at, z_at, core_at, pl.ds(part * size, size)]

    def remote(ref, send, recv, device):
        return pltpu.make_async_remote_copy(
            src_ref=ref, dst_ref=ref, send_sem=send, recv_sem=recv, device_id=device, device_id_type=MESH
        )

    own = (
        pltpu.make_async_copy(
            table_ref, table_out.at[z, core, :, pl.ds(dp * table_columns, table_columns)], own_sem.at[0]
        ),
        pltpu.make_async_copy(unit_ref, unit_out.at[:, dp, z, core], own_sem.at[1]),
    )
    for copy in own:
        copy.start()

    barrier = pltpu.get_barrier_semaphore()
    for device in (core_dev, x_dev, y_dev):
        pl.semaphore_signal(barrier, inc=1, device_id=device, device_id_type=MESH)

    @pl.when(has_up)
    def _():
        pl.semaphore_signal(barrier, inc=1, device_id=up_dev, device_id_type=MESH)

    @pl.when(has_down)
    def _():
        pl.semaphore_signal(barrier, inc=1, device_id=down_dev, device_id_type=MESH)

    for copy in own:
        copy.wait()
    pl.semaphore_wait(barrier, 3 + has_up.astype(jnp.int32) + has_down.astype(jnp.int32))

    def line_copies(view, k, step):
        s = step - 1
        return (
            (remote(view(jnp.maximum(z - s, 0)), line_send.at[0, s, k], line_recv.at[0, s, k], up_dev),
             has_up & (z >= s), has_down & (z >= s + 1)),
            (remote(view(jnp.minimum(z + s, Z - 1)), line_send.at[1, s, k], line_recv.at[1, s, k], down_dev),
             has_down & (z + s <= Z - 1), has_up & (z + s + 1 <= Z - 1)),
        )

    def line_start(view, k, step):
        for copy, sends, _ in line_copies(view, k, step):
            pl.when(sends)(copy.start)

    def line_wait(view, k, step):
        for copy, sends, receives in line_copies(view, k, step):
            pl.when(sends)(copy.wait_send)
            pl.when(receives)(copy.wait_recv)

    def to_core(ref, k, slot):
        return remote(ref, core_send.at[slot, k], core_recv.at[slot, k], core_dev)

    def square_copy(ref, k, slot):
        return remote(
            ref, square_send.at[slot, k], square_recv.at[slot, k], x_dev if slot % 2 == 0 else y_dev
        )

    def line_first(is_table):
        def view(k):
            return lambda place: at(is_table, k, dp, place, core)

        def row(k, dp_at):
            return at(is_table, k, dp_at, every, core)

        def ones(k):
            return square_copy(row(k, dp), k, 0), square_copy(row(k, dp), k, 1)

        def twos(k):
            return (
                square_copy(at(is_table, k, y_mate, pl.ds(0, half), core), k, 2),
                square_copy(at(is_table, k, x_mate, pl.ds(half, Z - half), core), k, 3),
            )

        def line(step):
            def run(k):
                if step > 1:
                    line_wait(view(k), k, step - 1)
                if step < Z:
                    line_start(view(k), k, step)
                else:
                    for copy in ones(k):
                        copy.start()
                    to_core(row(k, dp), k, 0).start()
            return run

        def after_one(k):
            for copy in ones(k):
                copy.wait()
            for copy in twos(k):
                copy.start()
            to_core(row(k, x_mate), k, 1).start()
            to_core(row(k, y_mate), k, 2).start()

        def after_two(k):
            for copy in twos(k):
                copy.wait()
            to_core(row(k, across_dp), k, 3).start()

        def finish(k):
            for slot in range(4):
                to_core(row(k, dp), k, slot).wait()

        return [line(step) for step in range(1, Z + 1)] + [after_one, after_two, finish]

    def square_first(is_table):
        def plane(k):
            return lambda place: at(is_table, k, every, place, core)

        def ones(k):
            ref = at(is_table, k, dp, z, core)
            return square_copy(ref, k, 0), square_copy(ref, k, 1)

        def twos(k):
            return (
                square_copy(at(is_table, k, y_mate, z, core, 0), k, 2),
                square_copy(at(is_table, k, x_mate, z, core, 1), k, 3),
            )

        def begin(k):
            for copy in ones(k):
                copy.start()

        def after_one(k):
            for copy in ones(k):
                copy.wait()
            for copy in twos(k):
                copy.start()

        def after_two(k):
            for copy in twos(k):
                copy.wait()
            line_start(plane(k), k, 1)
            to_core(plane(k)(z), k, z).start()

        def line(step):
            def run(k):
                line_wait(plane(k), k, step)
                if step + 1 < Z:
                    line_start(plane(k), k, step + 1)

                @pl.when(z - step >= 0)
                def _():
                    to_core(plane(k)(jnp.maximum(z - step, 0)), k, jnp.maximum(z - step, 0)).start()

                @pl.when(z + step <= Z - 1)
                def _():
                    to_core(plane(k)(jnp.minimum(z + step, Z - 1)), k, jnp.minimum(z + step, Z - 1)).start()
            return run

        def finish(k):
            for place in range(Z):
                to_core(plane(k)(place), k, place).wait()

        return [begin, after_one, after_two] + [line(step) for step in range(1, Z)] + [finish]

    forms = [(is_table, first, form(is_table))
             for is_table in (True, False) for first, form in ((True, line_first), (False, square_first))]
    n_stages = Z + 3

    def loop_step(j, carry):
        for place in reversed(range(n_stages)):
            k = j - place * LAG
            turn = k % 9
            by_line = (turn != 3) & (turn != 7)
            for is_table, first, stages in forms:
                here = (k >= 0) & (k < tables) if is_table else (k >= tables) & (k < total)
                here = here & (by_line if first else jnp.logical_not(by_line))

                @pl.when(here)
                def _(k=k, run=stages[place]):
                    run(k)

        return carry

    lax.fori_loop(0, total + (n_stages - 1) * LAG, loop_step, 0)


def spread(table, units, call_id):
    count, m, n = units.shape
    Z = lax.axis_size("fsdp") // 2
    if lax.axis_size("dp") != 4 or Z != 4 or m % 32:
        whole = lax.all_gather(lax.all_gather(table, "dp", axis=1, tiled=True), "fsdp", axis=0, tiled=True)
        return whole, lax.all_gather(units, AXES, axis=1, tiled=True)
    tables, dma = 8, pltpu.SemaphoreType.DMA
    total = tables + count
    whole, units = pl.pallas_call(
        partial(spread_kernel, tables, count, Z),
        out_shape=(
            jax.ShapeDtypeStruct((Z, 2, table.shape[0], 4 * table.shape[1]), BF),
            jax.ShapeDtypeStruct((count, 4, Z, 2, m, n), BF),
        ),
        in_specs=[pl.BlockSpec(memory_space=pltpu.VMEM)] * 2,
        out_specs=[pl.BlockSpec(memory_space=pl.ANY)] * 2,
        scratch_shapes=[
            dma((2,)),
            dma((2, Z - 1, total)),
            dma((2, Z - 1, total)),
            dma((4, total)),
            dma((4, total)),
            dma((4, total)),
            dma((4, total)),
        ],
        compiler_params=pltpu.CompilerParams(collective_id=call_id, has_side_effects=True),
    )(table, units)
    return whole.reshape(-1, 4 * table.shape[1]), units.reshape(count, -1, n)


def exchange_kernel(size, inner, in_ref, out_ref, send_sem, recv_sem):
    me = lax.axis_index("dp") * inner + lax.axis_index("fsdp")

    def peer(i):
        other = lax.rem(me + i, size)
        return other, (other // inner, lax.rem(other, inner))

    barrier = pltpu.get_barrier_semaphore()

    def greet(i, carry):
        pl.semaphore_signal(barrier, inc=1, device_id=peer(i)[1], device_id_type=MESH)
        return carry

    def copy(i):
        other, device = peer(i)
        return pltpu.make_async_remote_copy(
            src_ref=in_ref.at[other], dst_ref=out_ref.at[me], send_sem=send_sem.at[i],
            recv_sem=recv_sem.at[i], device_id=device, device_id_type=MESH,
        )

    def begin(i, carry):
        copy(i).start()
        return carry

    def end(i, carry):
        copy(i).wait()
        return carry

    lax.fori_loop(1, size, greet, 0)
    out_ref[me] = in_ref[me]
    pl.semaphore_wait(barrier, size - 1)
    lax.fori_loop(1, size, begin, 0)
    lax.fori_loop(1, size, end, 0)


def exchange(blocks, call_id):
    size, inner = blocks.shape[0], lax.axis_size("fsdp")
    return pl.pallas_call(
        partial(exchange_kernel, size, inner),
        out_shape=jax.ShapeDtypeStruct(blocks.shape, F32),
        in_specs=[pl.BlockSpec(memory_space=pltpu.VMEM)],
        out_specs=pl.BlockSpec(memory_space=pltpu.VMEM),
        scratch_shapes=[pltpu.SemaphoreType.DMA((size,)), pltpu.SemaphoreType.DMA((size,))],
        compiler_params=pltpu.CompilerParams(collective_id=call_id, has_side_effects=True),
    )(blocks)


def tiles(values, count):
    padded = jnp.pad(values, ((0, 1024 - values.shape[0]),)).reshape(1, 8, 128)
    return jnp.broadcast_to(padded, (count, 8, 128))


def layer_norm(stream, gain):
    centred = stream - jnp.mean(stream, axis=-1, keepdims=True)
    return centred * lax.rsqrt(jnp.mean(centred * centred, axis=-1, keepdims=True) + 1e-05) * gain


def norm_back(stream, gain, grad_out):
    _, pullback = jax.vjp(layer_norm, stream, gain)
    return pullback(grad_out)


def positions(length, width):
    position = jnp.arange(length, dtype=jnp.float32)[:, None]
    speeds = jnp.exp(
        -math.log(10000.0) * 2.0 * jnp.arange(width // 2, dtype=jnp.float32)[None, :] / width
    )
    return jnp.concatenate([jnp.sin(position * speeds), jnp.cos(position * speeds)], axis=1)


def matmul(first_op, second_op):
    return jnp.dot(first_op, second_op, preferred_element_type=jnp.float32)


def across(first_op, second_op):
    return lax.dot_general(
        first_op, second_op, (((0,), (0,)), ((), ())), preferred_element_type=jnp.float32
    )


def against(first_op, second_op):
    return lax.dot_general(
        first_op, second_op, (((1,), (1,)), ((), ())), preferred_element_type=jnp.float32
    )


def heads_first(matrix, blocks):
    return matrix.reshape(blocks, -1, HEADS, HEAD).transpose(0, 2, 1, 3)


def heads_last(array):
    return array.transpose(0, 2, 1, 3).reshape(-1, HEADS * HEAD)


def attention(queries, keys_in, values, visible):
    scores = jnp.einsum(
        "bhqd,bhkd->bhqk", queries, keys_in, preferred_element_type=F32
    ) * HEAD ** (-0.5)
    scores = jnp.where(visible[:, None], scores, MASKED)
    weights = jnp.exp(scores - jnp.max(scores, axis=-1, keepdims=True))
    shares = weights / jnp.sum(weights, axis=-1, keepdims=True)
    low = shares.astype(BF)
    attended = jnp.einsum("bhqk,bhkd->bhqd", low, values, preferred_element_type=F32)
    return heads_last(attended.astype(BF)), low


def attention_back(queries, keys_in, values, shares, grad_mixed):
    grad_heads = heads_first(grad_mixed, queries.shape[0])
    grad_shares = jnp.einsum(
        "bhqd,bhkd->bhqk", grad_heads, values, preferred_element_type=F32
    )
    wide = shares.astype(F32)
    grad_scores = (
        wide * (grad_shares - jnp.sum(wide * grad_shares, axis=-1, keepdims=True))
    ).astype(BF)
    grad_query = jnp.einsum(
        "bhqk,bhkd->bhqd", grad_scores, keys_in, preferred_element_type=F32
    ) * HEAD ** (-0.5)
    grad_keys = jnp.einsum(
        "bhqk,bhqd->bhkd", grad_scores, queries, preferred_element_type=F32
    ) * HEAD ** (-0.5)
    grad_values = jnp.einsum(
        "bhqk,bhqd->bhkd", shares, grad_heads, preferred_element_type=F32
    )
    return grad_query, grad_keys, grad_values


def layer_forward(stream, weights, gains, self_visible, memory, cross_visible):
    project, mix_out, cross, cross_out, ffn_up, ffn_down = weights
    blocks = self_visible.shape[0]
    stored = {"stream": stream}
    normed = layer_norm(stream, gains[0]).astype(BF)
    queries, keys_in, values = [
        heads_first(matmul(normed, project[i]).astype(BF), blocks) for i in range(3)
    ]
    attended, shares = attention(queries, keys_in, values, self_visible)
    stream = stream + matmul(attended, mix_out)
    stored.update(
        normed=normed, self_attention=(queries, keys_in, values, shares), attended=attended, after_self=stream
    )
    if memory is not None:
        cross_in = layer_norm(stream, gains[1]).astype(BF)
        cross_query = heads_first(matmul(cross_in, cross[0]).astype(BF), 1)
        memory_keys = heads_first(matmul(memory, cross[1]).astype(BF), 1)
        memory_values = heads_first(matmul(memory, cross[2]).astype(BF), 1)
        cross_mixed, cross_shares = attention(cross_query, memory_keys, memory_values, cross_visible)
        stream = stream + matmul(cross_mixed, cross_out)
        stored.update(
            cross_in=cross_in,
            cross_attention=(cross_query, memory_keys, memory_values, cross_shares),
            cross_mixed=cross_mixed,
        )
    stored["before_ffn"] = stream
    ffn_in = layer_norm(stream, gains[-2]).astype(BF)
    hidden_pre = [matmul(ffn_in, up) for up in ffn_up]
    hidden = [jax.nn.gelu(pre, approximate=True).astype(BF) for pre in hidden_pre]
    for low, down in zip(hidden, ffn_down):
        stream = stream + matmul(low, down)
    stored.update(ffn_in=ffn_in, hidden_pre=hidden_pre, hidden=hidden, before_final=stream)
    return layer_norm(stream, gains[-1]).astype(BF), stored


def layer_backward(grad_final, weights, gains, stored, memory):
    project, mix_out, cross, cross_out, ffn_up, ffn_down = weights
    gain_grads = [None] * len(gains)
    grad_stream, gain_grads[-1] = norm_back(stored["before_final"], gains[-1], grad_final)
    ffn_low = grad_stream.astype(BF)
    grad_pres = []
    grad_ffn = 0.0
    for pre, up, down in zip(stored["hidden_pre"], ffn_up, ffn_down):
        _, gelu_pull = jax.vjp(partial(jax.nn.gelu, approximate=True), pre)
        grad_pres.append(gelu_pull(against(ffn_low, down))[0].astype(BF))
        grad_ffn = grad_ffn + against(grad_pres[-1], up)
    grad_normed, gain_grads[-2] = norm_back(stored["before_ffn"], gains[-2], grad_ffn)
    grad_stream = grad_stream + grad_normed
    cross_inputs, cross_grads, memory_grads = [], [], []
    grad_memory = None
    if memory is not None:
        cross_low = grad_stream.astype(BF)
        grad_mixed = against(cross_low, cross_out).astype(BF)
        grads = [
            heads_last(grad.astype(BF)) for grad in attention_back(*stored["cross_attention"], grad_mixed)
        ]
        cross_inputs = [stored["cross_in"], stored["cross_mixed"]]
        cross_grads = [grads[0], cross_low]
        memory_grads = grads[1:]
        grad_memory = against(grads[1], cross[1]) + against(grads[2], cross[2])
        grad_normed, gain_grads[1] = norm_back(
            stored["after_self"], gains[1], against(grads[0], cross[0])
        )
        grad_stream = grad_stream + grad_normed
    self_low = grad_stream.astype(BF)
    grad_mixed = against(self_low, mix_out).astype(BF)
    grads = [
        heads_last(grad.astype(BF)) for grad in attention_back(*stored["self_attention"], grad_mixed)
    ]
    grad_normed, gain_grads[0] = norm_back(
        stored["stream"],
        gains[0],
        sum(against(grads[i], project[i]) for i in range(3)),
    )
    grad_stream = grad_stream + grad_normed
    inputs = [stored["normed"], stored["attended"], *cross_inputs, stored["ffn_in"], *stored["hidden"]]
    outputs = [*grads, self_low, *cross_grads, *grad_pres, ffn_low]
    parts = (inputs, outputs) if memory is None else (inputs, outputs, memory_grads)
    return grad_stream, grad_memory, gain_grads, parts


def adam_step(weight, moment_one, second, gradient, rate):
    moment_one = BETA_ONE * moment_one + (1.0 - BETA_ONE) * gradient
    second = BETA_TWO * second + (1.0 - BETA_TWO) * gradient * gradient
    first_hat = moment_one / (1.0 - BETA_ONE**STEP)
    second_hat = second / (1.0 - BETA_TWO**STEP)
    weight = weight - rate * (first_hat / (jnp.sqrt(second_hat) + ADAM_EPS) + WEIGHT_DECAY * weight)
    return (weight, moment_one, second)


def column_units(matrix):
    return matrix.reshape(matrix.shape[0], -1, D).transpose(1, 0, 2)


def from_column_units(units):
    return units.transpose(1, 0, 2).reshape(units.shape[1], -1)


def hidden_units(matrix, devices):
    rows, width = matrix.shape
    return (
        matrix.reshape(rows, devices, 4, width // devices // 4)
        .transpose(2, 0, 1, 3)
        .reshape(4, rows, width // 4)
    )


def from_hidden_units(units, devices):
    quarters, rows, width = units.shape
    return (
        units.reshape(quarters, rows, devices, width // devices)
        .transpose(1, 2, 0, 3)
        .reshape(rows, quarters * width)
    )


def on_device(
    text_ids,
    text_segments,
    codes,
    caption_of,
    mix_in,
    mix_out,
    ffn_up,
    ffn_down,
    norm_gains,
    text_table,
    code_table,
    mix_in_first,
    mix_out_first,
    ffn_up_first,
    ffn_down_first,
    gains_first,
    text_first,
    code_first,
    mix_in_second,
    mix_out_second,
    ffn_up_second,
    ffn_down_second,
    gains_second,
    text_second,
    code_second,
):
    image_count = codes.shape[0]
    dp_size, fsdp_size = lax.axis_size("dp"), lax.axis_size("fsdp")
    devices = dp_size * fsdp_size
    me = lax.axis_index("dp") * fsdp_size + lax.axis_index("fsdp")
    token_total = image_count * IMG_LEN * devices
    inverse = 1.0 / token_total
    scale_in = math.sqrt(D)
    rows = mix_in.shape[1]
    segments = text_segments[0]
    text_visible = (segments[:, None] == segments[None, :])[None]
    place = jnp.arange(IMG_LEN)
    self_visible = jnp.broadcast_to(
        place[None, :] <= place[:, None], (image_count, IMG_LEN, IMG_LEN)
    )
    wanted = jnp.repeat(caption_of, IMG_LEN)
    cross_visible = (segments[None, :] == wanted[:, None])[None]

    small = tiles(jnp.concatenate([text_ids[0].astype(F32), norm_gains.reshape(-1)]), devices)
    small = exchange(small, 3).reshape(devices, 1024)[:, : TXT_LEN + 7 * norm_gains.shape[1]]
    all_ids = small[:, :TXT_LEN].astype(jnp.int32).reshape(-1)
    gains = small[:, TXT_LEN:].reshape(devices, 7, -1).transpose(1, 0, 2).reshape(7, D)
    gains = gains.astype(BF).astype(F32)

    base = me * text_table.shape[0]
    owned = (all_ids[:, None] - base == jnp.arange(text_table.shape[0])[None, :]).astype(BF)
    looked = matmul(owned, text_table.astype(BF)).astype(BF)
    text_rows = lax.psum_scatter(looked, AXES, scatter_dimension=0, tiled=True)

    def layer_units(which):
        return [
            column_units(mix_in[which]),
            mix_out[which][None],
            hidden_units(ffn_up[min(which, 1)], devices),
            ffn_down[min(which, 1)].reshape(4, rows, D),
        ]

    shards = layer_units(0) + layer_units(1)[:2] + layer_units(2)
    code_full, units = spread(code_table.astype(BF), jnp.concatenate(shards).astype(BF), 4)
    enc_units, self_units, late_units = units[:12], units[12:16], units[16:]
    enc_weights = (enc_units[:3], enc_units[3], None, None, enc_units[4:8], enc_units[8:])
    dec_weights = (
        self_units[:3], self_units[3], late_units[:3], late_units[3], late_units[4:8], late_units[8:]
    )

    text_in = text_rows.astype(F32) * scale_in + positions(TXT_LEN, D)
    enc_gains = [gains[i] for i in range(3)]
    dec_gains = [gains[i] for i in range(3, 7)]
    memory, enc_stored = layer_forward(text_in, enc_weights, enc_gains, text_visible, None, None)

    image_rows = code_full[codes].astype(F32) * scale_in
    shifted = jnp.concatenate([jnp.zeros_like(image_rows[:, :1]), image_rows[:, :-1]], axis=1)
    image_in = (shifted + positions(IMG_LEN, D)[None]).reshape(-1, D)
    final_out, dec_stored = layer_forward(
        image_in, dec_weights, dec_gains, self_visible, memory, cross_visible
    )

    targets = codes.reshape(-1)
    logits = against(final_out, code_full)
    hit = targets[:, None] == jnp.arange(VOCAB)[None, :]
    top = jnp.max(logits, axis=1, keepdims=True)
    log_total = top + jnp.log(jnp.sum(jnp.exp(logits - top), axis=1, keepdims=True))
    weighted = jnp.sum(
        logits * jnp.where(hit, 1.0 - SMOOTH + SMOOTH / VOCAB, SMOOTH / VOCAB), axis=1, keepdims=True
    )
    loss_part = jnp.sum(log_total - weighted)
    grad_logits = (
        (jnp.exp(logits - log_total) - jnp.where(hit, 1.0 - SMOOTH, 0.0) - SMOOTH / VOCAB) * inverse
    ).astype(BF)
    grad_final = matmul(grad_logits, code_full)

    grad_image, grad_memory, dec_gain_grads, dec_parts = layer_backward(
        grad_final, dec_weights, dec_gains, dec_stored, memory
    )
    grad_text, _, enc_gain_grads, enc_parts = layer_backward(
        grad_memory, enc_weights, enc_gains, enc_stored, None
    )
    gain_part = jnp.stack(enc_gain_grads + dec_gain_grads)

    grad_rows = lax.all_gather((grad_text * scale_in).astype(BF), AXES, axis=0, tiled=True)
    text_grad = across(owned, grad_rows)

    grad_looked = grad_image.reshape(image_count, IMG_LEN, D)[:, 1:] * scale_in
    grad_looked = jnp.pad(grad_looked, ((0, 0), (0, 1), (0, 0))).reshape(-1, D).astype(BF)
    enc_x, enc_g = enc_parts
    dec_x, dec_g, memory_g = dec_parts
    plain_sum, code_sum = sum_products(
        dec_x, dec_g, [memory] + enc_x, memory_g + enc_g, grad_logits, targets, final_out, grad_looked, 1
    )
    code_grad = code_sum.T
    dec_sum, enc_sum = plain_sum[:14], plain_sum[14:]

    gain_blocks = gain_part.reshape(7, devices, rows).transpose(1, 0, 2).reshape(devices, 7 * rows)
    gain_blocks = jnp.concatenate([gain_blocks, jnp.full((devices, 1), loss_part)], axis=1)
    gain_blocks = jnp.pad(gain_blocks, ((0, 0), (0, 1024 - gain_blocks.shape[1])))
    small_sum = jnp.sum(exchange(gain_blocks.reshape(devices, 8, 128), 5), axis=0).reshape(-1)
    loss_sum = small_sum[7 * rows]
    gains_grad = small_sum[: 7 * rows].reshape(7, rows)
    gradients = (
        jnp.stack(
            [
                from_column_units(part)
                for part in (enc_sum[2:5], dec_sum[:3], jnp.concatenate([dec_sum[4:5], enc_sum[:2]]))
            ]
        ),
        jnp.stack([enc_sum[5], dec_sum[3], dec_sum[5]]),
        jnp.stack([from_hidden_units(part, devices) for part in (enc_sum[6:10], dec_sum[6:10])]),
        jnp.stack([part.reshape(-1, D) for part in (enc_sum[10:], dec_sum[10:])]),
        gains_grad,
        text_grad,
        code_grad,
    )
    square_part = sum((jnp.sum(gradient * gradient) for gradient in gradients))
    squares = exchange(tiles(square_part[None], devices), 6)[:, 0, 0]
    grad_norm = jnp.sqrt(jnp.sum(squares))
    factor = CLIP_NORM / jnp.maximum(grad_norm, CLIP_NORM)
    params = (mix_in, mix_out, ffn_up, ffn_down, norm_gains, text_table, code_table)
    firsts = (
        mix_in_first,
        mix_out_first,
        ffn_up_first,
        ffn_down_first,
        gains_first,
        text_first,
        code_first,
    )
    seconds = (
        mix_in_second,
        mix_out_second,
        ffn_up_second,
        ffn_down_second,
        gains_second,
        text_second,
        code_second,
    )
    updated = [
        adam_step(
            params[index],
            firsts[index],
            seconds[index],
            gradients[index] * factor,
            STEP_RATES[index],
        )
        for index in range(7)
    ]
    return (
        loss_sum,
        grad_norm,
        updated[0][0],
        updated[1][0],
        updated[2][0],
        updated[3][0],
        updated[4][0],
        updated[5][0],
        updated[6][0],
        updated[0][1],
        updated[1][1],
        updated[2][1],
        updated[3][1],
        updated[4][1],
        updated[5][1],
        updated[6][1],
        updated[0][2],
        updated[1][2],
        updated[2][2],
        updated[3][2],
        updated[4][2],
        updated[5][2],
        updated[6][2],
    )


def solution(mesh):
    return jax.shard_map(
        on_device,
        mesh=mesh,
        in_specs=(
            P(("dp", "fsdp"), None),
            P(("dp", "fsdp"), None),
            P(("dp", "fsdp"), None),
            P(("dp", "fsdp")),
            P(None, ("dp", "fsdp"), None),
            P(None, ("dp", "fsdp"), None),
            P(None, ("dp", "fsdp"), None),
            P(None, ("dp", "fsdp"), None),
            P(None, ("dp", "fsdp")),
            P(("dp", "fsdp"), None),
            P("fsdp", "dp"),
            P(None, ("dp", "fsdp"), None),
            P(None, ("dp", "fsdp"), None),
            P(None, ("dp", "fsdp"), None),
            P(None, ("dp", "fsdp"), None),
            P(None, ("dp", "fsdp")),
            P(("dp", "fsdp"), None),
            P("fsdp", "dp"),
            P(None, ("dp", "fsdp"), None),
            P(None, ("dp", "fsdp"), None),
            P(None, ("dp", "fsdp"), None),
            P(None, ("dp", "fsdp"), None),
            P(None, ("dp", "fsdp")),
            P(("dp", "fsdp"), None),
            P("fsdp", "dp"),
        ),
        out_specs=(
            P(),
            P(),
            P(None, ("dp", "fsdp"), None),
            P(None, ("dp", "fsdp"), None),
            P(None, ("dp", "fsdp"), None),
            P(None, ("dp", "fsdp"), None),
            P(None, ("dp", "fsdp")),
            P(("dp", "fsdp"), None),
            P("fsdp", "dp"),
            P(None, ("dp", "fsdp"), None),
            P(None, ("dp", "fsdp"), None),
            P(None, ("dp", "fsdp"), None),
            P(None, ("dp", "fsdp"), None),
            P(None, ("dp", "fsdp")),
            P(("dp", "fsdp"), None),
            P("fsdp", "dp"),
            P(None, ("dp", "fsdp"), None),
            P(None, ("dp", "fsdp"), None),
            P(None, ("dp", "fsdp"), None),
            P(None, ("dp", "fsdp"), None),
            P(None, ("dp", "fsdp")),
            P(("dp", "fsdp"), None),
            P("fsdp", "dp"),
        ),
        check_vma=False,
    )
```

```python
from functools import partial
import math

import jax
import jax.numpy as jnp
from jax import lax
from jax.experimental import pallas as pl
from jax.experimental.pallas import tpu as pltpu
from jax.sharding import PartitionSpec as P

D = 1024
HEADS = 16
HEAD = 64
VOCAB = 8192
TVOC = 16000
IMG_LEN = 256
TXT_LEN = 128
STEP = 5


SMOOTH = 0.1
BETA_ONE = 0.5
BETA_TWO = 0.5
WEIGHT_DECAY = 0.1
ADAM_EPS = 1e-08
CLIP_NORM = 0.02
MASKED = -1e30
STEP_RATES = (0.02, 0.15, 0.02, 0.01, 0.3, 0.02, 0.03)

BF = jnp.bfloat16
F32 = jnp.float32
AXES = ("dp", "fsdp")
MESH = pl.DeviceIdType.MESH
LAG = 2


DEC_INPUTS = (0, 0, 0, 1, 2, 3, 4, 4, 4, 4, 5, 6, 7, 8)
ENC_INPUTS = (0, 0, 1, 1, 1, 2, 3, 3, 3, 3, 4, 5, 6, 7)
CODE_UNITS = 8


def sum_kernel(Z, *refs):
    dec_x, refs = refs[:9], refs[9:]
    dec_g, refs = refs[:11], refs[11:]
    enc_x, refs = refs[:8], refs[8:]
    enc_g, refs = refs[:11], refs[11:]
    (
        code_x, targets, code_g, look_g, out_ref,
        dec_xs, dec_gs, dec_turned, enc_xs, enc_gs, enc_turned, code_xs, code_loaded, code_gs, to_core,
        own, from_core, held, from_x, from_y, all_x, all_y, kept, from_line,
        load_sem, code_sem, core_send, core_recv, one_send, one_recv, two_send, two_recv, line_send, line_recv,
    ) = refs
    dec_units, enc_units = len(DEC_INPUTS), len(ENC_INPUTS)
    plain_units = dec_units + enc_units
    units = plain_units + CODE_UNITS
    depth = 2 * LAG
    dp, fs = lax.axis_index("dp"), lax.axis_index("fsdp")
    z, core = fs // 2, fs % 2
    x_mate, y_mate = dp + 1 - 2 * (dp % 2), (dp + 2) % 4
    across_dp = (x_mate + 2) % 4
    core_dev, x_dev, y_dev = (dp, fs + 1 - 2 * core), (x_mate, fs), (y_mate, fs)
    up_dev, down_dev = (dp, fs + 2), (dp, fs - 2)
    has_up, has_down = z < Z - 1, z > 0

    barrier = pltpu.get_barrier_semaphore()
    for device in (core_dev, x_dev, y_dev):
        pl.semaphore_signal(barrier, inc=1, device_id=device, device_id_type=MESH)

    @pl.when(has_up)
    def _():
        pl.semaphore_signal(barrier, inc=1, device_id=up_dev, device_id_type=MESH)

    @pl.when(has_down)
    def _():
        pl.semaphore_signal(barrier, inc=1, device_id=down_dev, device_id_type=MESH)

    pl.semaphore_wait(barrier, 3 + has_up.astype(jnp.int32) + has_down.astype(jnp.int32))
    half = Z // 2
    own_slots, held_slots, kept_slots = own.shape[0], held.shape[0], kept.shape[0]

    def add(a, b):
        return (a.astype(F32) + b.astype(F32)).astype(BF)

    def remote(src, dst, send, recv, device):
        return pltpu.make_async_remote_copy(
            src_ref=src, dst_ref=dst, send_sem=send, recv_sem=recv, device_id=device, device_id_type=MESH
        )

    def pair(x, g, xs, gs, slot):
        return (
            pltpu.make_async_copy(x, xs.at[slot], load_sem.at[0, slot]),
            pltpu.make_async_copy(g, gs.at[slot], load_sem.at[1, slot]),
        )

    def start_loads(k):
        for i, place in enumerate(DEC_INPUTS):

            @pl.when(k == i)
            def _(i=i, place=place):
                for copy in pair(dec_x[place], dec_g[min(i, 10)], dec_xs, dec_gs, i % 2):
                    copy.start()

        for i, place in enumerate(ENC_INPUTS):

            @pl.when(k == dec_units + i)
            def _(i=i, place=place):
                for copy in pair(enc_x[place], enc_g[min(i, 10)], enc_xs, enc_gs, (dec_units + i) % 2):
                    copy.start()

    code_rows = code_x.shape[0]
    code_loads = [
        pltpu.make_async_copy(code_x, code_xs.at[pl.ds(0, code_rows)], code_sem.at[0]),
        pltpu.make_async_copy(code_g, code_loaded.at[0], code_sem.at[1]),
        pltpu.make_async_copy(look_g, code_loaded.at[1], code_sem.at[2]),
    ]
    for copy in code_loads:
        copy.start()
    start_loads(jnp.int32(0))

    def core_copy(k):
        s = k % depth
        return remote(
            to_core.at[k % own_slots], from_core.at[s], core_send.at[s], core_recv.at[s], core_dev
        )

    def one_copies(k):
        s, block = k % depth, held.at[k % held_slots, across_dp]
        return (
            remote(block.at[pl.ds(0, half)], from_x.at[s], one_send.at[0, s], one_recv.at[0, s], x_dev),
            remote(block.at[pl.ds(half, Z - half)], from_y.at[s], one_send.at[1, s], one_recv.at[1, s], y_dev),
        )

    def two_copies(k):
        s, h = k % depth, k % held_slots
        return (
            remote(held.at[h, x_mate], all_x.at[s], two_send.at[0, s], two_recv.at[0, s], x_dev),
            remote(held.at[h, y_mate], all_y.at[s], two_send.at[1, s], two_recv.at[1, s], y_dev),
        )

    def up_block(step):
        return jnp.minimum(z + Z - step, Z - 1)

    def down_block(step):
        return jnp.maximum(z - Z + step, 0)

    def up_copy(k, step):
        s = k % depth
        return remote(
            kept.at[k % kept_slots, up_block(step)], from_line.at[0, step - 1, s],
            line_send.at[0, step - 1, s], line_recv.at[0, step - 1, s], up_dev,
        )

    def down_copy(k, step):
        s = k % depth
        return remote(
            kept.at[k % kept_slots, down_block(step)], from_line.at[1, step - 1, s],
            line_send.at[1, step - 1, s], line_recv.at[1, step - 1, s], down_dev,
        )

    def line_start(k, step):
        @pl.when(has_up)
        def _():
            up_copy(k, step).start()

        @pl.when(has_down)
        def _():
            down_copy(k, step).start()

    def line_wait(k, step):
        @pl.when(has_down)
        def _():
            up_copy(k, step).wait_recv()
            down_copy(k, step).wait_send()

        @pl.when(has_up)
        def _():
            down_copy(k, step).wait_recv()
            up_copy(k, step).wait_send()

    def turn(xs, slot, turned):
        size = 256

        def columns(i, carry):
            part = xs[slot, :, pl.ds(pl.multiple_of(i * size, size), size)].T
            count = size // (2 * turned.shape[2])
            turned[pl.ds(i * count, count)] = part.reshape(count, *turned.shape[1:])
            return carry

        lax.fori_loop(0, xs.shape[2] // size, columns, 0)

    def product(turned, gs, slot, side, into):
        def rows(block, carry):
            value = turned[pl.ds(block * Z, Z), side].reshape(-1, turned.shape[-1])
            result = jnp.dot(value, gs[slot], preferred_element_type=F32).astype(BF)
            into[block] = result.reshape(into.shape[1:])
            return carry

        lax.fori_loop(0, 4, rows, 0)

    def code_inputs():
        for copy in code_loads:
            copy.wait()
        size = D // 4
        for half_rows in range(2):

            def turn_columns(i, carry, half_rows=half_rows):
                part = code_loaded[half_rows, :, pl.ds(pl.multiple_of(i * size, size), size)].T
                code_gs[i, :, :, pl.ds(half_rows * code_rows, code_rows)] = part.reshape(
                    CODE_UNITS, size // CODE_UNITS, code_rows
                )
                return carry

            lax.fori_loop(0, 4, turn_columns, 0)

        width = 512

        def hits(i, carry):
            start = pl.multiple_of(i * width, width)
            column = lax.broadcasted_iota(jnp.int32, (code_rows, width), 1) + i * width
            code_xs[pl.ds(code_rows, code_rows), pl.ds(start, width)] = jnp.where(
                targets[...] == column, 1.0, 0.0
            ).astype(BF)
            return carry

        lax.fori_loop(0, VOCAB // width, hits, 0)

    def code_product(k, side, into):
        value = code_gs[:, k - plain_units].reshape(-1, code_gs.shape[-1])
        width = into.shape[-1]

        def columns(place, carry):
            start = pl.multiple_of((2 * place + side) * width, width)
            result = jnp.dot(value, code_xs[:, pl.ds(start, width)], preferred_element_type=F32).astype(BF)
            into[:, place] = result.reshape(4, -1, width)
            return carry

        lax.fori_loop(0, Z, columns, 0)

    def begin(k):
        slot, o = k % 2, k % own_slots
        for here, x, g, xs, gs, turned in (
            (k < dec_units, dec_x[0], dec_g[0], dec_xs, dec_gs, dec_turned),
            ((k >= dec_units) & (k < plain_units), enc_x[0], enc_g[0], enc_xs, enc_gs, enc_turned),
        ):

            @pl.when(here)
            def _(x=x, g=g, xs=xs, gs=gs, turned=turned):
                for copy in pair(x, g, xs, gs, slot):
                    copy.wait()
                start_loads(k + 1)
                turn(xs, slot, turned)
                product(turned, gs, slot, 1 - core, to_core.at[o])
                core_copy(k).start()
                product(turned, gs, slot, core, own.at[o])

        @pl.when(k == dec_units)
        def _():
            code_inputs()

        @pl.when(k >= plain_units)
        def _():
            code_product(k, 1 - core, to_core.at[o])
            core_copy(k).start()
            code_product(k, core, own.at[o])

    def after_core(k):
        core_copy(k).wait()

        def one(block, carry):
            for q in range(Z):
                held[k % held_slots, block, q] = add(
                    own[k % own_slots, block, q], from_core[k % depth, block, q]
                )
            return carry

        lax.fori_loop(0, 4, one, 0)
        for copy in one_copies(k):
            copy.start()

    def after_one(k):
        s, h = k % depth, k % held_slots
        for copy in one_copies(k):
            copy.wait()
        for q in range(half):
            held[h, y_mate, q] = add(held[h, y_mate, q], from_x[s, q])
        for q in range(Z - half):
            held[h, x_mate, half + q] = add(held[h, x_mate, half + q], from_y[s, q])
        for copy in two_copies(k):
            copy.start()

    def after_two(k):
        s, h = k % depth, k % held_slots
        for copy in two_copies(k):
            copy.wait()
        for q in range(Z):
            kept[k % kept_slots, q] = (
                held[h, dp, q].astype(F32) + all_x[s, q].astype(F32) + all_y[s, q].astype(F32)
            ).astype(BF)
        line_start(k, 1)

    def along_line(step):
        def run(k):
            s, h = k % depth, k % kept_slots
            line_wait(k, step - 1)

            @pl.when(has_down & (z + Z - step <= Z - 1))
            def _():
                kept[h, up_block(step)] = add(kept[h, up_block(step)], from_line[0, step - 2, s])

            @pl.when(has_up & (z - Z + step >= 0))
            def _():
                kept[h, down_block(step)] = add(kept[h, down_block(step)], from_line[1, step - 2, s])

            line_start(k, step)

        return run

    def finish(k):
        s = k % depth
        line_wait(k, Z - 1)
        out_ref[k] = kept[k % kept_slots, z].astype(F32)

        @pl.when(has_down)
        def _():
            out_ref[k] = out_ref[k] + from_line[0, Z - 2, s].astype(F32)

        @pl.when(has_up)
        def _():
            out_ref[k] = out_ref[k] + from_line[1, Z - 2, s].astype(F32)

    stages = [begin, after_core, after_one, after_two]
    stages += [along_line(step) for step in range(2, Z)] + [finish]

    def loop_step(j, carry):
        for place in reversed(range(len(stages))):
            k = j - place * LAG

            @pl.when((k >= 0) & (k < units))
            def _(k=k, run=stages[place]):
                run(k)

        return carry

    lax.fori_loop(0, units + (len(stages) - 1) * LAG, loop_step, 0)


def sum_products(dec_x, dec_g, enc_x, enc_g, code_x, targets, code_g, look_g, call_id):
    dp_size, fsdp_size = lax.axis_size("dp"), lax.axis_size("fsdp")
    devices, Z = dp_size * fsdp_size, fsdp_size // 2
    m = D // devices
    if dp_size != 4 or Z != 4 or m % 32:
        products = [across(dec_x[i], dec_g[min(k, 10)]) for k, i in enumerate(DEC_INPUTS)]
        products += [across(enc_x[i], enc_g[min(k, 10)]) for k, i in enumerate(ENC_INPUTS)]
        plain = jnp.stack(products).astype(BF).reshape(len(products), devices, m, D)
        hit = (targets[:, None] == jnp.arange(VOCAB)[None, :]).astype(BF)
        code = across(jnp.concatenate([code_g, look_g]), jnp.concatenate([code_x, hit])).astype(BF)
        code = code.reshape(dp_size, D // dp_size, fsdp_size, VOCAB // fsdp_size)
        code = code.transpose(0, 2, 1, 3).reshape(devices, D // dp_size, VOCAB // fsdp_size)
        plain = lax.psum_scatter(plain, AXES, scatter_dimension=1, tiled=True)
        code = lax.psum_scatter(code, AXES, scatter_dimension=0, tiled=True)
        return plain.reshape(-1, m, D).astype(F32), code.reshape(D // dp_size, -1).astype(F32)
    n, units = D, len(DEC_INPUTS) + len(ENC_INPUTS) + CODE_UNITS
    depth, half = 2 * LAG, Z // 2
    own_slots, held_slots, kept_slots = LAG + 1, 2 * LAG + 1, Z * LAG + 1
    dec_rows, enc_rows, code_rows = dec_x[0].shape[0], enc_x[0].shape[0], code_x.shape[0]
    dma = pltpu.SemaphoreType.DMA
    whole = pl.BlockSpec(memory_space=pl.ANY)
    out = pl.pallas_call(
        partial(sum_kernel, Z),
        out_shape=jax.ShapeDtypeStruct((units, m, n), F32),
        in_specs=[whole] * 40 + [pl.BlockSpec(memory_space=pltpu.VMEM)] + [whole] * 2,
        out_specs=pl.BlockSpec(memory_space=pltpu.VMEM),
        scratch_shapes=[
            pltpu.VMEM((2, dec_rows, n), BF),
            pltpu.VMEM((2, dec_rows, n), BF),
            pltpu.VMEM((4 * Z, 2, m, dec_rows), BF),
            pltpu.VMEM((2, enc_rows, n), BF),
            pltpu.VMEM((2, enc_rows, n), BF),
            pltpu.VMEM((4 * Z, 2, m, enc_rows), BF),
            pltpu.VMEM((2 * code_rows, VOCAB), BF),
            pltpu.VMEM((2, code_rows, n), BF),
            pltpu.VMEM((4, CODE_UNITS, m, 2 * code_rows), BF),
            pltpu.VMEM((own_slots, 4, Z, m, n), BF),
            pltpu.VMEM((own_slots, 4, Z, m, n), BF),
            pltpu.VMEM((depth, 4, Z, m, n), BF),
            pltpu.VMEM((held_slots, 4, Z, m, n), BF),
            pltpu.VMEM((depth, half, m, n), BF),
            pltpu.VMEM((depth, Z - half, m, n), BF),
            pltpu.VMEM((depth, Z, m, n), BF),
            pltpu.VMEM((depth, Z, m, n), BF),
            pltpu.VMEM((kept_slots, Z, m, n), BF),
            pltpu.VMEM((2, Z - 1, depth, m, n), BF),
            dma((2, 2)),
            dma((3,)),
            dma((depth,)),
            dma((depth,)),
            dma((2, depth)),
            dma((2, depth)),
            dma((2, depth)),
            dma((2, depth)),
            dma((2, Z - 1, depth)),
            dma((2, Z - 1, depth)),
        ],
        compiler_params=pltpu.CompilerParams(
            collective_id=call_id, has_side_effects=True, vmem_limit_bytes=60 << 20
        ),
    )(*dec_x, *dec_g, *enc_x, *enc_g, code_x, targets[:, None], code_g, look_g)
    return out[:-CODE_UNITS], out[-CODE_UNITS:].reshape(-1, n)


def spread_kernel(
    tables, units, Z, table_ref, unit_ref, table_out, unit_out,
    own_sem, line_send, line_recv, square_send, square_recv, core_send, core_recv,
):
    dp, fs = lax.axis_index("dp"), lax.axis_index("fsdp")
    z, core = fs // 2, fs % 2
    x_mate, y_mate = dp + 1 - 2 * (dp % 2), (dp + 2) % 4
    across_dp = (x_mate + 2) % 4
    core_dev, x_dev, y_dev = (dp, fs + 1 - 2 * core), (x_mate, fs), (y_mate, fs)
    up_dev, down_dev = (dp, fs + 2), (dp, fs - 2)
    has_up, has_down = z < Z - 1, z > 0
    total, half = tables + units, Z // 2
    every = slice(None)
    table_rows, table_columns = table_out.shape[2] // tables, table_out.shape[3] // 4

    def at(is_table, k, dp_at, z_at, core_at, part=None):
        if is_table:
            size = table_rows if part is None else table_rows // 2
            rows = pl.ds(k * table_rows + (part or 0) * size, size)
            columns = every if isinstance(dp_at, slice) else pl.ds(dp_at * table_columns, table_columns)
            return table_out.at[z_at, core_at, rows, columns]
        if part is None:
            return unit_out.at[k - tables, dp_at, z_at, core_at]
        size = unit_out.shape[4] // 2
        return unit_out.at[k - tables, dp_at, z_at, core_at, pl.ds(part * size, size)]

    def remote(ref, send, recv, device):
        return pltpu.make_async_remote_copy(
            src_ref=ref, dst_ref=ref, send_sem=send, recv_sem=recv, device_id=device, device_id_type=MESH
        )

    own = (
        pltpu.make_async_copy(
            table_ref, table_out.at[z, core, :, pl.ds(dp * table_columns, table_columns)], own_sem.at[0]
        ),
        pltpu.make_async_copy(unit_ref, unit_out.at[:, dp, z, core], own_sem.at[1]),
    )
    for copy in own:
        copy.start()

    barrier = pltpu.get_barrier_semaphore()
    for device in (core_dev, x_dev, y_dev):
        pl.semaphore_signal(barrier, inc=1, device_id=device, device_id_type=MESH)

    @pl.when(has_up)
    def _():
        pl.semaphore_signal(barrier, inc=1, device_id=up_dev, device_id_type=MESH)

    @pl.when(has_down)
    def _():
        pl.semaphore_signal(barrier, inc=1, device_id=down_dev, device_id_type=MESH)

    for copy in own:
        copy.wait()
    pl.semaphore_wait(barrier, 3 + has_up.astype(jnp.int32) + has_down.astype(jnp.int32))

    def line_copies(view, k, step):
        s = step - 1
        return (
            (remote(view(jnp.maximum(z - s, 0)), line_send.at[0, s, k], line_recv.at[0, s, k], up_dev),
             has_up & (z >= s), has_down & (z >= s + 1)),
            (remote(view(jnp.minimum(z + s, Z - 1)), line_send.at[1, s, k], line_recv.at[1, s, k], down_dev),
             has_down & (z + s <= Z - 1), has_up & (z + s + 1 <= Z - 1)),
        )

    def line_start(view, k, step):
        for copy, sends, _ in line_copies(view, k, step):
            pl.when(sends)(copy.start)

    def line_wait(view, k, step):
        for copy, sends, receives in line_copies(view, k, step):
            pl.when(sends)(copy.wait_send)
            pl.when(receives)(copy.wait_recv)

    def to_core(ref, k, slot):
        return remote(ref, core_send.at[slot, k], core_recv.at[slot, k], core_dev)

    def square_copy(ref, k, slot):
        return remote(
            ref, square_send.at[slot, k], square_recv.at[slot, k], x_dev if slot % 2 == 0 else y_dev
        )

    def line_first(is_table):
        def view(k):
            return lambda place: at(is_table, k, dp, place, core)

        def row(k, dp_at):
            return at(is_table, k, dp_at, every, core)

        def ones(k):
            return square_copy(row(k, dp), k, 0), square_copy(row(k, dp), k, 1)

        def twos(k):
            return (
                square_copy(at(is_table, k, y_mate, pl.ds(0, half), core), k, 2),
                square_copy(at(is_table, k, x_mate, pl.ds(half, Z - half), core), k, 3),
            )

        def line(step):
            def run(k):
                if step > 1:
                    line_wait(view(k), k, step - 1)
                if step < Z:
                    line_start(view(k), k, step)
                else:
                    for copy in ones(k):
                        copy.start()
                    to_core(row(k, dp), k, 0).start()
            return run

        def after_one(k):
            for copy in ones(k):
                copy.wait()
            for copy in twos(k):
                copy.start()
            to_core(row(k, x_mate), k, 1).start()
            to_core(row(k, y_mate), k, 2).start()

        def after_two(k):
            for copy in twos(k):
                copy.wait()
            to_core(row(k, across_dp), k, 3).start()

        def finish(k):
            for slot in range(4):
                to_core(row(k, dp), k, slot).wait()

        return [line(step) for step in range(1, Z + 1)] + [after_one, after_two, finish]

    def square_first(is_table):
        def plane(k):
            return lambda place: at(is_table, k, every, place, core)

        def ones(k):
            ref = at(is_table, k, dp, z, core)
            return square_copy(ref, k, 0), square_copy(ref, k, 1)

        def twos(k):
            return (
                square_copy(at(is_table, k, y_mate, z, core, 0), k, 2),
                square_copy(at(is_table, k, x_mate, z, core, 1), k, 3),
            )

        def begin(k):
            for copy in ones(k):
                copy.start()

        def after_one(k):
            for copy in ones(k):
                copy.wait()
            for copy in twos(k):
                copy.start()

        def after_two(k):
            for copy in twos(k):
                copy.wait()
            line_start(plane(k), k, 1)
            to_core(plane(k)(z), k, z).start()

        def line(step):
            def run(k):
                line_wait(plane(k), k, step)
                if step + 1 < Z:
                    line_start(plane(k), k, step + 1)

                @pl.when(z - step >= 0)
                def _():
                    to_core(plane(k)(jnp.maximum(z - step, 0)), k, jnp.maximum(z - step, 0)).start()

                @pl.when(z + step <= Z - 1)
                def _():
                    to_core(plane(k)(jnp.minimum(z + step, Z - 1)), k, jnp.minimum(z + step, Z - 1)).start()
            return run

        def finish(k):
            for place in range(Z):
                to_core(plane(k)(place), k, place).wait()

        return [begin, after_one, after_two] + [line(step) for step in range(1, Z)] + [finish]

    forms = [(is_table, first, form(is_table))
             for is_table in (True, False) for first, form in ((True, line_first), (False, square_first))]
    n_stages = Z + 3

    def loop_step(j, carry):
        for place in reversed(range(n_stages)):
            k = j - place * LAG
            turn = k % 9
            by_line = (turn != 3) & (turn != 7)
            for is_table, first, stages in forms:
                here = (k >= 0) & (k < tables) if is_table else (k >= tables) & (k < total)
                here = here & (by_line if first else jnp.logical_not(by_line))

                @pl.when(here)
                def _(k=k, run=stages[place]):
                    run(k)

        return carry

    lax.fori_loop(0, total + (n_stages - 1) * LAG, loop_step, 0)


def spread(table, units, call_id):
    count, m, n = units.shape
    Z = lax.axis_size("fsdp") // 2
    if lax.axis_size("dp") != 4 or Z != 4 or m % 32:
        whole = lax.all_gather(lax.all_gather(table, "dp", axis=1, tiled=True), "fsdp", axis=0, tiled=True)
        return whole, lax.all_gather(units, AXES, axis=1, tiled=True)
    tables, dma = 8, pltpu.SemaphoreType.DMA
    total = tables + count
    whole, units = pl.pallas_call(
        partial(spread_kernel, tables, count, Z),
        out_shape=(
            jax.ShapeDtypeStruct((Z, 2, table.shape[0], 4 * table.shape[1]), BF),
            jax.ShapeDtypeStruct((count, 4, Z, 2, m, n), BF),
        ),
        in_specs=[pl.BlockSpec(memory_space=pltpu.VMEM)] * 2,
        out_specs=[pl.BlockSpec(memory_space=pl.ANY)] * 2,
        scratch_shapes=[
            dma((2,)),
            dma((2, Z - 1, total)),
            dma((2, Z - 1, total)),
            dma((4, total)),
            dma((4, total)),
            dma((4, total)),
            dma((4, total)),
        ],
        compiler_params=pltpu.CompilerParams(collective_id=call_id, has_side_effects=True),
    )(table, units)
    return whole.reshape(-1, 4 * table.shape[1]), units.reshape(count, -1, n)


def exchange_kernel(size, inner, in_ref, out_ref, send_sem, recv_sem):
    me = lax.axis_index("dp") * inner + lax.axis_index("fsdp")

    def peer(i):
        other = lax.rem(me + i, size)
        return other, (other // inner, lax.rem(other, inner))

    barrier = pltpu.get_barrier_semaphore()

    def greet(i, carry):
        pl.semaphore_signal(barrier, inc=1, device_id=peer(i)[1], device_id_type=MESH)
        return carry

    def copy(i):
        other, device = peer(i)
        return pltpu.make_async_remote_copy(
            src_ref=in_ref.at[other], dst_ref=out_ref.at[me], send_sem=send_sem.at[i],
            recv_sem=recv_sem.at[i], device_id=device, device_id_type=MESH,
        )

    def begin(i, carry):
        copy(i).start()
        return carry

    def end(i, carry):
        copy(i).wait()
        return carry

    lax.fori_loop(1, size, greet, 0)
    out_ref[me] = in_ref[me]
    pl.semaphore_wait(barrier, size - 1)
    lax.fori_loop(1, size, begin, 0)
    lax.fori_loop(1, size, end, 0)


def exchange(blocks, call_id):
    size, inner = blocks.shape[0], lax.axis_size("fsdp")
    return pl.pallas_call(
        partial(exchange_kernel, size, inner),
        out_shape=jax.ShapeDtypeStruct(blocks.shape, F32),
        in_specs=[pl.BlockSpec(memory_space=pltpu.VMEM)],
        out_specs=pl.BlockSpec(memory_space=pltpu.VMEM),
        scratch_shapes=[pltpu.SemaphoreType.DMA((size,)), pltpu.SemaphoreType.DMA((size,))],
        compiler_params=pltpu.CompilerParams(collective_id=call_id, has_side_effects=True),
    )(blocks)


def tiles(values, count):
    padded = jnp.pad(values, ((0, 1024 - values.shape[0]),)).reshape(1, 8, 128)
    return jnp.broadcast_to(padded, (count, 8, 128))


def swap_groups(parts):
    group = lax.broadcasted_iota(jnp.int32, parts[0].shape, 1) // 32
    results = []
    for i in range(4):
        total = parts[i]
        for j in range(4):
            if j != i:
                turned = pltpu.roll(parts[j], (32 * (j - i)) % 128, 1)
                total = jnp.where(group == j, turned, total)
        results.append(total)
    return results


def norm_kernel(size, inner, plain, code, text, gains, norm_out, squares, gathered, sum_scratch, send_sem, recv_sem):
    rows = plain.shape[1]
    text_rows = [(start, min(rows, text.shape[0] - start)) for start in range(0, text.shape[0], rows)]

    sum_scratch[...] = jnp.zeros_like(sum_scratch)

    def square(k, carry):
        sum_scratch[...] += plain[k] * plain[k]
        return carry

    lax.fori_loop(0, plain.shape[0], square, 0)

    def square_code(k, carry):
        part = code[pl.ds(pl.multiple_of(k * rows, rows), rows), :]
        sum_scratch[...] += part * part
        return carry

    lax.fori_loop(0, code.shape[0] // rows, square_code, 0)
    for start, count in text_rows:
        part = text[pl.ds(start, count), :]
        sum_scratch[pl.ds(0, count), :] += part * part
    own = jnp.sum(sum_scratch[...]) + jnp.sum(gains[...] * gains[...])
    squares[...] = jnp.full(squares.shape, own)

    me = lax.axis_index("dp") * inner + lax.axis_index("fsdp")

    def peer(i):
        other = lax.rem(me + i, size)
        return (other // inner, lax.rem(other, inner))

    def copy(i):
        return pltpu.make_async_remote_copy(
            src_ref=squares, dst_ref=gathered.at[me], send_sem=send_sem.at[i],
            recv_sem=recv_sem.at[i], device_id=peer(i), device_id_type=MESH,
        )

    barrier = pltpu.get_barrier_semaphore()

    def greet(i, carry):
        pl.semaphore_signal(barrier, inc=1, device_id=peer(i), device_id_type=MESH)
        return carry

    def begin(i, carry):
        copy(i).start()
        return carry

    def end(i, carry):
        copy(i).wait()
        return carry

    lax.fori_loop(1, size, greet, 0)
    gathered[me] = squares[...]
    pl.semaphore_wait(barrier, size - 1)
    lax.fori_loop(1, size, begin, 0)
    lax.fori_loop(1, size, end, 0)
    norm = jnp.sqrt(lax.fori_loop(0, size, lambda i, total: total + gathered[i], jnp.zeros_like(squares)))
    norm_out[...] = norm


def update_kernel(*refs):
    norm, plain, code, text, gains, *refs = refs
    weights, refs = refs[:7], refs[7:]
    firsts, refs = refs[:7], refs[7:]
    seconds, refs = refs[:7], refs[7:]
    new_weights, refs = refs[:7], refs[7:]
    new_firsts, new_seconds = refs[:7], refs[7:]
    rows = plain.shape[1]
    text_rows = [(start, min(rows, text.shape[0] - start)) for start in range(0, text.shape[0], rows)]
    factor = (CLIP_NORM / jnp.maximum(norm[...], CLIP_NORM))[:1, :1]

    def step(which, place, gradient):
        updated = adam_step(
            weights[which][place], firsts[which][place], seconds[which][place],
            gradient * factor, STEP_RATES[which],
        )
        for out, value in zip((new_weights, new_firsts, new_seconds), updated):
            out[which][place] = value

    enc = len(DEC_INPUTS)
    every = slice(None)
    for layer, units in enumerate(((enc + 2, enc + 3, enc + 4), (0, 1, 2), (4, enc, enc + 1))):
        for i, unit in enumerate(units):
            step(0, (layer, every, pl.ds(i * D, D)), plain[unit])
    for layer, unit in enumerate((enc + 5, 3, 5)):
        step(1, (layer,), plain[unit])
    for layer, first in enumerate((enc + 6, 6)):
        for g in range(8):
            parts = [plain[first + q, :, pl.ds(128 * g, 128)] for q in range(4)]
            for j, part in enumerate(swap_groups(parts)):
                step(2, (layer, every, pl.ds(128 * (4 * g + j), 128)), part)
    for layer, first in enumerate((enc + 10, 10)):
        for q in range(4):
            step(3, (layer, pl.ds(q * rows, rows), every), plain[first + q])
    step(4, (every, every), gains[...])
    for start, count in text_rows:
        step(5, (pl.ds(start, count), every), text[pl.ds(start, count), :])
    columns = 256
    for i in range(code.shape[1] // columns):
        step(6, (pl.ds(i * columns, columns), every), code[:, pl.ds(i * columns, columns)].T)


def update(plain, code, text, gains, weights, firsts, seconds, call_id):
    inner = lax.axis_size("fsdp")
    size = lax.axis_size("dp") * inner
    shapes = [jax.ShapeDtypeStruct(weight.shape, F32) for weight in weights]
    in_vmem = pl.BlockSpec(memory_space=pltpu.VMEM)
    dma = pltpu.SemaphoreType.DMA
    norm = pl.pallas_call(
        partial(norm_kernel, size, inner),
        out_shape=jax.ShapeDtypeStruct((8, 128), F32),
        in_specs=[in_vmem] * 4,
        out_specs=in_vmem,
        scratch_shapes=[
            pltpu.VMEM((8, 128), F32),
            pltpu.VMEM((size, 8, 128), F32),
            pltpu.VMEM(plain.shape[1:], F32),
            dma((size,)),
            dma((size,)),
        ],
        compiler_params=pltpu.CompilerParams(
            collective_id=call_id, has_side_effects=True, vmem_limit_bytes=32 << 20
        ),
    )(plain, code, text, gains)
    outs = pl.pallas_call(
        update_kernel,
        out_shape=shapes * 3,
        in_specs=[in_vmem] * 26,
        out_specs=[in_vmem] * 21,
        compiler_params=pltpu.CompilerParams(vmem_limit_bytes=60 << 20),
    )(norm, plain, code, text, gains, *weights, *firsts, *seconds)
    return norm[0, 0], list(zip(outs[:7], outs[7:14], outs[14:]))


def layer_norm(stream, gain):
    centred = stream - jnp.mean(stream, axis=-1, keepdims=True)
    return centred * lax.rsqrt(jnp.mean(centred * centred, axis=-1, keepdims=True) + 1e-05) * gain


def norm_back(stream, gain, grad_out):
    _, pullback = jax.vjp(layer_norm, stream, gain)
    return pullback(grad_out)


def positions(length, width):
    position = jnp.arange(length, dtype=jnp.float32)[:, None]
    speeds = jnp.exp(
        -math.log(10000.0) * 2.0 * jnp.arange(width // 2, dtype=jnp.float32)[None, :] / width
    )
    return jnp.concatenate([jnp.sin(position * speeds), jnp.cos(position * speeds)], axis=1)


def matmul(first_op, second_op):
    return jnp.dot(first_op, second_op, preferred_element_type=jnp.float32)


def across(first_op, second_op):
    return lax.dot_general(
        first_op, second_op, (((0,), (0,)), ((), ())), preferred_element_type=jnp.float32
    )


def against(first_op, second_op):
    return lax.dot_general(
        first_op, second_op, (((1,), (1,)), ((), ())), preferred_element_type=jnp.float32
    )


def heads_first(matrix, blocks):
    return matrix.reshape(blocks, -1, HEADS, HEAD).transpose(0, 2, 1, 3)


def heads_last(array):
    return array.transpose(0, 2, 1, 3).reshape(-1, HEADS * HEAD)


def attention(queries, keys_in, values, visible):
    scores = jnp.einsum(
        "bhqd,bhkd->bhqk", queries, keys_in, preferred_element_type=F32
    ) * HEAD ** (-0.5)
    scores = jnp.where(visible[:, None], scores, MASKED)
    weights = jnp.exp(scores - jnp.max(scores, axis=-1, keepdims=True))
    shares = weights / jnp.sum(weights, axis=-1, keepdims=True)
    low = shares.astype(BF)
    attended = jnp.einsum("bhqk,bhkd->bhqd", low, values, preferred_element_type=F32)
    return heads_last(attended.astype(BF)), low


def attention_back(queries, keys_in, values, shares, grad_mixed):
    grad_heads = heads_first(grad_mixed, queries.shape[0])
    grad_shares = jnp.einsum(
        "bhqd,bhkd->bhqk", grad_heads, values, preferred_element_type=F32
    )
    wide = shares.astype(F32)
    grad_scores = (
        wide * (grad_shares - jnp.sum(wide * grad_shares, axis=-1, keepdims=True))
    ).astype(BF)
    grad_query = jnp.einsum(
        "bhqk,bhkd->bhqd", grad_scores, keys_in, preferred_element_type=F32
    ) * HEAD ** (-0.5)
    grad_keys = jnp.einsum(
        "bhqk,bhqd->bhkd", grad_scores, queries, preferred_element_type=F32
    ) * HEAD ** (-0.5)
    grad_values = jnp.einsum(
        "bhqk,bhqd->bhkd", shares, grad_heads, preferred_element_type=F32
    )
    return grad_query, grad_keys, grad_values


def layer_forward(stream, weights, gains, self_visible, memory, cross_visible):
    project, mix_out, cross, cross_out, ffn_up, ffn_down = weights
    blocks = self_visible.shape[0]
    stored = {"stream": stream}
    normed = layer_norm(stream, gains[0]).astype(BF)
    queries, keys_in, values = [
        heads_first(matmul(normed, project[i]).astype(BF), blocks) for i in range(3)
    ]
    attended, shares = attention(queries, keys_in, values, self_visible)
    stream = stream + matmul(attended, mix_out)
    stored.update(
        normed=normed, self_attention=(queries, keys_in, values, shares), attended=attended, after_self=stream
    )
    if memory is not None:
        cross_in = layer_norm(stream, gains[1]).astype(BF)
        cross_query = heads_first(matmul(cross_in, cross[0]).astype(BF), 1)
        memory_keys = heads_first(matmul(memory, cross[1]).astype(BF), 1)
        memory_values = heads_first(matmul(memory, cross[2]).astype(BF), 1)
        cross_mixed, cross_shares = attention(cross_query, memory_keys, memory_values, cross_visible)
        stream = stream + matmul(cross_mixed, cross_out)
        stored.update(
            cross_in=cross_in,
            cross_attention=(cross_query, memory_keys, memory_values, cross_shares),
            cross_mixed=cross_mixed,
        )
    stored["before_ffn"] = stream
    ffn_in = layer_norm(stream, gains[-2]).astype(BF)
    hidden_pre = [matmul(ffn_in, up) for up in ffn_up]
    hidden = [jax.nn.gelu(pre, approximate=True).astype(BF) for pre in hidden_pre]
    for low, down in zip(hidden, ffn_down):
        stream = stream + matmul(low, down)
    stored.update(ffn_in=ffn_in, hidden_pre=hidden_pre, hidden=hidden, before_final=stream)
    return layer_norm(stream, gains[-1]).astype(BF), stored


def layer_backward(grad_final, weights, gains, stored, memory):
    project, mix_out, cross, cross_out, ffn_up, ffn_down = weights
    gain_grads = [None] * len(gains)
    grad_stream, gain_grads[-1] = norm_back(stored["before_final"], gains[-1], grad_final)
    ffn_low = grad_stream.astype(BF)
    grad_pres = []
    grad_ffn = 0.0
    for pre, up, down in zip(stored["hidden_pre"], ffn_up, ffn_down):
        _, gelu_pull = jax.vjp(partial(jax.nn.gelu, approximate=True), pre)
        grad_pres.append(gelu_pull(against(ffn_low, down))[0].astype(BF))
        grad_ffn = grad_ffn + against(grad_pres[-1], up)
    grad_normed, gain_grads[-2] = norm_back(stored["before_ffn"], gains[-2], grad_ffn)
    grad_stream = grad_stream + grad_normed
    cross_inputs, cross_grads, memory_grads = [], [], []
    grad_memory = None
    if memory is not None:
        cross_low = grad_stream.astype(BF)
        grad_mixed = against(cross_low, cross_out).astype(BF)
        grads = [
            heads_last(grad.astype(BF)) for grad in attention_back(*stored["cross_attention"], grad_mixed)
        ]
        cross_inputs = [stored["cross_in"], stored["cross_mixed"]]
        cross_grads = [grads[0], cross_low]
        memory_grads = grads[1:]
        grad_memory = against(grads[1], cross[1]) + against(grads[2], cross[2])
        grad_normed, gain_grads[1] = norm_back(
            stored["after_self"], gains[1], against(grads[0], cross[0])
        )
        grad_stream = grad_stream + grad_normed
    self_low = grad_stream.astype(BF)
    grad_mixed = against(self_low, mix_out).astype(BF)
    grads = [
        heads_last(grad.astype(BF)) for grad in attention_back(*stored["self_attention"], grad_mixed)
    ]
    grad_normed, gain_grads[0] = norm_back(
        stored["stream"],
        gains[0],
        sum(against(grads[i], project[i]) for i in range(3)),
    )
    grad_stream = grad_stream + grad_normed
    inputs = [stored["normed"], stored["attended"], *cross_inputs, stored["ffn_in"], *stored["hidden"]]
    outputs = [*grads, self_low, *cross_grads, *grad_pres, ffn_low]
    parts = (inputs, outputs) if memory is None else (inputs, outputs, memory_grads)
    return grad_stream, grad_memory, gain_grads, parts


def adam_step(weight, moment_one, second, gradient, rate):
    moment_one = BETA_ONE * moment_one + (1.0 - BETA_ONE) * gradient
    second = BETA_TWO * second + (1.0 - BETA_TWO) * gradient * gradient
    first_hat = moment_one / (1.0 - BETA_ONE**STEP)
    second_hat = second / (1.0 - BETA_TWO**STEP)
    weight = weight - rate * (first_hat / (jnp.sqrt(second_hat) + ADAM_EPS) + WEIGHT_DECAY * weight)
    return (weight, moment_one, second)


def column_units(matrix):
    return matrix.reshape(matrix.shape[0], -1, D).transpose(1, 0, 2)


def from_column_units(units):
    return units.transpose(1, 0, 2).reshape(units.shape[1], -1)


def hidden_units(matrix, devices):
    rows, width = matrix.shape
    return (
        matrix.reshape(rows, devices, 4, width // devices // 4)
        .transpose(2, 0, 1, 3)
        .reshape(4, rows, width // 4)
    )


def from_hidden_units(units, devices):
    quarters, rows, width = units.shape
    return (
        units.reshape(quarters, rows, devices, width // devices)
        .transpose(1, 2, 0, 3)
        .reshape(rows, quarters * width)
    )


def on_device(
    text_ids,
    text_segments,
    codes,
    caption_of,
    mix_in,
    mix_out,
    ffn_up,
    ffn_down,
    norm_gains,
    text_table,
    code_table,
    mix_in_first,
    mix_out_first,
    ffn_up_first,
    ffn_down_first,
    gains_first,
    text_first,
    code_first,
    mix_in_second,
    mix_out_second,
    ffn_up_second,
    ffn_down_second,
    gains_second,
    text_second,
    code_second,
):
    image_count = codes.shape[0]
    dp_size, fsdp_size = lax.axis_size("dp"), lax.axis_size("fsdp")
    devices = dp_size * fsdp_size
    me = lax.axis_index("dp") * fsdp_size + lax.axis_index("fsdp")
    token_total = image_count * IMG_LEN * devices
    inverse = 1.0 / token_total
    scale_in = math.sqrt(D)
    rows = mix_in.shape[1]
    segments = text_segments[0]
    text_visible = (segments[:, None] == segments[None, :])[None]
    place = jnp.arange(IMG_LEN)
    self_visible = jnp.broadcast_to(
        place[None, :] <= place[:, None], (image_count, IMG_LEN, IMG_LEN)
    )
    wanted = jnp.repeat(caption_of, IMG_LEN)
    cross_visible = (segments[None, :] == wanted[:, None])[None]

    small = tiles(jnp.concatenate([text_ids[0].astype(F32), norm_gains.reshape(-1)]), devices)
    small = exchange(small, 3).reshape(devices, 1024)[:, : TXT_LEN + 7 * norm_gains.shape[1]]
    all_ids = small[:, :TXT_LEN].astype(jnp.int32).reshape(-1)
    gains = small[:, TXT_LEN:].reshape(devices, 7, -1).transpose(1, 0, 2).reshape(7, D)
    gains = gains.astype(BF).astype(F32)

    base = me * text_table.shape[0]
    owned = (all_ids[:, None] - base == jnp.arange(text_table.shape[0])[None, :]).astype(BF)
    looked = matmul(owned, text_table.astype(BF)).astype(BF)
    text_rows = lax.psum_scatter(looked, AXES, scatter_dimension=0, tiled=True)

    def layer_units(which):
        return [
            column_units(mix_in[which]),
            mix_out[which][None],
            hidden_units(ffn_up[min(which, 1)], devices),
            ffn_down[min(which, 1)].reshape(4, rows, D),
        ]

    shards = layer_units(0) + layer_units(1)[:2] + layer_units(2)
    code_full, units = spread(code_table.astype(BF), jnp.concatenate(shards).astype(BF), 4)
    enc_units, self_units, late_units = units[:12], units[12:16], units[16:]
    enc_weights = (enc_units[:3], enc_units[3], None, None, enc_units[4:8], enc_units[8:])
    dec_weights = (
        self_units[:3], self_units[3], late_units[:3], late_units[3], late_units[4:8], late_units[8:]
    )

    text_in = text_rows.astype(F32) * scale_in + positions(TXT_LEN, D)
    enc_gains = [gains[i] for i in range(3)]
    dec_gains = [gains[i] for i in range(3, 7)]
    memory, enc_stored = layer_forward(text_in, enc_weights, enc_gains, text_visible, None, None)

    image_rows = code_full[codes].astype(F32) * scale_in
    shifted = jnp.concatenate([jnp.zeros_like(image_rows[:, :1]), image_rows[:, :-1]], axis=1)
    image_in = (shifted + positions(IMG_LEN, D)[None]).reshape(-1, D)
    final_out, dec_stored = layer_forward(
        image_in, dec_weights, dec_gains, self_visible, memory, cross_visible
    )

    targets = codes.reshape(-1)
    logits = against(final_out, code_full)
    hit = targets[:, None] == jnp.arange(VOCAB)[None, :]
    top = jnp.max(logits, axis=1, keepdims=True)
    log_total = top + jnp.log(jnp.sum(jnp.exp(logits - top), axis=1, keepdims=True))
    weighted = jnp.sum(
        logits * jnp.where(hit, 1.0 - SMOOTH + SMOOTH / VOCAB, SMOOTH / VOCAB), axis=1, keepdims=True
    )
    loss_part = jnp.sum(log_total - weighted)
    grad_logits = (
        (jnp.exp(logits - log_total) - jnp.where(hit, 1.0 - SMOOTH, 0.0) - SMOOTH / VOCAB) * inverse
    ).astype(BF)
    grad_final = matmul(grad_logits, code_full)

    grad_image, grad_memory, dec_gain_grads, dec_parts = layer_backward(
        grad_final, dec_weights, dec_gains, dec_stored, memory
    )
    grad_text, _, enc_gain_grads, enc_parts = layer_backward(
        grad_memory, enc_weights, enc_gains, enc_stored, None
    )
    gain_part = jnp.stack(enc_gain_grads + dec_gain_grads)

    grad_rows = lax.all_gather((grad_text * scale_in).astype(BF), AXES, axis=0, tiled=True)
    text_grad = across(owned, grad_rows)

    grad_looked = grad_image.reshape(image_count, IMG_LEN, D)[:, 1:] * scale_in
    grad_looked = jnp.pad(grad_looked, ((0, 0), (0, 1), (0, 0))).reshape(-1, D).astype(BF)
    enc_x, enc_g = enc_parts
    dec_x, dec_g, memory_g = dec_parts
    plain_sum, code_sum = sum_products(
        dec_x, dec_g, [memory] + enc_x, memory_g + enc_g, grad_logits, targets, final_out, grad_looked, 1
    )
    gain_blocks = gain_part.reshape(7, devices, rows).transpose(1, 0, 2).reshape(devices, 7 * rows)
    gain_blocks = jnp.concatenate([gain_blocks, jnp.full((devices, 1), loss_part)], axis=1)
    gain_blocks = jnp.pad(gain_blocks, ((0, 0), (0, 1024 - gain_blocks.shape[1])))
    small_sum = jnp.sum(exchange(gain_blocks.reshape(devices, 8, 128), 5), axis=0).reshape(-1)
    loss_sum = small_sum[7 * rows]
    gains_grad = small_sum[: 7 * rows].reshape(7, rows)
    params = (mix_in, mix_out, ffn_up, ffn_down, norm_gains, text_table, code_table)
    firsts = (
        mix_in_first,
        mix_out_first,
        ffn_up_first,
        ffn_down_first,
        gains_first,
        text_first,
        code_first,
    )
    seconds = (
        mix_in_second,
        mix_out_second,
        ffn_up_second,
        ffn_down_second,
        gains_second,
        text_second,
        code_second,
    )
    if rows == 32:
        grad_norm, updated = update(
            plain_sum, code_sum, text_grad, gains_grad, params, firsts, seconds, 6
        )
    else:
        dec_sum, enc_sum = plain_sum[:14], plain_sum[14:]
        gradients = (
            jnp.stack(
                [
                    from_column_units(part)
                    for part in (enc_sum[2:5], dec_sum[:3], jnp.concatenate([dec_sum[4:5], enc_sum[:2]]))
                ]
            ),
            jnp.stack([enc_sum[5], dec_sum[3], dec_sum[5]]),
            jnp.stack([from_hidden_units(part, devices) for part in (enc_sum[6:10], dec_sum[6:10])]),
            jnp.stack([part.reshape(-1, D) for part in (enc_sum[10:], dec_sum[10:])]),
            gains_grad,
            text_grad,
            code_sum.T,
        )
        square_part = sum((jnp.sum(gradient * gradient) for gradient in gradients))
        squares = exchange(tiles(square_part[None], devices), 6)[:, 0, 0]
        grad_norm = jnp.sqrt(jnp.sum(squares))
        factor = CLIP_NORM / jnp.maximum(grad_norm, CLIP_NORM)
        updated = [
            adam_step(
                params[index],
                firsts[index],
                seconds[index],
                gradients[index] * factor,
                STEP_RATES[index],
            )
            for index in range(7)
        ]
    return (
        loss_sum,
        grad_norm,
        updated[0][0],
        updated[1][0],
        updated[2][0],
        updated[3][0],
        updated[4][0],
        updated[5][0],
        updated[6][0],
        updated[0][1],
        updated[1][1],
        updated[2][1],
        updated[3][1],
        updated[4][1],
        updated[5][1],
        updated[6][1],
        updated[0][2],
        updated[1][2],
        updated[2][2],
        updated[3][2],
        updated[4][2],
        updated[5][2],
        updated[6][2],
    )


def solution(mesh):
    return jax.shard_map(
        on_device,
        mesh=mesh,
        in_specs=(
            P(("dp", "fsdp"), None),
            P(("dp", "fsdp"), None),
            P(("dp", "fsdp"), None),
            P(("dp", "fsdp")),
            P(None, ("dp", "fsdp"), None),
            P(None, ("dp", "fsdp"), None),
            P(None, ("dp", "fsdp"), None),
            P(None, ("dp", "fsdp"), None),
            P(None, ("dp", "fsdp")),
            P(("dp", "fsdp"), None),
            P("fsdp", "dp"),
            P(None, ("dp", "fsdp"), None),
            P(None, ("dp", "fsdp"), None),
            P(None, ("dp", "fsdp"), None),
            P(None, ("dp", "fsdp"), None),
            P(None, ("dp", "fsdp")),
            P(("dp", "fsdp"), None),
            P("fsdp", "dp"),
            P(None, ("dp", "fsdp"), None),
            P(None, ("dp", "fsdp"), None),
            P(None, ("dp", "fsdp"), None),
            P(None, ("dp", "fsdp"), None),
            P(None, ("dp", "fsdp")),
            P(("dp", "fsdp"), None),
            P("fsdp", "dp"),
        ),
        out_specs=(
            P(),
            P(),
            P(None, ("dp", "fsdp"), None),
            P(None, ("dp", "fsdp"), None),
            P(None, ("dp", "fsdp"), None),
            P(None, ("dp", "fsdp"), None),
            P(None, ("dp", "fsdp")),
            P(("dp", "fsdp"), None),
            P("fsdp", "dp"),
            P(None, ("dp", "fsdp"), None),
            P(None, ("dp", "fsdp"), None),
            P(None, ("dp", "fsdp"), None),
            P(None, ("dp", "fsdp"), None),
            P(None, ("dp", "fsdp")),
            P(("dp", "fsdp"), None),
            P("fsdp", "dp"),
            P(None, ("dp", "fsdp"), None),
            P(None, ("dp", "fsdp"), None),
            P(None, ("dp", "fsdp"), None),
            P(None, ("dp", "fsdp"), None),
            P(None, ("dp", "fsdp")),
            P(("dp", "fsdp"), None),
            P("fsdp", "dp"),
        ),
        check_vma=False,
    )
```

```python
from functools import partial
import math

import jax
import jax.numpy as jnp
from jax import lax
from jax.experimental import pallas as pl
from jax.experimental.pallas import tpu as pltpu
from jax.sharding import PartitionSpec as P

D = 1024
HEADS = 16
HEAD = 64
VOCAB = 8192
TVOC = 16000
IMG_LEN = 256
TXT_LEN = 128
STEP = 5


SMOOTH = 0.1
BETA_ONE = 0.5
BETA_TWO = 0.5
WEIGHT_DECAY = 0.1
ADAM_EPS = 1e-08
CLIP_NORM = 0.02
MASKED = -1e30
STEP_RATES = (0.02, 0.15, 0.02, 0.01, 0.3, 0.02, 0.03)

BF = jnp.bfloat16
F32 = jnp.float32
AXES = ("dp", "fsdp")
MESH = pl.DeviceIdType.MESH
LAG = 2


DEC_INPUTS = (0, 0, 0, 1, 2, 3, 4, 4, 4, 4, 5, 6, 7, 8)
ENC_INPUTS = (0, 0, 1, 1, 1, 2, 3, 3, 3, 3, 4, 5, 6, 7)
CODE_UNITS = 8


def place_of(Z):
    dp, fs = lax.axis_index("dp"), lax.axis_index("fsdp")
    z, core = fs // 2, fs % 2
    x_mate, y_mate = dp + 1 - 2 * (dp % 2), (dp + 2) % 4
    devices = ((dp, fs + 1 - 2 * core), (x_mate, fs), (y_mate, fs), (dp, fs + 2), (dp, fs - 2))
    return dp, z, core, x_mate, y_mate, (x_mate + 2) % 4, devices, z < Z - 1, z > 0


def add(a, b):
    return (a.astype(F32) + b.astype(F32)).astype(BF)


def remote(src, dst, send, recv, device):
    return pltpu.make_async_remote_copy(
        src_ref=src, dst_ref=dst, send_sem=send, recv_sem=recv, device_id=device, device_id_type=MESH
    )


def sum_scratch(Z, m, n):
    depth, half = 2 * LAG, Z // 2
    own_slots, held_slots, kept_slots = LAG + 1, 2 * LAG + 1, Z * LAG + 1
    return [
        pltpu.VMEM((own_slots, 4, Z, m, n), BF),
        pltpu.VMEM((depth, 4, Z, m, n), BF),
        pltpu.VMEM((held_slots, 4, Z, m, n), BF),
        pltpu.VMEM((depth, half, m, n), BF),
        pltpu.VMEM((depth, Z - half, m, n), BF),
        pltpu.VMEM((depth, Z, m, n), BF),
        pltpu.VMEM((depth, Z, m, n), BF),
        pltpu.VMEM((kept_slots, Z, m, n), BF),
        pltpu.VMEM((2, Z - 1, depth, m, n), BF),
    ]


def sum_semaphores(Z):
    depth, dma = 2 * LAG, pltpu.SemaphoreType.DMA
    return [
        dma((depth,)),
        dma((depth,)),
        dma((2, depth)),
        dma((2, depth)),
        dma((2, depth)),
        dma((2, depth)),
        dma((2, Z - 1, depth)),
        dma((2, Z - 1, depth)),
    ]


def sum_stages(Z, scratch, semaphores, arrive, out_ref):
    own, from_core, held, from_x, from_y, all_x, all_y, kept, from_line = scratch
    _, _, one_send, one_recv, two_send, two_recv, line_send, line_recv = semaphores
    dp, z, core, x_mate, y_mate, across_dp, devices, has_up, has_down = place_of(Z)
    _, x_dev, y_dev, up_dev, down_dev = devices
    depth, half = 2 * LAG, Z // 2
    own_slots, held_slots, kept_slots = own.shape[0], held.shape[0], kept.shape[0]

    def one_copies(k):
        s, block = k % depth, held.at[k % held_slots, across_dp]
        return (
            remote(block.at[pl.ds(0, half)], from_x.at[s], one_send.at[0, s], one_recv.at[0, s], x_dev),
            remote(block.at[pl.ds(half, Z - half)], from_y.at[s], one_send.at[1, s], one_recv.at[1, s], y_dev),
        )

    def two_copies(k):
        s, h = k % depth, k % held_slots
        return (
            remote(held.at[h, x_mate], all_x.at[s], two_send.at[0, s], two_recv.at[0, s], x_dev),
            remote(held.at[h, y_mate], all_y.at[s], two_send.at[1, s], two_recv.at[1, s], y_dev),
        )

    def up_block(step):
        return jnp.minimum(z + Z - step, Z - 1)

    def down_block(step):
        return jnp.maximum(z - Z + step, 0)

    def up_copy(k, step):
        s = k % depth
        return remote(
            kept.at[k % kept_slots, up_block(step)], from_line.at[0, step - 1, s],
            line_send.at[0, step - 1, s], line_recv.at[0, step - 1, s], up_dev,
        )

    def down_copy(k, step):
        s = k % depth
        return remote(
            kept.at[k % kept_slots, down_block(step)], from_line.at[1, step - 1, s],
            line_send.at[1, step - 1, s], line_recv.at[1, step - 1, s], down_dev,
        )

    def line_start(k, step):
        @pl.when(has_up)
        def _():
            up_copy(k, step).start()

        @pl.when(has_down)
        def _():
            down_copy(k, step).start()

    def line_wait(k, step):
        @pl.when(has_down)
        def _():
            up_copy(k, step).wait_recv()
            down_copy(k, step).wait_send()

        @pl.when(has_up)
        def _():
            down_copy(k, step).wait_recv()
            up_copy(k, step).wait_send()

    def after_core(k):
        arrive(k)

        def one(block, carry):
            for q in range(Z):
                held[k % held_slots, block, q] = add(
                    own[k % own_slots, block, q], from_core[k % depth, block, q]
                )
            return carry

        lax.fori_loop(0, 4, one, 0)
        for copy in one_copies(k):
            copy.start()

    def after_one(k):
        s, h = k % depth, k % held_slots
        for copy in one_copies(k):
            copy.wait()
        for q in range(half):
            held[h, y_mate, q] = add(held[h, y_mate, q], from_x[s, q])
        for q in range(Z - half):
            held[h, x_mate, half + q] = add(held[h, x_mate, half + q], from_y[s, q])
        for copy in two_copies(k):
            copy.start()

    def after_two(k):
        s, h = k % depth, k % held_slots
        for copy in two_copies(k):
            copy.wait()
        for q in range(Z):
            kept[k % kept_slots, q] = (
                held[h, dp, q].astype(F32) + all_x[s, q].astype(F32) + all_y[s, q].astype(F32)
            ).astype(BF)
        line_start(k, 1)

    def along_line(step):
        def run(k):
            s, h = k % depth, k % kept_slots
            line_wait(k, step - 1)

            @pl.when(has_down & (z + Z - step <= Z - 1))
            def _():
                kept[h, up_block(step)] = add(kept[h, up_block(step)], from_line[0, step - 2, s])

            @pl.when(has_up & (z - Z + step >= 0))
            def _():
                kept[h, down_block(step)] = add(kept[h, down_block(step)], from_line[1, step - 2, s])

            line_start(k, step)

        return run

    def finish(k):
        s = k % depth
        line_wait(k, Z - 1)
        out_ref[k] = kept[k % kept_slots, z].astype(F32)

        @pl.when(has_down)
        def _():
            out_ref[k] = out_ref[k] + from_line[0, Z - 2, s].astype(F32)

        @pl.when(has_up)
        def _():
            out_ref[k] = out_ref[k] + from_line[1, Z - 2, s].astype(F32)

    stages = [after_core, after_one, after_two]
    return stages + [along_line(step) for step in range(2, Z)] + [finish], up_block, down_block


def sum_kernel(Z, counts, *refs):
    groups = []
    for count in counts:
        groups.append([ref.at[i] for ref in refs[:count] for i in range(ref.shape[0])])
        refs = refs[count:]
    dec_x, dec_g, enc_x, enc_g = groups
    (
        code_x, targets, code_g, look_g, out_ref,
        dec_xs, dec_gs, dec_turned, enc_xs, enc_gs, enc_turned, code_xs, code_loaded, code_gs, to_core,
        own, from_core, held, from_x, from_y, all_x, all_y, kept, from_line,
        rare_held, rare_line, rare_kept, rare_x, rare_y, rare_all_x, rare_all_y,
        load_sem, code_sem, core_send, core_recv, one_send, one_recv, two_send, two_recv, line_send, line_recv,
        rare_line_send, rare_line_recv, rare_send, rare_recv,
    ) = refs
    dec_units, enc_units = len(DEC_INPUTS), len(ENC_INPUTS)
    plain_units = dec_units + enc_units
    units = plain_units + CODE_UNITS
    depth = 2 * LAG
    dp, fs = lax.axis_index("dp"), lax.axis_index("fsdp")
    z, core = fs // 2, fs % 2
    x_mate, y_mate = dp + 1 - 2 * (dp % 2), (dp + 2) % 4
    across_dp = (x_mate + 2) % 4
    core_dev, x_dev, y_dev = (dp, fs + 1 - 2 * core), (x_mate, fs), (y_mate, fs)
    up_dev, down_dev = (dp, fs + 2), (dp, fs - 2)
    has_up, has_down = z < Z - 1, z > 0

    barrier = pltpu.get_barrier_semaphore()
    for device in (core_dev, x_dev, y_dev):
        pl.semaphore_signal(barrier, inc=1, device_id=device, device_id_type=MESH)

    @pl.when(has_up)
    def _():
        pl.semaphore_signal(barrier, inc=1, device_id=up_dev, device_id_type=MESH)

    @pl.when(has_down)
    def _():
        pl.semaphore_signal(barrier, inc=1, device_id=down_dev, device_id_type=MESH)

    pl.semaphore_wait(barrier, 3 + has_up.astype(jnp.int32) + has_down.astype(jnp.int32))
    scratch = (own, from_core, held, from_x, from_y, all_x, all_y, kept, from_line)
    semaphores = (
        core_send, core_recv, one_send, one_recv, two_send, two_recv, line_send, line_recv
    )
    own_slots = own.shape[0]

    def pair(x, g, xs, gs, slot):
        return (
            pltpu.make_async_copy(x, xs.at[slot], load_sem.at[0, slot]),
            pltpu.make_async_copy(g, gs.at[slot], load_sem.at[1, slot]),
        )

    def start_loads(k):
        for i, place in enumerate(DEC_INPUTS):

            @pl.when(k == i)
            def _(i=i, place=place):
                for copy in pair(dec_x[place], dec_g[min(i, 10)], dec_xs, dec_gs, i % 2):
                    copy.start()

        for i, place in enumerate(ENC_INPUTS):

            @pl.when(k == dec_units + i)
            def _(i=i, place=place):
                for copy in pair(enc_x[place], enc_g[min(i, 10)], enc_xs, enc_gs, (dec_units + i) % 2):
                    copy.start()

    code_rows = code_x.shape[0]
    code_loads = [
        pltpu.make_async_copy(code_x, code_xs.at[pl.ds(0, code_rows)], code_sem.at[0]),
        pltpu.make_async_copy(code_g, code_loaded.at[0], code_sem.at[1]),
        pltpu.make_async_copy(look_g, code_loaded.at[1], code_sem.at[2]),
    ]
    for copy in code_loads:
        copy.start()
    start_loads(jnp.int32(0))

    def core_copy(k):
        s = k % depth
        return remote(
            to_core.at[k % own_slots], from_core.at[s], core_send.at[s], core_recv.at[s], core_dev
        )

    def turn(xs, slot, turned):
        size = 256

        def columns(i, carry):
            part = xs[slot, :, pl.ds(pl.multiple_of(i * size, size), size)].T
            count = size // (2 * turned.shape[2])
            turned[pl.ds(i * count, count)] = part.reshape(count, *turned.shape[1:])
            return carry

        lax.fori_loop(0, xs.shape[2] // size, columns, 0)

    def product(turned, gs, slot, side, into):
        def rows(block, carry):
            value = turned[pl.ds(block * Z, Z), side].reshape(-1, turned.shape[-1])
            result = jnp.dot(value, gs[slot], preferred_element_type=F32).astype(BF)
            into[block] = result.reshape(into.shape[1:])
            return carry

        lax.fori_loop(0, 4, rows, 0)

    def code_inputs():
        for copy in code_loads:
            copy.wait()
        size = D // 4
        for half_rows in range(2):

            def turn_columns(i, carry, half_rows=half_rows):
                part = code_loaded[half_rows, :, pl.ds(pl.multiple_of(i * size, size), size)].T
                code_gs[i, :, :, pl.ds(half_rows * code_rows, code_rows)] = part.reshape(
                    CODE_UNITS, size // CODE_UNITS, code_rows
                )
                return carry

            lax.fori_loop(0, 4, turn_columns, 0)

        width = 512

        def hits(i, carry):
            start = pl.multiple_of(i * width, width)
            column = lax.broadcasted_iota(jnp.int32, (code_rows, width), 1) + i * width
            code_xs[pl.ds(code_rows, code_rows), pl.ds(start, width)] = jnp.where(
                targets[...] == column, 1.0, 0.0
            ).astype(BF)
            return carry

        lax.fori_loop(0, VOCAB // width, hits, 0)

    def code_product(k, side, into):
        value = code_gs[:, k - plain_units].reshape(-1, code_gs.shape[-1])
        width = into.shape[-1]

        def columns(place, carry):
            start = pl.multiple_of((2 * place + side) * width, width)
            result = jnp.dot(value, code_xs[:, pl.ds(start, width)], preferred_element_type=F32).astype(BF)
            into[:, place] = result.reshape(4, -1, width)
            return carry

        lax.fori_loop(0, Z, columns, 0)

    def begin(k):
        slot, o = k % 2, k % own_slots
        for here, x, g, xs, gs, turned in (
            (k < dec_units, dec_x[0], dec_g[0], dec_xs, dec_gs, dec_turned),
            ((k >= dec_units) & (k < plain_units), enc_x[0], enc_g[0], enc_xs, enc_gs, enc_turned),
        ):

            @pl.when(here)
            def _(x=x, g=g, xs=xs, gs=gs, turned=turned):
                for copy in pair(x, g, xs, gs, slot):
                    copy.wait()
                start_loads(k + 1)
                turn(xs, slot, turned)
                product(turned, gs, slot, 1 - core, to_core.at[o])
                core_copy(k).start()
                product(turned, gs, slot, core, own.at[o])

        @pl.when(k == dec_units)
        def _():
            code_inputs()

        @pl.when(k >= plain_units)
        def _():
            code_product(k, 1 - core, to_core.at[o])
            core_copy(k).start()
            code_product(k, core, own.at[o])

    def arrive(k):
        core_copy(k).wait()

    later, up_block, down_block = sum_stages(Z, scratch, semaphores, arrive, out_ref)

    def turn_of(k):
        return (k // 9) * 2 + (k % 9 >= 7).astype(jnp.int32)

    def rare_slot(k):
        return turn_of(k) % rare_held.shape[0]

    def rare_line_copies(k, step):
        t, s = turn_of(k), rare_slot(k)
        return [
            remote(
                rare_held.at[s, :, block], rare_line.at[s, way, step - 1],
                rare_line_send.at[way, step - 1, t], rare_line_recv.at[way, step - 1, t], device,
            )
            for way, block, device in ((0, up_block(step), up_dev), (1, down_block(step), down_dev))
        ]

    def rare_valid(step):
        return (has_up & (z + Z - step <= Z - 1), has_down & (z - Z + step >= 0)), (
            has_down & (z - 1 + Z - step <= Z - 1),
            has_up & (z + 1 - Z + step >= 0),
        )

    def rare_line_start(k, step):
        for copy, sends in zip(rare_line_copies(k, step), rare_valid(step)[0]):
            pl.when(sends)(copy.start)

    def rare_line_wait(k, step):
        for copy, sends, receives in zip(rare_line_copies(k, step), *rare_valid(step)):
            pl.when(sends)(copy.wait_send)
            pl.when(receives)(copy.wait_recv)

    def rare_add(into, k, step):
        for way, receives in enumerate(rare_valid(step)[1]):

            @pl.when(receives)
            def _(way=way):
                for block in range(4):
                    ref = into(way, block)
                    ref[...] = add(ref[...], rare_line[rare_slot(k), way, step - 1, block])

    def rare_square(k, slot):
        t, s = turn_of(k), rare_slot(k)
        small = rare_kept.shape[2] // 2
        source, target, device = (
            (rare_kept.at[s, across_dp, pl.ds(0, small)], rare_x.at[s], x_dev),
            (rare_kept.at[s, across_dp, pl.ds(small, small)], rare_y.at[s], y_dev),
            (rare_kept.at[s, x_mate], rare_all_x.at[s], x_dev),
            (rare_kept.at[s, y_mate], rare_all_y.at[s], y_dev),
        )[slot]
        return remote(source, target, rare_send.at[slot, t], rare_recv.at[slot, t], device)

    def rare_after_core(k):
        core_copy(k).wait()

        def one(block, carry):
            for q in range(Z):
                rare_held[rare_slot(k), block, q] = add(
                    own[k % own_slots, block, q], from_core[k % depth, block, q]
                )
            return carry

        lax.fori_loop(0, 4, one, 0)
        rare_line_start(k, 1)

    def rare_along(step):
        def run(k):
            rare_line_wait(k, step - 1)
            s = rare_slot(k)
            rare_add(
                lambda way, block: rare_held.at[s, block, (up_block, down_block)[way](step)], k, step - 1
            )
            rare_line_start(k, step)

        return run

    def rare_after_line(k):
        rare_line_wait(k, Z - 1)
        s = rare_slot(k)
        for block in range(4):
            rare_kept[s, block] = rare_held[s, block, z]
        rare_add(lambda way, block: rare_kept.at[s, block], k, Z - 1)
        for slot in range(2):
            rare_square(k, slot).start()

    def rare_after_one(k):
        s, small = rare_slot(k), rare_kept.shape[2] // 2
        for slot in range(2):
            rare_square(k, slot).wait()
        first, second = pl.ds(0, small), pl.ds(small, small)
        rare_kept[s, y_mate, first] = add(rare_kept[s, y_mate, first], rare_x[s])
        rare_kept[s, x_mate, second] = add(rare_kept[s, x_mate, second], rare_y[s])
        for slot in range(2, 4):
            rare_square(k, slot).start()

    def rare_finish(k):
        s = rare_slot(k)
        for slot in range(2, 4):
            rare_square(k, slot).wait()
        out_ref[k] = (
            rare_kept[s, dp].astype(F32) + rare_all_x[s].astype(F32) + rare_all_y[s].astype(F32)
        )

    stages = [begin] + later
    rare_stages = [begin, rare_after_core] + [rare_along(step) for step in range(2, Z)]
    rare_stages += [rare_after_line, rare_after_one, rare_finish]

    def loop_step(j, carry):
        for place in reversed(range(len(stages))):
            k = j - place * LAG
            here = (k >= 0) & (k < units)
            rare = (k % 9 == 3) | (k % 9 == 7)
            if place == 0:
                pl.when(here)(partial(begin, k))
            else:
                pl.when(here & jnp.logical_not(rare))(partial(stages[place], k))
                pl.when(here & rare)(partial(rare_stages[place], k))
        return carry

    lax.fori_loop(0, units + (len(stages) - 1) * LAG, loop_step, 0)


def sum_products(dec_x, dec_g, enc_x, enc_g, code_x, targets, code_g, look_g, call_id):
    dp_size, fsdp_size = lax.axis_size("dp"), lax.axis_size("fsdp")
    devices, Z = dp_size * fsdp_size, fsdp_size // 2
    m = D // devices
    stacks = (dec_x, dec_g, enc_x, enc_g)
    if dp_size != 4 or Z != 4 or m % 32:
        dec_x, dec_g, enc_x, enc_g = [[row for stack in group for row in stack] for group in stacks]
        products = [across(dec_x[i], dec_g[min(k, 10)]) for k, i in enumerate(DEC_INPUTS)]
        products += [across(enc_x[i], enc_g[min(k, 10)]) for k, i in enumerate(ENC_INPUTS)]
        plain = jnp.stack(products).astype(BF).reshape(len(products), devices, m, D)
        hit = (targets[:, None] == jnp.arange(VOCAB)[None, :]).astype(BF)
        code = across(jnp.concatenate([code_g, look_g]), jnp.concatenate([code_x, hit])).astype(BF)
        code = code.reshape(dp_size, D // dp_size, fsdp_size, VOCAB // fsdp_size)
        code = code.transpose(0, 2, 1, 3).reshape(devices, D // dp_size, VOCAB // fsdp_size)
        plain = lax.psum_scatter(plain, AXES, scatter_dimension=1, tiled=True)
        code = lax.psum_scatter(code, AXES, scatter_dimension=0, tiled=True)
        return jnp.concatenate([plain.reshape(-1, m, D), code.reshape(-1, m, D)]).astype(F32)
    n, units = D, len(DEC_INPUTS) + len(ENC_INPUTS) + CODE_UNITS
    depth, half = 2 * LAG, Z // 2
    own_slots, held_slots, kept_slots = LAG + 1, 2 * LAG + 1, Z * LAG + 1
    dec_rows, enc_rows, code_rows = dec_x[0].shape[1], enc_x[0].shape[1], code_x.shape[0]
    counts = [len(group) for group in stacks]
    dma = pltpu.SemaphoreType.DMA
    whole = pl.BlockSpec(memory_space=pl.ANY)
    out = pl.pallas_call(
        partial(sum_kernel, Z, counts),
        out_shape=jax.ShapeDtypeStruct((units, m, n), F32),
        in_specs=[whole] * (sum(counts) + 1) + [pl.BlockSpec(memory_space=pltpu.VMEM)] + [whole] * 2,
        out_specs=pl.BlockSpec(memory_space=pltpu.VMEM),
        scratch_shapes=[
            pltpu.VMEM((2, dec_rows, n), BF),
            pltpu.VMEM((2, dec_rows, n), BF),
            pltpu.VMEM((4 * Z, 2, m, dec_rows), BF),
            pltpu.VMEM((2, enc_rows, n), BF),
            pltpu.VMEM((2, enc_rows, n), BF),
            pltpu.VMEM((4 * Z, 2, m, enc_rows), BF),
            pltpu.VMEM((2 * code_rows, VOCAB), BF),
            pltpu.VMEM((2, code_rows, n), BF),
            pltpu.VMEM((4, CODE_UNITS, m, 2 * code_rows), BF),
            pltpu.VMEM((own_slots, 4, Z, m, n), BF),
            pltpu.VMEM((own_slots, 4, Z, m, n), BF),
            pltpu.VMEM((depth, 4, Z, m, n), BF),
            pltpu.VMEM((held_slots, 4, Z, m, n), BF),
            pltpu.VMEM((depth, half, m, n), BF),
            pltpu.VMEM((depth, Z - half, m, n), BF),
            pltpu.VMEM((depth, Z, m, n), BF),
            pltpu.VMEM((depth, Z, m, n), BF),
            pltpu.VMEM((kept_slots, Z, m, n), BF),
            pltpu.VMEM((2, Z - 1, depth, m, n), BF),
            pltpu.VMEM((3, 4, Z, m, n), BF),
            pltpu.VMEM((3, 2, Z - 1, 4, m, n), BF),
            pltpu.VMEM((3, 4, m, n), BF),
            pltpu.VMEM((3, m // 2, n), BF),
            pltpu.VMEM((3, m // 2, n), BF),
            pltpu.VMEM((3, m, n), BF),
            pltpu.VMEM((3, m, n), BF),
            dma((2, 2)),
            dma((3,)),
            dma((depth,)),
            dma((depth,)),
            dma((2, depth)),
            dma((2, depth)),
            dma((2, depth)),
            dma((2, depth)),
            dma((2, Z - 1, depth)),
            dma((2, Z - 1, depth)),
            dma((2, Z - 1, 2 * (units // 9 + 1))),
            dma((2, Z - 1, 2 * (units // 9 + 1))),
            dma((4, 2 * (units // 9 + 1))),
            dma((4, 2 * (units // 9 + 1))),
        ],
        compiler_params=pltpu.CompilerParams(
            collective_id=call_id, has_side_effects=True, vmem_limit_bytes=62 << 20
        ),
    )(*dec_x, *dec_g, *enc_x, *enc_g, code_x, targets[:, None], code_g, look_g)
    return out


def spread_kernel(
    tables, units, Z, token_count, table_f32, mix_in, mix_out, ffn_up, ffn_down, text_table, small,
    table_out, unit_out, text_out, small_all,
    table_ref, unit_ref, looked, own_sem, line_send, line_recv, square_send, square_recv, core_send, core_recv,
    small_send, small_recv, text_sem, *sum_refs,
):
    dp, fs = lax.axis_index("dp"), lax.axis_index("fsdp")
    z, core = fs // 2, fs % 2
    x_mate, y_mate = dp + 1 - 2 * (dp % 2), (dp + 2) % 4
    across_dp = (x_mate + 2) % 4
    core_dev, x_dev, y_dev = (dp, fs + 1 - 2 * core), (x_mate, fs), (y_mate, fs)
    up_dev, down_dev = (dp, fs + 2), (dp, fs - 2)
    has_up, has_down = z < Z - 1, z > 0
    total, half = tables + units, Z // 2
    every = slice(None)
    table_rows, table_columns = table_out.shape[2] // tables, table_out.shape[3] // 4

    def at(is_table, k, dp_at, z_at, core_at, part=None):
        if is_table:
            size = table_rows if part is None else table_rows // 2
            rows = pl.ds(k * table_rows + (part or 0) * size, size)
            columns = every if isinstance(dp_at, slice) else pl.ds(dp_at * table_columns, table_columns)
            return table_out.at[z_at, core_at, rows, columns]
        if part is None:
            return unit_out.at[k - tables, dp_at, z_at, core_at]
        size = unit_out.shape[4] // 2
        return unit_out.at[k - tables, dp_at, z_at, core_at, pl.ds(part * size, size)]

    def passed(ref, send, recv, device):
        return remote(ref, ref, send, recv, device)

    size, inner = 8 * Z, 2 * Z
    me = dp * inner + fs

    def peer(i):
        other = lax.rem(me + i, size)
        return (other // inner, lax.rem(other, inner))

    def each(run):
        def one(i, carry):
            run(i)
            return carry

        lax.fori_loop(1, size, one, 0)

    def small_copy(i):
        return remote(small, small_all.at[me], small_send.at[i], small_recv.at[i], peer(i))

    barrier = pltpu.get_barrier_semaphore()
    each(lambda i: pl.semaphore_signal(barrier, inc=1, device_id=peer(i), device_id_type=MESH))
    small_all[me] = small[...]

    rows = unit_ref.shape[1]
    place = 0

    def put(value):
        nonlocal place
        unit_ref[place] = value.astype(BF)
        place += 1

    def put_ffn(layer, with_down):
        turned = [
            swap_groups([ffn_up[layer, :, pl.ds(128 * (4 * g + j), 128)] for j in range(4)]) for g in range(8)
        ]
        for q in range(4):
            put(jnp.concatenate([parts[q] for parts in turned], axis=1))
        for q in range(4 if with_down else 0):
            put(ffn_down[layer, pl.ds(q * rows, rows), :])

    for layer in range(3):
        for i in range(3):
            put(mix_in[layer, :, pl.ds(i * D, D)])
        put(mix_out[layer])
        if layer != 1:
            put_ffn(min(layer, 1), layer == 0)
    table_ref[...] = table_f32[...].astype(BF)

    own = (
        pltpu.make_async_copy(
            table_ref, table_out.at[z, core, :, pl.ds(dp * table_columns, table_columns)], own_sem.at[0]
        ),
        pltpu.make_async_copy(unit_ref, unit_out.at[:, dp, z, core], own_sem.at[1]),
    )
    for copy in own:
        copy.start()

    for copy in own:
        copy.wait()
    pl.semaphore_wait(barrier, size - 1)
    each(lambda i: small_copy(i).start())

    def line_copies(view, k, step):
        s = step - 1
        return (
            (passed(view(jnp.maximum(z - s, 0)), line_send.at[0, s, k], line_recv.at[0, s, k], up_dev),
             has_up & (z >= s), has_down & (z >= s + 1)),
            (passed(view(jnp.minimum(z + s, Z - 1)), line_send.at[1, s, k], line_recv.at[1, s, k], down_dev),
             has_down & (z + s <= Z - 1), has_up & (z + s + 1 <= Z - 1)),
        )

    def line_start(view, k, step):
        for copy, sends, _ in line_copies(view, k, step):
            pl.when(sends)(copy.start)

    def line_wait(view, k, step):
        for copy, sends, receives in line_copies(view, k, step):
            pl.when(sends)(copy.wait_send)
            pl.when(receives)(copy.wait_recv)

    def to_core(ref, k, slot):
        return passed(ref, core_send.at[slot, k], core_recv.at[slot, k], core_dev)

    def square_copy(ref, k, slot):
        return passed(
            ref, square_send.at[slot, k], square_recv.at[slot, k], x_dev if slot % 2 == 0 else y_dev
        )

    def line_first(is_table):
        def view(k):
            return lambda place: at(is_table, k, dp, place, core)

        def row(k, dp_at):
            return at(is_table, k, dp_at, every, core)

        def ones(k):
            return square_copy(row(k, dp), k, 0), square_copy(row(k, dp), k, 1)

        def twos(k):
            return (
                square_copy(at(is_table, k, y_mate, pl.ds(0, half), core), k, 2),
                square_copy(at(is_table, k, x_mate, pl.ds(half, Z - half), core), k, 3),
            )

        def line(step):
            def run(k):
                if step > 1:
                    line_wait(view(k), k, step - 1)
                if step < Z:
                    line_start(view(k), k, step)
                else:
                    for copy in ones(k):
                        copy.start()
                    to_core(row(k, dp), k, 0).start()
            return run

        def after_one(k):
            for copy in ones(k):
                copy.wait()
            for copy in twos(k):
                copy.start()
            to_core(row(k, x_mate), k, 1).start()
            to_core(row(k, y_mate), k, 2).start()

        def after_two(k):
            for copy in twos(k):
                copy.wait()
            to_core(row(k, across_dp), k, 3).start()

        def finish(k):
            for slot in range(4):
                to_core(row(k, dp), k, slot).wait()

        return [line(step) for step in range(1, Z + 1)] + [after_one, after_two, finish]

    def square_first(is_table):
        def plane(k):
            return lambda place: at(is_table, k, every, place, core)

        def ones(k):
            ref = at(is_table, k, dp, z, core)
            return square_copy(ref, k, 0), square_copy(ref, k, 1)

        def twos(k):
            return (
                square_copy(at(is_table, k, y_mate, z, core, 0), k, 2),
                square_copy(at(is_table, k, x_mate, z, core, 1), k, 3),
            )

        def begin(k):
            for copy in ones(k):
                copy.start()

        def after_one(k):
            for copy in ones(k):
                copy.wait()
            for copy in twos(k):
                copy.start()

        def after_two(k):
            for copy in twos(k):
                copy.wait()
            line_start(plane(k), k, 1)
            to_core(plane(k)(z), k, z).start()

        def line(step):
            def run(k):
                line_wait(plane(k), k, step)
                if step + 1 < Z:
                    line_start(plane(k), k, step + 1)

                @pl.when(z - step >= 0)
                def _():
                    to_core(plane(k)(jnp.maximum(z - step, 0)), k, jnp.maximum(z - step, 0)).start()

                @pl.when(z + step <= Z - 1)
                def _():
                    to_core(plane(k)(jnp.minimum(z + step, Z - 1)), k, jnp.minimum(z + step, Z - 1)).start()
            return run

        def finish(k):
            for place in range(Z):
                to_core(plane(k)(place), k, place).wait()

        return [begin, after_one, after_two] + [line(step) for step in range(1, Z)] + [finish]

    forms = [(is_table, first, form(is_table))
             for is_table in (True, False) for first, form in ((True, line_first), (False, square_first))]
    n_stages = Z + 3

    scratch, semaphores = sum_refs[:9], sum_refs[9:]
    own_slots, depth = scratch[0].shape[0], scratch[1].shape[0]

    def look_up():
        each(lambda i: small_copy(i).wait())
        owned_rows = text_table.shape[0]
        base = me * token_count

        def of_device(device, carry):
            ids = small_all[device][:1]
            row = lax.broadcasted_iota(jnp.int32, (owned_rows, ids.shape[1]), 0)
            hit = (row + base == ids.astype(jnp.int32)) & (row < token_count)
            found = across(jnp.where(hit, 1.0, 0.0).astype(BF), text_table[...]).astype(BF)
            dp_at, line_at, core_at = device // inner, lax.rem(device, inner) // 2, lax.rem(device, 2)
            for u in range(looked.shape[0]):
                looked[u, dp_at, line_at, core_at] = found[u * rows : (u + 1) * rows]
            return carry

        lax.fori_loop(0, size, of_device, 0)

    def text_own(k):
        return pltpu.make_async_copy(
            looked.at[k, :, :, core], scratch[0].at[k % own_slots], text_sem.at[k % own_slots]
        )

    def text_core(k):
        s = k % depth
        return remote(
            looked.at[k, :, :, 1 - core], scratch[1].at[s], semaphores[0].at[s], semaphores[1].at[s], core_dev
        )

    def text_begin(k):
        text_own(k).start()
        text_core(k).start()

    def text_arrive(k):
        text_own(k).wait()
        text_core(k).wait()

    text_stages = [text_begin] + sum_stages(Z, scratch, semaphores, text_arrive, text_out)[0]

    text_first = 3

    def loop_step(j, carry):
        pl.when(j == text_first)(look_up)
        for place in reversed(range(n_stages)):
            k = j - place * LAG
            turn = k - text_first
            pl.when((turn >= 0) & (turn < looked.shape[0]))(partial(text_stages[place], turn))
            turn = k % 9
            by_line = (turn != 3) & (turn != 7)
            for is_table, first, stages in forms:
                here = (k >= 0) & (k < tables) if is_table else (k >= tables) & (k < total)
                here = here & (by_line if first else jnp.logical_not(by_line))

                @pl.when(here)
                def _(k=k, run=stages[place]):
                    run(k)

        return carry

    lax.fori_loop(0, total + (n_stages - 1) * LAG, loop_step, 0)


def spread(table, weights, text_table, small, call_id):
    mix_in, mix_out, ffn_up, ffn_down = weights
    dp_size, fsdp_size = lax.axis_size("dp"), lax.axis_size("fsdp")
    m, Z = mix_in.shape[1], fsdp_size // 2
    if dp_size != 4 or Z != 4 or m != 32:
        shards = []
        for layer in range(3):
            shards += [column_units(mix_in[layer]), mix_out[layer][None]]
            if layer != 1:
                which = min(layer, 1)
                shards += [hidden_units(ffn_up[which], dp_size * fsdp_size)]
            if layer == 0:
                shards += [ffn_down[0].reshape(4, m, D)]
        table = lax.all_gather(table.astype(BF), "dp", axis=1, tiled=True)
        whole = lax.all_gather(table, "fsdp", axis=0, tiled=True)
        units = lax.all_gather(jnp.concatenate(shards).astype(BF), AXES, axis=1, tiled=True)
        devices, count = dp_size * fsdp_size, text_table.shape[0]
        small_all = exchange(jnp.broadcast_to(small[None], (devices, 8, 128)), 3)
        ids = small_all[:, 0].astype(jnp.int32).reshape(-1)
        base = (lax.axis_index("dp") * fsdp_size + lax.axis_index("fsdp")) * count
        owned = (ids[:, None] - base == jnp.arange(count)[None, :]).astype(BF)
        looked = matmul(owned, text_table.astype(BF)).astype(BF)
        text = lax.psum_scatter(looked, AXES, scatter_dimension=0, tiled=True).astype(F32)
        return whole, units, text, small_all
    text_units, token_count = TXT_LEN // m, text_table.shape[0]
    text_table = jnp.pad(text_table.astype(BF), ((0, -token_count % 128), (0, 0)))
    tables, count, dma = 8, 24, pltpu.SemaphoreType.DMA
    total = tables + count
    whole, units, text, small_all = pl.pallas_call(
        partial(spread_kernel, tables, count, Z, token_count),
        out_shape=(
            jax.ShapeDtypeStruct((Z, 2, table.shape[0], 4 * table.shape[1]), BF),
            jax.ShapeDtypeStruct((count, 4, Z, 2, m, D), BF),
            jax.ShapeDtypeStruct((text_units, m, D), F32),
            jax.ShapeDtypeStruct((8 * Z, *small.shape), F32),
        ),
        in_specs=[pl.BlockSpec(memory_space=pltpu.VMEM)] * 7,
        out_specs=[pl.BlockSpec(memory_space=pl.ANY)] * 2 + [pl.BlockSpec(memory_space=pltpu.VMEM)] * 2,
        scratch_shapes=[
            pltpu.VMEM(table.shape, BF),
            pltpu.VMEM((count, m, D), BF),
            pltpu.VMEM((text_units, 4, Z, 2, m, D), BF),
            dma((2,)),
            dma((2, Z - 1, total)),
            dma((2, Z - 1, total)),
            dma((4, total)),
            dma((4, total)),
            dma((4, total)),
            dma((4, total)),
            dma((8 * Z,)),
            dma((8 * Z,)),
            dma((LAG + 1,)),
            *sum_scratch(Z, m, D),
            *sum_semaphores(Z),
        ],
        compiler_params=pltpu.CompilerParams(
            collective_id=call_id, has_side_effects=True, vmem_limit_bytes=48 << 20
        ),
    )(table, *weights, text_table, small)
    return whole.reshape(-1, 4 * table.shape[1]), units.reshape(count, -1, D), text.reshape(-1, D), small_all


def exchange_kernel(size, inner, in_ref, out_ref, send_sem, recv_sem):
    me = lax.axis_index("dp") * inner + lax.axis_index("fsdp")

    def peer(i):
        other = lax.rem(me + i, size)
        return other, (other // inner, lax.rem(other, inner))

    barrier = pltpu.get_barrier_semaphore()

    def greet(i, carry):
        pl.semaphore_signal(barrier, inc=1, device_id=peer(i)[1], device_id_type=MESH)
        return carry

    def copy(i):
        other, device = peer(i)
        return pltpu.make_async_remote_copy(
            src_ref=in_ref.at[other], dst_ref=out_ref.at[me], send_sem=send_sem.at[i],
            recv_sem=recv_sem.at[i], device_id=device, device_id_type=MESH,
        )

    def begin(i, carry):
        copy(i).start()
        return carry

    def end(i, carry):
        copy(i).wait()
        return carry

    lax.fori_loop(1, size, greet, 0)
    out_ref[me] = in_ref[me]
    pl.semaphore_wait(barrier, size - 1)
    lax.fori_loop(1, size, begin, 0)
    lax.fori_loop(1, size, end, 0)


def exchange(blocks, call_id):
    size, inner = blocks.shape[0], lax.axis_size("fsdp")
    return pl.pallas_call(
        partial(exchange_kernel, size, inner),
        out_shape=jax.ShapeDtypeStruct(blocks.shape, F32),
        in_specs=[pl.BlockSpec(memory_space=pltpu.VMEM)],
        out_specs=pl.BlockSpec(memory_space=pltpu.VMEM),
        scratch_shapes=[pltpu.SemaphoreType.DMA((size,)), pltpu.SemaphoreType.DMA((size,))],
        compiler_params=pltpu.CompilerParams(collective_id=call_id, has_side_effects=True),
    )(blocks)


def tiles(values, count):
    padded = jnp.pad(values, ((0, 1024 - values.shape[0]),)).reshape(1, 8, 128)
    return jnp.broadcast_to(padded, (count, 8, 128))


def swap_groups(parts):
    group = lax.broadcasted_iota(jnp.int32, parts[0].shape, 1) // 32
    results = []
    for i in range(4):
        total = parts[i]
        for j in range(4):
            if j != i:
                turned = pltpu.roll(parts[j], (32 * (j - i)) % 128, 1)
                total = jnp.where(group == j, turned, total)
        results.append(total)
    return results


def norm_kernel(
    size, inner, count, sums, text, small, small_out, norm_out,
    squares, small_all, squares_all, sum_scratch, small_send, small_recv, square_send, square_recv,
):
    rows = sums.shape[1]
    text_rows = [(start, min(rows, text.shape[0] - start)) for start in range(0, text.shape[0], rows)]
    me = lax.axis_index("dp") * inner + lax.axis_index("fsdp")

    def peer(i):
        other = lax.rem(me + i, size)
        return other, (other // inner, lax.rem(other, inner))

    def small_copy(i):
        other, device = peer(i)
        return remote(small.at[other], small_all.at[me], small_send.at[i], small_recv.at[i], device)

    def square_copy(i):
        return remote(squares, squares_all.at[me], square_send.at[i], square_recv.at[i], peer(i)[1])

    def each(run):
        def one(i, carry):
            run(i)
            return carry

        lax.fori_loop(1, size, one, 0)

    barrier = pltpu.get_barrier_semaphore()
    each(lambda i: pl.semaphore_signal(barrier, inc=1, device_id=peer(i)[1], device_id_type=MESH))
    small_all[me] = small[me]
    pl.semaphore_wait(barrier, size - 1)
    each(lambda i: small_copy(i).start())

    sum_scratch[...] = jnp.zeros_like(sum_scratch)

    def square(k, carry):
        sum_scratch[...] += sums[k] * sums[k]
        return carry

    lax.fori_loop(0, sums.shape[0], square, 0)
    for start, length in text_rows:
        part = text[pl.ds(start, length), :]
        sum_scratch[pl.ds(0, length), :] += part * part

    each(lambda i: small_copy(i).wait())
    total = lax.fori_loop(0, size, lambda i, total: total + small_all[i], jnp.zeros_like(squares))
    small_out[...] = total
    place = lax.broadcasted_iota(jnp.int32, total.shape, 0) * 128 + lax.broadcasted_iota(jnp.int32, total.shape, 1)
    gains = jnp.where(place < count, total, 0.0)
    squares[...] = jnp.full(squares.shape, jnp.sum(sum_scratch[...]) + jnp.sum(gains * gains))

    squares_all[me] = squares[...]
    each(lambda i: square_copy(i).start())
    each(lambda i: square_copy(i).wait())
    norm_out[...] = jnp.sqrt(
        lax.fori_loop(0, size, lambda i, total: total + squares_all[i], jnp.zeros_like(squares))
    )


def update_kernel(*refs):
    norm, plain, text, gains, *refs = refs
    weights, refs = refs[:7], refs[7:]
    firsts, refs = refs[:7], refs[7:]
    seconds, refs = refs[:7], refs[7:]
    new_weights, refs = refs[:7], refs[7:]
    new_firsts, new_seconds = refs[:7], refs[7:]
    rows = plain.shape[1]
    text_rows = [(start, min(rows, text.shape[0] - start)) for start in range(0, text.shape[0], rows)]
    factor = (CLIP_NORM / jnp.maximum(norm[...], CLIP_NORM))[:1, :1]

    def step(which, place, gradient):
        updated = adam_step(
            weights[which][place], firsts[which][place], seconds[which][place],
            gradient * factor, STEP_RATES[which],
        )
        for out, value in zip((new_weights, new_firsts, new_seconds), updated):
            out[which][place] = value

    enc = len(DEC_INPUTS)
    every = slice(None)
    for layer, units in enumerate(((enc + 2, enc + 3, enc + 4), (0, 1, 2), (4, enc, enc + 1))):
        for i, unit in enumerate(units):
            step(0, (layer, every, pl.ds(i * D, D)), plain[unit])
    for layer, unit in enumerate((enc + 5, 3, 5)):
        step(1, (layer,), plain[unit])
    for layer, first in enumerate((enc + 6, 6)):
        for g in range(8):
            parts = [plain[first + q, :, pl.ds(128 * g, 128)] for q in range(4)]
            for j, part in enumerate(swap_groups(parts)):
                step(2, (layer, every, pl.ds(128 * (4 * g + j), 128)), part)
    for layer, first in enumerate((enc + 10, 10)):
        for q in range(4):
            step(3, (layer, pl.ds(q * rows, rows), every), plain[first + q])
    step(4, (every, every), gains[...])
    for start, count in text_rows:
        step(5, (pl.ds(start, count), every), text[pl.ds(start, count), :])
    columns, first = 256, len(DEC_INPUTS) + len(ENC_INPUTS)
    for i in range(D // columns):
        part = plain[pl.ds(first, CODE_UNITS), :, pl.ds(i * columns, columns)]
        step(6, (pl.ds(i * columns, columns), every), part.reshape(-1, columns).T)


def update(sums, text, small, weights, firsts, seconds, call_id):
    inner = lax.axis_size("fsdp")
    size = lax.axis_size("dp") * inner
    shapes = [jax.ShapeDtypeStruct(weight.shape, F32) for weight in weights]
    gains_shape = weights[4].shape
    count = gains_shape[0] * gains_shape[1]
    in_vmem = pl.BlockSpec(memory_space=pltpu.VMEM)
    dma, tile = pltpu.SemaphoreType.DMA, jax.ShapeDtypeStruct((8, 128), F32)
    small, norm = pl.pallas_call(
        partial(norm_kernel, size, inner, count),
        out_shape=[tile, tile],
        in_specs=[in_vmem] * 3,
        out_specs=[in_vmem] * 2,
        scratch_shapes=[
            pltpu.VMEM((8, 128), F32),
            pltpu.VMEM((size, 8, 128), F32),
            pltpu.VMEM((size, 8, 128), F32),
            pltpu.VMEM(sums.shape[1:], F32),
            dma((size,)),
            dma((size,)),
            dma((size,)),
            dma((size,)),
        ],
        compiler_params=pltpu.CompilerParams(
            collective_id=call_id, has_side_effects=True, vmem_limit_bytes=32 << 20
        ),
    )(sums, text, small)
    small = small.reshape(-1)
    outs = pl.pallas_call(
        update_kernel,
        out_shape=shapes * 3,
        in_specs=[in_vmem] * 25,
        out_specs=[in_vmem] * 21,
        compiler_params=pltpu.CompilerParams(vmem_limit_bytes=60 << 20),
    )(norm, sums, text, small[:count].reshape(gains_shape), *weights, *firsts, *seconds)
    return small[count], norm[0, 0], list(zip(outs[:7], outs[7:14], outs[14:]))


def layer_norm(stream, gain):
    centred = stream - jnp.mean(stream, axis=-1, keepdims=True)
    return centred * lax.rsqrt(jnp.mean(centred * centred, axis=-1, keepdims=True) + 1e-05) * gain


def norm_back(stream, gain, grad_out):
    centred = stream - jnp.mean(stream, axis=-1, keepdims=True)
    inverse = lax.rsqrt(jnp.mean(centred * centred, axis=-1, keepdims=True) + 1e-05)
    plain = centred * inverse
    scaled = grad_out * gain
    inner = jnp.mean(scaled * plain, axis=-1, keepdims=True)
    grad = inverse * (scaled - jnp.mean(scaled, axis=-1, keepdims=True) - plain * inner)
    return grad, jnp.sum(grad_out * plain, axis=0, keepdims=True)


def positions(length, width):
    position = jnp.arange(length, dtype=jnp.float32)[:, None]
    speeds = jnp.exp(
        -math.log(10000.0) * 2.0 * jnp.arange(width // 2, dtype=jnp.float32)[None, :] / width
    )
    return jnp.concatenate([jnp.sin(position * speeds), jnp.cos(position * speeds)], axis=1)


def matmul(first_op, second_op):
    return jnp.dot(first_op, second_op, preferred_element_type=jnp.float32)


def across(first_op, second_op):
    return lax.dot_general(
        first_op, second_op, (((0,), (0,)), ((), ())), preferred_element_type=jnp.float32
    )


def against(first_op, second_op):
    return lax.dot_general(
        first_op, second_op, (((1,), (1,)), ((), ())), preferred_element_type=jnp.float32
    )


LOCAL = 56 << 20


def gain_at(i):
    return pl.BlockSpec((1, 1, D), lambda *_: (i, 0, 0))


def fixed(shape):
    return pl.BlockSpec(shape, lambda *_: (0,) * len(shape))


def turns(shape):
    return pl.BlockSpec((1, *shape[1:]), lambda i: (i,) + (0,) * (len(shape) - 1))


def unit_from(first):
    return pl.BlockSpec((1, D, D), lambda i: (first + i, 0, 0))


def cost(rows, count):
    return pl.CostEstimate(flops=2 * rows * D * D * count, bytes_accessed=2 * D * D * count + 8 * rows * D, transcendentals=0)


def steps(kernel, count, rows, in_specs, out_specs, out_shape, scratch, *args):
    return pl.pallas_call(
        kernel,
        grid=(count,),
        in_specs=in_specs,
        out_specs=out_specs,
        out_shape=out_shape,
        scratch_shapes=scratch,
        cost_estimate=cost(rows, count),
        compiler_params=pltpu.CompilerParams(vmem_limit_bytes=LOCAL),
    )(*args)


def shaped(shape, kind):
    return jax.ShapeDtypeStruct(shape, kind)


def project(stream, gain, units, first, count):
    rows = stream.shape[0]

    def kernel(x, g, w, normed, out):
        @pl.when(pl.program_id(0) == 0)
        def _():
            normed[...] = layer_norm(x[...], g[0]).astype(BF)

        out[0] = matmul(normed[...], w[0]).astype(BF)

    whole = (count, rows, D)
    return steps(
        kernel, count, rows,
        [fixed((rows, D)), gain_at(gain[1]), unit_from(first)],
        [fixed((rows, D)), turns(whole)],
        [shaped((rows, D), BF), shaped(whole, BF)], [],
        stream, gain[0], units,
    )


def products(value, units, first, count):
    rows = value.shape[0]

    def kernel(x, w, out):
        out[0] = matmul(x[...], w[0]).astype(BF)

    whole = (count, rows, D)
    return steps(
        kernel, count, rows, [fixed((rows, D)), unit_from(first)], turns(whole), shaped(whole, BF), [],
        value, units,
    )


def add_products(stream, parts, units, first):
    count, rows, _ = parts.shape

    def kernel(x, a, w, out):
        @pl.when(pl.program_id(0) == 0)
        def _():
            out[...] = x[...]

        out[...] += matmul(a[0], w[0])

    return steps(
        kernel, count, rows,
        [fixed((rows, D)), turns(parts.shape), unit_from(first)], fixed((rows, D)), shaped((rows, D), F32), [],
        stream, parts, units,
    )


def hidden_layer(stream, gain, units, first):
    rows = stream.shape[0]
    bend, rate = 0.044715, math.sqrt(2.0 / math.pi)

    def kernel(x, g, w, normed, out, slope):
        @pl.when(pl.program_id(0) == 0)
        def _():
            normed[...] = layer_norm(x[...], g[0]).astype(BF)

        for start in range(0, rows, 128):
            at = pl.ds(start, 128)
            z = matmul(normed[at], w[0])
            square = z * z
            flat = jnp.tanh(rate * z * (1.0 + bend * square))
            out[0, at] = (0.5 * z * (1.0 + flat)).astype(BF)
            slope[0, at] = (
                0.5 * (1.0 + flat) + 0.5 * z * (1.0 - flat * flat) * rate * (1.0 + 3.0 * bend * square)
            ).astype(BF)

    whole = (4, rows, D)
    return steps(
        kernel, 4, rows,
        [fixed((rows, D)), gain_at(gain[1]), unit_from(first)],
        [fixed((rows, D)), turns(whole), turns(whole)],
        [shaped((rows, D), BF), shaped(whole, BF), shaped(whole, BF)], [],
        stream, gain[0], units,
    )


def norm_only(stream, gain):
    def kernel(x, g, out):
        out[...] = layer_norm(x[...], g[0]).astype(BF)

    return steps(
        kernel, 1, 8, [fixed(stream.shape), gain_at(gain[1])], fixed(stream.shape), shaped(stream.shape, BF), [],
        stream, gain[0],
    )


def norm_only_back(grad, stream, gain):
    shape = stream.shape

    def kernel(d, x, g, out, low, gain_out):
        out[...], gain_out[...] = norm_back(x[...], g[0], d[...])
        low[...] = out[...].astype(BF)

    return steps(
        kernel, 1, 8, [fixed(shape), fixed(shape), gain_at(gain[1])],
        [fixed(shape), fixed(shape), fixed((1, D))],
        [shaped(shape, F32), shaped(shape, BF), shaped((1, D), F32)], [],
        grad, stream, gain[0],
    )


def project_back(parts, units, first, stream, gain, grad):
    count, rows, _ = parts.shape
    shape = (rows, D)

    def kernel(d, w, x, g, above, out, low, gain_out, total):
        @pl.when(pl.program_id(0) == 0)
        def _():
            total[...] = jnp.zeros_like(total)

        total[...] += against(d[0], w[0])

        @pl.when(pl.program_id(0) == count - 1)
        def _():
            part, gain_out[...] = norm_back(x[...], g[0], total[...])
            out[...] = above[...] + part
            low[...] = out[...].astype(BF)

    return steps(
        kernel, count, rows,
        [turns(parts.shape), unit_from(first), fixed(shape), gain_at(gain[1]), fixed(shape)],
        [fixed(shape), fixed(shape), fixed((1, D))],
        [shaped(shape, F32), shaped(shape, BF), shaped((1, D), F32)], [pltpu.VMEM(shape, F32)],
        parts, units, stream, gain[0], grad,
    )


def products_back(parts, units, first):
    count, rows, _ = parts.shape
    shape = (rows, D)

    def kernel(d, w, out):
        @pl.when(pl.program_id(0) == 0)
        def _():
            out[...] = jnp.zeros_like(out)

        out[...] += against(d[0], w[0])

    return steps(
        kernel, count, rows, [turns(parts.shape), unit_from(first)], fixed(shape), shaped(shape, F32), [],
        parts, units,
    )


def mix_back(low, units, first):
    rows = low.shape[0]

    def kernel(d, w, out):
        out[...] = against(d[...], w[0]).astype(BF)

    return steps(
        kernel, 1, rows, [fixed((rows, D)), unit_from(first)], fixed((rows, D)), shaped((rows, D), BF), [],
        low, units,
    )


def hidden_back(low, slope, units, up_first, down_units, down_first, stream, gain, grad):
    rows = low.shape[0]
    shape = (rows, D)

    def kernel(d, s, up, down, x, g, above, hidden, out, out_low, gain_out, total):
        @pl.when(pl.program_id(0) == 0)
        def _():
            total[...] = jnp.zeros_like(total)

        for start in range(0, rows, 128):
            at = pl.ds(start, 128)
            hidden[0, at] = (against(d[at], down[0]) * s[0, at].astype(F32)).astype(BF)
            total[at] += against(hidden[0, at], up[0])

        @pl.when(pl.program_id(0) == 3)
        def _():
            part, gain_out[...] = norm_back(x[...], g[0], total[...])
            out[...] = above[...] + part
            out_low[...] = out[...].astype(BF)

    return steps(
        kernel, 4, 2 * rows,
        [fixed(shape), turns(slope.shape), unit_from(up_first), unit_from(down_first),
         fixed(shape), gain_at(gain[1]), fixed(shape)],
        [turns(slope.shape), fixed(shape), fixed(shape), fixed((1, D))],
        [shaped(slope.shape, BF), shaped(shape, F32), shaped(shape, BF), shaped((1, D), F32)],
        [pltpu.VMEM(shape, F32)],
        low, slope, units, down_units, stream, gain[0], grad,
    )


PAIR = 2 * HEAD
PAIRS = 4


def head_lanes(value, head):
    lane = lax.broadcasted_iota(jnp.int32, value.shape, 1)
    return jnp.where(lane // HEAD == head, value, jnp.zeros_like(value))


def head_shares(query, key, labels, head):
    scores = against(head_lanes(query, head), key) * HEAD ** (-0.5)
    if labels is None:
        row = lax.broadcasted_iota(jnp.int32, scores.shape, 0)
        visible = lax.broadcasted_iota(jnp.int32, scores.shape, 1) <= row
    else:
        visible = labels[0][...] == labels[1][...]
    scores = jnp.where(visible, scores, MASKED)
    weights = jnp.exp(scores - jnp.max(scores, axis=-1, keepdims=True))
    return weights / jnp.sum(weights, axis=-1, keepdims=True)


def attention_specs(blocks, parts, labels):
    def one(array, place):
        return pl.BlockSpec((1, array.shape[1] // blocks, PAIRS * PAIR), lambda b, h: (place, b, h))

    marks = [] if labels is None else [fixed(label.shape) for label in labels]
    return (blocks, D // (PAIRS * PAIR)), [one(*part) for part in parts], marks


def pair_columns(count, rows, blocks):
    return pl.BlockSpec((count, rows // blocks, PAIRS * PAIR), lambda b, h: (0, b, h))


def attention(parts, blocks, labels):
    grid, specs, marks = attention_specs(blocks, parts, labels)
    rows = parts[0][0].shape[1]

    def kernel(q, k, v, *rest):
        seen, out = (rest[:-1] or None), rest[-1]
        for pair in range(PAIRS):
            at = pl.ds(pair * PAIR, PAIR)
            query, key, value = q[0, :, at], k[0, :, at], v[0, :, at]
            total = 0.0
            for head in range(2):
                shares = head_shares(query, key, seen, head).astype(BF)
                total = total + matmul(shares, head_lanes(value, head))
            out[0, :, at] = total.astype(BF)

    return pl.pallas_call(
        kernel,
        grid=grid,
        in_specs=[*specs, *marks],
        out_specs=pair_columns(1, rows, blocks),
        out_shape=shaped((1, rows, D), BF),
        compiler_params=pltpu.CompilerParams(vmem_limit_bytes=LOCAL),
    )(*[array for array, _ in parts], *(labels or ()))


def attention_back(parts, grad, blocks, labels):
    grid, specs, marks = attention_specs(blocks, parts, labels)
    rows, keys = parts[0][0].shape[1], parts[1][0].shape[1]
    counts = [(3, rows)] if rows == keys else [(1, rows), (2, keys)]

    def kernel(q, k, v, d, *rest):
        seen, outs = (rest[: -len(counts)] or None), rest[-len(counts) :]
        places = [(out, i) for out in outs for i in range(out.shape[0])]
        for pair in range(PAIRS):
            at = pl.ds(pair * PAIR, PAIR)
            query, key, value, grads = q[0, :, at], k[0, :, at], v[0, :, at], d[:, at]
            grad_query = grad_key = grad_value = 0.0
            for head in range(2):
                shares = head_shares(query, key, seen, head)
                above = head_lanes(grads, head)
                grad_shares = against(above, value)
                inner = jnp.sum(shares * grad_shares, axis=-1, keepdims=True)
                grad_scores = (shares * (grad_shares - inner)).astype(BF)
                grad_query = grad_query + matmul(grad_scores, head_lanes(key, head))
                grad_key = grad_key + across(grad_scores, head_lanes(query, head))
                grad_value = grad_value + across(shares.astype(BF), above)
            results = (grad_query * HEAD ** (-0.5), grad_key * HEAD ** (-0.5), grad_value)
            for (out, i), result in zip(places, results):
                out[i, :, at] = result.astype(BF)

    return pl.pallas_call(
        kernel,
        grid=grid,
        in_specs=[*specs, pl.BlockSpec((rows // blocks, PAIRS * PAIR), lambda b, h: (b, h)), *marks],
        out_specs=[pair_columns(count, length, blocks) for count, length in counts],
        out_shape=[shaped((count, length, D), BF) for count, length in counts],
        compiler_params=pltpu.CompilerParams(vmem_limit_bytes=LOCAL),
    )(*[array for array, _ in parts], grad, *(labels or ()))


def layer_forward(stream, units, first, down_units, down, gains, blocks, labels, memory, cross_labels):
    stored = {"stream": stream}
    stored["normed"], qkv = project(stream, gains[0], units, first, 3)
    stored["self"] = [(qkv, i) for i in range(3)]
    stored["attended"] = attention(stored["self"], blocks, labels)
    stream = add_products(stream, stored["attended"], units, first + 3)
    last = first + 4
    if memory is not None:
        stored["after_self"] = stream
        stored["cross_in"], cross_query = project(stream, gains[1], units, first + 4, 1)
        memory_kv = products(memory, units, first + 5, 2)
        stored["cross"] = [(cross_query, 0), (memory_kv, 0), (memory_kv, 1)]
        stored["cross_mixed"] = attention(stored["cross"], 1, cross_labels)
        stream = add_products(stream, stored["cross_mixed"], units, first + 7)
        last = first + 8
    stored["before_ffn"] = stream
    stored["ffn_in"], stored["hidden"], stored["slope"] = hidden_layer(stream, gains[-2], units, last)
    stream = add_products(stream, stored["hidden"], down_units, down)
    stored["before_final"] = stream
    return norm_only(stream, gains[-1]), stored


def layer_backward(
    grad_final, units, first, down_units, down, gains, blocks, labels, stored, memory, cross_labels
):
    gain_grads = [None] * len(gains)
    last = first + (4 if memory is None else 8)
    grad, ffn_low, gain_grads[-1] = norm_only_back(grad_final, stored["before_final"], gains[-1])
    hidden_grads, grad, low, gain_grads[-2] = hidden_back(
        ffn_low, stored["slope"], units, last, down_units, down, stored["before_ffn"], gains[-2], grad
    )
    cross_inputs, cross_grads, memory_grads = [], [], []
    grad_memory = None
    if memory is not None:
        grad_query, grad_memory_kv = attention_back(
            stored["cross"], mix_back(low, units, first + 7), 1, cross_labels
        )
        cross_inputs = [stored["cross_in"][None], stored["cross_mixed"]]
        cross_grads = [grad_query, low[None]]
        memory_grads = [grad_memory_kv]
        grad_memory = products_back(grad_memory_kv, units, first + 5)
        grad, low, gain_grads[1] = project_back(
            grad_query, units, first + 4, stored["after_self"], gains[1], grad
        )
    (grads,) = attention_back(stored["self"], mix_back(low, units, first + 3), blocks, labels)
    inputs = [stored["normed"][None], stored["attended"], *cross_inputs, stored["ffn_in"][None], stored["hidden"]]
    outputs = [grads, low[None], *cross_grads, hidden_grads, ffn_low[None]]
    grad, _, gain_grads[0] = project_back(grads, units, first, stored["stream"], gains[0], grad)
    parts = (inputs, outputs) if memory is None else (inputs, outputs, memory_grads)
    return grad, grad_memory, gain_grads, parts


def adam_step(weight, moment_one, second, gradient, rate):
    moment_one = BETA_ONE * moment_one + (1.0 - BETA_ONE) * gradient
    second = BETA_TWO * second + (1.0 - BETA_TWO) * gradient * gradient
    first_hat = moment_one / (1.0 - BETA_ONE**STEP)
    second_hat = second / (1.0 - BETA_TWO**STEP)
    weight = weight - rate * (first_hat / (jnp.sqrt(second_hat) + ADAM_EPS) + WEIGHT_DECAY * weight)
    return (weight, moment_one, second)


def column_units(matrix):
    return matrix.reshape(matrix.shape[0], -1, D).transpose(1, 0, 2)


def from_column_units(units):
    return units.transpose(1, 0, 2).reshape(units.shape[1], -1)


def hidden_units(matrix, devices):
    rows, width = matrix.shape
    return (
        matrix.reshape(rows, devices, 4, width // devices // 4)
        .transpose(2, 0, 1, 3)
        .reshape(4, rows, width // 4)
    )


def from_hidden_units(units, devices):
    quarters, rows, width = units.shape
    return (
        units.reshape(quarters, rows, devices, width // devices)
        .transpose(1, 2, 0, 3)
        .reshape(rows, quarters * width)
    )


def on_device(
    text_ids,
    text_segments,
    codes,
    caption_of,
    mix_in,
    mix_out,
    ffn_up,
    ffn_down,
    norm_gains,
    text_table,
    code_table,
    mix_in_first,
    mix_out_first,
    ffn_up_first,
    ffn_down_first,
    gains_first,
    text_first,
    code_first,
    mix_in_second,
    mix_out_second,
    ffn_up_second,
    ffn_down_second,
    gains_second,
    text_second,
    code_second,
):
    image_count = codes.shape[0]
    dp_size, fsdp_size = lax.axis_size("dp"), lax.axis_size("fsdp")
    devices = dp_size * fsdp_size
    me = lax.axis_index("dp") * fsdp_size + lax.axis_index("fsdp")
    token_total = image_count * IMG_LEN * devices
    inverse = 1.0 / token_total
    scale_in = math.sqrt(D)
    rows = mix_in.shape[1]
    segments = text_segments[0]
    text_labels = (segments[:, None], segments[None, :])
    cross_labels = (jnp.repeat(caption_of, IMG_LEN)[:, None], segments[None, :])

    small = tiles(jnp.concatenate([text_ids[0].astype(F32), norm_gains.reshape(-1)]), 1)[0]
    code_full, units, text_rows, small = spread(
        code_table, (mix_in, mix_out, ffn_up, ffn_down), text_table, small, 4
    )
    small = small.reshape(devices, 1024)[:, : TXT_LEN + 7 * norm_gains.shape[1]]
    all_ids = small[:, :TXT_LEN].astype(jnp.int32).reshape(-1)
    gains = small[:, TXT_LEN:].reshape(devices, 7, -1).transpose(1, 0, 2).reshape(7, 1, D)
    gains = gains.astype(BF).astype(F32)
    base = me * text_table.shape[0]
    owned = (all_ids[:, None] - base == jnp.arange(text_table.shape[0])[None, :]).astype(BF)
    last = ffn_down[1].reshape(4, rows, D).astype(BF)
    last = lax.optimization_barrier((last, text_rows))[0]
    down_units = lax.all_gather(last, AXES, axis=1, tiled=True)
    text_in = text_rows * scale_in + positions(TXT_LEN, D)
    enc_gains = [(gains, i) for i in range(3)]
    dec_gains = [(gains, i) for i in range(3, 7)]
    memory, enc_stored = layer_forward(text_in, units, 0, units, 8, enc_gains, 1, text_labels, None, None)

    image_rows = code_full[codes].astype(F32) * scale_in
    shifted = jnp.concatenate([jnp.zeros_like(image_rows[:, :1]), image_rows[:, :-1]], axis=1)
    image_in = (shifted + positions(IMG_LEN, D)[None]).reshape(-1, D)
    final_out, dec_stored = layer_forward(
        image_in, units, 12, down_units, 0, dec_gains, image_count, None, memory, cross_labels
    )

    targets = codes.reshape(-1)
    logits = against(final_out, code_full)
    hit = targets[:, None] == jnp.arange(VOCAB)[None, :]
    top = jnp.max(logits, axis=1, keepdims=True)
    log_total = top + jnp.log(jnp.sum(jnp.exp(logits - top), axis=1, keepdims=True))
    weighted = jnp.sum(
        logits * jnp.where(hit, 1.0 - SMOOTH + SMOOTH / VOCAB, SMOOTH / VOCAB), axis=1, keepdims=True
    )
    loss_part = jnp.sum(log_total - weighted)
    grad_logits = (
        (jnp.exp(logits - log_total) - jnp.where(hit, 1.0 - SMOOTH, 0.0) - SMOOTH / VOCAB) * inverse
    ).astype(BF)
    grad_final = matmul(grad_logits, code_full)

    grad_image, grad_memory, dec_gain_grads, dec_parts = layer_backward(
        grad_final, units, 12, down_units, 0, dec_gains, image_count, None, dec_stored, memory, cross_labels
    )
    grad_text, _, enc_gain_grads, enc_parts = layer_backward(
        grad_memory, units, 0, units, 8, enc_gains, 1, text_labels, enc_stored, None, None
    )
    gain_part = jnp.concatenate(enc_gain_grads + dec_gain_grads)

    grad_rows = lax.all_gather((grad_text * scale_in).astype(BF), AXES, axis=0, tiled=True)
    text_grad = across(owned, grad_rows)

    grad_looked = grad_image.reshape(image_count, IMG_LEN, D)[:, 1:] * scale_in
    grad_looked = jnp.pad(grad_looked, ((0, 0), (0, 1), (0, 0))).reshape(-1, D).astype(BF)
    enc_x, enc_g = enc_parts
    dec_x, dec_g, memory_g = dec_parts
    sums = sum_products(
        dec_x, dec_g, [memory[None]] + enc_x, memory_g + enc_g, grad_logits, targets, final_out, grad_looked, 1
    )
    gain_blocks = gain_part.reshape(7, devices, rows).transpose(1, 0, 2).reshape(devices, 7 * rows)
    gain_blocks = jnp.concatenate([gain_blocks, jnp.full((devices, 1), loss_part)], axis=1)
    gain_blocks = jnp.pad(gain_blocks, ((0, 0), (0, 1024 - gain_blocks.shape[1])))
    gain_blocks = gain_blocks.reshape(devices, 8, 128)
    params = (mix_in, mix_out, ffn_up, ffn_down, norm_gains, text_table, code_table)
    firsts = (
        mix_in_first,
        mix_out_first,
        ffn_up_first,
        ffn_down_first,
        gains_first,
        text_first,
        code_first,
    )
    seconds = (
        mix_in_second,
        mix_out_second,
        ffn_up_second,
        ffn_down_second,
        gains_second,
        text_second,
        code_second,
    )
    if rows == 32:
        loss_sum, grad_norm, updated = update(sums, text_grad, gain_blocks, params, firsts, seconds, 6)
    else:
        small_sum = jnp.sum(exchange(gain_blocks, 5), axis=0).reshape(-1)
        loss_sum = small_sum[7 * rows]
        gains_grad = small_sum[: 7 * rows].reshape(7, rows)
        dec_sum, enc_sum = sums[:14], sums[14:28]
        gradients = (
            jnp.stack(
                [
                    from_column_units(part)
                    for part in (enc_sum[2:5], dec_sum[:3], jnp.concatenate([dec_sum[4:5], enc_sum[:2]]))
                ]
            ),
            jnp.stack([enc_sum[5], dec_sum[3], dec_sum[5]]),
            jnp.stack([from_hidden_units(part, devices) for part in (enc_sum[6:10], dec_sum[6:10])]),
            jnp.stack([part.reshape(-1, D) for part in (enc_sum[10:], dec_sum[10:])]),
            gains_grad,
            text_grad,
            sums[28:].reshape(D // dp_size, -1).T,
        )
        square_part = sum((jnp.sum(gradient * gradient) for gradient in gradients))
        squares = exchange(tiles(square_part[None], devices), 6)[:, 0, 0]
        grad_norm = jnp.sqrt(jnp.sum(squares))
        factor = CLIP_NORM / jnp.maximum(grad_norm, CLIP_NORM)
        updated = [
            adam_step(
                params[index],
                firsts[index],
                seconds[index],
                gradients[index] * factor,
                STEP_RATES[index],
            )
            for index in range(7)
        ]
    return (
        loss_sum,
        grad_norm,
        updated[0][0],
        updated[1][0],
        updated[2][0],
        updated[3][0],
        updated[4][0],
        updated[5][0],
        updated[6][0],
        updated[0][1],
        updated[1][1],
        updated[2][1],
        updated[3][1],
        updated[4][1],
        updated[5][1],
        updated[6][1],
        updated[0][2],
        updated[1][2],
        updated[2][2],
        updated[3][2],
        updated[4][2],
        updated[5][2],
        updated[6][2],
    )


def solution(mesh):
    return jax.shard_map(
        on_device,
        mesh=mesh,
        in_specs=(
            P(("dp", "fsdp"), None),
            P(("dp", "fsdp"), None),
            P(("dp", "fsdp"), None),
            P(("dp", "fsdp")),
            P(None, ("dp", "fsdp"), None),
            P(None, ("dp", "fsdp"), None),
            P(None, ("dp", "fsdp"), None),
            P(None, ("dp", "fsdp"), None),
            P(None, ("dp", "fsdp")),
            P(("dp", "fsdp"), None),
            P("fsdp", "dp"),
            P(None, ("dp", "fsdp"), None),
            P(None, ("dp", "fsdp"), None),
            P(None, ("dp", "fsdp"), None),
            P(None, ("dp", "fsdp"), None),
            P(None, ("dp", "fsdp")),
            P(("dp", "fsdp"), None),
            P("fsdp", "dp"),
            P(None, ("dp", "fsdp"), None),
            P(None, ("dp", "fsdp"), None),
            P(None, ("dp", "fsdp"), None),
            P(None, ("dp", "fsdp"), None),
            P(None, ("dp", "fsdp")),
            P(("dp", "fsdp"), None),
            P("fsdp", "dp"),
        ),
        out_specs=(
            P(),
            P(),
            P(None, ("dp", "fsdp"), None),
            P(None, ("dp", "fsdp"), None),
            P(None, ("dp", "fsdp"), None),
            P(None, ("dp", "fsdp"), None),
            P(None, ("dp", "fsdp")),
            P(("dp", "fsdp"), None),
            P("fsdp", "dp"),
            P(None, ("dp", "fsdp"), None),
            P(None, ("dp", "fsdp"), None),
            P(None, ("dp", "fsdp"), None),
            P(None, ("dp", "fsdp"), None),
            P(None, ("dp", "fsdp")),
            P(("dp", "fsdp"), None),
            P("fsdp", "dp"),
            P(None, ("dp", "fsdp"), None),
            P(None, ("dp", "fsdp"), None),
            P(None, ("dp", "fsdp"), None),
            P(None, ("dp", "fsdp"), None),
            P(None, ("dp", "fsdp")),
            P(("dp", "fsdp"), None),
            P("fsdp", "dp"),
        ),
        check_vma=False,
    )
```

```python
from functools import partial
import math

import jax
import jax.numpy as jnp
from jax import lax
from jax.experimental import pallas as pl
from jax.experimental.pallas import tpu as pltpu
from jax.sharding import PartitionSpec as P

D = 1024
HEADS = 16
HEAD = 64
VOCAB = 8192
TVOC = 16000
IMG_LEN = 256
TXT_LEN = 128
STEP = 5


SMOOTH = 0.1
BETA_ONE = 0.5
BETA_TWO = 0.5
WEIGHT_DECAY = 0.1
ADAM_EPS = 1e-08
CLIP_NORM = 0.02
MASKED = -1e30
STEP_RATES = (0.02, 0.15, 0.02, 0.01, 0.3, 0.02, 0.03)

BF = jnp.bfloat16
F32 = jnp.float32
AXES = ("dp", "fsdp")
MESH = pl.DeviceIdType.MESH
LAG = 2


DEC_INPUTS = (0, 0, 0, 1, 2, 3, 4, 4, 4, 4, 5, 6, 7, 8)
ENC_INPUTS = (0, 0, 1, 1, 1, 2, 3, 3, 3, 3, 4, 5, 6, 7)
CODE_UNITS = 8


def place_of(Z):
    dp, fs = lax.axis_index("dp"), lax.axis_index("fsdp")
    z, core = fs // 2, fs % 2
    x_mate, y_mate = dp + 1 - 2 * (dp % 2), (dp + 2) % 4
    devices = ((dp, fs + 1 - 2 * core), (x_mate, fs), (y_mate, fs), (dp, fs + 2), (dp, fs - 2))
    return dp, z, core, x_mate, y_mate, (x_mate + 2) % 4, devices, z < Z - 1, z > 0


def add(a, b):
    return (a.astype(F32) + b.astype(F32)).astype(BF)


def remote(src, dst, send, recv, device):
    return pltpu.make_async_remote_copy(
        src_ref=src, dst_ref=dst, send_sem=send, recv_sem=recv, device_id=device, device_id_type=MESH
    )


def sum_scratch(Z, m, n):
    depth, half = 2 * LAG, Z // 2
    own_slots, held_slots, kept_slots = LAG + 1, 2 * LAG + 1, Z * LAG + 1
    return [
        pltpu.VMEM((own_slots, 4, Z, m, n), BF),
        pltpu.VMEM((depth, 4, Z, m, n), BF),
        pltpu.VMEM((held_slots, 4, Z, m, n), BF),
        pltpu.VMEM((depth, half, m, n), BF),
        pltpu.VMEM((depth, Z - half, m, n), BF),
        pltpu.VMEM((depth, Z, m, n), BF),
        pltpu.VMEM((depth, Z, m, n), BF),
        pltpu.VMEM((kept_slots, Z, m, n), BF),
        pltpu.VMEM((2, Z - 1, depth, m, n), BF),
    ]


def sum_semaphores(Z):
    depth, dma = 2 * LAG, pltpu.SemaphoreType.DMA
    return [
        dma((depth,)),
        dma((depth,)),
        dma((2, depth)),
        dma((2, depth)),
        dma((2, depth)),
        dma((2, depth)),
        dma((2, Z - 1, depth)),
        dma((2, Z - 1, depth)),
    ]


def sum_stages(Z, scratch, semaphores, arrive, out_ref):
    own, from_core, held, from_x, from_y, all_x, all_y, kept, from_line = scratch
    _, _, one_send, one_recv, two_send, two_recv, line_send, line_recv = semaphores
    dp, z, core, x_mate, y_mate, across_dp, devices, has_up, has_down = place_of(Z)
    _, x_dev, y_dev, up_dev, down_dev = devices
    depth, half = 2 * LAG, Z // 2
    own_slots, held_slots, kept_slots = own.shape[0], held.shape[0], kept.shape[0]

    def one_copies(k):
        s, block = k % depth, held.at[k % held_slots, across_dp]
        return (
            remote(block.at[pl.ds(0, half)], from_x.at[s], one_send.at[0, s], one_recv.at[0, s], x_dev),
            remote(block.at[pl.ds(half, Z - half)], from_y.at[s], one_send.at[1, s], one_recv.at[1, s], y_dev),
        )

    def two_copies(k):
        s, h = k % depth, k % held_slots
        return (
            remote(held.at[h, x_mate], all_x.at[s], two_send.at[0, s], two_recv.at[0, s], x_dev),
            remote(held.at[h, y_mate], all_y.at[s], two_send.at[1, s], two_recv.at[1, s], y_dev),
        )

    def up_block(step):
        return jnp.minimum(z + Z - step, Z - 1)

    def down_block(step):
        return jnp.maximum(z - Z + step, 0)

    def up_copy(k, step):
        s = k % depth
        return remote(
            kept.at[k % kept_slots, up_block(step)], from_line.at[0, step - 1, s],
            line_send.at[0, step - 1, s], line_recv.at[0, step - 1, s], up_dev,
        )

    def down_copy(k, step):
        s = k % depth
        return remote(
            kept.at[k % kept_slots, down_block(step)], from_line.at[1, step - 1, s],
            line_send.at[1, step - 1, s], line_recv.at[1, step - 1, s], down_dev,
        )

    def line_start(k, step):
        @pl.when(has_up)
        def _():
            up_copy(k, step).start()

        @pl.when(has_down)
        def _():
            down_copy(k, step).start()

    def line_wait(k, step):
        @pl.when(has_down)
        def _():
            up_copy(k, step).wait_recv()
            down_copy(k, step).wait_send()

        @pl.when(has_up)
        def _():
            down_copy(k, step).wait_recv()
            up_copy(k, step).wait_send()

    def after_core(k):
        arrive(k)

        def one(block, carry):
            for q in range(Z):
                held[k % held_slots, block, q] = add(
                    own[k % own_slots, block, q], from_core[k % depth, block, q]
                )
            return carry

        lax.fori_loop(0, 4, one, 0)
        for copy in one_copies(k):
            copy.start()

    def after_one(k):
        s, h = k % depth, k % held_slots
        for copy in one_copies(k):
            copy.wait()
        for q in range(half):
            held[h, y_mate, q] = add(held[h, y_mate, q], from_x[s, q])
        for q in range(Z - half):
            held[h, x_mate, half + q] = add(held[h, x_mate, half + q], from_y[s, q])
        for copy in two_copies(k):
            copy.start()

    def after_two(k):
        s, h = k % depth, k % held_slots
        for copy in two_copies(k):
            copy.wait()
        for q in range(Z):
            kept[k % kept_slots, q] = (
                held[h, dp, q].astype(F32) + all_x[s, q].astype(F32) + all_y[s, q].astype(F32)
            ).astype(BF)
        line_start(k, 1)

    def along_line(step):
        def run(k):
            s, h = k % depth, k % kept_slots
            line_wait(k, step - 1)

            @pl.when(has_down & (z + Z - step <= Z - 1))
            def _():
                kept[h, up_block(step)] = add(kept[h, up_block(step)], from_line[0, step - 2, s])

            @pl.when(has_up & (z - Z + step >= 0))
            def _():
                kept[h, down_block(step)] = add(kept[h, down_block(step)], from_line[1, step - 2, s])

            line_start(k, step)

        return run

    def finish(k):
        s = k % depth
        line_wait(k, Z - 1)
        out_ref[k] = kept[k % kept_slots, z].astype(F32)

        @pl.when(has_down)
        def _():
            out_ref[k] = out_ref[k] + from_line[0, Z - 2, s].astype(F32)

        @pl.when(has_up)
        def _():
            out_ref[k] = out_ref[k] + from_line[1, Z - 2, s].astype(F32)

    stages = [after_core, after_one, after_two]
    return stages + [along_line(step) for step in range(2, Z)] + [finish], up_block, down_block


def sum_kernel(Z, counts, *refs):
    groups = []
    for count in counts:
        groups.append([ref.at[i] for ref in refs[:count] for i in range(ref.shape[0])])
        refs = refs[count:]
    dec_x, dec_g, enc_x, enc_g = groups
    (
        code_x, targets, code_g, look_g, out_ref,
        dec_xs, dec_gs, dec_turned, enc_xs, enc_gs, enc_turned, code_xs, code_loaded, code_gs, to_core,
        own, from_core, held, from_x, from_y, all_x, all_y, kept, from_line,
        rare_held, rare_line, rare_kept, rare_x, rare_y, rare_all_x, rare_all_y,
        load_sem, code_sem, core_send, core_recv, one_send, one_recv, two_send, two_recv, line_send, line_recv,
        rare_line_send, rare_line_recv, rare_send, rare_recv,
    ) = refs
    dec_units, enc_units = len(DEC_INPUTS), len(ENC_INPUTS)
    plain_units = dec_units + enc_units
    units = plain_units + CODE_UNITS
    depth = 2 * LAG
    dp, fs = lax.axis_index("dp"), lax.axis_index("fsdp")
    z, core = fs // 2, fs % 2
    x_mate, y_mate = dp + 1 - 2 * (dp % 2), (dp + 2) % 4
    across_dp = (x_mate + 2) % 4
    core_dev, x_dev, y_dev = (dp, fs + 1 - 2 * core), (x_mate, fs), (y_mate, fs)
    up_dev, down_dev = (dp, fs + 2), (dp, fs - 2)
    has_up, has_down = z < Z - 1, z > 0

    barrier = pltpu.get_barrier_semaphore()
    for device in (core_dev, x_dev, y_dev):
        pl.semaphore_signal(barrier, inc=1, device_id=device, device_id_type=MESH)

    @pl.when(has_up)
    def _():
        pl.semaphore_signal(barrier, inc=1, device_id=up_dev, device_id_type=MESH)

    @pl.when(has_down)
    def _():
        pl.semaphore_signal(barrier, inc=1, device_id=down_dev, device_id_type=MESH)

    pl.semaphore_wait(barrier, 3 + has_up.astype(jnp.int32) + has_down.astype(jnp.int32))
    scratch = (own, from_core, held, from_x, from_y, all_x, all_y, kept, from_line)
    semaphores = (
        core_send, core_recv, one_send, one_recv, two_send, two_recv, line_send, line_recv
    )
    own_slots = own.shape[0]

    def pair(x, g, xs, gs, slot):
        return (
            pltpu.make_async_copy(x, xs.at[slot], load_sem.at[0, slot]),
            pltpu.make_async_copy(g, gs.at[slot], load_sem.at[1, slot]),
        )

    def start_loads(k):
        for i, place in enumerate(DEC_INPUTS):

            @pl.when(k == i)
            def _(i=i, place=place):
                for copy in pair(dec_x[place], dec_g[min(i, 10)], dec_xs, dec_gs, i % 2):
                    copy.start()

        for i, place in enumerate(ENC_INPUTS):

            @pl.when(k == dec_units + i)
            def _(i=i, place=place):
                for copy in pair(enc_x[place], enc_g[min(i, 10)], enc_xs, enc_gs, (dec_units + i) % 2):
                    copy.start()

    code_rows = code_x.shape[0]
    code_loads = [
        pltpu.make_async_copy(code_x, code_xs.at[pl.ds(0, code_rows)], code_sem.at[0]),
        pltpu.make_async_copy(code_g, code_loaded.at[0], code_sem.at[1]),
        pltpu.make_async_copy(look_g, code_loaded.at[1], code_sem.at[2]),
    ]
    for copy in code_loads:
        copy.start()
    start_loads(jnp.int32(0))

    def core_copy(k):
        s = k % depth
        return remote(
            to_core.at[k % own_slots], from_core.at[s], core_send.at[s], core_recv.at[s], core_dev
        )

    def turn(xs, slot, turned):
        size = 256

        def columns(i, carry):
            part = xs[slot, :, pl.ds(pl.multiple_of(i * size, size), size)].T
            count = size // (2 * turned.shape[2])
            turned[pl.ds(i * count, count)] = part.reshape(count, *turned.shape[1:])
            return carry

        lax.fori_loop(0, xs.shape[2] // size, columns, 0)

    def product(turned, gs, slot, side, into):
        def rows(block, carry):
            value = turned[pl.ds(block * Z, Z), side].reshape(-1, turned.shape[-1])
            result = jnp.dot(value, gs[slot], preferred_element_type=F32).astype(BF)
            into[block] = result.reshape(into.shape[1:])
            return carry

        lax.fori_loop(0, 4, rows, 0)

    def code_inputs():
        for copy in code_loads:
            copy.wait()
        size = D // 4
        for half_rows in range(2):

            def turn_columns(i, carry, half_rows=half_rows):
                part = code_loaded[half_rows, :, pl.ds(pl.multiple_of(i * size, size), size)].T
                code_gs[i, :, :, pl.ds(half_rows * code_rows, code_rows)] = part.reshape(
                    CODE_UNITS, size // CODE_UNITS, code_rows
                )
                return carry

            lax.fori_loop(0, 4, turn_columns, 0)

        width = 512

        def hits(i, carry):
            start = pl.multiple_of(i * width, width)
            column = lax.broadcasted_iota(jnp.int32, (code_rows, width), 1) + i * width
            code_xs[pl.ds(code_rows, code_rows), pl.ds(start, width)] = jnp.where(
                targets[...] == column, 1.0, 0.0
            ).astype(BF)
            return carry

        lax.fori_loop(0, VOCAB // width, hits, 0)

    def code_product(k, side, into):
        value = code_gs[:, k - plain_units].reshape(-1, code_gs.shape[-1])
        width = into.shape[-1]

        def columns(place, carry):
            start = pl.multiple_of((2 * place + side) * width, width)
            result = jnp.dot(value, code_xs[:, pl.ds(start, width)], preferred_element_type=F32).astype(BF)
            into[:, place] = result.reshape(4, -1, width)
            return carry

        lax.fori_loop(0, Z, columns, 0)

    def begin(k):
        slot, o = k % 2, k % own_slots
        for here, x, g, xs, gs, turned in (
            (k < dec_units, dec_x[0], dec_g[0], dec_xs, dec_gs, dec_turned),
            ((k >= dec_units) & (k < plain_units), enc_x[0], enc_g[0], enc_xs, enc_gs, enc_turned),
        ):

            @pl.when(here)
            def _(x=x, g=g, xs=xs, gs=gs, turned=turned):
                for copy in pair(x, g, xs, gs, slot):
                    copy.wait()
                start_loads(k + 1)
                turn(xs, slot, turned)
                product(turned, gs, slot, 1 - core, to_core.at[o])
                core_copy(k).start()
                product(turned, gs, slot, core, own.at[o])

        @pl.when(k == dec_units)
        def _():
            code_inputs()

        @pl.when(k >= plain_units)
        def _():
            code_product(k, 1 - core, to_core.at[o])
            core_copy(k).start()
            code_product(k, core, own.at[o])

    def arrive(k):
        core_copy(k).wait()

    later, up_block, down_block = sum_stages(Z, scratch, semaphores, arrive, out_ref)

    def turn_of(k):
        return (k // 9) * 2 + (k % 9 >= 7).astype(jnp.int32)

    def rare_slot(k):
        return turn_of(k) % rare_held.shape[0]

    def rare_line_copies(k, step):
        t, s = turn_of(k), rare_slot(k)
        return [
            remote(
                rare_held.at[s, :, block], rare_line.at[s, way, step - 1],
                rare_line_send.at[way, step - 1, t], rare_line_recv.at[way, step - 1, t], device,
            )
            for way, block, device in ((0, up_block(step), up_dev), (1, down_block(step), down_dev))
        ]

    def rare_valid(step):
        return (has_up & (z + Z - step <= Z - 1), has_down & (z - Z + step >= 0)), (
            has_down & (z - 1 + Z - step <= Z - 1),
            has_up & (z + 1 - Z + step >= 0),
        )

    def rare_line_start(k, step):
        for copy, sends in zip(rare_line_copies(k, step), rare_valid(step)[0]):
            pl.when(sends)(copy.start)

    def rare_line_wait(k, step):
        for copy, sends, receives in zip(rare_line_copies(k, step), *rare_valid(step)):
            pl.when(sends)(copy.wait_send)
            pl.when(receives)(copy.wait_recv)

    def rare_add(into, k, step):
        for way, receives in enumerate(rare_valid(step)[1]):

            @pl.when(receives)
            def _(way=way):
                for block in range(4):
                    ref = into(way, block)
                    ref[...] = add(ref[...], rare_line[rare_slot(k), way, step - 1, block])

    def rare_square(k, slot):
        t, s = turn_of(k), rare_slot(k)
        small = rare_kept.shape[2] // 2
        source, target, device = (
            (rare_kept.at[s, across_dp, pl.ds(0, small)], rare_x.at[s], x_dev),
            (rare_kept.at[s, across_dp, pl.ds(small, small)], rare_y.at[s], y_dev),
            (rare_kept.at[s, x_mate], rare_all_x.at[s], x_dev),
            (rare_kept.at[s, y_mate], rare_all_y.at[s], y_dev),
        )[slot]
        return remote(source, target, rare_send.at[slot, t], rare_recv.at[slot, t], device)

    def rare_after_core(k):
        core_copy(k).wait()

        def one(block, carry):
            for q in range(Z):
                rare_held[rare_slot(k), block, q] = add(
                    own[k % own_slots, block, q], from_core[k % depth, block, q]
                )
            return carry

        lax.fori_loop(0, 4, one, 0)
        rare_line_start(k, 1)

    def rare_along(step):
        def run(k):
            rare_line_wait(k, step - 1)
            s = rare_slot(k)
            rare_add(
                lambda way, block: rare_held.at[s, block, (up_block, down_block)[way](step)], k, step - 1
            )
            rare_line_start(k, step)

        return run

    def rare_after_line(k):
        rare_line_wait(k, Z - 1)
        s = rare_slot(k)
        for block in range(4):
            rare_kept[s, block] = rare_held[s, block, z]
        rare_add(lambda way, block: rare_kept.at[s, block], k, Z - 1)
        for slot in range(2):
            rare_square(k, slot).start()

    def rare_after_one(k):
        s, small = rare_slot(k), rare_kept.shape[2] // 2
        for slot in range(2):
            rare_square(k, slot).wait()
        first, second = pl.ds(0, small), pl.ds(small, small)
        rare_kept[s, y_mate, first] = add(rare_kept[s, y_mate, first], rare_x[s])
        rare_kept[s, x_mate, second] = add(rare_kept[s, x_mate, second], rare_y[s])
        for slot in range(2, 4):
            rare_square(k, slot).start()

    def rare_finish(k):
        s = rare_slot(k)
        for slot in range(2, 4):
            rare_square(k, slot).wait()
        out_ref[k] = (
            rare_kept[s, dp].astype(F32) + rare_all_x[s].astype(F32) + rare_all_y[s].astype(F32)
        )

    stages = [begin] + later
    rare_stages = [begin, rare_after_core] + [rare_along(step) for step in range(2, Z)]
    rare_stages += [rare_after_line, rare_after_one, rare_finish]

    def loop_step(j, carry):
        for place in reversed(range(len(stages))):
            k = j - place * LAG
            here = (k >= 0) & (k < units)
            rare = (k % 9 == 3) | (k % 9 == 7)
            if place == 0:
                pl.when(here)(partial(begin, k))
            else:
                pl.when(here & jnp.logical_not(rare))(partial(stages[place], k))
                pl.when(here & rare)(partial(rare_stages[place], k))
        return carry

    lax.fori_loop(0, units + (len(stages) - 1) * LAG, loop_step, 0)


def sum_products(dec_x, dec_g, enc_x, enc_g, code_x, targets, code_g, look_g, call_id):
    dp_size, fsdp_size = lax.axis_size("dp"), lax.axis_size("fsdp")
    devices, Z = dp_size * fsdp_size, fsdp_size // 2
    m = D // devices
    stacks = (dec_x, dec_g, enc_x, enc_g)
    if dp_size != 4 or Z != 4 or m % 32:
        dec_x, dec_g, enc_x, enc_g = [[row for stack in group for row in stack] for group in stacks]
        products = [across(dec_x[i], dec_g[min(k, 10)]) for k, i in enumerate(DEC_INPUTS)]
        products += [across(enc_x[i], enc_g[min(k, 10)]) for k, i in enumerate(ENC_INPUTS)]
        plain = jnp.stack(products).astype(BF).reshape(len(products), devices, m, D)
        hit = (targets[:, None] == jnp.arange(VOCAB)[None, :]).astype(BF)
        code = across(jnp.concatenate([code_g, look_g]), jnp.concatenate([code_x, hit])).astype(BF)
        code = code.reshape(dp_size, D // dp_size, fsdp_size, VOCAB // fsdp_size)
        code = code.transpose(0, 2, 1, 3).reshape(devices, D // dp_size, VOCAB // fsdp_size)
        plain = lax.psum_scatter(plain, AXES, scatter_dimension=1, tiled=True)
        code = lax.psum_scatter(code, AXES, scatter_dimension=0, tiled=True)
        return jnp.concatenate([plain.reshape(-1, m, D), code.reshape(-1, m, D)]).astype(F32)
    n, units = D, len(DEC_INPUTS) + len(ENC_INPUTS) + CODE_UNITS
    depth, half = 2 * LAG, Z // 2
    own_slots, held_slots, kept_slots = LAG + 1, 2 * LAG + 1, Z * LAG + 1
    dec_rows, enc_rows, code_rows = dec_x[0].shape[1], enc_x[0].shape[1], code_x.shape[0]
    counts = [len(group) for group in stacks]
    dma = pltpu.SemaphoreType.DMA
    whole = pl.BlockSpec(memory_space=pl.ANY)
    out = pl.pallas_call(
        partial(sum_kernel, Z, counts),
        out_shape=jax.ShapeDtypeStruct((units, m, n), F32),
        in_specs=[whole] * (sum(counts) + 1) + [pl.BlockSpec(memory_space=pltpu.VMEM)] + [whole] * 2,
        out_specs=pl.BlockSpec(memory_space=pltpu.VMEM),
        scratch_shapes=[
            pltpu.VMEM((2, dec_rows, n), BF),
            pltpu.VMEM((2, dec_rows, n), BF),
            pltpu.VMEM((4 * Z, 2, m, dec_rows), BF),
            pltpu.VMEM((2, enc_rows, n), BF),
            pltpu.VMEM((2, enc_rows, n), BF),
            pltpu.VMEM((4 * Z, 2, m, enc_rows), BF),
            pltpu.VMEM((2 * code_rows, VOCAB), BF),
            pltpu.VMEM((2, code_rows, n), BF),
            pltpu.VMEM((4, CODE_UNITS, m, 2 * code_rows), BF),
            pltpu.VMEM((own_slots, 4, Z, m, n), BF),
            pltpu.VMEM((own_slots, 4, Z, m, n), BF),
            pltpu.VMEM((depth, 4, Z, m, n), BF),
            pltpu.VMEM((held_slots, 4, Z, m, n), BF),
            pltpu.VMEM((depth, half, m, n), BF),
            pltpu.VMEM((depth, Z - half, m, n), BF),
            pltpu.VMEM((depth, Z, m, n), BF),
            pltpu.VMEM((depth, Z, m, n), BF),
            pltpu.VMEM((kept_slots, Z, m, n), BF),
            pltpu.VMEM((2, Z - 1, depth, m, n), BF),
            pltpu.VMEM((3, 4, Z, m, n), BF),
            pltpu.VMEM((3, 2, Z - 1, 4, m, n), BF),
            pltpu.VMEM((3, 4, m, n), BF),
            pltpu.VMEM((3, m // 2, n), BF),
            pltpu.VMEM((3, m // 2, n), BF),
            pltpu.VMEM((3, m, n), BF),
            pltpu.VMEM((3, m, n), BF),
            dma((2, 2)),
            dma((3,)),
            dma((depth,)),
            dma((depth,)),
            dma((2, depth)),
            dma((2, depth)),
            dma((2, depth)),
            dma((2, depth)),
            dma((2, Z - 1, depth)),
            dma((2, Z - 1, depth)),
            dma((2, Z - 1, 2 * (units // 9 + 1))),
            dma((2, Z - 1, 2 * (units // 9 + 1))),
            dma((4, 2 * (units // 9 + 1))),
            dma((4, 2 * (units // 9 + 1))),
        ],
        compiler_params=pltpu.CompilerParams(
            collective_id=call_id, has_side_effects=True, vmem_limit_bytes=62 << 20
        ),
    )(*dec_x, *dec_g, *enc_x, *enc_g, code_x, targets[:, None], code_g, look_g)
    return out


def spread_kernel(
    tables, units, Z, token_count, table_f32, mix_in, mix_out, ffn_up, ffn_down, text_table, small, codes,
    table_out, unit_out, text_out, small_all, code_rows,
    table_ref, unit_ref, looked, chunk, chunk_sem, own_sem, line_send, line_recv, square_send, square_recv, core_send, core_recv,
    small_send, small_recv, text_sem, *sum_refs,
):
    dp, fs = lax.axis_index("dp"), lax.axis_index("fsdp")
    z, core = fs // 2, fs % 2
    x_mate, y_mate = dp + 1 - 2 * (dp % 2), (dp + 2) % 4
    across_dp = (x_mate + 2) % 4
    core_dev, x_dev, y_dev = (dp, fs + 1 - 2 * core), (x_mate, fs), (y_mate, fs)
    up_dev, down_dev = (dp, fs + 2), (dp, fs - 2)
    has_up, has_down = z < Z - 1, z > 0
    total, half = tables + units, Z // 2
    every = slice(None)
    table_rows, table_columns = table_out.shape[2] // tables, table_out.shape[3] // 4

    def at(is_table, k, dp_at, z_at, core_at, part=None):
        if is_table:
            size = table_rows if part is None else table_rows // 2
            rows = pl.ds(k * table_rows + (part or 0) * size, size)
            columns = every if isinstance(dp_at, slice) else pl.ds(dp_at * table_columns, table_columns)
            return table_out.at[z_at, core_at, rows, columns]
        if part is None:
            return unit_out.at[k - tables, dp_at, z_at, core_at]
        size = unit_out.shape[4] // 2
        return unit_out.at[k - tables, dp_at, z_at, core_at, pl.ds(part * size, size)]

    def passed(ref, send, recv, device):
        return remote(ref, ref, send, recv, device)

    size, inner = 8 * Z, 2 * Z
    me = dp * inner + fs

    def peer(i):
        other = lax.rem(me + i, size)
        return (other // inner, lax.rem(other, inner))

    def each(run):
        def one(i, carry):
            run(i)
            return carry

        lax.fori_loop(1, size, one, 0)

    def small_copy(i):
        return remote(small, small_all.at[me], small_send.at[i], small_recv.at[i], peer(i))

    barrier = pltpu.get_barrier_semaphore()
    each(lambda i: pl.semaphore_signal(barrier, inc=1, device_id=peer(i), device_id_type=MESH))
    small_all[me] = small[...]

    rows = unit_ref.shape[1]
    place = 0

    def put(value):
        nonlocal place
        unit_ref[place] = value.astype(BF)
        place += 1

    def put_ffn(layer, with_down):
        turned = [
            swap_groups([ffn_up[layer, :, pl.ds(128 * (4 * g + j), 128)] for j in range(4)]) for g in range(8)
        ]
        for q in range(4):
            put(jnp.concatenate([parts[q] for parts in turned], axis=1))
        for q in range(4 if with_down else 0):
            put(ffn_down[layer, pl.ds(q * rows, rows), :])

    for layer in range(3):
        for i in range(3):
            put(mix_in[layer, :, pl.ds(i * D, D)])
        put(mix_out[layer])
        if layer != 1:
            put_ffn(min(layer, 1), layer == 0)
    table_ref[...] = table_f32[...].astype(BF)

    own = (
        pltpu.make_async_copy(
            table_ref, table_out.at[z, core, :, pl.ds(dp * table_columns, table_columns)], own_sem.at[0]
        ),
        pltpu.make_async_copy(unit_ref, unit_out.at[:, dp, z, core], own_sem.at[1]),
    )
    for copy in own:
        copy.start()

    for copy in own:
        copy.wait()
    pl.semaphore_wait(barrier, size - 1)
    each(lambda i: small_copy(i).start())

    def line_copies(view, k, step):
        s = step - 1
        return (
            (passed(view(jnp.maximum(z - s, 0)), line_send.at[0, s, k], line_recv.at[0, s, k], up_dev),
             has_up & (z >= s), has_down & (z >= s + 1)),
            (passed(view(jnp.minimum(z + s, Z - 1)), line_send.at[1, s, k], line_recv.at[1, s, k], down_dev),
             has_down & (z + s <= Z - 1), has_up & (z + s + 1 <= Z - 1)),
        )

    def line_start(view, k, step):
        for copy, sends, _ in line_copies(view, k, step):
            pl.when(sends)(copy.start)

    def line_wait(view, k, step):
        for copy, sends, receives in line_copies(view, k, step):
            pl.when(sends)(copy.wait_send)
            pl.when(receives)(copy.wait_recv)

    def to_core(ref, k, slot):
        return passed(ref, core_send.at[slot, k], core_recv.at[slot, k], core_dev)

    def square_copy(ref, k, slot):
        return passed(
            ref, square_send.at[slot, k], square_recv.at[slot, k], x_dev if slot % 2 == 0 else y_dev
        )

    def line_first(is_table):
        def view(k):
            return lambda place: at(is_table, k, dp, place, core)

        def row(k, dp_at):
            return at(is_table, k, dp_at, every, core)

        def ones(k):
            return square_copy(row(k, dp), k, 0), square_copy(row(k, dp), k, 1)

        def twos(k):
            return (
                square_copy(at(is_table, k, y_mate, pl.ds(0, half), core), k, 2),
                square_copy(at(is_table, k, x_mate, pl.ds(half, Z - half), core), k, 3),
            )

        def line(step):
            def run(k):
                if step > 1:
                    line_wait(view(k), k, step - 1)
                if step < Z:
                    line_start(view(k), k, step)
                else:
                    for copy in ones(k):
                        copy.start()
                    to_core(row(k, dp), k, 0).start()
            return run

        def after_one(k):
            for copy in ones(k):
                copy.wait()
            for copy in twos(k):
                copy.start()
            to_core(row(k, x_mate), k, 1).start()
            to_core(row(k, y_mate), k, 2).start()

        def after_two(k):
            for copy in twos(k):
                copy.wait()
            to_core(row(k, across_dp), k, 3).start()

        def finish(k):
            for slot in range(4):
                to_core(row(k, dp), k, slot).wait()

        return [line(step) for step in range(1, Z + 1)] + [after_one, after_two, finish]

    def square_first(is_table):
        def plane(k):
            return lambda place: at(is_table, k, every, place, core)

        def ones(k):
            ref = at(is_table, k, dp, z, core)
            return square_copy(ref, k, 0), square_copy(ref, k, 1)

        def twos(k):
            return (
                square_copy(at(is_table, k, y_mate, z, core, 0), k, 2),
                square_copy(at(is_table, k, x_mate, z, core, 1), k, 3),
            )

        def begin(k):
            for copy in ones(k):
                copy.start()

        def after_one(k):
            for copy in ones(k):
                copy.wait()
            for copy in twos(k):
                copy.start()

        def after_two(k):
            for copy in twos(k):
                copy.wait()
            line_start(plane(k), k, 1)
            to_core(plane(k)(z), k, z).start()

        def line(step):
            def run(k):
                line_wait(plane(k), k, step)
                if step + 1 < Z:
                    line_start(plane(k), k, step + 1)

                @pl.when(z - step >= 0)
                def _():
                    to_core(plane(k)(jnp.maximum(z - step, 0)), k, jnp.maximum(z - step, 0)).start()

                @pl.when(z + step <= Z - 1)
                def _():
                    to_core(plane(k)(jnp.minimum(z + step, Z - 1)), k, jnp.minimum(z + step, Z - 1)).start()
            return run

        def finish(k):
            for place in range(Z):
                to_core(plane(k)(place), k, place).wait()

        return [begin, after_one, after_two] + [line(step) for step in range(1, Z)] + [finish]

    forms = [(is_table, first, form(is_table))
             for is_table in (True, False) for first, form in ((True, line_first), (False, square_first))]
    n_stages = Z + 3

    scratch, semaphores = sum_refs[:9], sum_refs[9:]
    own_slots, depth = scratch[0].shape[0], scratch[1].shape[0]

    look_ups, text_first = 8, 9

    def look_up(part):
        owned_rows = text_table.shape[0]
        base = me * token_count

        def of_device(i, carry):
            device = part * (size // look_ups) + i
            ids = small_all[device].T[:, :1]
            row = lax.broadcasted_iota(jnp.int32, (ids.shape[0], owned_rows), 1)
            hit = (row + base == ids.astype(jnp.int32)) & (row < token_count)
            found = matmul(jnp.where(hit, 1.0, 0.0).astype(BF), text_table[...]).astype(BF)
            dp_at, line_at, core_at = device // inner, lax.rem(device, inner) // 2, lax.rem(device, 2)
            for u in range(looked.shape[0]):
                looked[u, dp_at, line_at, core_at] = found[u * rows : (u + 1) * rows]
            return carry

        lax.fori_loop(0, size // look_ups, of_device, 0)

    def text_own(k):
        return pltpu.make_async_copy(
            looked.at[k, :, :, core], scratch[0].at[k % own_slots], text_sem.at[k % own_slots]
        )

    def text_core(k):
        s = k % depth
        return remote(
            looked.at[k, :, :, 1 - core], scratch[1].at[s], semaphores[0].at[s], semaphores[1].at[s], core_dev
        )

    def text_begin(k):
        text_own(k).start()
        text_core(k).start()

    def text_arrive(k):
        text_own(k).wait()
        text_core(k).wait()

    text_stages = [text_begin] + sum_stages(Z, scratch, semaphores, text_arrive, text_out)[0]

    code_first = (n_stages - 1) * LAG + 1

    def chunk_copy(k):
        source = table_out.at[:, :, pl.ds(k * table_rows, table_rows), :]
        return pltpu.make_async_copy(source, chunk.at[k % 2], chunk_sem.at[k % 2])

    def find_codes(k):
        chunk_copy(k).wait()
        pl.when(k + 1 < tables)(lambda: chunk_copy(k + 1).start())
        place = lax.broadcasted_iota(jnp.int32, (codes.shape[0], inner * table_rows), 1)
        code = (place // table_rows) * table_out.shape[2] + k * table_rows + place % table_rows
        hit = jnp.where(codes[...] == code, 1.0, 0.0).astype(BF)
        code_rows[...] += matmul(hit, chunk[k % 2].reshape(-1, chunk.shape[-1]))

    code_rows[...] = jnp.zeros_like(code_rows)

    def loop_step(j, carry):
        @pl.when(j == 1)
        def _():
            each(lambda i: small_copy(i).wait())

        pl.when((j >= 1) & (j < 1 + look_ups))(lambda: look_up(j - 1))
        for place in reversed(range(n_stages)):
            k = j - place * LAG
            turn = k - text_first
            pl.when((turn >= 0) & (turn < looked.shape[0]))(partial(text_stages[place], turn))
            turn = k % 9
            by_line = (turn != 3) & (turn != 7)
            for is_table, first, stages in forms:
                here = (k >= 0) & (k < tables) if is_table else (k >= tables) & (k < total)
                here = here & (by_line if first else jnp.logical_not(by_line))

                @pl.when(here)
                def _(k=k, run=stages[place]):
                    run(k)

        found = j - code_first

        @pl.when(found == -1)
        def _():
            chunk_copy(0).start()

        pl.when((found >= 0) & (found < tables))(lambda: find_codes(found))
        return carry

    lax.fori_loop(0, total + (n_stages - 1) * LAG, loop_step, 0)


def spread(table, weights, text_table, small, codes, call_id):
    mix_in, mix_out, ffn_up, ffn_down = weights
    dp_size, fsdp_size = lax.axis_size("dp"), lax.axis_size("fsdp")
    m, Z = mix_in.shape[1], fsdp_size // 2
    if dp_size != 4 or Z != 4 or m != 32:
        shards = []
        for layer in range(3):
            shards += [column_units(mix_in[layer]), mix_out[layer][None]]
            if layer != 1:
                which = min(layer, 1)
                shards += [hidden_units(ffn_up[which], dp_size * fsdp_size)]
            if layer == 0:
                shards += [ffn_down[0].reshape(4, m, D)]
        table = lax.all_gather(table.astype(BF), "dp", axis=1, tiled=True)
        whole = lax.all_gather(table, "fsdp", axis=0, tiled=True)
        units = lax.all_gather(jnp.concatenate(shards).astype(BF), AXES, axis=1, tiled=True)
        devices, count = dp_size * fsdp_size, text_table.shape[0]
        small_all = exchange(jnp.broadcast_to(small[None], (devices, 8, 128)), 3)
        ids = small_all[:, 0].astype(jnp.int32).reshape(-1)
        base = (lax.axis_index("dp") * fsdp_size + lax.axis_index("fsdp")) * count
        owned = (ids[:, None] - base == jnp.arange(count)[None, :]).astype(BF)
        looked = matmul(owned, text_table.astype(BF)).astype(BF)
        text = lax.psum_scatter(looked, AXES, scatter_dimension=0, tiled=True).astype(F32)
        found = jnp.where(codes[:, None] >= 0, whole[jnp.maximum(codes, 0)].astype(F32), 0.0)
        return whole, units, text, small_all, found
    text_units, token_count = TXT_LEN // m, text_table.shape[0]
    text_table = jnp.pad(text_table.astype(BF), ((0, -token_count % 128), (0, 0)))
    tables, count, dma = 8, 24, pltpu.SemaphoreType.DMA
    total = tables + count
    whole, units, text, small_all, found = pl.pallas_call(
        partial(spread_kernel, tables, count, Z, token_count),
        out_shape=(
            jax.ShapeDtypeStruct((Z, 2, table.shape[0], 4 * table.shape[1]), BF),
            jax.ShapeDtypeStruct((count, 4, Z, 2, m, D), BF),
            jax.ShapeDtypeStruct((text_units, m, D), F32),
            jax.ShapeDtypeStruct((8 * Z, *small.shape), F32),
            jax.ShapeDtypeStruct((codes.shape[0], D), F32),
        ),
        in_specs=[pl.BlockSpec(memory_space=pltpu.VMEM)] * 8,
        out_specs=[pl.BlockSpec(memory_space=pl.ANY)] * 2 + [pl.BlockSpec(memory_space=pltpu.VMEM)] * 3,
        scratch_shapes=[
            pltpu.VMEM(table.shape, BF),
            pltpu.VMEM((count, m, D), BF),
            pltpu.VMEM((text_units, 4, Z, 2, m, D), BF),
            pltpu.VMEM((2, Z, 2, table.shape[0] // tables, D), BF),
            dma((2,)),
            dma((2,)),
            dma((2, Z - 1, total)),
            dma((2, Z - 1, total)),
            dma((4, total)),
            dma((4, total)),
            dma((4, total)),
            dma((4, total)),
            dma((8 * Z,)),
            dma((8 * Z,)),
            dma((LAG + 1,)),
            *sum_scratch(Z, m, D),
            *sum_semaphores(Z),
        ],
        compiler_params=pltpu.CompilerParams(
            collective_id=call_id, has_side_effects=True, vmem_limit_bytes=48 << 20
        ),
    )(table, *weights, text_table, small, codes[:, None])
    whole, units = whole.reshape(-1, 4 * table.shape[1]), units.reshape(count, -1, D)
    return whole, units, text.reshape(-1, D), small_all, found


def exchange_kernel(size, inner, in_ref, out_ref, send_sem, recv_sem):
    me = lax.axis_index("dp") * inner + lax.axis_index("fsdp")

    def peer(i):
        other = lax.rem(me + i, size)
        return other, (other // inner, lax.rem(other, inner))

    barrier = pltpu.get_barrier_semaphore()

    def greet(i, carry):
        pl.semaphore_signal(barrier, inc=1, device_id=peer(i)[1], device_id_type=MESH)
        return carry

    def copy(i):
        other, device = peer(i)
        return pltpu.make_async_remote_copy(
            src_ref=in_ref.at[other], dst_ref=out_ref.at[me], send_sem=send_sem.at[i],
            recv_sem=recv_sem.at[i], device_id=device, device_id_type=MESH,
        )

    def begin(i, carry):
        copy(i).start()
        return carry

    def end(i, carry):
        copy(i).wait()
        return carry

    lax.fori_loop(1, size, greet, 0)
    out_ref[me] = in_ref[me]
    pl.semaphore_wait(barrier, size - 1)
    lax.fori_loop(1, size, begin, 0)
    lax.fori_loop(1, size, end, 0)


def exchange(blocks, call_id):
    size, inner = blocks.shape[0], lax.axis_size("fsdp")
    return pl.pallas_call(
        partial(exchange_kernel, size, inner),
        out_shape=jax.ShapeDtypeStruct(blocks.shape, F32),
        in_specs=[pl.BlockSpec(memory_space=pltpu.VMEM)],
        out_specs=pl.BlockSpec(memory_space=pltpu.VMEM),
        scratch_shapes=[pltpu.SemaphoreType.DMA((size,)), pltpu.SemaphoreType.DMA((size,))],
        compiler_params=pltpu.CompilerParams(collective_id=call_id, has_side_effects=True),
    )(blocks)


def tiles(values, count):
    padded = jnp.pad(values, ((0, 1024 - values.shape[0]),)).reshape(1, 8, 128)
    return jnp.broadcast_to(padded, (count, 8, 128))


def swap_groups(parts):
    group = lax.broadcasted_iota(jnp.int32, parts[0].shape, 1) // 32
    results = []
    for i in range(4):
        total = parts[i]
        for j in range(4):
            if j != i:
                turned = pltpu.roll(parts[j], (32 * (j - i)) % 128, 1)
                total = jnp.where(group == j, turned, total)
        results.append(total)
    return results


def norm_kernel(
    size, inner, count, sums, text, small, small_out, norm_out,
    squares, small_all, squares_all, sum_scratch, small_send, small_recv, square_send, square_recv,
):
    rows = sums.shape[1]
    text_rows = [(start, min(rows, text.shape[0] - start)) for start in range(0, text.shape[0], rows)]
    me = lax.axis_index("dp") * inner + lax.axis_index("fsdp")

    def peer(i):
        other = lax.rem(me + i, size)
        return other, (other // inner, lax.rem(other, inner))

    def small_copy(i):
        other, device = peer(i)
        return remote(small.at[other], small_all.at[me], small_send.at[i], small_recv.at[i], device)

    def square_copy(i):
        return remote(squares, squares_all.at[me], square_send.at[i], square_recv.at[i], peer(i)[1])

    def each(run):
        def one(i, carry):
            run(i)
            return carry

        lax.fori_loop(1, size, one, 0)

    barrier = pltpu.get_barrier_semaphore()
    each(lambda i: pl.semaphore_signal(barrier, inc=1, device_id=peer(i)[1], device_id_type=MESH))
    small_all[me] = small[me]
    pl.semaphore_wait(barrier, size - 1)
    each(lambda i: small_copy(i).start())

    sum_scratch[...] = jnp.zeros_like(sum_scratch)

    def square(k, carry):
        sum_scratch[...] += sums[k] * sums[k]
        return carry

    lax.fori_loop(0, sums.shape[0], square, 0)
    for start, length in text_rows:
        part = text[pl.ds(start, length), :]
        sum_scratch[pl.ds(0, length), :] += part * part

    each(lambda i: small_copy(i).wait())
    total = lax.fori_loop(0, size, lambda i, total: total + small_all[i], jnp.zeros_like(squares))
    small_out[...] = total
    place = lax.broadcasted_iota(jnp.int32, total.shape, 0) * 128 + lax.broadcasted_iota(jnp.int32, total.shape, 1)
    gains = jnp.where(place < count, total, 0.0)
    squares[...] = jnp.full(squares.shape, jnp.sum(sum_scratch[...]) + jnp.sum(gains * gains))

    squares_all[me] = squares[...]
    each(lambda i: square_copy(i).start())
    each(lambda i: square_copy(i).wait())
    norm_out[...] = jnp.sqrt(
        lax.fori_loop(0, size, lambda i, total: total + squares_all[i], jnp.zeros_like(squares))
    )


def update_kernel(*refs):
    norm, plain, text, gains, *refs = refs
    weights, refs = refs[:7], refs[7:]
    firsts, refs = refs[:7], refs[7:]
    seconds, refs = refs[:7], refs[7:]
    new_weights, refs = refs[:7], refs[7:]
    new_firsts, new_seconds = refs[:7], refs[7:]
    rows = plain.shape[1]
    text_rows = [(start, min(rows, text.shape[0] - start)) for start in range(0, text.shape[0], rows)]
    factor = (CLIP_NORM / jnp.maximum(norm[...], CLIP_NORM))[:1, :1]

    def step(which, place, gradient):
        updated = adam_step(
            weights[which][place], firsts[which][place], seconds[which][place],
            gradient * factor, STEP_RATES[which],
        )
        for out, value in zip((new_weights, new_firsts, new_seconds), updated):
            out[which][place] = value

    enc = len(DEC_INPUTS)
    every = slice(None)
    for layer, units in enumerate(((enc + 2, enc + 3, enc + 4), (0, 1, 2), (4, enc, enc + 1))):
        for i, unit in enumerate(units):
            step(0, (layer, every, pl.ds(i * D, D)), plain[unit])
    for layer, unit in enumerate((enc + 5, 3, 5)):
        step(1, (layer,), plain[unit])
    for layer, first in enumerate((enc + 6, 6)):
        for g in range(8):
            parts = [plain[first + q, :, pl.ds(128 * g, 128)] for q in range(4)]
            for j, part in enumerate(swap_groups(parts)):
                step(2, (layer, every, pl.ds(128 * (4 * g + j), 128)), part)
    for layer, first in enumerate((enc + 10, 10)):
        for q in range(4):
            step(3, (layer, pl.ds(q * rows, rows), every), plain[first + q])
    step(4, (every, every), gains[...])
    for start, count in text_rows:
        step(5, (pl.ds(start, count), every), text[pl.ds(start, count), :])
    columns, first = 256, len(DEC_INPUTS) + len(ENC_INPUTS)
    for i in range(D // columns):
        part = plain[pl.ds(first, CODE_UNITS), :, pl.ds(i * columns, columns)]
        step(6, (pl.ds(i * columns, columns), every), part.reshape(-1, columns).T)


def update(sums, text, small, weights, firsts, seconds, call_id):
    inner = lax.axis_size("fsdp")
    size = lax.axis_size("dp") * inner
    shapes = [jax.ShapeDtypeStruct(weight.shape, F32) for weight in weights]
    gains_shape = weights[4].shape
    count = gains_shape[0] * gains_shape[1]
    in_vmem = pl.BlockSpec(memory_space=pltpu.VMEM)
    dma, tile = pltpu.SemaphoreType.DMA, jax.ShapeDtypeStruct((8, 128), F32)
    small, norm = pl.pallas_call(
        partial(norm_kernel, size, inner, count),
        out_shape=[tile, tile],
        in_specs=[in_vmem] * 3,
        out_specs=[in_vmem] * 2,
        scratch_shapes=[
            pltpu.VMEM((8, 128), F32),
            pltpu.VMEM((size, 8, 128), F32),
            pltpu.VMEM((size, 8, 128), F32),
            pltpu.VMEM(sums.shape[1:], F32),
            dma((size,)),
            dma((size,)),
            dma((size,)),
            dma((size,)),
        ],
        compiler_params=pltpu.CompilerParams(
            collective_id=call_id, has_side_effects=True, vmem_limit_bytes=32 << 20
        ),
    )(sums, text, small)
    small = small.reshape(-1)
    outs = pl.pallas_call(
        update_kernel,
        out_shape=shapes * 3,
        in_specs=[in_vmem] * 25,
        out_specs=[in_vmem] * 21,
        compiler_params=pltpu.CompilerParams(vmem_limit_bytes=60 << 20),
    )(norm, sums, text, small[:count].reshape(gains_shape), *weights, *firsts, *seconds)
    return small[count], norm[0, 0], list(zip(outs[:7], outs[7:14], outs[14:]))


def layer_norm(stream, gain):
    centred = stream - jnp.mean(stream, axis=-1, keepdims=True)
    return centred * lax.rsqrt(jnp.mean(centred * centred, axis=-1, keepdims=True) + 1e-05) * gain


def norm_back(stream, gain, grad_out):
    centred = stream - jnp.mean(stream, axis=-1, keepdims=True)
    inverse = lax.rsqrt(jnp.mean(centred * centred, axis=-1, keepdims=True) + 1e-05)
    plain = centred * inverse
    scaled = grad_out * gain
    inner = jnp.mean(scaled * plain, axis=-1, keepdims=True)
    grad = inverse * (scaled - jnp.mean(scaled, axis=-1, keepdims=True) - plain * inner)
    return grad, jnp.sum(grad_out * plain, axis=0, keepdims=True)


def positions(length, width):
    position = jnp.arange(length, dtype=jnp.float32)[:, None]
    speeds = jnp.exp(
        -math.log(10000.0) * 2.0 * jnp.arange(width // 2, dtype=jnp.float32)[None, :] / width
    )
    return jnp.concatenate([jnp.sin(position * speeds), jnp.cos(position * speeds)], axis=1)


def matmul(first_op, second_op):
    return jnp.dot(first_op, second_op, preferred_element_type=jnp.float32)


def across(first_op, second_op):
    return lax.dot_general(
        first_op, second_op, (((0,), (0,)), ((), ())), preferred_element_type=jnp.float32
    )


def against(first_op, second_op):
    return lax.dot_general(
        first_op, second_op, (((1,), (1,)), ((), ())), preferred_element_type=jnp.float32
    )


LOCAL = 56 << 20


def gain_at(i):
    return pl.BlockSpec((1, 1, D), lambda *_: (i, 0, 0))


def fixed(shape):
    return pl.BlockSpec(shape, lambda *_: (0,) * len(shape))


def turns(shape):
    return pl.BlockSpec((1, *shape[1:]), lambda i: (i,) + (0,) * (len(shape) - 1))


def unit_from(first):
    return pl.BlockSpec((1, D, D), lambda i: (first + i, 0, 0))


def cost(rows, count):
    return pl.CostEstimate(flops=2 * rows * D * D * count, bytes_accessed=2 * D * D * count + 8 * rows * D, transcendentals=0)


def steps(kernel, count, rows, in_specs, out_specs, out_shape, scratch, *args):
    return pl.pallas_call(
        kernel,
        grid=(count,),
        in_specs=in_specs,
        out_specs=out_specs,
        out_shape=out_shape,
        scratch_shapes=scratch,
        cost_estimate=cost(rows, count),
        compiler_params=pltpu.CompilerParams(vmem_limit_bytes=LOCAL),
    )(*args)


def shaped(shape, kind):
    return jax.ShapeDtypeStruct(shape, kind)


def project(stream, gain, units, first, count):
    rows = stream.shape[0]

    def kernel(x, g, w, normed, out):
        @pl.when(pl.program_id(0) == 0)
        def _():
            normed[...] = layer_norm(x[...], g[0]).astype(BF)

        out[0] = matmul(normed[...], w[0]).astype(BF)

    whole = (count, rows, D)
    return steps(
        kernel, count, rows,
        [fixed((rows, D)), gain_at(gain[1]), unit_from(first)],
        [fixed((rows, D)), turns(whole)],
        [shaped((rows, D), BF), shaped(whole, BF)], [],
        stream, gain[0], units,
    )


def products(value, units, first, count):
    rows = value.shape[0]

    def kernel(x, w, out):
        out[0] = matmul(x[...], w[0]).astype(BF)

    whole = (count, rows, D)
    return steps(
        kernel, count, rows, [fixed((rows, D)), unit_from(first)], turns(whole), shaped(whole, BF), [],
        value, units,
    )


def add_products(stream, parts, units, first):
    count, rows, _ = parts.shape

    def kernel(x, a, w, out):
        @pl.when(pl.program_id(0) == 0)
        def _():
            out[...] = x[...]

        out[...] += matmul(a[0], w[0])

    return steps(
        kernel, count, rows,
        [fixed((rows, D)), turns(parts.shape), unit_from(first)], fixed((rows, D)), shaped((rows, D), F32), [],
        stream, parts, units,
    )


def hidden_layer(stream, gain, units, first):
    rows = stream.shape[0]
    bend, rate = 0.044715, math.sqrt(2.0 / math.pi)

    def kernel(x, g, w, normed, out, slope):
        @pl.when(pl.program_id(0) == 0)
        def _():
            normed[...] = layer_norm(x[...], g[0]).astype(BF)

        for start in range(0, rows, 128):
            at = pl.ds(start, 128)
            z = matmul(normed[at], w[0])
            square = z * z
            flat = jnp.tanh(rate * z * (1.0 + bend * square))
            out[0, at] = (0.5 * z * (1.0 + flat)).astype(BF)
            slope[0, at] = (
                0.5 * (1.0 + flat) + 0.5 * z * (1.0 - flat * flat) * rate * (1.0 + 3.0 * bend * square)
            ).astype(BF)

    whole = (4, rows, D)
    return steps(
        kernel, 4, rows,
        [fixed((rows, D)), gain_at(gain[1]), unit_from(first)],
        [fixed((rows, D)), turns(whole), turns(whole)],
        [shaped((rows, D), BF), shaped(whole, BF), shaped(whole, BF)], [],
        stream, gain[0], units,
    )


def norm_only(stream, gain):
    def kernel(x, g, out):
        out[...] = layer_norm(x[...], g[0]).astype(BF)

    return steps(
        kernel, 1, 8, [fixed(stream.shape), gain_at(gain[1])], fixed(stream.shape), shaped(stream.shape, BF), [],
        stream, gain[0],
    )


def norm_only_back(grad, stream, gain):
    shape = stream.shape

    def kernel(d, x, g, out, low, gain_out):
        out[...], gain_out[...] = norm_back(x[...], g[0], d[...])
        low[...] = out[...].astype(BF)

    return steps(
        kernel, 1, 8, [fixed(shape), fixed(shape), gain_at(gain[1])],
        [fixed(shape), fixed(shape), fixed((1, D))],
        [shaped(shape, F32), shaped(shape, BF), shaped((1, D), F32)], [],
        grad, stream, gain[0],
    )


def project_back(parts, units, first, stream, gain, grad):
    count, rows, _ = parts.shape
    shape = (rows, D)

    def kernel(d, w, x, g, above, out, low, gain_out, total):
        @pl.when(pl.program_id(0) == 0)
        def _():
            total[...] = jnp.zeros_like(total)

        total[...] += against(d[0], w[0])

        @pl.when(pl.program_id(0) == count - 1)
        def _():
            part, gain_out[...] = norm_back(x[...], g[0], total[...])
            out[...] = above[...] + part
            low[...] = out[...].astype(BF)

    return steps(
        kernel, count, rows,
        [turns(parts.shape), unit_from(first), fixed(shape), gain_at(gain[1]), fixed(shape)],
        [fixed(shape), fixed(shape), fixed((1, D))],
        [shaped(shape, F32), shaped(shape, BF), shaped((1, D), F32)], [pltpu.VMEM(shape, F32)],
        parts, units, stream, gain[0], grad,
    )


def products_back(parts, units, first):
    count, rows, _ = parts.shape
    shape = (rows, D)

    def kernel(d, w, out):
        @pl.when(pl.program_id(0) == 0)
        def _():
            out[...] = jnp.zeros_like(out)

        out[...] += against(d[0], w[0])

    return steps(
        kernel, count, rows, [turns(parts.shape), unit_from(first)], fixed(shape), shaped(shape, F32), [],
        parts, units,
    )


def mix_back(low, units, first):
    rows = low.shape[0]

    def kernel(d, w, out):
        out[...] = against(d[...], w[0]).astype(BF)

    return steps(
        kernel, 1, rows, [fixed((rows, D)), unit_from(first)], fixed((rows, D)), shaped((rows, D), BF), [],
        low, units,
    )


def hidden_back(low, slope, units, up_first, down_units, down_first, stream, gain, grad):
    rows = low.shape[0]
    shape = (rows, D)

    def kernel(d, s, up, down, x, g, above, hidden, out, out_low, gain_out, total):
        @pl.when(pl.program_id(0) == 0)
        def _():
            total[...] = jnp.zeros_like(total)

        hidden[0] = (against(d[...], down[0]) * s[0].astype(F32)).astype(BF)
        total[...] += against(hidden[0], up[0])

        @pl.when(pl.program_id(0) == 3)
        def _():
            part, gain_out[...] = norm_back(x[...], g[0], total[...])
            out[...] = above[...] + part
            out_low[...] = out[...].astype(BF)

    return steps(
        kernel, 4, 2 * rows,
        [fixed(shape), turns(slope.shape), unit_from(up_first), unit_from(down_first),
         fixed(shape), gain_at(gain[1]), fixed(shape)],
        [turns(slope.shape), fixed(shape), fixed(shape), fixed((1, D))],
        [shaped(slope.shape, BF), shaped(shape, F32), shaped(shape, BF), shaped((1, D), F32)],
        [pltpu.VMEM(shape, F32)],
        low, slope, units, down_units, stream, gain[0], grad,
    )


PAIR = 2 * HEAD
PAIRS = 4


def head_lanes(value, head):
    lane = lax.broadcasted_iota(jnp.int32, value.shape, 1)
    return jnp.where(lane // HEAD == head, value, jnp.zeros_like(value))


def head_shares(query, key, labels, head):
    scores = against(head_lanes(query, head), key) * HEAD ** (-0.5)
    if labels is None:
        row = lax.broadcasted_iota(jnp.int32, scores.shape, 0)
        visible = lax.broadcasted_iota(jnp.int32, scores.shape, 1) <= row
    else:
        visible = labels[0][...] == labels[1][...]
    scores = jnp.where(visible, scores, MASKED)
    weights = jnp.exp(scores - jnp.max(scores, axis=-1, keepdims=True))
    return weights / jnp.sum(weights, axis=-1, keepdims=True)


def attention_specs(blocks, parts, labels):
    def one(array, place):
        return pl.BlockSpec((1, array.shape[1] // blocks, PAIRS * PAIR), lambda b, h: (place, b, h))

    marks = [] if labels is None else [fixed(label.shape) for label in labels]
    return (blocks, D // (PAIRS * PAIR)), [one(*part) for part in parts], marks


def pair_columns(count, rows, blocks):
    return pl.BlockSpec((count, rows // blocks, PAIRS * PAIR), lambda b, h: (0, b, h))


def attention(parts, blocks, labels):
    grid, specs, marks = attention_specs(blocks, parts, labels)
    rows = parts[0][0].shape[1]

    def kernel(q, k, v, *rest):
        seen, out = (rest[:-1] or None), rest[-1]
        for pair in range(PAIRS):
            at = pl.ds(pair * PAIR, PAIR)
            query, key, value = q[0, :, at], k[0, :, at], v[0, :, at]
            total = 0.0
            for head in range(2):
                shares = head_shares(query, key, seen, head).astype(BF)
                total = total + matmul(shares, head_lanes(value, head))
            out[0, :, at] = total.astype(BF)

    return pl.pallas_call(
        kernel,
        grid=grid,
        in_specs=[*specs, *marks],
        out_specs=pair_columns(1, rows, blocks),
        out_shape=shaped((1, rows, D), BF),
        compiler_params=pltpu.CompilerParams(vmem_limit_bytes=LOCAL),
    )(*[array for array, _ in parts], *(labels or ()))


def attention_back(parts, grad, blocks, labels):
    grid, specs, marks = attention_specs(blocks, parts, labels)
    rows, keys = parts[0][0].shape[1], parts[1][0].shape[1]
    counts = [(3, rows)] if rows == keys else [(1, rows), (2, keys)]

    def kernel(q, k, v, d, *rest):
        seen, outs = (rest[: -len(counts)] or None), rest[-len(counts) :]
        places = [(out, i) for out in outs for i in range(out.shape[0])]
        for pair in range(PAIRS):
            at = pl.ds(pair * PAIR, PAIR)
            query, key, value, grads = q[0, :, at], k[0, :, at], v[0, :, at], d[:, at]
            grad_query = grad_key = grad_value = 0.0
            for head in range(2):
                shares = head_shares(query, key, seen, head)
                above = head_lanes(grads, head)
                grad_shares = against(above, value)
                inner = jnp.sum(shares * grad_shares, axis=-1, keepdims=True)
                grad_scores = (shares * (grad_shares - inner)).astype(BF)
                grad_query = grad_query + matmul(grad_scores, head_lanes(key, head))
                grad_key = grad_key + across(grad_scores, head_lanes(query, head))
                grad_value = grad_value + across(shares.astype(BF), above)
            results = (grad_query * HEAD ** (-0.5), grad_key * HEAD ** (-0.5), grad_value)
            for (out, i), result in zip(places, results):
                out[i, :, at] = result.astype(BF)

    return pl.pallas_call(
        kernel,
        grid=grid,
        in_specs=[*specs, pl.BlockSpec((rows // blocks, PAIRS * PAIR), lambda b, h: (b, h)), *marks],
        out_specs=[pair_columns(count, length, blocks) for count, length in counts],
        out_shape=[shaped((count, length, D), BF) for count, length in counts],
        compiler_params=pltpu.CompilerParams(vmem_limit_bytes=LOCAL),
    )(*[array for array, _ in parts], grad, *(labels or ()))


def layer_forward(stream, units, first, down_units, down, gains, blocks, labels, memory, cross_labels):
    stored = {"stream": stream}
    stored["normed"], qkv = project(stream, gains[0], units, first, 3)
    stored["self"] = [(qkv, i) for i in range(3)]
    stored["attended"] = attention(stored["self"], blocks, labels)
    stream = add_products(stream, stored["attended"], units, first + 3)
    last = first + 4
    if memory is not None:
        stored["after_self"] = stream
        stored["cross_in"], cross_query = project(stream, gains[1], units, first + 4, 1)
        memory_kv = products(memory, units, first + 5, 2)
        stored["cross"] = [(cross_query, 0), (memory_kv, 0), (memory_kv, 1)]
        stored["cross_mixed"] = attention(stored["cross"], 1, cross_labels)
        stream = add_products(stream, stored["cross_mixed"], units, first + 7)
        last = first + 8
    stored["before_ffn"] = stream
    stored["ffn_in"], stored["hidden"], stored["slope"] = hidden_layer(stream, gains[-2], units, last)
    stream = add_products(stream, stored["hidden"], down_units, down)
    stored["before_final"] = stream
    return norm_only(stream, gains[-1]), stored


def layer_backward(
    grad_final, units, first, down_units, down, gains, blocks, labels, stored, memory, cross_labels
):
    gain_grads = [None] * len(gains)
    last = first + (4 if memory is None else 8)
    grad, ffn_low, gain_grads[-1] = norm_only_back(grad_final, stored["before_final"], gains[-1])
    hidden_grads, grad, low, gain_grads[-2] = hidden_back(
        ffn_low, stored["slope"], units, last, down_units, down, stored["before_ffn"], gains[-2], grad
    )
    cross_inputs, cross_grads, memory_grads = [], [], []
    grad_memory = None
    if memory is not None:
        grad_query, grad_memory_kv = attention_back(
            stored["cross"], mix_back(low, units, first + 7), 1, cross_labels
        )
        cross_inputs = [stored["cross_in"][None], stored["cross_mixed"]]
        cross_grads = [grad_query, low[None]]
        memory_grads = [grad_memory_kv]
        grad_memory = products_back(grad_memory_kv, units, first + 5)
        grad, low, gain_grads[1] = project_back(
            grad_query, units, first + 4, stored["after_self"], gains[1], grad
        )
    (grads,) = attention_back(stored["self"], mix_back(low, units, first + 3), blocks, labels)
    inputs = [stored["normed"][None], stored["attended"], *cross_inputs, stored["ffn_in"][None], stored["hidden"]]
    outputs = [grads, low[None], *cross_grads, hidden_grads, ffn_low[None]]
    grad, _, gain_grads[0] = project_back(grads, units, first, stored["stream"], gains[0], grad)
    parts = (inputs, outputs) if memory is None else (inputs, outputs, memory_grads)
    return grad, grad_memory, gain_grads, parts


def adam_step(weight, moment_one, second, gradient, rate):
    moment_one = BETA_ONE * moment_one + (1.0 - BETA_ONE) * gradient
    second = BETA_TWO * second + (1.0 - BETA_TWO) * gradient * gradient
    first_hat = moment_one / (1.0 - BETA_ONE**STEP)
    second_hat = second / (1.0 - BETA_TWO**STEP)
    weight = weight - rate * (first_hat / (jnp.sqrt(second_hat) + ADAM_EPS) + WEIGHT_DECAY * weight)
    return (weight, moment_one, second)


def column_units(matrix):
    return matrix.reshape(matrix.shape[0], -1, D).transpose(1, 0, 2)


def from_column_units(units):
    return units.transpose(1, 0, 2).reshape(units.shape[1], -1)


def hidden_units(matrix, devices):
    rows, width = matrix.shape
    return (
        matrix.reshape(rows, devices, 4, width // devices // 4)
        .transpose(2, 0, 1, 3)
        .reshape(4, rows, width // 4)
    )


def from_hidden_units(units, devices):
    quarters, rows, width = units.shape
    return (
        units.reshape(quarters, rows, devices, width // devices)
        .transpose(1, 2, 0, 3)
        .reshape(rows, quarters * width)
    )


def on_device(
    text_ids,
    text_segments,
    codes,
    caption_of,
    mix_in,
    mix_out,
    ffn_up,
    ffn_down,
    norm_gains,
    text_table,
    code_table,
    mix_in_first,
    mix_out_first,
    ffn_up_first,
    ffn_down_first,
    gains_first,
    text_first,
    code_first,
    mix_in_second,
    mix_out_second,
    ffn_up_second,
    ffn_down_second,
    gains_second,
    text_second,
    code_second,
):
    image_count = codes.shape[0]
    dp_size, fsdp_size = lax.axis_size("dp"), lax.axis_size("fsdp")
    devices = dp_size * fsdp_size
    me = lax.axis_index("dp") * fsdp_size + lax.axis_index("fsdp")
    token_total = image_count * IMG_LEN * devices
    inverse = 1.0 / token_total
    scale_in = math.sqrt(D)
    rows = mix_in.shape[1]
    segments = text_segments[0]
    text_labels = (segments[:, None], segments[None, :])
    cross_labels = (jnp.repeat(caption_of, IMG_LEN)[:, None], segments[None, :])

    small = tiles(jnp.concatenate([text_ids[0].astype(F32), norm_gains.reshape(-1)]), 1)[0]
    before = jnp.pad(codes[:, :-1], ((0, 0), (1, 0)), constant_values=-1).reshape(-1)
    code_full, units, text_rows, small, image_rows = spread(
        code_table, (mix_in, mix_out, ffn_up, ffn_down), text_table, small, before, 4
    )
    small = small.reshape(devices, 1024)[:, : TXT_LEN + 7 * norm_gains.shape[1]]
    all_ids = small[:, :TXT_LEN].astype(jnp.int32).reshape(-1)
    gains = small[:, TXT_LEN:].reshape(devices, 7, -1).transpose(1, 0, 2).reshape(7, 1, D)
    gains = gains.astype(BF).astype(F32)
    base = me * text_table.shape[0]
    owned = (all_ids[:, None] - base == jnp.arange(text_table.shape[0])[None, :]).astype(BF)
    last = ffn_down[1].reshape(4, rows, D).astype(BF)
    last = lax.optimization_barrier((last, text_rows))[0]
    down_units = lax.all_gather(last, AXES, axis=1, tiled=True)
    text_in = text_rows * scale_in + positions(TXT_LEN, D)
    enc_gains = [(gains, i) for i in range(3)]
    dec_gains = [(gains, i) for i in range(3, 7)]
    memory, enc_stored = layer_forward(text_in, units, 0, units, 8, enc_gains, 1, text_labels, None, None)

    image_in = image_rows.reshape(image_count, IMG_LEN, D) * scale_in + positions(IMG_LEN, D)[None]
    image_in = image_in.reshape(-1, D)
    final_out, dec_stored = layer_forward(
        image_in, units, 12, down_units, 0, dec_gains, image_count, None, memory, cross_labels
    )

    targets = codes.reshape(-1)
    logits = against(final_out, code_full)
    hit = targets[:, None] == jnp.arange(VOCAB)[None, :]
    top = jnp.max(logits, axis=1, keepdims=True)
    log_total = top + jnp.log(jnp.sum(jnp.exp(logits - top), axis=1, keepdims=True))
    weighted = jnp.sum(
        logits * jnp.where(hit, 1.0 - SMOOTH + SMOOTH / VOCAB, SMOOTH / VOCAB), axis=1, keepdims=True
    )
    loss_part = jnp.sum(log_total - weighted)
    grad_logits = (
        (jnp.exp(logits - log_total) - jnp.where(hit, 1.0 - SMOOTH, 0.0) - SMOOTH / VOCAB) * inverse
    ).astype(BF)
    grad_final = matmul(grad_logits, code_full)

    grad_image, grad_memory, dec_gain_grads, dec_parts = layer_backward(
        grad_final, units, 12, down_units, 0, dec_gains, image_count, None, dec_stored, memory, cross_labels
    )
    grad_text, _, enc_gain_grads, enc_parts = layer_backward(
        grad_memory, units, 0, units, 8, enc_gains, 1, text_labels, enc_stored, None, None
    )
    gain_part = jnp.concatenate(enc_gain_grads + dec_gain_grads)

    grad_rows = lax.all_gather((grad_text * scale_in).astype(BF), AXES, axis=0, tiled=True)
    text_grad = across(owned, grad_rows)

    grad_looked = grad_image.reshape(image_count, IMG_LEN, D)[:, 1:] * scale_in
    grad_looked = jnp.pad(grad_looked, ((0, 0), (0, 1), (0, 0))).reshape(-1, D).astype(BF)
    enc_x, enc_g = enc_parts
    dec_x, dec_g, memory_g = dec_parts
    sums = sum_products(
        dec_x, dec_g, [memory[None]] + enc_x, memory_g + enc_g, grad_logits, targets, final_out, grad_looked, 1
    )
    gain_blocks = gain_part.reshape(7, devices, rows).transpose(1, 0, 2).reshape(devices, 7 * rows)
    gain_blocks = jnp.concatenate([gain_blocks, jnp.full((devices, 1), loss_part)], axis=1)
    gain_blocks = jnp.pad(gain_blocks, ((0, 0), (0, 1024 - gain_blocks.shape[1])))
    gain_blocks = gain_blocks.reshape(devices, 8, 128)
    params = (mix_in, mix_out, ffn_up, ffn_down, norm_gains, text_table, code_table)
    firsts = (
        mix_in_first,
        mix_out_first,
        ffn_up_first,
        ffn_down_first,
        gains_first,
        text_first,
        code_first,
    )
    seconds = (
        mix_in_second,
        mix_out_second,
        ffn_up_second,
        ffn_down_second,
        gains_second,
        text_second,
        code_second,
    )
    if rows == 32:
        loss_sum, grad_norm, updated = update(sums, text_grad, gain_blocks, params, firsts, seconds, 6)
    else:
        small_sum = jnp.sum(exchange(gain_blocks, 5), axis=0).reshape(-1)
        loss_sum = small_sum[7 * rows]
        gains_grad = small_sum[: 7 * rows].reshape(7, rows)
        dec_sum, enc_sum = sums[:14], sums[14:28]
        gradients = (
            jnp.stack(
                [
                    from_column_units(part)
                    for part in (enc_sum[2:5], dec_sum[:3], jnp.concatenate([dec_sum[4:5], enc_sum[:2]]))
                ]
            ),
            jnp.stack([enc_sum[5], dec_sum[3], dec_sum[5]]),
            jnp.stack([from_hidden_units(part, devices) for part in (enc_sum[6:10], dec_sum[6:10])]),
            jnp.stack([part.reshape(-1, D) for part in (enc_sum[10:], dec_sum[10:])]),
            gains_grad,
            text_grad,
            sums[28:].reshape(D // dp_size, -1).T,
        )
        square_part = sum((jnp.sum(gradient * gradient) for gradient in gradients))
        squares = exchange(tiles(square_part[None], devices), 6)[:, 0, 0]
        grad_norm = jnp.sqrt(jnp.sum(squares))
        factor = CLIP_NORM / jnp.maximum(grad_norm, CLIP_NORM)
        updated = [
            adam_step(
                params[index],
                firsts[index],
                seconds[index],
                gradients[index] * factor,
                STEP_RATES[index],
            )
            for index in range(7)
        ]
    return (
        loss_sum,
        grad_norm,
        updated[0][0],
        updated[1][0],
        updated[2][0],
        updated[3][0],
        updated[4][0],
        updated[5][0],
        updated[6][0],
        updated[0][1],
        updated[1][1],
        updated[2][1],
        updated[3][1],
        updated[4][1],
        updated[5][1],
        updated[6][1],
        updated[0][2],
        updated[1][2],
        updated[2][2],
        updated[3][2],
        updated[4][2],
        updated[5][2],
        updated[6][2],
    )


def solution(mesh):
    return jax.shard_map(
        on_device,
        mesh=mesh,
        in_specs=(
            P(("dp", "fsdp"), None),
            P(("dp", "fsdp"), None),
            P(("dp", "fsdp"), None),
            P(("dp", "fsdp")),
            P(None, ("dp", "fsdp"), None),
            P(None, ("dp", "fsdp"), None),
            P(None, ("dp", "fsdp"), None),
            P(None, ("dp", "fsdp"), None),
            P(None, ("dp", "fsdp")),
            P(("dp", "fsdp"), None),
            P("fsdp", "dp"),
            P(None, ("dp", "fsdp"), None),
            P(None, ("dp", "fsdp"), None),
            P(None, ("dp", "fsdp"), None),
            P(None, ("dp", "fsdp"), None),
            P(None, ("dp", "fsdp")),
            P(("dp", "fsdp"), None),
            P("fsdp", "dp"),
            P(None, ("dp", "fsdp"), None),
            P(None, ("dp", "fsdp"), None),
            P(None, ("dp", "fsdp"), None),
            P(None, ("dp", "fsdp"), None),
            P(None, ("dp", "fsdp")),
            P(("dp", "fsdp"), None),
            P("fsdp", "dp"),
        ),
        out_specs=(
            P(),
            P(),
            P(None, ("dp", "fsdp"), None),
            P(None, ("dp", "fsdp"), None),
            P(None, ("dp", "fsdp"), None),
            P(None, ("dp", "fsdp"), None),
            P(None, ("dp", "fsdp")),
            P(("dp", "fsdp"), None),
            P("fsdp", "dp"),
            P(None, ("dp", "fsdp"), None),
            P(None, ("dp", "fsdp"), None),
            P(None, ("dp", "fsdp"), None),
            P(None, ("dp", "fsdp"), None),
            P(None, ("dp", "fsdp")),
            P(("dp", "fsdp"), None),
            P("fsdp", "dp"),
            P(None, ("dp", "fsdp"), None),
            P(None, ("dp", "fsdp"), None),
            P(None, ("dp", "fsdp"), None),
            P(None, ("dp", "fsdp"), None),
            P(None, ("dp", "fsdp")),
            P(("dp", "fsdp"), None),
            P("fsdp", "dp"),
        ),
        check_vma=False,
    )
```

```python
from functools import partial
import math

import jax
import jax.numpy as jnp
from jax import lax
from jax.experimental import pallas as pl
from jax.experimental.pallas import tpu as pltpu
from jax.sharding import PartitionSpec as P

D = 1024
HEADS = 16
HEAD = 64
VOCAB = 8192
TVOC = 16000
IMG_LEN = 256
TXT_LEN = 128
STEP = 5


SMOOTH = 0.1
BETA_ONE = 0.5
BETA_TWO = 0.5
WEIGHT_DECAY = 0.1
ADAM_EPS = 1e-08
CLIP_NORM = 0.02
MASKED = -1e30
STEP_RATES = (0.02, 0.15, 0.02, 0.01, 0.3, 0.02, 0.03)

BF = jnp.bfloat16
F32 = jnp.float32
AXES = ("dp", "fsdp")
MESH = pl.DeviceIdType.MESH
LAG = 2


DEC_INPUTS = (0, 0, 0, 1, 2, 3, 4, 4, 4, 4, 5, 6, 7, 8)
ENC_INPUTS = (0, 0, 1, 1, 1, 2, 3, 3, 3, 3, 4, 5, 6, 7)
CODE_UNITS = 8


def place_of(Z):
    dp, fs = lax.axis_index("dp"), lax.axis_index("fsdp")
    z, core = fs // 2, fs % 2
    x_mate, y_mate = dp + 1 - 2 * (dp % 2), (dp + 2) % 4
    devices = ((dp, fs + 1 - 2 * core), (x_mate, fs), (y_mate, fs), (dp, fs + 2), (dp, fs - 2))
    return dp, z, core, x_mate, y_mate, (x_mate + 2) % 4, devices, z < Z - 1, z > 0


def add(a, b):
    return (a.astype(F32) + b.astype(F32)).astype(BF)


def remote(src, dst, send, recv, device):
    return pltpu.make_async_remote_copy(
        src_ref=src, dst_ref=dst, send_sem=send, recv_sem=recv, device_id=device, device_id_type=MESH
    )


def sum_scratch(Z, m, n):
    depth, half = 2 * LAG, Z // 2
    own_slots, held_slots, kept_slots = LAG + 1, 2 * LAG + 1, Z * LAG + 1
    return [
        pltpu.VMEM((own_slots, 4, Z, m, n), BF),
        pltpu.VMEM((depth, 4, Z, m, n), BF),
        pltpu.VMEM((held_slots, 4, Z, m, n), BF),
        pltpu.VMEM((depth, half, m, n), BF),
        pltpu.VMEM((depth, Z - half, m, n), BF),
        pltpu.VMEM((depth, Z, m, n), BF),
        pltpu.VMEM((depth, Z, m, n), BF),
        pltpu.VMEM((kept_slots, Z, m, n), BF),
        pltpu.VMEM((2, Z - 1, depth, m, n), BF),
    ]


def sum_semaphores(Z):
    depth, dma = 2 * LAG, pltpu.SemaphoreType.DMA
    return [
        dma((depth,)),
        dma((depth,)),
        dma((2, depth)),
        dma((2, depth)),
        dma((2, depth)),
        dma((2, depth)),
        dma((2, Z - 1, depth)),
        dma((2, Z - 1, depth)),
    ]


def sum_stages(Z, scratch, semaphores, arrive, out_ref):
    own, from_core, held, from_x, from_y, all_x, all_y, kept, from_line = scratch
    _, _, one_send, one_recv, two_send, two_recv, line_send, line_recv = semaphores
    dp, z, core, x_mate, y_mate, across_dp, devices, has_up, has_down = place_of(Z)
    _, x_dev, y_dev, up_dev, down_dev = devices
    depth, half = 2 * LAG, Z // 2
    own_slots, held_slots, kept_slots = own.shape[0], held.shape[0], kept.shape[0]

    def one_copies(k):
        s, block = k % depth, held.at[k % held_slots, across_dp]
        return (
            remote(block.at[pl.ds(0, half)], from_x.at[s], one_send.at[0, s], one_recv.at[0, s], x_dev),
            remote(block.at[pl.ds(half, Z - half)], from_y.at[s], one_send.at[1, s], one_recv.at[1, s], y_dev),
        )

    def two_copies(k):
        s, h = k % depth, k % held_slots
        return (
            remote(held.at[h, x_mate], all_x.at[s], two_send.at[0, s], two_recv.at[0, s], x_dev),
            remote(held.at[h, y_mate], all_y.at[s], two_send.at[1, s], two_recv.at[1, s], y_dev),
        )

    def up_block(step):
        return jnp.minimum(z + Z - step, Z - 1)

    def down_block(step):
        return jnp.maximum(z - Z + step, 0)

    def up_copy(k, step):
        s = k % depth
        return remote(
            kept.at[k % kept_slots, up_block(step)], from_line.at[0, step - 1, s],
            line_send.at[0, step - 1, s], line_recv.at[0, step - 1, s], up_dev,
        )

    def down_copy(k, step):
        s = k % depth
        return remote(
            kept.at[k % kept_slots, down_block(step)], from_line.at[1, step - 1, s],
            line_send.at[1, step - 1, s], line_recv.at[1, step - 1, s], down_dev,
        )

    def line_start(k, step):
        @pl.when(has_up)
        def _():
            up_copy(k, step).start()

        @pl.when(has_down)
        def _():
            down_copy(k, step).start()

    def line_wait(k, step):
        @pl.when(has_down)
        def _():
            up_copy(k, step).wait_recv()
            down_copy(k, step).wait_send()

        @pl.when(has_up)
        def _():
            down_copy(k, step).wait_recv()
            up_copy(k, step).wait_send()

    def after_core(k):
        arrive(k)

        def one(block, carry):
            for q in range(Z):
                held[k % held_slots, block, q] = add(
                    own[k % own_slots, block, q], from_core[k % depth, block, q]
                )
            return carry

        lax.fori_loop(0, 4, one, 0)
        for copy in one_copies(k):
            copy.start()

    def after_one(k):
        s, h = k % depth, k % held_slots
        for copy in one_copies(k):
            copy.wait()
        for q in range(half):
            held[h, y_mate, q] = add(held[h, y_mate, q], from_x[s, q])
        for q in range(Z - half):
            held[h, x_mate, half + q] = add(held[h, x_mate, half + q], from_y[s, q])
        for copy in two_copies(k):
            copy.start()

    def after_two(k):
        s, h = k % depth, k % held_slots
        for copy in two_copies(k):
            copy.wait()
        for q in range(Z):
            kept[k % kept_slots, q] = (
                held[h, dp, q].astype(F32) + all_x[s, q].astype(F32) + all_y[s, q].astype(F32)
            ).astype(BF)
        line_start(k, 1)

    def along_line(step):
        def run(k):
            s, h = k % depth, k % kept_slots
            line_wait(k, step - 1)

            @pl.when(has_down & (z + Z - step <= Z - 1))
            def _():
                kept[h, up_block(step)] = add(kept[h, up_block(step)], from_line[0, step - 2, s])

            @pl.when(has_up & (z - Z + step >= 0))
            def _():
                kept[h, down_block(step)] = add(kept[h, down_block(step)], from_line[1, step - 2, s])

            line_start(k, step)

        return run

    def finish(k):
        s = k % depth
        line_wait(k, Z - 1)
        out_ref[k] = kept[k % kept_slots, z].astype(F32)

        @pl.when(has_down)
        def _():
            out_ref[k] = out_ref[k] + from_line[0, Z - 2, s].astype(F32)

        @pl.when(has_up)
        def _():
            out_ref[k] = out_ref[k] + from_line[1, Z - 2, s].astype(F32)

    stages = [after_core, after_one, after_two]
    return stages + [along_line(step) for step in range(2, Z)] + [finish], up_block, down_block


def sum_kernel(Z, counts, *refs):
    groups = []
    for count in counts:
        groups.append([ref.at[i] for ref in refs[:count] for i in range(ref.shape[0])])
        refs = refs[count:]
    dec_x, dec_g, enc_x, enc_g = groups
    (
        code_x, targets, code_g, look_g, out_ref,
        dec_xs, dec_gs, dec_turned, enc_xs, enc_gs, enc_turned, code_xs, code_loaded, code_gs, to_core,
        own, from_core, held, from_x, from_y, all_x, all_y, kept, from_line,
        rare_held, rare_line, rare_kept, rare_x, rare_y, rare_all_x, rare_all_y,
        load_sem, code_sem, core_send, core_recv, one_send, one_recv, two_send, two_recv, line_send, line_recv,
        rare_line_send, rare_line_recv, rare_send, rare_recv,
    ) = refs
    dec_units, enc_units = len(DEC_INPUTS), len(ENC_INPUTS)
    plain_units = dec_units + enc_units
    units = plain_units + CODE_UNITS
    depth = 2 * LAG
    dp, fs = lax.axis_index("dp"), lax.axis_index("fsdp")
    z, core = fs // 2, fs % 2
    x_mate, y_mate = dp + 1 - 2 * (dp % 2), (dp + 2) % 4
    across_dp = (x_mate + 2) % 4
    core_dev, x_dev, y_dev = (dp, fs + 1 - 2 * core), (x_mate, fs), (y_mate, fs)
    up_dev, down_dev = (dp, fs + 2), (dp, fs - 2)
    has_up, has_down = z < Z - 1, z > 0

    barrier = pltpu.get_barrier_semaphore()
    for device in (core_dev, x_dev, y_dev):
        pl.semaphore_signal(barrier, inc=1, device_id=device, device_id_type=MESH)

    @pl.when(has_up)
    def _():
        pl.semaphore_signal(barrier, inc=1, device_id=up_dev, device_id_type=MESH)

    @pl.when(has_down)
    def _():
        pl.semaphore_signal(barrier, inc=1, device_id=down_dev, device_id_type=MESH)

    pl.semaphore_wait(barrier, 3 + has_up.astype(jnp.int32) + has_down.astype(jnp.int32))
    scratch = (own, from_core, held, from_x, from_y, all_x, all_y, kept, from_line)
    semaphores = (
        core_send, core_recv, one_send, one_recv, two_send, two_recv, line_send, line_recv
    )
    own_slots = own.shape[0]

    def pair(x, g, xs, gs, slot):
        return (
            pltpu.make_async_copy(x, xs.at[slot], load_sem.at[0, slot]),
            pltpu.make_async_copy(g, gs.at[slot], load_sem.at[1, slot]),
        )

    def start_loads(k):
        for i, place in enumerate(DEC_INPUTS):

            @pl.when(k == i)
            def _(i=i, place=place):
                for copy in pair(dec_x[place], dec_g[min(i, 10)], dec_xs, dec_gs, i % 2):
                    copy.start()

        for i, place in enumerate(ENC_INPUTS):

            @pl.when(k == dec_units + i)
            def _(i=i, place=place):
                for copy in pair(enc_x[place], enc_g[min(i, 10)], enc_xs, enc_gs, (dec_units + i) % 2):
                    copy.start()

    code_rows = code_x.shape[0]
    code_loads = [
        pltpu.make_async_copy(code_x, code_xs.at[pl.ds(0, code_rows)], code_sem.at[0]),
        pltpu.make_async_copy(code_g, code_loaded.at[0], code_sem.at[1]),
        pltpu.make_async_copy(look_g, code_loaded.at[1], code_sem.at[2]),
    ]
    for copy in code_loads:
        copy.start()
    start_loads(jnp.int32(0))

    def core_copy(k):
        s = k % depth
        return remote(
            to_core.at[k % own_slots], from_core.at[s], core_send.at[s], core_recv.at[s], core_dev
        )

    def turn(xs, slot, turned):
        size = 256

        def columns(i, carry):
            part = xs[slot, :, pl.ds(pl.multiple_of(i * size, size), size)].T
            count = size // (2 * turned.shape[2])
            turned[pl.ds(i * count, count)] = part.reshape(count, *turned.shape[1:])
            return carry

        lax.fori_loop(0, xs.shape[2] // size, columns, 0)

    def product(turned, gs, slot, side, into):
        def rows(block, carry):
            value = turned[pl.ds(block * Z, Z), side].reshape(-1, turned.shape[-1])
            result = jnp.dot(value, gs[slot], preferred_element_type=F32).astype(BF)
            into[block] = result.reshape(into.shape[1:])
            return carry

        lax.fori_loop(0, 4, rows, 0)

    def code_inputs():
        for copy in code_loads:
            copy.wait()
        size = D // 4
        for half_rows in range(2):

            def turn_columns(i, carry, half_rows=half_rows):
                part = code_loaded[half_rows, :, pl.ds(pl.multiple_of(i * size, size), size)].T
                code_gs[i, :, :, pl.ds(half_rows * code_rows, code_rows)] = part.reshape(
                    CODE_UNITS, size // CODE_UNITS, code_rows
                )
                return carry

            lax.fori_loop(0, 4, turn_columns, 0)

        width = 512

        def hits(i, carry):
            start = pl.multiple_of(i * width, width)
            column = lax.broadcasted_iota(jnp.int32, (code_rows, width), 1) + i * width
            code_xs[pl.ds(code_rows, code_rows), pl.ds(start, width)] = jnp.where(
                targets[...] == column, 1.0, 0.0
            ).astype(BF)
            return carry

        lax.fori_loop(0, VOCAB // width, hits, 0)

    def code_product(k, side, into):
        value = code_gs[:, k - plain_units].reshape(-1, code_gs.shape[-1])
        width = into.shape[-1]

        def columns(place, carry):
            start = pl.multiple_of((2 * place + side) * width, width)
            result = jnp.dot(value, code_xs[:, pl.ds(start, width)], preferred_element_type=F32).astype(BF)
            into[:, place] = result.reshape(4, -1, width)
            return carry

        lax.fori_loop(0, Z, columns, 0)

    def begin(k):
        slot, o = k % 2, k % own_slots
        for here, x, g, xs, gs, turned in (
            (k < dec_units, dec_x[0], dec_g[0], dec_xs, dec_gs, dec_turned),
            ((k >= dec_units) & (k < plain_units), enc_x[0], enc_g[0], enc_xs, enc_gs, enc_turned),
        ):

            @pl.when(here)
            def _(x=x, g=g, xs=xs, gs=gs, turned=turned):
                for copy in pair(x, g, xs, gs, slot):
                    copy.wait()
                start_loads(k + 1)
                turn(xs, slot, turned)
                product(turned, gs, slot, 1 - core, to_core.at[o])
                core_copy(k).start()
                product(turned, gs, slot, core, own.at[o])

        @pl.when(k == dec_units)
        def _():
            code_inputs()

        @pl.when(k >= plain_units)
        def _():
            code_product(k, 1 - core, to_core.at[o])
            core_copy(k).start()
            code_product(k, core, own.at[o])

    def arrive(k):
        core_copy(k).wait()

    later, up_block, down_block = sum_stages(Z, scratch, semaphores, arrive, out_ref)

    def turn_of(k):
        return (k // 9) * 2 + (k % 9 >= 7).astype(jnp.int32)

    def rare_slot(k):
        return turn_of(k) % rare_held.shape[0]

    def rare_line_copies(k, step):
        t, s = turn_of(k), rare_slot(k)
        return [
            remote(
                rare_held.at[s, :, block], rare_line.at[s, way, step - 1],
                rare_line_send.at[way, step - 1, t], rare_line_recv.at[way, step - 1, t], device,
            )
            for way, block, device in ((0, up_block(step), up_dev), (1, down_block(step), down_dev))
        ]

    def rare_valid(step):
        return (has_up & (z + Z - step <= Z - 1), has_down & (z - Z + step >= 0)), (
            has_down & (z - 1 + Z - step <= Z - 1),
            has_up & (z + 1 - Z + step >= 0),
        )

    def rare_line_start(k, step):
        for copy, sends in zip(rare_line_copies(k, step), rare_valid(step)[0]):
            pl.when(sends)(copy.start)

    def rare_line_wait(k, step):
        for copy, sends, receives in zip(rare_line_copies(k, step), *rare_valid(step)):
            pl.when(sends)(copy.wait_send)
            pl.when(receives)(copy.wait_recv)

    def rare_add(into, k, step):
        for way, receives in enumerate(rare_valid(step)[1]):

            @pl.when(receives)
            def _(way=way):
                for block in range(4):
                    ref = into(way, block)
                    ref[...] = add(ref[...], rare_line[rare_slot(k), way, step - 1, block])

    def rare_square(k, slot):
        t, s = turn_of(k), rare_slot(k)
        small = rare_kept.shape[2] // 2
        source, target, device = (
            (rare_kept.at[s, across_dp, pl.ds(0, small)], rare_x.at[s], x_dev),
            (rare_kept.at[s, across_dp, pl.ds(small, small)], rare_y.at[s], y_dev),
            (rare_kept.at[s, x_mate], rare_all_x.at[s], x_dev),
            (rare_kept.at[s, y_mate], rare_all_y.at[s], y_dev),
        )[slot]
        return remote(source, target, rare_send.at[slot, t], rare_recv.at[slot, t], device)

    def rare_after_core(k):
        core_copy(k).wait()

        def one(block, carry):
            for q in range(Z):
                rare_held[rare_slot(k), block, q] = add(
                    own[k % own_slots, block, q], from_core[k % depth, block, q]
                )
            return carry

        lax.fori_loop(0, 4, one, 0)
        rare_line_start(k, 1)

    def rare_along(step):
        def run(k):
            rare_line_wait(k, step - 1)
            s = rare_slot(k)
            rare_add(
                lambda way, block: rare_held.at[s, block, (up_block, down_block)[way](step)], k, step - 1
            )
            rare_line_start(k, step)

        return run

    def rare_after_line(k):
        rare_line_wait(k, Z - 1)
        s = rare_slot(k)
        for block in range(4):
            rare_kept[s, block] = rare_held[s, block, z]
        rare_add(lambda way, block: rare_kept.at[s, block], k, Z - 1)
        for slot in range(2):
            rare_square(k, slot).start()

    def rare_after_one(k):
        s, small = rare_slot(k), rare_kept.shape[2] // 2
        for slot in range(2):
            rare_square(k, slot).wait()
        first, second = pl.ds(0, small), pl.ds(small, small)
        rare_kept[s, y_mate, first] = add(rare_kept[s, y_mate, first], rare_x[s])
        rare_kept[s, x_mate, second] = add(rare_kept[s, x_mate, second], rare_y[s])
        for slot in range(2, 4):
            rare_square(k, slot).start()

    def rare_finish(k):
        s = rare_slot(k)
        for slot in range(2, 4):
            rare_square(k, slot).wait()
        out_ref[k] = (
            rare_kept[s, dp].astype(F32) + rare_all_x[s].astype(F32) + rare_all_y[s].astype(F32)
        )

    stages = [begin] + later
    rare_stages = [begin, rare_after_core] + [rare_along(step) for step in range(2, Z)]
    rare_stages += [rare_after_line, rare_after_one, rare_finish]

    def loop_step(j, carry):
        for place in reversed(range(len(stages))):
            k = j - place * LAG
            here = (k >= 0) & (k < units)
            rare = (k % 9 == 3) | (k % 9 == 7)
            if place == 0:
                pl.when(here)(partial(begin, k))
            else:
                pl.when(here & jnp.logical_not(rare))(partial(stages[place], k))
                pl.when(here & rare)(partial(rare_stages[place], k))
        return carry

    lax.fori_loop(0, units + (len(stages) - 1) * LAG, loop_step, 0)


def sum_products(dec_x, dec_g, enc_x, enc_g, code_x, targets, code_g, look_g, call_id):
    dp_size, fsdp_size = lax.axis_size("dp"), lax.axis_size("fsdp")
    devices, Z = dp_size * fsdp_size, fsdp_size // 2
    m = D // devices
    stacks = (dec_x, dec_g, enc_x, enc_g)
    if dp_size != 4 or Z != 4 or m % 32:
        dec_x, dec_g, enc_x, enc_g = [[row for stack in group for row in stack] for group in stacks]
        products = [across(dec_x[i], dec_g[min(k, 10)]) for k, i in enumerate(DEC_INPUTS)]
        products += [across(enc_x[i], enc_g[min(k, 10)]) for k, i in enumerate(ENC_INPUTS)]
        plain = jnp.stack(products).astype(BF).reshape(len(products), devices, m, D)
        hit = (targets[:, None] == jnp.arange(VOCAB)[None, :]).astype(BF)
        code = across(jnp.concatenate([code_g, look_g]), jnp.concatenate([code_x, hit])).astype(BF)
        code = code.reshape(dp_size, D // dp_size, fsdp_size, VOCAB // fsdp_size)
        code = code.transpose(0, 2, 1, 3).reshape(devices, D // dp_size, VOCAB // fsdp_size)
        plain = lax.psum_scatter(plain, AXES, scatter_dimension=1, tiled=True)
        code = lax.psum_scatter(code, AXES, scatter_dimension=0, tiled=True)
        return jnp.concatenate([plain.reshape(-1, m, D), code.reshape(-1, m, D)]).astype(F32)
    n, units = D, len(DEC_INPUTS) + len(ENC_INPUTS) + CODE_UNITS
    depth, half = 2 * LAG, Z // 2
    own_slots, held_slots, kept_slots = LAG + 1, 2 * LAG + 1, Z * LAG + 1
    dec_rows, enc_rows, code_rows = dec_x[0].shape[1], enc_x[0].shape[1], code_x.shape[0]
    counts = [len(group) for group in stacks]
    dma = pltpu.SemaphoreType.DMA
    whole = pl.BlockSpec(memory_space=pl.ANY)
    out = pl.pallas_call(
        partial(sum_kernel, Z, counts),
        out_shape=jax.ShapeDtypeStruct((units, m, n), F32),
        in_specs=[whole] * (sum(counts) + 1) + [pl.BlockSpec(memory_space=pltpu.VMEM)] + [whole] * 2,
        out_specs=pl.BlockSpec(memory_space=pltpu.VMEM),
        scratch_shapes=[
            pltpu.VMEM((2, dec_rows, n), BF),
            pltpu.VMEM((2, dec_rows, n), BF),
            pltpu.VMEM((4 * Z, 2, m, dec_rows), BF),
            pltpu.VMEM((2, enc_rows, n), BF),
            pltpu.VMEM((2, enc_rows, n), BF),
            pltpu.VMEM((4 * Z, 2, m, enc_rows), BF),
            pltpu.VMEM((2 * code_rows, VOCAB), BF),
            pltpu.VMEM((2, code_rows, n), BF),
            pltpu.VMEM((4, CODE_UNITS, m, 2 * code_rows), BF),
            pltpu.VMEM((own_slots, 4, Z, m, n), BF),
            pltpu.VMEM((own_slots, 4, Z, m, n), BF),
            pltpu.VMEM((depth, 4, Z, m, n), BF),
            pltpu.VMEM((held_slots, 4, Z, m, n), BF),
            pltpu.VMEM((depth, half, m, n), BF),
            pltpu.VMEM((depth, Z - half, m, n), BF),
            pltpu.VMEM((depth, Z, m, n), BF),
            pltpu.VMEM((depth, Z, m, n), BF),
            pltpu.VMEM((kept_slots, Z, m, n), BF),
            pltpu.VMEM((2, Z - 1, depth, m, n), BF),
            pltpu.VMEM((3, 4, Z, m, n), BF),
            pltpu.VMEM((3, 2, Z - 1, 4, m, n), BF),
            pltpu.VMEM((3, 4, m, n), BF),
            pltpu.VMEM((3, m // 2, n), BF),
            pltpu.VMEM((3, m // 2, n), BF),
            pltpu.VMEM((3, m, n), BF),
            pltpu.VMEM((3, m, n), BF),
            dma((2, 2)),
            dma((3,)),
            dma((depth,)),
            dma((depth,)),
            dma((2, depth)),
            dma((2, depth)),
            dma((2, depth)),
            dma((2, depth)),
            dma((2, Z - 1, depth)),
            dma((2, Z - 1, depth)),
            dma((2, Z - 1, 2 * (units // 9 + 1))),
            dma((2, Z - 1, 2 * (units // 9 + 1))),
            dma((4, 2 * (units // 9 + 1))),
            dma((4, 2 * (units // 9 + 1))),
        ],
        compiler_params=pltpu.CompilerParams(
            collective_id=call_id, has_side_effects=True, vmem_limit_bytes=62 << 20
        ),
    )(*dec_x, *dec_g, *enc_x, *enc_g, code_x, targets[:, None], code_g, look_g)
    return out


def spread_kernel(
    tables, units, Z, token_count, table_f32, mix_in, mix_out, ffn_up, ffn_down, text_table, small, codes,
    table_out, unit_out, text_out, small_all, code_rows,
    table_ref, unit_ref, looked, chunk, chunk_sem, own_sem, line_send, line_recv, square_send, square_recv, core_send, core_recv,
    small_send, small_recv, text_sem, *sum_refs,
):
    dp, fs = lax.axis_index("dp"), lax.axis_index("fsdp")
    z, core = fs // 2, fs % 2
    x_mate, y_mate = dp + 1 - 2 * (dp % 2), (dp + 2) % 4
    across_dp = (x_mate + 2) % 4
    core_dev, x_dev, y_dev = (dp, fs + 1 - 2 * core), (x_mate, fs), (y_mate, fs)
    up_dev, down_dev = (dp, fs + 2), (dp, fs - 2)
    has_up, has_down = z < Z - 1, z > 0
    total, half = tables + units, Z // 2
    every = slice(None)
    table_rows, table_columns = table_out.shape[2] // tables, table_out.shape[3] // 4

    def at(is_table, k, dp_at, z_at, core_at, part=None):
        if is_table:
            size = table_rows if part is None else table_rows // 2
            rows = pl.ds(k * table_rows + (part or 0) * size, size)
            columns = every if isinstance(dp_at, slice) else pl.ds(dp_at * table_columns, table_columns)
            return table_out.at[z_at, core_at, rows, columns]
        if part is None:
            return unit_out.at[k - tables, dp_at, z_at, core_at]
        size = unit_out.shape[4] // 2
        return unit_out.at[k - tables, dp_at, z_at, core_at, pl.ds(part * size, size)]

    def passed(ref, send, recv, device):
        return remote(ref, ref, send, recv, device)

    size, inner = 8 * Z, 2 * Z
    me = dp * inner + fs

    def peer(i):
        other = lax.rem(me + i, size)
        return (other // inner, lax.rem(other, inner))

    def each(run):
        def one(i, carry):
            run(i)
            return carry

        lax.fori_loop(1, size, one, 0)

    def small_copy(i):
        return remote(small, small_all.at[me], small_send.at[i], small_recv.at[i], peer(i))

    barrier = pltpu.get_barrier_semaphore()
    each(lambda i: pl.semaphore_signal(barrier, inc=1, device_id=peer(i), device_id_type=MESH))
    small_all[me] = small[...]

    rows = unit_ref.shape[1]
    place = 0

    def put(value):
        nonlocal place
        unit_ref[place] = value.astype(BF)
        place += 1

    def put_ffn(layer, with_down):
        turned = [
            swap_groups([ffn_up[layer, :, pl.ds(128 * (4 * g + j), 128)] for j in range(4)]) for g in range(8)
        ]
        for q in range(4):
            put(jnp.concatenate([parts[q] for parts in turned], axis=1))
        for q in range(4 if with_down else 0):
            put(ffn_down[layer, pl.ds(q * rows, rows), :])

    for layer in range(3):
        for i in range(3):
            put(mix_in[layer, :, pl.ds(i * D, D)])
        put(mix_out[layer])
        if layer != 1:
            put_ffn(min(layer, 1), layer == 0)
    table_ref[...] = table_f32[...].astype(BF)

    own = (
        pltpu.make_async_copy(
            table_ref, table_out.at[z, core, :, pl.ds(dp * table_columns, table_columns)], own_sem.at[0]
        ),
        pltpu.make_async_copy(unit_ref, unit_out.at[:, dp, z, core], own_sem.at[1]),
    )
    for copy in own:
        copy.start()

    for copy in own:
        copy.wait()
    pl.semaphore_wait(barrier, size - 1)
    each(lambda i: small_copy(i).start())

    def line_copies(view, k, step):
        s = step - 1
        return (
            (passed(view(jnp.maximum(z - s, 0)), line_send.at[0, s, k], line_recv.at[0, s, k], up_dev),
             has_up & (z >= s), has_down & (z >= s + 1)),
            (passed(view(jnp.minimum(z + s, Z - 1)), line_send.at[1, s, k], line_recv.at[1, s, k], down_dev),
             has_down & (z + s <= Z - 1), has_up & (z + s + 1 <= Z - 1)),
        )

    def line_start(view, k, step):
        for copy, sends, _ in line_copies(view, k, step):
            pl.when(sends)(copy.start)

    def line_wait(view, k, step):
        for copy, sends, receives in line_copies(view, k, step):
            pl.when(sends)(copy.wait_send)
            pl.when(receives)(copy.wait_recv)

    def to_core(ref, k, slot):
        return passed(ref, core_send.at[slot, k], core_recv.at[slot, k], core_dev)

    def square_copy(ref, k, slot):
        return passed(
            ref, square_send.at[slot, k], square_recv.at[slot, k], x_dev if slot % 2 == 0 else y_dev
        )

    def line_first(is_table):
        def view(k):
            return lambda place: at(is_table, k, dp, place, core)

        def row(k, dp_at):
            return at(is_table, k, dp_at, every, core)

        def ones(k):
            return square_copy(row(k, dp), k, 0), square_copy(row(k, dp), k, 1)

        def twos(k):
            return (
                square_copy(at(is_table, k, y_mate, pl.ds(0, half), core), k, 2),
                square_copy(at(is_table, k, x_mate, pl.ds(half, Z - half), core), k, 3),
            )

        def line(step):
            def run(k):
                if step > 1:
                    line_wait(view(k), k, step - 1)
                if step < Z:
                    line_start(view(k), k, step)
                else:
                    for copy in ones(k):
                        copy.start()
                    to_core(row(k, dp), k, 0).start()
            return run

        def after_one(k):
            for copy in ones(k):
                copy.wait()
            for copy in twos(k):
                copy.start()
            to_core(row(k, x_mate), k, 1).start()
            to_core(row(k, y_mate), k, 2).start()

        def after_two(k):
            for copy in twos(k):
                copy.wait()
            to_core(row(k, across_dp), k, 3).start()

        def finish(k):
            for slot in range(4):
                to_core(row(k, dp), k, slot).wait()

        return [line(step) for step in range(1, Z + 1)] + [after_one, after_two, finish]

    def square_first(is_table):
        def plane(k):
            return lambda place: at(is_table, k, every, place, core)

        def ones(k):
            ref = at(is_table, k, dp, z, core)
            return square_copy(ref, k, 0), square_copy(ref, k, 1)

        def twos(k):
            return (
                square_copy(at(is_table, k, y_mate, z, core, 0), k, 2),
                square_copy(at(is_table, k, x_mate, z, core, 1), k, 3),
            )

        def begin(k):
            for copy in ones(k):
                copy.start()

        def after_one(k):
            for copy in ones(k):
                copy.wait()
            for copy in twos(k):
                copy.start()

        def after_two(k):
            for copy in twos(k):
                copy.wait()
            line_start(plane(k), k, 1)
            to_core(plane(k)(z), k, z).start()

        def line(step):
            def run(k):
                line_wait(plane(k), k, step)
                if step + 1 < Z:
                    line_start(plane(k), k, step + 1)

                @pl.when(z - step >= 0)
                def _():
                    to_core(plane(k)(jnp.maximum(z - step, 0)), k, jnp.maximum(z - step, 0)).start()

                @pl.when(z + step <= Z - 1)
                def _():
                    to_core(plane(k)(jnp.minimum(z + step, Z - 1)), k, jnp.minimum(z + step, Z - 1)).start()
            return run

        def finish(k):
            for place in range(Z):
                to_core(plane(k)(place), k, place).wait()

        return [begin, after_one, after_two] + [line(step) for step in range(1, Z)] + [finish]

    forms = [(is_table, first, form(is_table))
             for is_table in (True, False) for first, form in ((True, line_first), (False, square_first))]
    n_stages = Z + 3

    scratch, semaphores = sum_refs[:9], sum_refs[9:]
    own_slots, depth = scratch[0].shape[0], scratch[1].shape[0]

    small_turn, look_ups = 9, 8
    text_first = small_turn + look_ups

    def look_up(part):
        owned_rows = text_table.shape[0]
        base = me * token_count

        def of_device(i, carry):
            device = part * (size // look_ups) + i
            ids = small_all[device].T[:, :1]
            row = lax.broadcasted_iota(jnp.int32, (ids.shape[0], owned_rows), 1)
            hit = (row + base == ids.astype(jnp.int32)) & (row < token_count)
            found = matmul(jnp.where(hit, 1.0, 0.0).astype(BF), text_table[...]).astype(BF)
            dp_at, line_at, core_at = device // inner, lax.rem(device, inner) // 2, lax.rem(device, 2)
            for u in range(looked.shape[0]):
                looked[u, dp_at, line_at, core_at] = found[u * rows : (u + 1) * rows]
            return carry

        lax.fori_loop(0, size // look_ups, of_device, 0)

    def text_own(k):
        return pltpu.make_async_copy(
            looked.at[k, :, :, core], scratch[0].at[k % own_slots], text_sem.at[k % own_slots]
        )

    def text_core(k):
        s = k % depth
        return remote(
            looked.at[k, :, :, 1 - core], scratch[1].at[s], semaphores[0].at[s], semaphores[1].at[s], core_dev
        )

    def text_begin(k):
        text_own(k).start()
        text_core(k).start()

    def text_arrive(k):
        text_own(k).wait()
        text_core(k).wait()

    text_stages = [text_begin] + sum_stages(Z, scratch, semaphores, text_arrive, text_out)[0]

    code_first = (n_stages - 1) * LAG + 1

    def chunk_copy(k):
        source = table_out.at[:, :, pl.ds(k * table_rows, table_rows), :]
        return pltpu.make_async_copy(source, chunk.at[k % 2], chunk_sem.at[k % 2])

    def find_codes(k):
        chunk_copy(k).wait()
        pl.when(k + 1 < tables)(lambda: chunk_copy(k + 1).start())
        place = lax.broadcasted_iota(jnp.int32, (codes.shape[0], inner * table_rows), 1)
        code = (place // table_rows) * table_out.shape[2] + k * table_rows + place % table_rows
        hit = jnp.where(codes[...] == code, 1.0, 0.0).astype(BF)
        code_rows[...] += matmul(hit, chunk[k % 2].reshape(-1, chunk.shape[-1]))

    code_rows[...] = jnp.zeros_like(code_rows)

    def loop_step(j, carry):
        @pl.when(j == small_turn)
        def _():
            each(lambda i: small_copy(i).wait())

        pl.when((j >= small_turn) & (j < text_first))(lambda: look_up(j - small_turn))
        for place in reversed(range(n_stages)):
            k = j - place * LAG
            turn = k - text_first
            pl.when((turn >= 0) & (turn < looked.shape[0]))(partial(text_stages[place], turn))
            turn = k % 9
            by_line = (turn != 3) & (turn != 7)
            for is_table, first, stages in forms:
                here = (k >= 0) & (k < tables) if is_table else (k >= tables) & (k < total)
                here = here & (by_line if first else jnp.logical_not(by_line))

                @pl.when(here)
                def _(k=k, run=stages[place]):
                    run(k)

        found = j - code_first

        @pl.when(found == -1)
        def _():
            chunk_copy(0).start()

        pl.when((found >= 0) & (found < tables))(lambda: find_codes(found))
        return carry

    lax.fori_loop(0, total + (n_stages - 1) * LAG, loop_step, 0)


def spread(table, weights, text_table, small, codes, call_id):
    mix_in, mix_out, ffn_up, ffn_down = weights
    dp_size, fsdp_size = lax.axis_size("dp"), lax.axis_size("fsdp")
    m, Z = mix_in.shape[1], fsdp_size // 2
    if dp_size != 4 or Z != 4 or m != 32:
        shards = []
        for layer in range(3):
            shards += [column_units(mix_in[layer]), mix_out[layer][None]]
            if layer != 1:
                which = min(layer, 1)
                shards += [hidden_units(ffn_up[which], dp_size * fsdp_size)]
            if layer == 0:
                shards += [ffn_down[0].reshape(4, m, D)]
        table = lax.all_gather(table.astype(BF), "dp", axis=1, tiled=True)
        whole = lax.all_gather(table, "fsdp", axis=0, tiled=True)
        units = lax.all_gather(jnp.concatenate(shards).astype(BF), AXES, axis=1, tiled=True)
        devices, count = dp_size * fsdp_size, text_table.shape[0]
        small_all = exchange(jnp.broadcast_to(small[None], (devices, 8, 128)), 3)
        ids = small_all[:, 0].astype(jnp.int32).reshape(-1)
        base = (lax.axis_index("dp") * fsdp_size + lax.axis_index("fsdp")) * count
        owned = (ids[:, None] - base == jnp.arange(count)[None, :]).astype(BF)
        looked = matmul(owned, text_table.astype(BF)).astype(BF)
        text = lax.psum_scatter(looked, AXES, scatter_dimension=0, tiled=True).astype(F32)
        found = jnp.where(codes[:, None] >= 0, whole[jnp.maximum(codes, 0)].astype(F32), 0.0)
        return whole, units, text, small_all, found
    text_units, token_count = TXT_LEN // m, text_table.shape[0]
    text_table = jnp.pad(text_table.astype(BF), ((0, -token_count % 128), (0, 0)))
    tables, count, dma = 8, 24, pltpu.SemaphoreType.DMA
    total = tables + count
    whole, units, text, small_all, found = pl.pallas_call(
        partial(spread_kernel, tables, count, Z, token_count),
        out_shape=(
            jax.ShapeDtypeStruct((Z, 2, table.shape[0], 4 * table.shape[1]), BF),
            jax.ShapeDtypeStruct((count, 4, Z, 2, m, D), BF),
            jax.ShapeDtypeStruct((text_units, m, D), F32),
            jax.ShapeDtypeStruct((8 * Z, *small.shape), F32),
            jax.ShapeDtypeStruct((codes.shape[0], D), F32),
        ),
        in_specs=[pl.BlockSpec(memory_space=pltpu.VMEM)] * 8,
        out_specs=[pl.BlockSpec(memory_space=pl.ANY)] * 2 + [pl.BlockSpec(memory_space=pltpu.VMEM)] * 3,
        scratch_shapes=[
            pltpu.VMEM(table.shape, BF),
            pltpu.VMEM((count, m, D), BF),
            pltpu.VMEM((text_units, 4, Z, 2, m, D), BF),
            pltpu.VMEM((2, Z, 2, table.shape[0] // tables, D), BF),
            dma((2,)),
            dma((2,)),
            dma((2, Z - 1, total)),
            dma((2, Z - 1, total)),
            dma((4, total)),
            dma((4, total)),
            dma((4, total)),
            dma((4, total)),
            dma((8 * Z,)),
            dma((8 * Z,)),
            dma((LAG + 1,)),
            *sum_scratch(Z, m, D),
            *sum_semaphores(Z),
        ],
        compiler_params=pltpu.CompilerParams(
            collective_id=call_id, has_side_effects=True, vmem_limit_bytes=48 << 20
        ),
    )(table, *weights, text_table, small, codes[:, None])
    whole, units = whole.reshape(-1, 4 * table.shape[1]), units.reshape(count, -1, D)
    return whole, units, text.reshape(-1, D), small_all, found


def exchange_kernel(size, inner, in_ref, out_ref, send_sem, recv_sem):
    me = lax.axis_index("dp") * inner + lax.axis_index("fsdp")

    def peer(i):
        other = lax.rem(me + i, size)
        return other, (other // inner, lax.rem(other, inner))

    barrier = pltpu.get_barrier_semaphore()

    def greet(i, carry):
        pl.semaphore_signal(barrier, inc=1, device_id=peer(i)[1], device_id_type=MESH)
        return carry

    def copy(i):
        other, device = peer(i)
        return pltpu.make_async_remote_copy(
            src_ref=in_ref.at[other], dst_ref=out_ref.at[me], send_sem=send_sem.at[i],
            recv_sem=recv_sem.at[i], device_id=device, device_id_type=MESH,
        )

    def begin(i, carry):
        copy(i).start()
        return carry

    def end(i, carry):
        copy(i).wait()
        return carry

    lax.fori_loop(1, size, greet, 0)
    out_ref[me] = in_ref[me]
    pl.semaphore_wait(barrier, size - 1)
    lax.fori_loop(1, size, begin, 0)
    lax.fori_loop(1, size, end, 0)


def exchange(blocks, call_id):
    size, inner = blocks.shape[0], lax.axis_size("fsdp")
    return pl.pallas_call(
        partial(exchange_kernel, size, inner),
        out_shape=jax.ShapeDtypeStruct(blocks.shape, F32),
        in_specs=[pl.BlockSpec(memory_space=pltpu.VMEM)],
        out_specs=pl.BlockSpec(memory_space=pltpu.VMEM),
        scratch_shapes=[pltpu.SemaphoreType.DMA((size,)), pltpu.SemaphoreType.DMA((size,))],
        compiler_params=pltpu.CompilerParams(collective_id=call_id, has_side_effects=True),
    )(blocks)


def tiles(values, count):
    padded = jnp.pad(values, ((0, 1024 - values.shape[0]),)).reshape(1, 8, 128)
    return jnp.broadcast_to(padded, (count, 8, 128))


def swap_groups(parts):
    group = lax.broadcasted_iota(jnp.int32, parts[0].shape, 1) // 32
    results = []
    for i in range(4):
        total = parts[i]
        for j in range(4):
            if j != i:
                turned = pltpu.roll(parts[j], (32 * (j - i)) % 128, 1)
                total = jnp.where(group == j, turned, total)
        results.append(total)
    return results


def norm_kernel(
    size, inner, count, sums, text, small, small_out, norm_out,
    squares, small_all, squares_all, sum_scratch, small_send, small_recv, square_send, square_recv,
):
    rows = sums.shape[1]
    text_rows = [(start, min(rows, text.shape[0] - start)) for start in range(0, text.shape[0], rows)]
    me = lax.axis_index("dp") * inner + lax.axis_index("fsdp")

    def peer(i):
        other = lax.rem(me + i, size)
        return other, (other // inner, lax.rem(other, inner))

    def small_copy(i):
        other, device = peer(i)
        return remote(small.at[other], small_all.at[me], small_send.at[i], small_recv.at[i], device)

    def square_copy(i):
        return remote(squares, squares_all.at[me], square_send.at[i], square_recv.at[i], peer(i)[1])

    def each(run):
        def one(i, carry):
            run(i)
            return carry

        lax.fori_loop(1, size, one, 0)

    barrier = pltpu.get_barrier_semaphore()
    each(lambda i: pl.semaphore_signal(barrier, inc=1, device_id=peer(i)[1], device_id_type=MESH))
    small_all[me] = small[me]
    pl.semaphore_wait(barrier, size - 1)
    each(lambda i: small_copy(i).start())

    sum_scratch[...] = jnp.zeros_like(sum_scratch)

    def square(k, carry):
        sum_scratch[...] += sums[k] * sums[k]
        return carry

    lax.fori_loop(0, sums.shape[0], square, 0)
    for start, length in text_rows:
        part = text[pl.ds(start, length), :]
        sum_scratch[pl.ds(0, length), :] += part * part

    each(lambda i: small_copy(i).wait())
    total = lax.fori_loop(0, size, lambda i, total: total + small_all[i], jnp.zeros_like(squares))
    small_out[...] = total
    place = lax.broadcasted_iota(jnp.int32, total.shape, 0) * 128 + lax.broadcasted_iota(jnp.int32, total.shape, 1)
    gains = jnp.where(place < count, total, 0.0)
    squares[...] = jnp.full(squares.shape, jnp.sum(sum_scratch[...]) + jnp.sum(gains * gains))

    squares_all[me] = squares[...]
    each(lambda i: square_copy(i).start())
    each(lambda i: square_copy(i).wait())
    norm_out[...] = jnp.sqrt(
        lax.fori_loop(0, size, lambda i, total: total + squares_all[i], jnp.zeros_like(squares))
    )


def update_kernel(*refs):
    norm, plain, text, gains, *refs = refs
    weights, refs = refs[:7], refs[7:]
    firsts, refs = refs[:7], refs[7:]
    seconds, refs = refs[:7], refs[7:]
    new_weights, refs = refs[:7], refs[7:]
    new_firsts, new_seconds = refs[:7], refs[7:]
    rows = plain.shape[1]
    text_rows = [(start, min(rows, text.shape[0] - start)) for start in range(0, text.shape[0], rows)]
    factor = (CLIP_NORM / jnp.maximum(norm[...], CLIP_NORM))[:1, :1]

    def step(which, place, gradient):
        updated = adam_step(
            weights[which][place], firsts[which][place], seconds[which][place],
            gradient * factor, STEP_RATES[which],
        )
        for out, value in zip((new_weights, new_firsts, new_seconds), updated):
            out[which][place] = value

    enc = len(DEC_INPUTS)
    every = slice(None)
    for layer, units in enumerate(((enc + 2, enc + 3, enc + 4), (0, 1, 2), (4, enc, enc + 1))):
        for i, unit in enumerate(units):
            step(0, (layer, every, pl.ds(i * D, D)), plain[unit])
    for layer, unit in enumerate((enc + 5, 3, 5)):
        step(1, (layer,), plain[unit])
    for layer, first in enumerate((enc + 6, 6)):
        for g in range(8):
            parts = [plain[first + q, :, pl.ds(128 * g, 128)] for q in range(4)]
            for j, part in enumerate(swap_groups(parts)):
                step(2, (layer, every, pl.ds(128 * (4 * g + j), 128)), part)
    for layer, first in enumerate((enc + 10, 10)):
        for q in range(4):
            step(3, (layer, pl.ds(q * rows, rows), every), plain[first + q])
    step(4, (every, every), gains[...])
    for start, count in text_rows:
        step(5, (pl.ds(start, count), every), text[pl.ds(start, count), :])
    columns, first = 256, len(DEC_INPUTS) + len(ENC_INPUTS)
    for i in range(D // columns):
        part = plain[pl.ds(first, CODE_UNITS), :, pl.ds(i * columns, columns)]
        step(6, (pl.ds(i * columns, columns), every), part.reshape(-1, columns).T)


def update(sums, text, small, weights, firsts, seconds, call_id):
    inner = lax.axis_size("fsdp")
    size = lax.axis_size("dp") * inner
    shapes = [jax.ShapeDtypeStruct(weight.shape, F32) for weight in weights]
    gains_shape = weights[4].shape
    count = gains_shape[0] * gains_shape[1]
    in_vmem = pl.BlockSpec(memory_space=pltpu.VMEM)
    dma, tile = pltpu.SemaphoreType.DMA, jax.ShapeDtypeStruct((8, 128), F32)
    small, norm = pl.pallas_call(
        partial(norm_kernel, size, inner, count),
        out_shape=[tile, tile],
        in_specs=[in_vmem] * 3,
        out_specs=[in_vmem] * 2,
        scratch_shapes=[
            pltpu.VMEM((8, 128), F32),
            pltpu.VMEM((size, 8, 128), F32),
            pltpu.VMEM((size, 8, 128), F32),
            pltpu.VMEM(sums.shape[1:], F32),
            dma((size,)),
            dma((size,)),
            dma((size,)),
            dma((size,)),
        ],
        compiler_params=pltpu.CompilerParams(
            collective_id=call_id, has_side_effects=True, vmem_limit_bytes=32 << 20
        ),
    )(sums, text, small)
    small = small.reshape(-1)
    outs = pl.pallas_call(
        update_kernel,
        out_shape=shapes * 3,
        in_specs=[in_vmem] * 25,
        out_specs=[in_vmem] * 21,
        compiler_params=pltpu.CompilerParams(vmem_limit_bytes=60 << 20),
    )(norm, sums, text, small[:count].reshape(gains_shape), *weights, *firsts, *seconds)
    return small[count], norm[0, 0], list(zip(outs[:7], outs[7:14], outs[14:]))


def layer_norm(stream, gain):
    centred = stream - jnp.mean(stream, axis=-1, keepdims=True)
    return centred * lax.rsqrt(jnp.mean(centred * centred, axis=-1, keepdims=True) + 1e-05) * gain


def norm_back(stream, gain, grad_out):
    centred = stream - jnp.mean(stream, axis=-1, keepdims=True)
    inverse = lax.rsqrt(jnp.mean(centred * centred, axis=-1, keepdims=True) + 1e-05)
    plain = centred * inverse
    scaled = grad_out * gain
    inner = jnp.mean(scaled * plain, axis=-1, keepdims=True)
    grad = inverse * (scaled - jnp.mean(scaled, axis=-1, keepdims=True) - plain * inner)
    return grad, jnp.sum(grad_out * plain, axis=0, keepdims=True)


def positions(length, width):
    position = jnp.arange(length, dtype=jnp.float32)[:, None]
    speeds = jnp.exp(
        -math.log(10000.0) * 2.0 * jnp.arange(width // 2, dtype=jnp.float32)[None, :] / width
    )
    return jnp.concatenate([jnp.sin(position * speeds), jnp.cos(position * speeds)], axis=1)


def matmul(first_op, second_op):
    return jnp.dot(first_op, second_op, preferred_element_type=jnp.float32)


def across(first_op, second_op):
    return lax.dot_general(
        first_op, second_op, (((0,), (0,)), ((), ())), preferred_element_type=jnp.float32
    )


def against(first_op, second_op):
    return lax.dot_general(
        first_op, second_op, (((1,), (1,)), ((), ())), preferred_element_type=jnp.float32
    )


LOCAL = 56 << 20


def gain_at(i):
    return pl.BlockSpec((1, 1, D), lambda *_: (i, 0, 0))


def fixed(shape):
    return pl.BlockSpec(shape, lambda *_: (0,) * len(shape))


def turns(shape):
    return pl.BlockSpec((1, *shape[1:]), lambda i: (i,) + (0,) * (len(shape) - 1))


def unit_from(first):
    return pl.BlockSpec((1, D, D), lambda i: (first + i, 0, 0))


def cost(rows, count):
    return pl.CostEstimate(flops=2 * rows * D * D * count, bytes_accessed=2 * D * D * count + 8 * rows * D, transcendentals=0)


def steps(kernel, count, rows, in_specs, out_specs, out_shape, scratch, *args):
    return pl.pallas_call(
        kernel,
        grid=(count,),
        in_specs=in_specs,
        out_specs=out_specs,
        out_shape=out_shape,
        scratch_shapes=scratch,
        cost_estimate=cost(rows, count),
        compiler_params=pltpu.CompilerParams(vmem_limit_bytes=LOCAL),
    )(*args)


def shaped(shape, kind):
    return jax.ShapeDtypeStruct(shape, kind)


def project(stream, gain, units, first, count):
    rows = stream.shape[0]

    def kernel(x, g, w, normed, out):
        @pl.when(pl.program_id(0) == 0)
        def _():
            normed[...] = layer_norm(x[...], g[0]).astype(BF)

        out[0] = matmul(normed[...], w[0]).astype(BF)

    whole = (count, rows, D)
    return steps(
        kernel, count, rows,
        [fixed((rows, D)), gain_at(gain[1]), unit_from(first)],
        [fixed((rows, D)), turns(whole)],
        [shaped((rows, D), BF), shaped(whole, BF)], [],
        stream, gain[0], units,
    )


def products(value, units, first, count):
    rows = value.shape[0]

    def kernel(x, w, out):
        out[0] = matmul(x[...], w[0]).astype(BF)

    whole = (count, rows, D)
    return steps(
        kernel, count, rows, [fixed((rows, D)), unit_from(first)], turns(whole), shaped(whole, BF), [],
        value, units,
    )


def add_products(stream, parts, units, first):
    count, rows, _ = parts.shape

    def kernel(x, a, w, out):
        @pl.when(pl.program_id(0) == 0)
        def _():
            out[...] = x[...]

        out[...] += matmul(a[0], w[0])

    return steps(
        kernel, count, rows,
        [fixed((rows, D)), turns(parts.shape), unit_from(first)], fixed((rows, D)), shaped((rows, D), F32), [],
        stream, parts, units,
    )


def hidden_layer(stream, gain, units, first):
    rows = stream.shape[0]
    bend, rate = 0.044715, math.sqrt(2.0 / math.pi)

    def kernel(x, g, w, normed, out, slope):
        @pl.when(pl.program_id(0) == 0)
        def _():
            normed[...] = layer_norm(x[...], g[0]).astype(BF)

        for start in range(0, rows, 128):
            at = pl.ds(start, 128)
            z = matmul(normed[at], w[0])
            square = z * z
            flat = jnp.tanh(rate * z * (1.0 + bend * square))
            out[0, at] = (0.5 * z * (1.0 + flat)).astype(BF)
            slope[0, at] = (
                0.5 * (1.0 + flat) + 0.5 * z * (1.0 - flat * flat) * rate * (1.0 + 3.0 * bend * square)
            ).astype(BF)

    whole = (4, rows, D)
    return steps(
        kernel, 4, rows,
        [fixed((rows, D)), gain_at(gain[1]), unit_from(first)],
        [fixed((rows, D)), turns(whole), turns(whole)],
        [shaped((rows, D), BF), shaped(whole, BF), shaped(whole, BF)], [],
        stream, gain[0], units,
    )


def norm_only(stream, gain):
    def kernel(x, g, out):
        out[...] = layer_norm(x[...], g[0]).astype(BF)

    return steps(
        kernel, 1, 8, [fixed(stream.shape), gain_at(gain[1])], fixed(stream.shape), shaped(stream.shape, BF), [],
        stream, gain[0],
    )


def norm_only_back(grad, stream, gain):
    shape = stream.shape

    def kernel(d, x, g, out, low, gain_out):
        out[...], gain_out[...] = norm_back(x[...], g[0], d[...])
        low[...] = out[...].astype(BF)

    return steps(
        kernel, 1, 8, [fixed(shape), fixed(shape), gain_at(gain[1])],
        [fixed(shape), fixed(shape), fixed((1, D))],
        [shaped(shape, F32), shaped(shape, BF), shaped((1, D), F32)], [],
        grad, stream, gain[0],
    )


def project_back(parts, units, first, stream, gain, grad):
    count, rows, _ = parts.shape
    shape = (rows, D)

    def kernel(d, w, x, g, above, out, low, gain_out, total):
        @pl.when(pl.program_id(0) == 0)
        def _():
            total[...] = jnp.zeros_like(total)

        total[...] += against(d[0], w[0])

        @pl.when(pl.program_id(0) == count - 1)
        def _():
            part, gain_out[...] = norm_back(x[...], g[0], total[...])
            out[...] = above[...] + part
            low[...] = out[...].astype(BF)

    return steps(
        kernel, count, rows,
        [turns(parts.shape), unit_from(first), fixed(shape), gain_at(gain[1]), fixed(shape)],
        [fixed(shape), fixed(shape), fixed((1, D))],
        [shaped(shape, F32), shaped(shape, BF), shaped((1, D), F32)], [pltpu.VMEM(shape, F32)],
        parts, units, stream, gain[0], grad,
    )


def products_back(parts, units, first):
    count, rows, _ = parts.shape
    shape = (rows, D)

    def kernel(d, w, out):
        @pl.when(pl.program_id(0) == 0)
        def _():
            out[...] = jnp.zeros_like(out)

        out[...] += against(d[0], w[0])

    return steps(
        kernel, count, rows, [turns(parts.shape), unit_from(first)], fixed(shape), shaped(shape, F32), [],
        parts, units,
    )


def mix_back(low, units, first):
    rows = low.shape[0]

    def kernel(d, w, out):
        out[...] = against(d[...], w[0]).astype(BF)

    return steps(
        kernel, 1, rows, [fixed((rows, D)), unit_from(first)], fixed((rows, D)), shaped((rows, D), BF), [],
        low, units,
    )


def hidden_back(low, slope, units, up_first, down_units, down_first, stream, gain, grad):
    rows = low.shape[0]
    shape = (rows, D)

    def kernel(d, s, up, down, x, g, above, hidden, out, out_low, gain_out, total):
        @pl.when(pl.program_id(0) == 0)
        def _():
            total[...] = jnp.zeros_like(total)

        hidden[0] = (against(d[...], down[0]) * s[0].astype(F32)).astype(BF)
        total[...] += against(hidden[0], up[0])

        @pl.when(pl.program_id(0) == 3)
        def _():
            part, gain_out[...] = norm_back(x[...], g[0], total[...])
            out[...] = above[...] + part
            out_low[...] = out[...].astype(BF)

    return steps(
        kernel, 4, 2 * rows,
        [fixed(shape), turns(slope.shape), unit_from(up_first), unit_from(down_first),
         fixed(shape), gain_at(gain[1]), fixed(shape)],
        [turns(slope.shape), fixed(shape), fixed(shape), fixed((1, D))],
        [shaped(slope.shape, BF), shaped(shape, F32), shaped(shape, BF), shaped((1, D), F32)],
        [pltpu.VMEM(shape, F32)],
        low, slope, units, down_units, stream, gain[0], grad,
    )


PAIR = 2 * HEAD
PAIRS = 4


def head_lanes(value, head):
    lane = lax.broadcasted_iota(jnp.int32, value.shape, 1)
    return jnp.where(lane // HEAD == head, value, jnp.zeros_like(value))


def head_shares(query, key, labels, head):
    scores = against(head_lanes(query, head), key) * HEAD ** (-0.5)
    if labels is None:
        row = lax.broadcasted_iota(jnp.int32, scores.shape, 0)
        visible = lax.broadcasted_iota(jnp.int32, scores.shape, 1) <= row
    else:
        visible = labels[0][...] == labels[1][...]
    scores = jnp.where(visible, scores, MASKED)
    weights = jnp.exp(scores - jnp.max(scores, axis=-1, keepdims=True))
    return weights / jnp.sum(weights, axis=-1, keepdims=True)


def attention_specs(blocks, parts, labels):
    def one(array, place):
        return pl.BlockSpec((1, array.shape[1] // blocks, PAIRS * PAIR), lambda b, h: (place, b, h))

    marks = [] if labels is None else [fixed(label.shape) for label in labels]
    return (blocks, D // (PAIRS * PAIR)), [one(*part) for part in parts], marks


def pair_columns(count, rows, blocks):
    return pl.BlockSpec((count, rows // blocks, PAIRS * PAIR), lambda b, h: (0, b, h))


def attention(parts, blocks, labels):
    grid, specs, marks = attention_specs(blocks, parts, labels)
    rows = parts[0][0].shape[1]

    def kernel(q, k, v, *rest):
        seen, out = (rest[:-1] or None), rest[-1]
        for pair in range(PAIRS):
            at = pl.ds(pair * PAIR, PAIR)
            query, key, value = q[0, :, at], k[0, :, at], v[0, :, at]
            total = 0.0
            for head in range(2):
                shares = head_shares(query, key, seen, head).astype(BF)
                total = total + matmul(shares, head_lanes(value, head))
            out[0, :, at] = total.astype(BF)

    return pl.pallas_call(
        kernel,
        grid=grid,
        in_specs=[*specs, *marks],
        out_specs=pair_columns(1, rows, blocks),
        out_shape=shaped((1, rows, D), BF),
        compiler_params=pltpu.CompilerParams(vmem_limit_bytes=LOCAL),
    )(*[array for array, _ in parts], *(labels or ()))


def attention_back(parts, grad, blocks, labels):
    grid, specs, marks = attention_specs(blocks, parts, labels)
    rows, keys = parts[0][0].shape[1], parts[1][0].shape[1]
    counts = [(3, rows)] if rows == keys else [(1, rows), (2, keys)]

    def kernel(q, k, v, d, *rest):
        seen, outs = (rest[: -len(counts)] or None), rest[-len(counts) :]
        places = [(out, i) for out in outs for i in range(out.shape[0])]
        for pair in range(PAIRS):
            at = pl.ds(pair * PAIR, PAIR)
            query, key, value, grads = q[0, :, at], k[0, :, at], v[0, :, at], d[:, at]
            grad_query = grad_key = grad_value = 0.0
            for head in range(2):
                shares = head_shares(query, key, seen, head)
                above = head_lanes(grads, head)
                grad_shares = against(above, value)
                inner = jnp.sum(shares * grad_shares, axis=-1, keepdims=True)
                grad_scores = (shares * (grad_shares - inner)).astype(BF)
                grad_query = grad_query + matmul(grad_scores, head_lanes(key, head))
                grad_key = grad_key + across(grad_scores, head_lanes(query, head))
                grad_value = grad_value + across(shares.astype(BF), above)
            results = (grad_query * HEAD ** (-0.5), grad_key * HEAD ** (-0.5), grad_value)
            for (out, i), result in zip(places, results):
                out[i, :, at] = result.astype(BF)

    return pl.pallas_call(
        kernel,
        grid=grid,
        in_specs=[*specs, pl.BlockSpec((rows // blocks, PAIRS * PAIR), lambda b, h: (b, h)), *marks],
        out_specs=[pair_columns(count, length, blocks) for count, length in counts],
        out_shape=[shaped((count, length, D), BF) for count, length in counts],
        compiler_params=pltpu.CompilerParams(vmem_limit_bytes=LOCAL),
    )(*[array for array, _ in parts], grad, *(labels or ()))


def layer_forward(stream, units, first, down_units, down, gains, blocks, labels, memory, cross_labels):
    stored = {"stream": stream}
    stored["normed"], qkv = project(stream, gains[0], units, first, 3)
    stored["self"] = [(qkv, i) for i in range(3)]
    stored["attended"] = attention(stored["self"], blocks, labels)
    stream = add_products(stream, stored["attended"], units, first + 3)
    last = first + 4
    if memory is not None:
        stored["after_self"] = stream
        stored["cross_in"], cross_query = project(stream, gains[1], units, first + 4, 1)
        memory_kv = products(memory, units, first + 5, 2)
        stored["cross"] = [(cross_query, 0), (memory_kv, 0), (memory_kv, 1)]
        stored["cross_mixed"] = attention(stored["cross"], 1, cross_labels)
        stream = add_products(stream, stored["cross_mixed"], units, first + 7)
        last = first + 8
    stored["before_ffn"] = stream
    stored["ffn_in"], stored["hidden"], stored["slope"] = hidden_layer(stream, gains[-2], units, last)
    stream = add_products(stream, stored["hidden"], down_units, down)
    stored["before_final"] = stream
    return norm_only(stream, gains[-1]), stored


def layer_backward(
    grad_final, units, first, down_units, down, gains, blocks, labels, stored, memory, cross_labels
):
    gain_grads = [None] * len(gains)
    last = first + (4 if memory is None else 8)
    grad, ffn_low, gain_grads[-1] = norm_only_back(grad_final, stored["before_final"], gains[-1])
    hidden_grads, grad, low, gain_grads[-2] = hidden_back(
        ffn_low, stored["slope"], units, last, down_units, down, stored["before_ffn"], gains[-2], grad
    )
    cross_inputs, cross_grads, memory_grads = [], [], []
    grad_memory = None
    if memory is not None:
        grad_query, grad_memory_kv = attention_back(
            stored["cross"], mix_back(low, units, first + 7), 1, cross_labels
        )
        cross_inputs = [stored["cross_in"][None], stored["cross_mixed"]]
        cross_grads = [grad_query, low[None]]
        memory_grads = [grad_memory_kv]
        grad_memory = products_back(grad_memory_kv, units, first + 5)
        grad, low, gain_grads[1] = project_back(
            grad_query, units, first + 4, stored["after_self"], gains[1], grad
        )
    (grads,) = attention_back(stored["self"], mix_back(low, units, first + 3), blocks, labels)
    inputs = [stored["normed"][None], stored["attended"], *cross_inputs, stored["ffn_in"][None], stored["hidden"]]
    outputs = [grads, low[None], *cross_grads, hidden_grads, ffn_low[None]]
    grad, _, gain_grads[0] = project_back(grads, units, first, stored["stream"], gains[0], grad)
    parts = (inputs, outputs) if memory is None else (inputs, outputs, memory_grads)
    return grad, grad_memory, gain_grads, parts


def adam_step(weight, moment_one, second, gradient, rate):
    moment_one = BETA_ONE * moment_one + (1.0 - BETA_ONE) * gradient
    second = BETA_TWO * second + (1.0 - BETA_TWO) * gradient * gradient
    first_hat = moment_one / (1.0 - BETA_ONE**STEP)
    second_hat = second / (1.0 - BETA_TWO**STEP)
    weight = weight - rate * (first_hat / (jnp.sqrt(second_hat) + ADAM_EPS) + WEIGHT_DECAY * weight)
    return (weight, moment_one, second)


def column_units(matrix):
    return matrix.reshape(matrix.shape[0], -1, D).transpose(1, 0, 2)


def from_column_units(units):
    return units.transpose(1, 0, 2).reshape(units.shape[1], -1)


def hidden_units(matrix, devices):
    rows, width = matrix.shape
    return (
        matrix.reshape(rows, devices, 4, width // devices // 4)
        .transpose(2, 0, 1, 3)
        .reshape(4, rows, width // 4)
    )


def from_hidden_units(units, devices):
    quarters, rows, width = units.shape
    return (
        units.reshape(quarters, rows, devices, width // devices)
        .transpose(1, 2, 0, 3)
        .reshape(rows, quarters * width)
    )


def on_device(
    text_ids,
    text_segments,
    codes,
    caption_of,
    mix_in,
    mix_out,
    ffn_up,
    ffn_down,
    norm_gains,
    text_table,
    code_table,
    mix_in_first,
    mix_out_first,
    ffn_up_first,
    ffn_down_first,
    gains_first,
    text_first,
    code_first,
    mix_in_second,
    mix_out_second,
    ffn_up_second,
    ffn_down_second,
    gains_second,
    text_second,
    code_second,
):
    image_count = codes.shape[0]
    dp_size, fsdp_size = lax.axis_size("dp"), lax.axis_size("fsdp")
    devices = dp_size * fsdp_size
    me = lax.axis_index("dp") * fsdp_size + lax.axis_index("fsdp")
    token_total = image_count * IMG_LEN * devices
    inverse = 1.0 / token_total
    scale_in = math.sqrt(D)
    rows = mix_in.shape[1]
    segments = text_segments[0]
    text_labels = (segments[:, None], segments[None, :])
    cross_labels = (jnp.repeat(caption_of, IMG_LEN)[:, None], segments[None, :])

    small = tiles(jnp.concatenate([text_ids[0].astype(F32), norm_gains.reshape(-1)]), 1)[0]
    before = jnp.pad(codes[:, :-1], ((0, 0), (1, 0)), constant_values=-1).reshape(-1)
    code_full, units, text_rows, small, image_rows = spread(
        code_table, (mix_in, mix_out, ffn_up, ffn_down), text_table, small, before, 4
    )
    small = small.reshape(devices, 1024)[:, : TXT_LEN + 7 * norm_gains.shape[1]]
    all_ids = small[:, :TXT_LEN].astype(jnp.int32).reshape(-1)
    gains = small[:, TXT_LEN:].reshape(devices, 7, -1).transpose(1, 0, 2).reshape(7, 1, D)
    gains = gains.astype(BF).astype(F32)
    base = me * text_table.shape[0]
    owned = (all_ids[:, None] - base == jnp.arange(text_table.shape[0])[None, :]).astype(BF)
    last = ffn_down[1].reshape(4, rows, D).astype(BF)
    last = lax.optimization_barrier((last, text_rows))[0]
    down_units = lax.all_gather(last, AXES, axis=1, tiled=True)
    text_in = text_rows * scale_in + positions(TXT_LEN, D)
    enc_gains = [(gains, i) for i in range(3)]
    dec_gains = [(gains, i) for i in range(3, 7)]
    memory, enc_stored = layer_forward(text_in, units, 0, units, 8, enc_gains, 1, text_labels, None, None)

    image_in = image_rows.reshape(image_count, IMG_LEN, D) * scale_in + positions(IMG_LEN, D)[None]
    image_in = image_in.reshape(-1, D)
    final_out, dec_stored = layer_forward(
        image_in, units, 12, down_units, 0, dec_gains, image_count, None, memory, cross_labels
    )

    targets = codes.reshape(-1)
    logits = against(final_out, code_full)
    hit = targets[:, None] == jnp.arange(VOCAB)[None, :]
    top = jnp.max(logits, axis=1, keepdims=True)
    log_total = top + jnp.log(jnp.sum(jnp.exp(logits - top), axis=1, keepdims=True))
    weighted = jnp.sum(
        logits * jnp.where(hit, 1.0 - SMOOTH + SMOOTH / VOCAB, SMOOTH / VOCAB), axis=1, keepdims=True
    )
    loss_part = jnp.sum(log_total - weighted)
    grad_logits = (
        (jnp.exp(logits - log_total) - jnp.where(hit, 1.0 - SMOOTH, 0.0) - SMOOTH / VOCAB) * inverse
    ).astype(BF)
    grad_final = matmul(grad_logits, code_full)

    grad_image, grad_memory, dec_gain_grads, dec_parts = layer_backward(
        grad_final, units, 12, down_units, 0, dec_gains, image_count, None, dec_stored, memory, cross_labels
    )
    grad_text, _, enc_gain_grads, enc_parts = layer_backward(
        grad_memory, units, 0, units, 8, enc_gains, 1, text_labels, enc_stored, None, None
    )
    gain_part = jnp.concatenate(enc_gain_grads + dec_gain_grads)

    grad_rows = lax.all_gather((grad_text * scale_in).astype(BF), AXES, axis=0, tiled=True)
    text_grad = across(owned, grad_rows)

    grad_looked = grad_image.reshape(image_count, IMG_LEN, D)[:, 1:] * scale_in
    grad_looked = jnp.pad(grad_looked, ((0, 0), (0, 1), (0, 0))).reshape(-1, D).astype(BF)
    enc_x, enc_g = enc_parts
    dec_x, dec_g, memory_g = dec_parts
    sums = sum_products(
        dec_x, dec_g, [memory[None]] + enc_x, memory_g + enc_g, grad_logits, targets, final_out, grad_looked, 1
    )
    gain_blocks = gain_part.reshape(7, devices, rows).transpose(1, 0, 2).reshape(devices, 7 * rows)
    gain_blocks = jnp.concatenate([gain_blocks, jnp.full((devices, 1), loss_part)], axis=1)
    gain_blocks = jnp.pad(gain_blocks, ((0, 0), (0, 1024 - gain_blocks.shape[1])))
    gain_blocks = gain_blocks.reshape(devices, 8, 128)
    params = (mix_in, mix_out, ffn_up, ffn_down, norm_gains, text_table, code_table)
    firsts = (
        mix_in_first,
        mix_out_first,
        ffn_up_first,
        ffn_down_first,
        gains_first,
        text_first,
        code_first,
    )
    seconds = (
        mix_in_second,
        mix_out_second,
        ffn_up_second,
        ffn_down_second,
        gains_second,
        text_second,
        code_second,
    )
    if rows == 32:
        loss_sum, grad_norm, updated = update(sums, text_grad, gain_blocks, params, firsts, seconds, 6)
    else:
        small_sum = jnp.sum(exchange(gain_blocks, 5), axis=0).reshape(-1)
        loss_sum = small_sum[7 * rows]
        gains_grad = small_sum[: 7 * rows].reshape(7, rows)
        dec_sum, enc_sum = sums[:14], sums[14:28]
        gradients = (
            jnp.stack(
                [
                    from_column_units(part)
                    for part in (enc_sum[2:5], dec_sum[:3], jnp.concatenate([dec_sum[4:5], enc_sum[:2]]))
                ]
            ),
            jnp.stack([enc_sum[5], dec_sum[3], dec_sum[5]]),
            jnp.stack([from_hidden_units(part, devices) for part in (enc_sum[6:10], dec_sum[6:10])]),
            jnp.stack([part.reshape(-1, D) for part in (enc_sum[10:], dec_sum[10:])]),
            gains_grad,
            text_grad,
            sums[28:].reshape(D // dp_size, -1).T,
        )
        square_part = sum((jnp.sum(gradient * gradient) for gradient in gradients))
        squares = exchange(tiles(square_part[None], devices), 6)[:, 0, 0]
        grad_norm = jnp.sqrt(jnp.sum(squares))
        factor = CLIP_NORM / jnp.maximum(grad_norm, CLIP_NORM)
        updated = [
            adam_step(
                params[index],
                firsts[index],
                seconds[index],
                gradients[index] * factor,
                STEP_RATES[index],
            )
            for index in range(7)
        ]
    return (
        loss_sum,
        grad_norm,
        updated[0][0],
        updated[1][0],
        updated[2][0],
        updated[3][0],
        updated[4][0],
        updated[5][0],
        updated[6][0],
        updated[0][1],
        updated[1][1],
        updated[2][1],
        updated[3][1],
        updated[4][1],
        updated[5][1],
        updated[6][1],
        updated[0][2],
        updated[1][2],
        updated[2][2],
        updated[3][2],
        updated[4][2],
        updated[5][2],
        updated[6][2],
    )


def solution(mesh):
    return jax.shard_map(
        on_device,
        mesh=mesh,
        in_specs=(
            P(("dp", "fsdp"), None),
            P(("dp", "fsdp"), None),
            P(("dp", "fsdp"), None),
            P(("dp", "fsdp")),
            P(None, ("dp", "fsdp"), None),
            P(None, ("dp", "fsdp"), None),
            P(None, ("dp", "fsdp"), None),
            P(None, ("dp", "fsdp"), None),
            P(None, ("dp", "fsdp")),
            P(("dp", "fsdp"), None),
            P("fsdp", "dp"),
            P(None, ("dp", "fsdp"), None),
            P(None, ("dp", "fsdp"), None),
            P(None, ("dp", "fsdp"), None),
            P(None, ("dp", "fsdp"), None),
            P(None, ("dp", "fsdp")),
            P(("dp", "fsdp"), None),
            P("fsdp", "dp"),
            P(None, ("dp", "fsdp"), None),
            P(None, ("dp", "fsdp"), None),
            P(None, ("dp", "fsdp"), None),
            P(None, ("dp", "fsdp"), None),
            P(None, ("dp", "fsdp")),
            P(("dp", "fsdp"), None),
            P("fsdp", "dp"),
        ),
        out_specs=(
            P(),
            P(),
            P(None, ("dp", "fsdp"), None),
            P(None, ("dp", "fsdp"), None),
            P(None, ("dp", "fsdp"), None),
            P(None, ("dp", "fsdp"), None),
            P(None, ("dp", "fsdp")),
            P(("dp", "fsdp"), None),
            P("fsdp", "dp"),
            P(None, ("dp", "fsdp"), None),
            P(None, ("dp", "fsdp"), None),
            P(None, ("dp", "fsdp"), None),
            P(None, ("dp", "fsdp"), None),
            P(None, ("dp", "fsdp")),
            P(("dp", "fsdp"), None),
            P("fsdp", "dp"),
            P(None, ("dp", "fsdp"), None),
            P(None, ("dp", "fsdp"), None),
            P(None, ("dp", "fsdp"), None),
            P(None, ("dp", "fsdp"), None),
            P(None, ("dp", "fsdp")),
            P(("dp", "fsdp"), None),
            P("fsdp", "dp"),
        ),
        check_vma=False,
    )
```
